32 devices in a mesh: dp: 8 (over y, x, core), mp: 4 (over z).
Axes of the slice: x: 2, y: 2, z: 4, core: 2. Of those that a mesh axis runs over, the one named last changes fastest.
Arguments:
- frames: bfloat16 [18432, 768], P(('dp', 'mp')), may hold values from -6 to 6
- segment_ids: int32 [18432], P('dp'), may hold values from 0 to 255, as said below
- qkv_weight: bfloat16 [1, 3, 768, 768], P(None, None, None, 'mp'), may hold values from -0.21875 to 0.21875
- q_bias: bfloat16 [1, 768], P(None, 'mp'), may hold values from -1.5 to 1.5
- v_bias: bfloat16 [1, 768], P(None, 'mp'), may hold values from -0.14941406 to 0.14941406
- out_weight: bfloat16 [1, 768, 768], P(None, 'mp'), may hold values from -3.5 to 3.5
- out_bias: bfloat16 [1, 768], replicated, may hold values from -0.5 to 0.5
- ff_in_weight: bfloat16 [1, 768, 3072], P(None, None, 'mp'), may hold values from -0.21875 to 0.21875
- ff_in_bias: bfloat16 [1, 3072], P(None, 'mp'), may hold values from -1.5 to 1.5
- ff_out_weight: bfloat16 [1, 3072, 768], P(None, 'mp'), may hold values from -0.109375 to 0.109375
- ff_out_bias: bfloat16 [1, 768], replicated, may hold values from -0.5 to 0.5
- norm_gain: bfloat16 [1, 2, 768], replicated, may hold values from 0.5 to 1.5
- norm_shift: bfloat16 [1, 2, 768], replicated, may hold values from -0.5 to 0.5
- out_grad: bfloat16 [18432, 768], P(('dp', 'mp')), may hold values from -6 to 6
Outputs:
- block_out: float32 [18432, 768], P(('dp', 'mp'))
- frames_grad: float32 [18432, 768], P(('dp', 'mp'))
- qkv_weight_grad: float32 [1, 3, 768, 768], P(None, None, None, 'mp')
- q_bias_grad: float32 [1, 768], P(None, 'mp')
- v_bias_grad: float32 [1, 768], P(None, 'mp')
- out_weight_grad: float32 [1, 768, 768], P(None, 'mp')
- out_bias_grad: float32 [1, 768], replicated
- ff_in_weight_grad: float32 [1, 768, 3072], P(None, None, 'mp')
- ff_in_bias_grad: float32 [1, 3072], P(None, 'mp')
- ff_out_weight_grad: float32 [1, 3072, 768], P(None, 'mp')
- ff_out_bias_grad: float32 [1, 768], replicated
- norm_gain_grad: float32 [1, 2, 768], replicated
- norm_shift_grad: float32 [1, 2, 768], replicated
The draws below stay inside these ranges and needn't reach their ends.
Inputs may be any that keep to these rules, and one draw needn't show every extreme that they name: `segment_ids`: in each packed row of 2304 frames an utterance is a run of consecutive frames sharing one id, and different utterances of a row have different ids. Ids of different rows are unrelated.
All inputs are finite; a program needn't handle non-finite values.
Results may differ from the reference program's by a relative error of at most 0.014.
The reference program's roundings to bfloat16 on the way count: a program that leaves them out, or rounds other values in their place, can miss the bound.
Values may be sent and summed in bfloat16 or wider, within the bound.
A program may use at most 192 MiB of HBM per device.

```python
import jax
import jax.numpy as jnp
from jax import lax

D = 768
HEADS = 12
HEAD_DIM = 64
FF = 3072
LAYERS = 1
ROW_LEN = 2304
TOKENS = 18432


def draw_segment_ids(key, part):
    key = jax.random.fold_in(key, 7)
    row_total = TOKENS // ROW_LEN
    lead_key, span_key, head_key, tail_key = jax.random.split(key, 4)
    lead_len = jax.random.randint(lead_key, (row_total, 1), ROW_LEN // 16, ROW_LEN // 8 + 1)
    span_len = jax.random.randint(span_key, (row_total, 1), 3 * ROW_LEN // 4, 13 * ROW_LEN // 16 + 1)
    head_piece = jax.random.randint(head_key, (row_total, 1), ROW_LEN // 32, ROW_LEN // 16 + 1)
    tail_piece = jax.random.randint(tail_key, (row_total, 1), ROW_LEN // 32, ROW_LEN // 16 + 1)
    position = jnp.arange(ROW_LEN, dtype=jnp.int32)[None, :]
    head_ids = position // head_piece
    tail_ids = 201 + (position - lead_len - span_len) // tail_piece
    tail_ids = jnp.where(position >= ROW_LEN - ROW_LEN // 32, 255, tail_ids)
    utter_ids = jnp.where(position < lead_len, head_ids, jnp.where(position < lead_len + span_len, 200, tail_ids))
    return utter_ids.reshape(-1).astype(jnp.int32)


def level_of(own_key, shape, cuts, smallest, high):
    factor_of = 1.0
    for dim, blocks in cuts:
        steps = jax.random.uniform(jax.random.fold_in(jax.random.fold_in(own_key, 6), dim), (blocks,), jnp.float32, smallest / len(cuts), high / len(cuts))
        factor_of = factor_of * jnp.repeat(jnp.exp(steps), shape[dim] // blocks).reshape((-1,) + (1,) * (len(shape) - 1 - dim))
    return factor_of


def noise(own_key, extent, spread, limit, cuts=(), kind=jnp.bfloat16):
    values = spread * jax.random.normal(own_key, extent, jnp.float32)
    if cuts:
        values = values * level_of(own_key, extent, cuts, -0.22, 0.18)
    return jnp.clip(values, -limit, limit).astype(kind)


def setup_inputs(seed: int = 0) -> dict:
    arg_keys = jax.random.split(jax.random.key(seed), 15)
    frames = noise(arg_keys[0], (TOKENS, D), 1.0, 6.0, ((0, 32),))
    segment_ids = draw_segment_ids(jax.random.fold_in(arg_keys[14], 71), 0)
    qkv_weight = noise(arg_keys[2], (LAYERS, 3, D, D), D ** -0.5, 0.21875, ((3, 4),))
    q_bias = noise(arg_keys[3], (LAYERS, D), 0.3, 1.5, ((1, 4),))
    v_bias = noise(arg_keys[4], (LAYERS, D), 0.03, 0.14941406, ((1, 4),))
    out_weight = noise(arg_keys[5], (LAYERS, D, D), (max(1, D // 256)) ** -0.5, 3.5, ((1, 4),))
    out_bias = noise(arg_keys[6], (LAYERS, D), 0.1, 0.5)
    ff_in_weight = noise(arg_keys[7], (LAYERS, D, FF), D ** -0.5, 0.21875, ((2, 4),))
    ff_in_bias = noise(arg_keys[8], (LAYERS, FF), 0.3, 1.5, ((1, 4),))
    ff_out_weight = noise(arg_keys[9], (LAYERS, FF, D), FF ** -0.5, 0.109375, ((1, 4),))
    ff_out_bias = noise(arg_keys[10], (LAYERS, D), 0.1, 0.5)
    norm_gain = jnp.clip(1.0 + 0.1 * jax.random.normal(arg_keys[11], (LAYERS, 2, D), jnp.float32), 0.5, 1.5).astype(jnp.bfloat16)
    norm_shift = noise(arg_keys[12], (LAYERS, 2, D), 0.1, 0.5)
    out_grad = noise(arg_keys[13], (TOKENS, D), 1.0, 6.0, ((0, 32),))
    return {"frames": frames, "segment_ids": segment_ids, "qkv_weight": qkv_weight, "q_bias": q_bias, "v_bias": v_bias, "out_weight": out_weight, "out_bias": out_bias, "ff_in_weight": ff_in_weight, "ff_in_bias": ff_in_bias, "ff_out_weight": ff_out_weight, "ff_out_bias": ff_out_bias, "norm_gain": norm_gain, "norm_shift": norm_shift, "out_grad": out_grad}


precise = lax.Precision.HIGHEST

@jax.custom_vjp
def low(v):
    return lax.optimization_barrier(v.astype(jnp.bfloat16)).astype(jnp.float32)

@jax.custom_vjp
def low_back(v):
    return v

def low_keep(v):
    return (low(v), None)

def low_pass(kept, grad):
    return (grad,)

def back_keep(v):
    return (v, None)

def back_low(kept, grad):
    return (low(grad),)
low.defvjp(low_keep, low_pass)
low_back.defvjp(back_keep, back_low)

def matmul(left, right):
    return jnp.dot(left, right, precision=precise)

def layer_norm(inputs, norm_gain, norm_shift):
    row_mean = lax.optimization_barrier(jnp.mean(inputs, axis=-1, keepdims=True))
    centred = inputs - row_mean
    variance = lax.optimization_barrier(jnp.mean(centred * centred, axis=-1, keepdims=True))
    normed = centred * lax.rsqrt(variance + 1e-05)
    return normed * norm_gain + norm_shift

def attend(query_heads, key_heads, value_heads, seg_query, seg_keys):
    scores = jnp.einsum('bhe,khe->hbk', query_heads, key_heads, precision=precise) * HEAD_DIM ** (-0.5)
    scores = low_back(scores)
    same_utter = seg_query[:, None] == seg_keys[None, :]
    scores = jnp.where(same_utter[None], scores, -1e+30)
    row_max = lax.optimization_barrier(jnp.max(scores, axis=-1, keepdims=True))
    exponent = jnp.exp(scores - row_max)
    soft = exponent / lax.optimization_barrier(jnp.sum(exponent, axis=-1, keepdims=True))
    return jnp.einsum('hbk,khe->bhe', low(soft), value_heads, precision=precise)

def row_layer(stream, seg_row, layer_params):
    proj_weight, query_bias, value_bias, head_weight, head_bias, in_weight, in_bias, down_weight, down_bias, norm_gain, norm_shift = layer_params
    input_low = low(stream)
    projected = jnp.einsum('td,cde->cte', input_low, proj_weight, precision=precise)
    queries = low(low_back(projected[0] + query_bias))
    key_rows = low(low_back(projected[1]))
    value_rows = low(low_back(projected[2] + value_bias))
    block_len = min(768, ROW_LEN)
    block_count = ROW_LEN // block_len
    key_heads = key_rows.reshape(ROW_LEN, HEADS, HEAD_DIM)
    value_heads = value_rows.reshape(ROW_LEN, HEADS, HEAD_DIM)

    def one_block(block_in):
        return attend(block_in[0], key_heads, value_heads, block_in[1], seg_row).reshape(block_len, D)
    heads_out = lax.map(jax.checkpoint(one_block), (queries.reshape(block_count, block_len, HEADS, HEAD_DIM), seg_row.reshape(block_count, block_len)))
    heads_low = low(low_back(heads_out.reshape(ROW_LEN, D)))
    residual = stream + low_back(matmul(heads_low, head_weight) + head_bias)
    mid = layer_norm(residual, norm_gain[0], norm_shift[0])
    pre_act = low_back(matmul(low(mid), in_weight) + in_bias)
    hidden = low(jax.nn.gelu(pre_act, approximate=False))
    summed = mid + low_back(matmul(hidden, down_weight) + down_bias)
    return layer_norm(summed, norm_gain[1], norm_shift[1])

def row_layers(stream, seg_row, params):
    for which_layer in range(LAYERS):
        stream = row_layer(stream, seg_row, tuple((param[which_layer] for param in params)))
    return stream

def reference(frames, segment_ids, qkv_weight, q_bias, v_bias, out_weight, out_bias, ff_in_weight, ff_in_bias, ff_out_weight, ff_out_bias, norm_gain, norm_shift, out_grad):
    params = tuple((param.astype(jnp.float32) for param in (qkv_weight, q_bias, v_bias, out_weight, out_bias, ff_in_weight, ff_in_bias, ff_out_weight, ff_out_bias, norm_gain, norm_shift)))
    row_total = frames.shape[0] // ROW_LEN
    stream = frames.astype(jnp.float32).reshape(row_total, ROW_LEN, D)
    seg_rows = segment_ids.reshape(row_total, ROW_LEN)
    checked = jax.checkpoint(row_layers)

    def forward(stream_in, params_in):

        def step(running, packed):
            return (running, checked(packed[0], packed[1], params_in))
        return lax.scan(step, jnp.zeros((), jnp.float32), (stream_in, seg_rows))[1]
    output, pull_back = jax.vjp(forward, stream, params)
    stream_grad, param_grads = pull_back(out_grad.astype(jnp.float32).reshape(row_total, ROW_LEN, D))
    return (output.reshape(-1, D), stream_grad.reshape(-1, D), param_grads[0], param_grads[1], param_grads[2], param_grads[3], param_grads[4], param_grads[5], param_grads[6], param_grads[7], param_grads[8], param_grads[9], param_grads[10])
```

```python
from functools import partial

import jax
import jax.numpy as jnp
from jax import lax
from jax.experimental import pallas as pl
from jax.experimental.pallas import tpu as pltpu
from jax.sharding import PartitionSpec as P

HEAD_DIM = 64
ROW_LEN = 2304
TILE = 256
STEP = 2
TILES = ROW_LEN // TILE
PADDED = TILES + 1
SCALE = HEAD_DIM ** (-0.5)
MASKED = -1e30
F32 = jnp.float32
BF16 = jnp.bfloat16
VMEM_BYTES = 56 * 1024 * 1024


def dot_rows(left, right):
    return lax.dot_general(left, right, (((1,), (1,)), ((), ())), preferred_element_type=F32)


def dot_cols(left, right):
    return lax.dot_general(left, right, (((0,), (0,)), ((), ())), preferred_element_type=F32)


def dot(left, right):
    return jnp.dot(left, right, preferred_element_type=F32)


def fold_max(tile):
    return jnp.max(tile.reshape(-1, 8, tile.shape[1]), axis=0)


def fold_sum(tile):
    return jnp.sum(tile.reshape(-1, 8, tile.shape[1]), axis=0)


def tile_rows(tile):
    return pl.ds(pl.multiple_of(tile * TILE, TILE), TILE)


def attend_kernel(
    limits, seg_row, seg_col, qkv, out, out_cols, log_total, key_buf, value_buf, score_buf
):
    for head in range(qkv.shape[2] // HEAD_DIM):
        cols = slice(head * HEAD_DIM, (head + 1) * HEAD_DIM)
        key_buf[:ROW_LEN] = qkv[1, :, cols]
        key_buf[ROW_LEN:] = jnp.zeros((TILE, HEAD_DIM), BF16)
        for tile in range(TILES):
            value_buf[tile] = qkv[2, tile * TILE : (tile + 1) * TILE, cols].T
        value_buf[TILES] = jnp.zeros((HEAD_DIM, TILE), BF16)

        def query_tile(tile, _):
            rows = tile_rows(tile)
            queries = qkv[0, rows, cols] * SCALE
            seg_query = seg_row[tile]
            first, count = limits[tile, 0], limits[tile, 1]

            def score(step, peak):
                for part in range(STEP):
                    key_rows = tile_rows(first + step * STEP + part)
                    scores = dot_rows(key_buf[key_rows], queries)
                    scores = jnp.where(seg_col[key_rows] == seg_query, scores, MASKED)
                    score_buf[tile_rows(step * STEP + part)] = scores
                    peak = jnp.maximum(peak, fold_max(scores))
                return peak

            peak = lax.fori_loop(0, count, score, jnp.full((8, TILE), MASKED, F32))
            peak = jnp.max(peak, axis=0, keepdims=True)

            def mix(step, carry):
                total, mixed = carry
                for part in range(STEP):
                    soft = jnp.exp(score_buf[tile_rows(step * STEP + part)] - peak)
                    total = total + fold_sum(soft)
                    mixed = mixed + dot(value_buf[first + step * STEP + part], soft.astype(BF16))
                return total, mixed

            total, mixed = lax.fori_loop(
                0,
                count,
                mix,
                (jnp.zeros((8, TILE), F32), jnp.zeros((HEAD_DIM, TILE), F32)),
            )
            total = jnp.sum(total, axis=0, keepdims=True)
            mixed = mixed / total
            out_cols[head, tile] = mixed
            log_total[head, tile] = peak + jnp.log(total)
            out[rows, cols] = mixed.T.astype(BF16)
            return 0

        lax.fori_loop(0, TILES, query_tile, 0)


def attend_back_kernel(
    head,
    limits,
    seg_row,
    seg_col,
    qkv,
    out_cols,
    log_total,
    heads_grad,
    qkv_grad,
    key_buf,
    key_cols,
    value_buf,
    key_sum,
    value_sum,
):
    cols = slice(head * HEAD_DIM, (head + 1) * HEAD_DIM)
    key_buf[:ROW_LEN] = qkv[1, :, cols]
    key_buf[ROW_LEN:] = jnp.zeros((TILE, HEAD_DIM), BF16)
    value_buf[:ROW_LEN] = qkv[2, :, cols]
    value_buf[ROW_LEN:] = jnp.zeros((TILE, HEAD_DIM), BF16)
    for tile in range(TILES):
        key_cols[tile] = qkv[1, tile * TILE : (tile + 1) * TILE, cols].T
    key_cols[TILES] = jnp.zeros((HEAD_DIM, TILE), BF16)
    key_sum[...] = jnp.zeros_like(key_sum)
    value_sum[...] = jnp.zeros_like(value_sum)

    def query_tile(tile, _):
        rows = tile_rows(tile)
        queries = qkv[0, rows, cols] * SCALE
        grads = heads_grad[rows, cols]
        seg_query = seg_row[tile]
        logs = log_total[head, tile]
        grad_cols = grads.astype(F32).T
        row_dot = jnp.sum(grad_cols * out_cols[head, tile], axis=0, keepdims=True)
        first, count = limits[tile, 0], limits[tile, 1]

        def step_back(step, query_grad):
            for part in range(STEP):
                key_tile = first + step * STEP + part
                key_rows = tile_rows(key_tile)
                scores = dot_rows(key_buf[key_rows], queries)
                same = seg_col[key_rows] == seg_query
                soft = jnp.exp(jnp.where(same, scores - logs, MASKED))
                soft_grad = dot_rows(value_buf[key_rows], grads)
                score_grad = (soft * (soft_grad - row_dot)).astype(BF16)
                value_sum[key_rows] += dot(soft.astype(BF16), grads)
                key_sum[key_rows] += dot(score_grad, queries)
                query_grad = query_grad + dot(key_cols[key_tile], score_grad)
            return query_grad

        query_grad = lax.fori_loop(0, count, step_back, jnp.zeros((HEAD_DIM, TILE), F32))
        qkv_grad[rows, 0:HEAD_DIM] = (query_grad * SCALE).T.astype(BF16)
        return 0

    lax.fori_loop(0, TILES, query_tile, 0)
    qkv_grad[:, HEAD_DIM : 2 * HEAD_DIM] = key_sum[:ROW_LEN].astype(BF16)
    qkv_grad[:, 2 * HEAD_DIM : 3 * HEAD_DIM] = value_sum[:ROW_LEN].astype(BF16)


def tile_limits(segments):
    places = jnp.arange(ROW_LEN, dtype=jnp.int32)
    first_ids = segments[::TILE]
    last_ids = segments[TILE - 1 :: TILE]
    low = jnp.min(jnp.where(segments[None] == first_ids[:, None], places[None], ROW_LEN), axis=1)
    high = jnp.max(jnp.where(segments[None] == last_ids[:, None], places[None], -1), axis=1) + 1
    first = low // TILE
    count = (-(-high // TILE) - first + STEP - 1) // STEP
    first = jnp.minimum(first, PADDED - STEP * count)
    return jnp.stack([first, count], axis=1)


def whole(memory_space=pltpu.VMEM):
    return pl.BlockSpec(memory_space=memory_space)


def attend(limits, seg_row, seg_col, qkv_low):
    head_total = qkv_low.shape[2] // HEAD_DIM
    return pl.pallas_call(
        attend_kernel,
        out_shape=(
            jax.ShapeDtypeStruct(qkv_low.shape[1:], BF16),
            jax.ShapeDtypeStruct((head_total, TILES, HEAD_DIM, TILE), F32),
            jax.ShapeDtypeStruct((head_total, TILES, 1, TILE), F32),
        ),
        in_specs=[whole(pltpu.SMEM), whole(), whole(), whole()],
        out_specs=(whole(), whole(), whole()),
        scratch_shapes=[
            pltpu.VMEM((PADDED * TILE, HEAD_DIM), BF16),
            pltpu.VMEM((PADDED, HEAD_DIM, TILE), BF16),
            pltpu.VMEM((PADDED * TILE, TILE), F32),
        ],
        compiler_params=pltpu.CompilerParams(vmem_limit_bytes=VMEM_BYTES),
        cost_estimate=pl.CostEstimate(
            flops=16 * head_total * ROW_LEN * ROW_LEN * HEAD_DIM,
            bytes_accessed=8 * ROW_LEN * 256 * 3,
            transcendentals=head_total * ROW_LEN * ROW_LEN,
        ),
        name="attend",
    )(limits, seg_row, seg_col, qkv_low)


def attend_back(head, limits, seg_row, seg_col, qkv_low, out_cols, log_total, heads_grad):
    return pl.pallas_call(
        partial(attend_back_kernel, head),
        out_shape=jax.ShapeDtypeStruct((ROW_LEN, 3 * HEAD_DIM), BF16),
        in_specs=[whole(pltpu.SMEM)] + [whole()] * 6,
        out_specs=whole(),
        scratch_shapes=[
            pltpu.VMEM((PADDED * TILE, HEAD_DIM), BF16),
            pltpu.VMEM((PADDED, HEAD_DIM, TILE), BF16),
            pltpu.VMEM((PADDED * TILE, HEAD_DIM), BF16),
            pltpu.VMEM((PADDED * TILE, HEAD_DIM), F32),
            pltpu.VMEM((PADDED * TILE, HEAD_DIM), F32),
        ],
        compiler_params=pltpu.CompilerParams(vmem_limit_bytes=VMEM_BYTES),
        cost_estimate=pl.CostEstimate(
            flops=40 * ROW_LEN * ROW_LEN * HEAD_DIM,
            bytes_accessed=8 * ROW_LEN * 256 * 3,
            transcendentals=ROW_LEN * ROW_LEN,
        ),
        name="attend_back_" + str(head),
    )(limits, seg_row, seg_col, qkv_low, out_cols, log_total, heads_grad)


def norm_rows(inputs, norm_gain, norm_shift):
    row_mean = jnp.mean(inputs, axis=-1, keepdims=True)
    centred = inputs - row_mean
    variance = jnp.mean(centred * centred, axis=-1, keepdims=True)
    inv_std = lax.rsqrt(variance + 1e-05)
    normed = centred * inv_std
    return (normed * norm_gain + norm_shift, normed, inv_std)


def norm_back(cotangent, normed, inv_std, norm_gain):
    scaled = cotangent * norm_gain
    adjusted = (
        scaled
        - jnp.mean(scaled, axis=-1, keepdims=True)
        - normed * jnp.mean(scaled * normed, axis=-1, keepdims=True)
    )
    return (adjusted * inv_std, jnp.sum(cotangent * normed, axis=0), jnp.sum(cotangent, axis=0))


def ring_perm(size, offset):
    return [(place, (place + offset) % size) for place in range(size)]


def exchange(pieces):
    size = lax.axis_size("mp")
    me = lax.axis_index("mp")
    own = lax.dynamic_index_in_dim(pieces, me, 0, keepdims=True)
    gathered = lax.dynamic_update_slice_in_dim(pieces, own, me, 0)
    for offset in range(1, size):
        piece = lax.dynamic_index_in_dim(pieces, (me + offset) % size, 0, keepdims=True)
        arrived = lax.ppermute(piece, "mp", ring_perm(size, offset))
        gathered = lax.dynamic_update_slice_in_dim(
            gathered, arrived, (me + size - offset) % size, 0
        )
    return gathered


def dp_groups():
    total = lax.axis_size("dp")
    size = min(8, total)
    groups = [list(range(start, start + size)) for start in range(0, total, size)]
    return (size, groups)


def on_device(
    frames,
    segment_ids,
    qkv_weight,
    q_bias,
    v_bias,
    out_weight,
    out_bias,
    ff_in_weight,
    ff_in_bias,
    ff_out_weight,
    ff_out_bias,
    norm_gain,
    norm_shift,
    out_grad,
):
    local_rows, width = frames.shape
    mp_size = lax.axis_size("mp")
    group, groups = dp_groups()
    place = lax.axis_index("dp") % group
    head_cols = qkv_weight.shape[3]
    head_total = head_cols // HEAD_DIM
    units = ff_in_weight.shape[2]

    input_all = lax.all_gather(frames, "mp", axis=0, tiled=True)
    qkv_rows = (
        qkv_weight[0].reshape(3, width, head_total, HEAD_DIM).transpose(2, 0, 3, 1)
    ).reshape(-1, width)
    packed = jnp.concatenate([out_weight[0], ff_in_weight[0].T, ff_out_weight[0], qkv_rows])
    share = packed.shape[0] // group
    part = lax.dynamic_slice_in_dim(packed, place * share, share, 0)
    part = lax.all_gather(part, "mp", axis=0)
    parts = lax.all_gather(part, "dp", axis=0, axis_index_groups=groups)
    packed_all = parts.transpose(1, 0, 2, 3).reshape(mp_size, packed.shape[0], width)
    ends = [0, head_cols, head_cols + units, head_cols + 2 * units, packed.shape[0]]
    out_all, in_rows, down_all, qkv_all = (
        packed_all[:, ends[at] : ends[at + 1]].reshape(-1, width) for at in range(4)
    )

    seg_row = segment_ids.reshape(TILES, 1, TILE)
    seg_col = jnp.pad(segment_ids, (0, TILE), constant_values=-1)[:, None]
    limits = tile_limits(segment_ids)
    projected = jnp.einsum("td,cde->cte", input_all, qkv_weight[0], preferred_element_type=F32)
    bias_rows = jnp.stack([q_bias[0], jnp.zeros_like(q_bias[0]), v_bias[0]]).astype(F32)
    qkv_low = (projected + bias_rows[:, None, :]).astype(BF16)
    heads_out, out_cols, log_total = attend(limits, seg_row, seg_col, qkv_low)
    heads_low = exchange(heads_out.reshape(mp_size, local_rows, head_cols))
    heads_low = heads_low.transpose(1, 0, 2).reshape(local_rows, width)

    gains = norm_gain[0].astype(F32)
    shifts = norm_shift[0].astype(F32)
    residual = frames.astype(F32) + (dot(heads_low, out_all) + out_bias[0].astype(F32))
    mid, normed_mid, inv_std_mid = norm_rows(residual, gains[0], shifts[0])
    mid_low = mid.astype(BF16)
    in_bias_all = lax.all_gather(ff_in_bias[0], "mp", axis=0, tiled=True).astype(F32)
    pre_act = dot_rows(mid_low, in_rows) + in_bias_all
    unit_cdf = 0.5 * (1.0 + lax.erf(pre_act * 0.5**0.5))
    hidden = (pre_act * unit_cdf).astype(BF16)
    slope = unit_cdf + pre_act * jnp.exp(-0.5 * pre_act * pre_act) * (2.0 * jnp.pi) ** (-0.5)
    summed = mid + (dot(hidden, down_all) + ff_out_bias[0].astype(F32))
    block_out, normed_out, inv_std_out = norm_rows(summed, gains[1], shifts[1])

    sum_grad, gain_out_grad, shift_out_grad = norm_back(
        out_grad.astype(F32), normed_out, inv_std_out, gains[1]
    )
    ffn_grad_low = sum_grad.astype(BF16)
    down_bias_grad = jnp.sum(ffn_grad_low, axis=0, dtype=F32)
    pre_grad_low = (dot_rows(ffn_grad_low, down_all) * slope).astype(BF16)
    in_bias_grad = jnp.sum(pre_grad_low, axis=0, dtype=F32)
    mid_grad = sum_grad + dot(pre_grad_low, in_rows)
    resid_grad, gain_mid_grad, shift_mid_grad = norm_back(
        mid_grad, normed_mid, inv_std_mid, gains[0]
    )
    attn_grad_low = resid_grad.astype(BF16)
    head_bias_grad = jnp.sum(attn_grad_low, axis=0, dtype=F32)
    heads_grad_low = dot_rows(attn_grad_low, out_all).astype(BF16)
    heads_grad = exchange(
        heads_grad_low.reshape(local_rows, mp_size, head_cols).transpose(1, 0, 2)
    ).reshape(-1, head_cols)

    grad_rows = jnp.concatenate(
        [
            dot_cols(heads_low, attn_grad_low).astype(BF16).reshape(mp_size, head_cols, width),
            dot_cols(pre_grad_low, mid_low).astype(BF16).reshape(mp_size, units, width),
            dot_cols(hidden, ffn_grad_low).astype(BF16).reshape(mp_size, units, width),
        ],
        axis=1,
    )
    grad_rows = grad_rows.reshape(mp_size * lax.axis_size("dp"), -1, width)
    grad_sum = lax.psum_scatter(grad_rows, ("mp", "dp"), scatter_dimension=0, tiled=False)
    grad_sum = lax.all_gather(
        grad_sum, "dp", axis=0, tiled=True
    ).astype(F32)
    out_weight_grad = grad_sum[: ends[1]][None]
    in_weight_grad = grad_sum[ends[1] : ends[2]].T[None]
    down_weight_grad = grad_sum[ends[2] : ends[3]][None]

    stream_grad = resid_grad
    weight_sums = []
    bias_sums = []
    qkv_blocks = qkv_all.reshape(mp_size, head_total, 3 * HEAD_DIM, width)
    for head in range(head_total):
        qkv_grad = attend_back(
            head, limits, seg_row, seg_col, qkv_low, out_cols, log_total, heads_grad
        )
        arrived = exchange(qkv_grad.reshape(mp_size, local_rows, 3 * HEAD_DIM))
        for source in range(mp_size):
            stream_grad = stream_grad + dot(arrived[source], qkv_blocks[source, head])
        weight_sums.append(dot_cols(input_all, qkv_grad))
        bias_sums.append(jnp.sum(qkv_grad, axis=0, dtype=F32))
    weight_sums = lax.psum(jnp.stack(weight_sums).astype(BF16), "dp").astype(F32)
    qkv_weight_grad = (
        weight_sums.reshape(head_total, width, 3, HEAD_DIM)
        .transpose(2, 1, 0, 3)
        .reshape(1, 3, width, head_cols)
    )
    bias_sums = lax.psum(jnp.stack(bias_sums), "dp").reshape(head_total, 3, HEAD_DIM)
    query_bias_grad = bias_sums[:, 0].reshape(1, head_cols)
    value_bias_grad = bias_sums[:, 2].reshape(1, head_cols)

    gain_grad, shift_grad, head_bias_grad, down_bias_grad, in_bias_grad = lax.psum(
        (
            jnp.stack([gain_mid_grad, gain_out_grad])[None],
            jnp.stack([shift_mid_grad, shift_out_grad])[None],
            head_bias_grad[None],
            down_bias_grad[None],
            in_bias_grad,
        ),
        ("dp", "mp"),
    )
    in_bias_grad = lax.dynamic_slice_in_dim(
        in_bias_grad, lax.axis_index("mp") * units, units, 0
    )[None]
    return (
        block_out,
        stream_grad,
        qkv_weight_grad,
        query_bias_grad,
        value_bias_grad,
        out_weight_grad,
        head_bias_grad,
        in_weight_grad,
        in_bias_grad,
        down_weight_grad,
        down_bias_grad,
        gain_grad,
        shift_grad,
    )


def solution(mesh):
    return jax.shard_map(
        on_device,
        mesh=mesh,
        in_specs=(
            P(("dp", "mp"), None),
            P("dp"),
            P(None, None, None, "mp"),
            P(None, "mp"),
            P(None, "mp"),
            P(None, "mp", None),
            P(),
            P(None, None, "mp"),
            P(None, "mp"),
            P(None, "mp", None),
            P(),
            P(),
            P(),
            P(("dp", "mp"), None),
        ),
        out_specs=(
            P(("dp", "mp"), None),
            P(("dp", "mp"), None),
            P(None, None, None, "mp"),
            P(None, "mp"),
            P(None, "mp"),
            P(None, "mp", None),
            P(),
            P(None, None, "mp"),
            P(None, "mp"),
            P(None, "mp", None),
            P(),
            P(),
            P(),
        ),
        check_vma=False,
    )
```

```python
from functools import partial

import jax
import jax.numpy as jnp
from jax import lax
from jax.experimental import pallas as pl
from jax.experimental.pallas import tpu as pltpu
from jax.sharding import PartitionSpec as P

HEAD_DIM = 64
ROW_LEN = 2304
TILE = 256
STEP = 2
TILES = ROW_LEN // TILE
PADDED = TILES + 1
BACK_STEP = 3
EXTRA = 16
SCALE = HEAD_DIM ** (-0.5)
MASKED = -1e30
F32 = jnp.float32
BF16 = jnp.bfloat16
VMEM_BYTES = 56 * 1024 * 1024


def dot_rows(left, right):
    return lax.dot_general(left, right, (((1,), (1,)), ((), ())), preferred_element_type=F32)


def dot_cols(left, right):
    return lax.dot_general(left, right, (((0,), (0,)), ((), ())), preferred_element_type=F32)


def dot(left, right):
    return jnp.dot(left, right, preferred_element_type=F32)


def tile_rows(tile):
    return pl.ds(pl.multiple_of(tile * TILE, TILE), TILE)


def as_pieces(row):
    high = row.astype(BF16).astype(F32)
    middle = (row - high).astype(BF16).astype(F32)
    last = row - high - middle
    place = lax.broadcasted_iota(jnp.int32, (EXTRA, row.shape[1]), 0)
    pieces = jnp.where(place == 0, high, jnp.where(place == 1, middle, jnp.where(place == 2, last, 0.0)))
    return pieces.astype(BF16)


def ones_columns(rows):
    place = lax.broadcasted_iota(jnp.int32, (rows, EXTRA), 1)
    return jnp.where(place < 3, 1.0, 0.0).astype(BF16)


def same_utter(seg_keys, seg_query):
    return jnp.concatenate([seg_keys] * (TILE // 128), axis=1) == seg_query


def attend_kernel(
    limits, seg_row, seg_col, qkv, out, out_cols, log_total, key_buf, value_buf, peak_buf
):
    head_total = qkv.shape[2] // HEAD_DIM
    key_peak = []
    for head in range(head_total):
        cols = slice(head * HEAD_DIM, (head + 1) * HEAD_DIM)
        key_buf[head, :ROW_LEN, :HEAD_DIM] = qkv[1, :, cols]
        key_buf[head, ROW_LEN:, :HEAD_DIM] = jnp.zeros((TILE, HEAD_DIM), BF16)
        key_buf[head, :, HEAD_DIM:] = ones_columns(PADDED * TILE)
        peak = jnp.zeros((1, TILE), F32)
        for tile in range(TILES):
            rows = slice(tile * TILE, (tile + 1) * TILE)
            value_buf[head, tile, :HEAD_DIM] = qkv[2, rows, cols].T
            keys = qkv[1, rows, cols].astype(F32).T
            peak = jnp.maximum(peak, jnp.sum(keys * keys, axis=0, keepdims=True))
        value_buf[head, TILES, :HEAD_DIM] = jnp.zeros((HEAD_DIM, TILE), BF16)
        place = lax.broadcasted_iota(jnp.int32, (EXTRA, TILE), 0)
        for tile in range(PADDED):
            value_buf[head, tile, HEAD_DIM:] = jnp.where(place == 0, 1.0, 0.0).astype(BF16)
        key_peak.append(jnp.max(peak, axis=1, keepdims=True))

    def query_tile(tile, _):
        rows = tile_rows(tile)
        seg_query = seg_row[tile]
        first, count = limits[tile, 0], limits[tile, 1]
        query_cols = []
        bounds = []
        for head in range(head_total):
            cols = slice(head * HEAD_DIM, (head + 1) * HEAD_DIM)
            queries = qkv[0, rows, cols].astype(F32).T * SCALE
            length = jnp.sum(queries * queries, axis=0, keepdims=True)
            bound = jnp.sqrt(length * key_peak[head]).astype(BF16).astype(F32)
            bounds.append(bound)
            query_cols.append(jnp.concatenate([queries.astype(BF16), as_pieces(-bound)], axis=0))

        def scores_of(head, step):
            key_rows = pl.ds(pl.multiple_of((first + step * STEP) * TILE, TILE), STEP * TILE)
            same = same_utter(seg_col[key_rows], seg_query)
            scores = dot(key_buf[head, key_rows], query_cols[head])
            return jnp.where(same, scores, MASKED)

        def mixed_in(head, step, soft):
            soft_low = soft.astype(BF16)
            gained = 0.0
            for part in range(STEP):
                values = value_buf[head, first + step * STEP + part]
                gained = gained + dot(values, soft_low[part * TILE : (part + 1) * TILE])
            return gained

        def mix(step, carry):
            return tuple(
                mixed + mixed_in(head, step, jnp.exp(scores_of(head, step)))
                for head, mixed in enumerate(carry)
            )

        empty = tuple(jnp.zeros((HEAD_DIM + EXTRA, TILE), F32) for _ in range(head_total))
        gathered = lax.fori_loop(0, count, mix, empty)
        for head in range(head_total):
            cols = slice(head * HEAD_DIM, (head + 1) * HEAD_DIM)

            def store(mixed, shift):
                total = mixed[HEAD_DIM : HEAD_DIM + 1]
                mixed = mixed[:HEAD_DIM] / total
                out_cols[head, tile] = mixed
                log_total[head, tile] = shift + jnp.log(total)
                out[rows, cols] = mixed.T.astype(BF16)

            store(gathered[head], bounds[head])

            @pl.when(jnp.min(gathered[head][HEAD_DIM : HEAD_DIM + 1]) < 2.0**-64)
            def _():
                def top(step, peak):
                    scores = scores_of(head, step)
                    return jnp.maximum(peak, jnp.max(scores, axis=0, keepdims=True))

                peak_buf[...] = lax.fori_loop(0, count, top, jnp.full((1, TILE), MASKED, F32))

                def mix_again(step, mixed):
                    soft = jnp.exp(scores_of(head, step) - peak_buf[...])
                    return mixed + mixed_in(head, step, soft)

                mixed = lax.fori_loop(0, count, mix_again, empty[0])
                store(mixed, bounds[head] + peak_buf[...])

        return 0

    lax.fori_loop(0, TILES, query_tile, 0)


def attend_back_kernel(
    head,
    seg_row,
    seg_col,
    qkv,
    out_cols,
    log_total,
    heads_grad,
    qkv_grad,
    key_buf,
    key_cols,
    value_buf,
    key_sum,
    value_sum,
):
    cols = slice(head * HEAD_DIM, (head + 1) * HEAD_DIM)
    key_buf[:, :HEAD_DIM] = qkv[1, :, cols]
    key_buf[:, HEAD_DIM:] = ones_columns(ROW_LEN)
    value_buf[:, :HEAD_DIM] = qkv[2, :, cols]
    value_buf[:, HEAD_DIM:] = ones_columns(ROW_LEN)
    for tile in range(TILES):
        key_cols[tile] = qkv[1, tile * TILE : (tile + 1) * TILE, cols].T
    key_sum[...] = jnp.zeros_like(key_sum)
    value_sum[...] = jnp.zeros_like(value_sum)

    def query_tile(tile, _):
        rows = tile_rows(tile)
        queries = qkv[0, rows, cols] * SCALE
        grads = heads_grad[rows, cols]
        seg_query = seg_row[tile]
        grad_cols = grads.astype(F32).T
        row_dot = jnp.sum(grad_cols * out_cols[head, tile], axis=0, keepdims=True)
        grad_cols = jnp.concatenate([grad_cols.astype(BF16), as_pieces(-row_dot)], axis=0)
        query_cols = jnp.concatenate(
            [queries.astype(F32).T.astype(BF16), as_pieces(-log_total[head, tile])], axis=0
        )

        def step_back(step, query_grad):
            key_rows = pl.ds(pl.multiple_of(step * BACK_STEP * TILE, TILE), BACK_STEP * TILE)
            same = same_utter(seg_col[key_rows], seg_query)
            scores = dot(key_buf[key_rows], query_cols)
            soft = jnp.exp(jnp.where(same, scores, MASKED))
            soft_grad = dot(value_buf[key_rows], grad_cols)
            score_grad = (soft * soft_grad).astype(BF16)
            value_sum[key_rows] += dot(soft.astype(BF16), grads)
            key_sum[key_rows] += dot(score_grad, queries)
            for part in range(BACK_STEP):
                piece = score_grad[part * TILE : (part + 1) * TILE]
                query_grad = query_grad + dot(key_cols[step * BACK_STEP + part], piece)
            return query_grad

        query_grad = lax.fori_loop(
            0, TILES // BACK_STEP, step_back, jnp.zeros((HEAD_DIM, TILE), F32)
        )
        qkv_grad[rows, 0:HEAD_DIM] = (query_grad * SCALE).T.astype(BF16)
        return 0

    lax.fori_loop(0, TILES, query_tile, 0)
    qkv_grad[:, HEAD_DIM : 2 * HEAD_DIM] = key_sum[...].astype(BF16)
    qkv_grad[:, 2 * HEAD_DIM : 3 * HEAD_DIM] = value_sum[...].astype(BF16)


def tile_limits(segments):
    places = jnp.arange(ROW_LEN, dtype=jnp.int32)
    first_ids = segments[::TILE]
    last_ids = segments[TILE - 1 :: TILE]
    low = jnp.min(jnp.where(segments[None] == first_ids[:, None], places[None], ROW_LEN), axis=1)
    high = jnp.max(jnp.where(segments[None] == last_ids[:, None], places[None], -1), axis=1) + 1
    first = low // TILE
    count = (-(-high // TILE) - first + STEP - 1) // STEP
    first = jnp.minimum(first, PADDED - STEP * count)
    return jnp.stack([first, count], axis=1)


def whole(memory_space=pltpu.VMEM):
    return pl.BlockSpec(memory_space=memory_space)


def attend(limits, seg_row, seg_col, qkv_low):
    head_total = qkv_low.shape[2] // HEAD_DIM
    return pl.pallas_call(
        attend_kernel,
        out_shape=(
            jax.ShapeDtypeStruct(qkv_low.shape[1:], BF16),
            jax.ShapeDtypeStruct((head_total, TILES, HEAD_DIM, TILE), F32),
            jax.ShapeDtypeStruct((head_total, TILES, 1, TILE), F32),
        ),
        in_specs=[whole(pltpu.SMEM), whole(), whole(), whole()],
        out_specs=(whole(), whole(), whole()),
        scratch_shapes=[
            pltpu.VMEM((head_total, PADDED * TILE, HEAD_DIM + EXTRA), BF16),
            pltpu.VMEM((head_total, PADDED, HEAD_DIM + EXTRA, TILE), BF16),
            pltpu.VMEM((1, TILE), F32),
        ],
        compiler_params=pltpu.CompilerParams(vmem_limit_bytes=VMEM_BYTES),
        cost_estimate=pl.CostEstimate(
            flops=16 * head_total * ROW_LEN * ROW_LEN * HEAD_DIM,
            bytes_accessed=8 * ROW_LEN * 256 * 3,
            transcendentals=head_total * ROW_LEN * ROW_LEN,
        ),
        name="attend",
    )(limits, seg_row, seg_col, qkv_low)


def attend_back(head, seg_row, seg_col, qkv_low, out_cols, log_total, heads_grad):
    return pl.pallas_call(
        partial(attend_back_kernel, head),
        out_shape=jax.ShapeDtypeStruct((ROW_LEN, 3 * HEAD_DIM), BF16),
        in_specs=[whole()] * 6,
        out_specs=whole(),
        scratch_shapes=[
            pltpu.VMEM((ROW_LEN, HEAD_DIM + EXTRA), BF16),
            pltpu.VMEM((TILES, HEAD_DIM, TILE), BF16),
            pltpu.VMEM((ROW_LEN, HEAD_DIM + EXTRA), BF16),
            pltpu.VMEM((ROW_LEN, HEAD_DIM), F32),
            pltpu.VMEM((ROW_LEN, HEAD_DIM), F32),
        ],
        compiler_params=pltpu.CompilerParams(vmem_limit_bytes=VMEM_BYTES),
        cost_estimate=pl.CostEstimate(
            flops=40 * ROW_LEN * ROW_LEN * HEAD_DIM,
            bytes_accessed=8 * ROW_LEN * 256 * 3,
            transcendentals=ROW_LEN * ROW_LEN,
        ),
        name="attend_back_" + str(head),
    )(seg_row, seg_col, qkv_low, out_cols, log_total, heads_grad)


def norm_rows(inputs, norm_gain, norm_shift):
    row_mean = jnp.mean(inputs, axis=-1, keepdims=True)
    centred = inputs - row_mean
    variance = jnp.mean(centred * centred, axis=-1, keepdims=True)
    inv_std = lax.rsqrt(variance + 1e-05)
    normed = centred * inv_std
    return (normed * norm_gain + norm_shift, normed, inv_std)


def norm_back(cotangent, normed, inv_std, norm_gain):
    scaled = cotangent * norm_gain
    adjusted = (
        scaled
        - jnp.mean(scaled, axis=-1, keepdims=True)
        - normed * jnp.mean(scaled * normed, axis=-1, keepdims=True)
    )
    return (adjusted * inv_std, jnp.sum(cotangent * normed, axis=0), jnp.sum(cotangent, axis=0))


def ring_perm(size, offset):
    return [(place, (place + offset) % size) for place in range(size)]


def exchange(pieces):
    size = lax.axis_size("mp")
    me = lax.axis_index("mp")
    own = lax.dynamic_index_in_dim(pieces, me, 0, keepdims=True)
    gathered = lax.dynamic_update_slice_in_dim(pieces, own, me, 0)
    for offset in range(1, size):
        piece = lax.dynamic_index_in_dim(pieces, (me + offset) % size, 0, keepdims=True)
        arrived = lax.ppermute(piece, "mp", ring_perm(size, offset))
        gathered = lax.dynamic_update_slice_in_dim(
            gathered, arrived, (me + size - offset) % size, 0
        )
    return gathered


def dp_groups():
    total = lax.axis_size("dp")
    size = min(8, total)
    groups = [list(range(start, start + size)) for start in range(0, total, size)]
    return (size, groups)


def on_device(
    frames,
    segment_ids,
    qkv_weight,
    q_bias,
    v_bias,
    out_weight,
    out_bias,
    ff_in_weight,
    ff_in_bias,
    ff_out_weight,
    ff_out_bias,
    norm_gain,
    norm_shift,
    out_grad,
):
    local_rows, width = frames.shape
    mp_size = lax.axis_size("mp")
    group, groups = dp_groups()
    place = lax.axis_index("dp") % group
    head_cols = qkv_weight.shape[3]
    head_total = head_cols // HEAD_DIM
    units = ff_in_weight.shape[2]

    input_all = lax.all_gather(frames, "mp", axis=0, tiled=True)
    qkv_rows = (
        qkv_weight[0].reshape(3, width, head_total, HEAD_DIM).transpose(2, 0, 3, 1)
    ).reshape(-1, width)
    packed = jnp.concatenate([out_weight[0], ff_in_weight[0].T, ff_out_weight[0], qkv_rows])
    share = packed.shape[0] // group
    part = lax.dynamic_slice_in_dim(packed, place * share, share, 0)
    part = lax.all_gather(part, "mp", axis=0)
    parts = lax.all_gather(part, "dp", axis=0, axis_index_groups=groups)
    packed_all = parts.transpose(1, 0, 2, 3).reshape(mp_size, packed.shape[0], width)
    ends = [0, head_cols, head_cols + units, head_cols + 2 * units, packed.shape[0]]
    out_all, in_rows, down_all, qkv_all = (
        packed_all[:, ends[at] : ends[at + 1]].reshape(-1, width) for at in range(4)
    )

    seg_row = segment_ids.reshape(TILES, 1, TILE)
    seg_col = jnp.pad(segment_ids, (0, TILE), constant_values=-1)[:, None]
    seg_col = jnp.broadcast_to(seg_col, (seg_col.shape[0], 128))
    limits = tile_limits(segment_ids)
    projected = jnp.einsum("td,cde->cte", input_all, qkv_weight[0], preferred_element_type=F32)
    bias_rows = jnp.stack([q_bias[0], jnp.zeros_like(q_bias[0]), v_bias[0]]).astype(F32)
    qkv_low = (projected + bias_rows[:, None, :]).astype(BF16)
    heads_out, out_cols, log_total = attend(limits, seg_row, seg_col, qkv_low)
    heads_low = exchange(heads_out.reshape(mp_size, local_rows, head_cols))
    heads_low = heads_low.transpose(1, 0, 2).reshape(local_rows, width)

    gains = norm_gain[0].astype(F32)
    shifts = norm_shift[0].astype(F32)
    residual = frames.astype(F32) + (dot(heads_low, out_all) + out_bias[0].astype(F32))
    mid, normed_mid, inv_std_mid = norm_rows(residual, gains[0], shifts[0])
    mid_low = mid.astype(BF16)
    in_bias_all = lax.all_gather(ff_in_bias[0], "mp", axis=0, tiled=True).astype(F32)
    pre_act = dot_rows(mid_low, in_rows) + in_bias_all
    unit_cdf = 0.5 * (1.0 + lax.erf(pre_act * 0.5**0.5))
    hidden = (pre_act * unit_cdf).astype(BF16)
    slope = unit_cdf + pre_act * jnp.exp(-0.5 * pre_act * pre_act) * (2.0 * jnp.pi) ** (-0.5)
    summed = mid + (dot(hidden, down_all) + ff_out_bias[0].astype(F32))
    block_out, normed_out, inv_std_out = norm_rows(summed, gains[1], shifts[1])

    sum_grad, gain_out_grad, shift_out_grad = norm_back(
        out_grad.astype(F32), normed_out, inv_std_out, gains[1]
    )
    ffn_grad_low = sum_grad.astype(BF16)
    down_bias_grad = jnp.sum(ffn_grad_low, axis=0, dtype=F32)
    pre_grad_low = (dot_rows(ffn_grad_low, down_all) * slope).astype(BF16)
    in_bias_grad = jnp.sum(pre_grad_low, axis=0, dtype=F32)
    mid_grad = sum_grad + dot(pre_grad_low, in_rows)
    resid_grad, gain_mid_grad, shift_mid_grad = norm_back(
        mid_grad, normed_mid, inv_std_mid, gains[0]
    )
    attn_grad_low = resid_grad.astype(BF16)
    head_bias_grad = jnp.sum(attn_grad_low, axis=0, dtype=F32)
    heads_grad_low = dot_rows(attn_grad_low, out_all).astype(BF16)
    heads_grad = exchange(
        heads_grad_low.reshape(local_rows, mp_size, head_cols).transpose(1, 0, 2)
    ).reshape(-1, head_cols)

    grad_rows = jnp.concatenate(
        [
            dot_cols(heads_low, attn_grad_low).astype(BF16).reshape(mp_size, head_cols, width),
            dot_cols(pre_grad_low, mid_low).astype(BF16).reshape(mp_size, units, width),
            dot_cols(hidden, ffn_grad_low).astype(BF16).reshape(mp_size, units, width),
        ],
        axis=1,
    )
    grad_rows = grad_rows.reshape(mp_size * lax.axis_size("dp"), -1, width)
    grad_sum = lax.psum_scatter(grad_rows, ("mp", "dp"), scatter_dimension=0, tiled=False)
    grad_sum = lax.all_gather(
        grad_sum, "dp", axis=0, tiled=True
    ).astype(F32)
    out_weight_grad = grad_sum[: ends[1]][None]
    in_weight_grad = grad_sum[ends[1] : ends[2]].T[None]
    down_weight_grad = grad_sum[ends[2] : ends[3]][None]

    stream_grad = resid_grad
    weight_sums = []
    bias_sums = []
    qkv_blocks = qkv_all.reshape(mp_size, head_total, 3 * HEAD_DIM, width)
    for head in range(head_total):
        qkv_grad = attend_back(
            head, seg_row, seg_col, qkv_low, out_cols, log_total, heads_grad
        )
        arrived = exchange(qkv_grad.reshape(mp_size, local_rows, 3 * HEAD_DIM))
        for source in range(mp_size):
            stream_grad = stream_grad + dot(arrived[source], qkv_blocks[source, head])
        weight_sums.append(dot_cols(input_all, qkv_grad))
        bias_sums.append(jnp.sum(qkv_grad, axis=0, dtype=F32))
    weight_sums = lax.psum(jnp.stack(weight_sums).astype(BF16), "dp").astype(F32)
    qkv_weight_grad = (
        weight_sums.reshape(head_total, width, 3, HEAD_DIM)
        .transpose(2, 1, 0, 3)
        .reshape(1, 3, width, head_cols)
    )
    bias_sums = lax.psum(jnp.stack(bias_sums), "dp").reshape(head_total, 3, HEAD_DIM)
    query_bias_grad = bias_sums[:, 0].reshape(1, head_cols)
    value_bias_grad = bias_sums[:, 2].reshape(1, head_cols)

    gain_grad, shift_grad, head_bias_grad, down_bias_grad, in_bias_grad = lax.psum(
        (
            jnp.stack([gain_mid_grad, gain_out_grad])[None],
            jnp.stack([shift_mid_grad, shift_out_grad])[None],
            head_bias_grad[None],
            down_bias_grad[None],
            in_bias_grad,
        ),
        ("dp", "mp"),
    )
    in_bias_grad = lax.dynamic_slice_in_dim(
        in_bias_grad, lax.axis_index("mp") * units, units, 0
    )[None]
    return (
        block_out,
        stream_grad,
        qkv_weight_grad,
        query_bias_grad,
        value_bias_grad,
        out_weight_grad,
        head_bias_grad,
        in_weight_grad,
        in_bias_grad,
        down_weight_grad,
        down_bias_grad,
        gain_grad,
        shift_grad,
    )


def solution(mesh):
    return jax.shard_map(
        on_device,
        mesh=mesh,
        in_specs=(
            P(("dp", "mp"), None),
            P("dp"),
            P(None, None, None, "mp"),
            P(None, "mp"),
            P(None, "mp"),
            P(None, "mp", None),
            P(),
            P(None, None, "mp"),
            P(None, "mp"),
            P(None, "mp", None),
            P(),
            P(),
            P(),
            P(("dp", "mp"), None),
        ),
        out_specs=(
            P(("dp", "mp"), None),
            P(("dp", "mp"), None),
            P(None, None, None, "mp"),
            P(None, "mp"),
            P(None, "mp"),
            P(None, "mp", None),
            P(),
            P(None, None, "mp"),
            P(None, "mp"),
            P(None, "mp", None),
            P(),
            P(),
            P(),
        ),
        check_vma=False,
    )
```

```python
from functools import partial

import jax
import jax.numpy as jnp
from jax import lax
from jax.experimental import pallas as pl
from jax.experimental.pallas import tpu as pltpu
from jax.sharding import PartitionSpec as P

HEAD_DIM = 64
ROW_LEN = 2304
TILE = 256
STEP = 3
TILES = ROW_LEN // TILE
EXTRA = 16
SCALE = HEAD_DIM ** (-0.5)
MASKED = -1e30
F32 = jnp.float32
BF16 = jnp.bfloat16
VMEM_BYTES = 56 * 1024 * 1024


def dot_rows(left, right):
    return lax.dot_general(left, right, (((1,), (1,)), ((), ())), preferred_element_type=F32)


def dot_cols(left, right):
    return lax.dot_general(left, right, (((0,), (0,)), ((), ())), preferred_element_type=F32)


def dot(left, right):
    return jnp.dot(left, right, preferred_element_type=F32)


def tile_rows(tile):
    return pl.ds(pl.multiple_of(tile * TILE, TILE), TILE)


def as_pieces(row):
    high = row.astype(BF16).astype(F32)
    middle = (row - high).astype(BF16).astype(F32)
    last = row - high - middle
    place = lax.broadcasted_iota(jnp.int32, (EXTRA, row.shape[1]), 0)
    pieces = jnp.where(place == 0, high, jnp.where(place == 1, middle, jnp.where(place == 2, last, 0.0)))
    return pieces.astype(BF16)


def ones_columns(rows):
    place = lax.broadcasted_iota(jnp.int32, (rows, EXTRA), 1)
    return jnp.where(place < 3, 1.0, 0.0).astype(BF16)


def attend_kernel(
    limits, seg_row, seg_col, qkv, out, out_cols, log_total, key_cols, value_buf, query_buf, peak_buf
):
    head_total = qkv.shape[2] // HEAD_DIM
    width = HEAD_DIM + EXTRA
    lane = lax.broadcasted_iota(jnp.int32, (TILE, EXTRA), 1)
    place = lax.broadcasted_iota(jnp.int32, (EXTRA, STEP * TILE), 0)
    for head in range(head_total):
        cols = slice(head * HEAD_DIM, (head + 1) * HEAD_DIM)
        value_buf[:, :HEAD_DIM] = qkv[2, :, cols]
        for tile in range(TILES):
            value_buf[tile * TILE : (tile + 1) * TILE, HEAD_DIM:] = jnp.where(
                lane == 0, 1.0, 0.0
            ).astype(BF16)
        key_peak = jnp.zeros((1, STEP * TILE), F32)
        for step in range(TILES // STEP):
            rows = slice(step * STEP * TILE, (step + 1) * STEP * TILE)
            keys = qkv[1, rows, cols].astype(F32).T
            key_peak = jnp.maximum(key_peak, jnp.sum(keys * keys, axis=0, keepdims=True))
            key_cols[step, :HEAD_DIM] = keys.astype(BF16)
            key_cols[step, HEAD_DIM:] = jnp.where(place == 0, 1.0, 0.0).astype(BF16)
        key_peak = jnp.max(key_peak, axis=1, keepdims=True)

        def query_tile(tile, _):
            rows = tile_rows(tile)
            seg_query = seg_col[rows]
            first, count = limits[tile, 0], limits[tile, 1]
            queries = qkv[0, rows, cols].astype(F32) * SCALE
            length = jnp.sum(queries * queries, axis=1, keepdims=True)
            bound = jnp.sqrt(length * key_peak).astype(BF16).astype(F32)
            query_buf[:, :HEAD_DIM] = queries.astype(BF16)
            query_buf[:, HEAD_DIM:] = jnp.where(lane == 0, -bound, 0.0).astype(BF16)

            def scores_of(step):
                same = jnp.concatenate([seg_query] * (STEP * TILE // 128), axis=1) == seg_row[step]
                scores = dot(query_buf[...], key_cols[step])
                return jnp.where(same, scores, MASKED)

            def mixed_in(step, soft):
                key_rows = pl.ds(pl.multiple_of(step * STEP * TILE, STEP * TILE), STEP * TILE)
                return dot(soft.astype(BF16), value_buf[key_rows])

            def mix(step, mixed):
                return mixed + mixed_in(step, jnp.exp(scores_of(step)))

            def store(mixed, shift):
                total = mixed[:, HEAD_DIM : HEAD_DIM + 1]
                mixed = mixed[:, :HEAD_DIM] / total
                logs = jnp.broadcast_to(shift + jnp.log(total), (TILE, HEAD_DIM))
                both = jnp.concatenate([mixed, logs], axis=1).T
                out_cols[head, tile] = both[:HEAD_DIM]
                log_total[head, tile] = both[HEAD_DIM : HEAD_DIM + 1]
                out[rows, cols] = mixed.astype(BF16)

            empty = jnp.zeros((TILE, width), F32)
            mixed = lax.fori_loop(first, first + count, mix, empty)
            store(mixed, bound)

            @pl.when(jnp.min(mixed[:, HEAD_DIM : HEAD_DIM + 1]) < 2.0**-64)
            def _():
                def top(step, peak):
                    return jnp.maximum(peak, jnp.max(scores_of(step), axis=1, keepdims=True))

                peak = jnp.full((TILE, 1), MASKED, F32)
                peak_buf[...] = lax.fori_loop(first, first + count, top, peak)

                def mix_again(step, mixed):
                    return mixed + mixed_in(step, jnp.exp(scores_of(step) - peak_buf[...]))

                mixed = lax.fori_loop(first, first + count, mix_again, empty)
                store(mixed, bound + peak_buf[...])

            return 0

        lax.fori_loop(0, TILES, query_tile, 0)


def attend_back_kernel(
    head,
    seg_row,
    seg_col,
    qkv,
    out_cols,
    log_total,
    heads_grad,
    qkv_grad,
    key_buf,
    key_cols,
    value_buf,
    key_sum,
    value_sum,
):
    cols = slice(head * HEAD_DIM, (head + 1) * HEAD_DIM)
    block = STEP * TILE
    key_buf[:, :HEAD_DIM] = qkv[1, :, cols]
    key_buf[:, HEAD_DIM:] = ones_columns(ROW_LEN)
    value_buf[:, :HEAD_DIM] = qkv[2, :, cols]
    value_buf[:, HEAD_DIM:] = ones_columns(ROW_LEN)
    for step in range(TILES // STEP):
        key_cols[step] = qkv[1, step * block : (step + 1) * block, cols].T
    key_sum[...] = jnp.zeros_like(key_sum)
    value_sum[...] = jnp.zeros_like(value_sum)

    def query_block(number, _):
        rows = pl.ds(pl.multiple_of(number * block, block), block)
        queries = qkv[0, rows, cols] * SCALE
        grads = heads_grad[rows, cols]
        seg_query = seg_row[number]
        outs = jnp.concatenate([out_cols[head, number * STEP + part] for part in range(STEP)], axis=1)
        logs = jnp.concatenate([log_total[head, number * STEP + part] for part in range(STEP)], axis=1)
        grad_cols = grads.astype(F32).T
        row_dot = jnp.sum(grad_cols * outs, axis=0, keepdims=True)
        grad_cols = jnp.concatenate([grad_cols.astype(BF16), as_pieces(-row_dot)], axis=0)
        query_cols = jnp.concatenate(
            [queries.astype(F32).T.astype(BF16), as_pieces(-logs)], axis=0
        )

        def step_back(step, query_grad):
            key_rows = pl.ds(pl.multiple_of(step * block, block), block)
            same = jnp.concatenate([seg_col[key_rows]] * (block // 128), axis=1) == seg_query
            scores = dot(key_buf[key_rows], query_cols)
            soft = jnp.exp(jnp.where(same, scores, MASKED))
            soft_grad = dot(value_buf[key_rows], grad_cols)
            score_grad = (soft * soft_grad).astype(BF16)
            value_sum[key_rows] += dot(soft.astype(BF16), grads)
            key_sum[key_rows] += dot(score_grad, queries)
            return query_grad + dot(key_cols[step], score_grad)

        query_grad = lax.fori_loop(0, TILES // STEP, step_back, jnp.zeros((HEAD_DIM, block), F32))
        qkv_grad[rows, 0:HEAD_DIM] = (query_grad * SCALE).T.astype(BF16)
        return 0

    lax.fori_loop(0, TILES // STEP, query_block, 0)
    qkv_grad[:, HEAD_DIM : 2 * HEAD_DIM] = key_sum[...].astype(BF16)
    qkv_grad[:, 2 * HEAD_DIM : 3 * HEAD_DIM] = value_sum[...].astype(BF16)


def tile_limits(segments):
    places = jnp.arange(ROW_LEN, dtype=jnp.int32)
    first_ids = segments[::TILE]
    last_ids = segments[TILE - 1 :: TILE]
    low = jnp.min(jnp.where(segments[None] == first_ids[:, None], places[None], ROW_LEN), axis=1)
    high = jnp.max(jnp.where(segments[None] == last_ids[:, None], places[None], -1), axis=1)
    first = low // (STEP * TILE)
    return jnp.stack([first, high // (STEP * TILE) + 1 - first], axis=1)


def whole(memory_space=pltpu.VMEM):
    return pl.BlockSpec(memory_space=memory_space)


def attend(limits, seg_row, seg_col, qkv_low):
    head_total = qkv_low.shape[2] // HEAD_DIM
    return pl.pallas_call(
        attend_kernel,
        out_shape=(
            jax.ShapeDtypeStruct(qkv_low.shape[1:], BF16),
            jax.ShapeDtypeStruct((head_total, TILES, HEAD_DIM, TILE), F32),
            jax.ShapeDtypeStruct((head_total, TILES, 1, TILE), F32),
        ),
        in_specs=[whole(pltpu.SMEM), whole(), whole(), whole()],
        out_specs=(whole(), whole(), whole()),
        scratch_shapes=[
            pltpu.VMEM((TILES // STEP, HEAD_DIM + EXTRA, STEP * TILE), BF16),
            pltpu.VMEM((ROW_LEN, HEAD_DIM + EXTRA), BF16),
            pltpu.VMEM((TILE, HEAD_DIM + EXTRA), BF16),
            pltpu.VMEM((TILE, 1), F32),
        ],
        compiler_params=pltpu.CompilerParams(vmem_limit_bytes=VMEM_BYTES),
        cost_estimate=pl.CostEstimate(
            flops=16 * head_total * ROW_LEN * ROW_LEN * HEAD_DIM,
            bytes_accessed=8 * ROW_LEN * 256 * 3,
            transcendentals=head_total * ROW_LEN * ROW_LEN,
        ),
        name="attend",
    )(limits, seg_row, seg_col, qkv_low)


def attend_back(head, seg_row, seg_col, qkv_low, out_cols, log_total, heads_grad):
    return pl.pallas_call(
        partial(attend_back_kernel, head),
        out_shape=jax.ShapeDtypeStruct((ROW_LEN, 3 * HEAD_DIM), BF16),
        in_specs=[whole()] * 6,
        out_specs=whole(),
        scratch_shapes=[
            pltpu.VMEM((ROW_LEN, HEAD_DIM + EXTRA), BF16),
            pltpu.VMEM((TILES // STEP, HEAD_DIM, STEP * TILE), BF16),
            pltpu.VMEM((ROW_LEN, HEAD_DIM + EXTRA), BF16),
            pltpu.VMEM((ROW_LEN, HEAD_DIM), F32),
            pltpu.VMEM((ROW_LEN, HEAD_DIM), F32),
        ],
        compiler_params=pltpu.CompilerParams(vmem_limit_bytes=VMEM_BYTES),
        cost_estimate=pl.CostEstimate(
            flops=40 * ROW_LEN * ROW_LEN * HEAD_DIM,
            bytes_accessed=8 * ROW_LEN * 256 * 3,
            transcendentals=ROW_LEN * ROW_LEN,
        ),
        name="attend_back_" + str(head),
    )(seg_row, seg_col, qkv_low, out_cols, log_total, heads_grad)


MESH = pl.DeviceIdType.MESH


def group_bits(dp_size):
    return min(3, dp_size.bit_length() - 1)


def place_in(dp_index, order):
    slot = 0
    for at, bit in enumerate(order):
        slot = slot + (dp_index // 2**bit) % 2 * 2**at
    return slot


def partner_of(dp_index, bit):
    return dp_index + (1 - 2 * ((dp_index // 2**bit) % 2)) * 2**bit


def enter(dp_index, mp_index, mp_size, bits):
    barrier = pltpu.get_barrier_semaphore()
    for offset in range(1, mp_size):
        pl.semaphore_signal(
            barrier, device_id={"mp": lax.rem(mp_index + offset, mp_size)}, device_id_type=MESH
        )
    for bit in range(bits):
        pl.semaphore_signal(
            barrier, device_id={"dp": partner_of(dp_index, bit)}, device_id_type=MESH
        )
    pl.semaphore_wait(barrier, mp_size - 1 + bits)


def send(src, dst, sems, at, device_id):
    return pltpu.make_async_remote_copy(
        src_ref=src,
        dst_ref=dst,
        send_sem=sems[0].at[at],
        recv_sem=sems[1].at[at],
        device_id=device_id,
        device_id_type=MESH,
    )


def gather_orders(bits):
    if bits == 3:
        return ((1, 2, 0), (2, 1, 0), (1, 2))
    return (tuple(range(bits)),) * 3


def gather_kernel(
    bits,
    frames,
    qkv_weight,
    bias_rows,
    in_weight,
    down_weight,
    head_weight,
    in_bias,
    input_all,
    qkv_low,
    in_all,
    down_all,
    head_all,
    bias_all,
    own_sems,
    frame_send,
    frame_recv,
    bias_send,
    bias_recv,
    first_send,
    first_recv,
    later_send,
    later_recv,
):
    mp_size = in_all.shape[0]
    me = lax.axis_index("mp")
    dp_index = lax.axis_index("dp")
    local_rows = frames.shape[0]
    orders = gather_orders(bits)
    shares = (in_weight, down_weight, head_weight)
    wholes = (in_all, down_all, head_all)
    enter(dp_index, me, mp_size, bits)

    def slots(which, level):
        order = orders[which]
        count = shares[which].shape[0] // 2 ** len(order)
        start = place_in(dp_index, order) // 2**level * 2**level
        return pl.ds(pl.multiple_of(start * count, 16), count * 2**level)

    def first_copy(which, offset):
        rows = slots(which, 0)
        return send(
            shares[which].at[rows],
            wholes[which].at[me, rows],
            (first_send, first_recv),
            (which, offset - 1),
            {"mp": lax.rem(me + offset, mp_size)},
        )

    def later_copy(which, level, offset):
        rows = slots(which, level)
        held = wholes[which].at[lax.rem(me + mp_size - offset, mp_size), rows]
        return send(
            held,
            held,
            (later_send, later_recv),
            (which, level, offset - 1),
            {"dp": partner_of(dp_index, orders[which][level])},
        )

    def frame_rows(index):
        return pl.ds(pl.multiple_of(index * local_rows, local_rows), local_rows)

    def frame_copy(offset):
        return send(
            frames,
            input_all.at[frame_rows(me)],
            (frame_send, frame_recv),
            offset - 1,
            {"mp": lax.rem(me + offset, mp_size)},
        )

    def bias_copy(offset):
        return send(
            in_bias,
            bias_all.at[me],
            (bias_send, bias_recv),
            offset - 1,
            {"mp": lax.rem(me + offset, mp_size)},
        )

    def project(index):
        rows = frame_rows(index)
        inputs = input_all[rows]
        for part in range(3):
            products = dot(inputs, qkv_weight[part]) + bias_rows[part : part + 1]
            qkv_low[part, rows] = products.astype(BF16)

    offsets = range(1, mp_size)
    for which in range(3):
        for offset in offsets:
            first_copy(which, offset).start()
    for offset in offsets:
        frame_copy(offset).start()
        bias_copy(offset).start()
    own = [
        pltpu.make_async_copy(shares[which], wholes[which].at[me], own_sems.at[which])
        for which in range(3)
    ]
    own.append(pltpu.make_async_copy(in_bias, bias_all.at[me], own_sems.at[3]))
    for copy in own:
        copy.start()
    input_all[frame_rows(me)] = frames[...]
    project(me)

    waited = 0
    for level in range(bits + 1):
        for which in range(3):
            depth = len(orders[which])
            for offset in offsets:
                if level == 0:
                    first_copy(which, offset).wait_recv()
                elif level <= depth:
                    later_copy(which, level - 1, offset).wait_recv()
                if level < depth:
                    later_copy(which, level, offset).start()
        if level > 0 and waited < mp_size - 1:
            waited += 1
            frame_copy(waited).wait_recv()
            project(lax.rem(me + mp_size - waited, mp_size))
    while waited < mp_size - 1:
        waited += 1
        frame_copy(waited).wait_recv()
        project(lax.rem(me + mp_size - waited, mp_size))
    for offset in offsets:
        bias_copy(offset).wait_recv()
        bias_copy(offset).wait_send()
        frame_copy(offset).wait_send()
        for which in range(3):
            first_copy(which, offset).wait_send()
            for level in range(len(orders[which])):
                later_copy(which, level, offset).wait_send()
    for copy in own:
        copy.wait()


def gather_inputs(
    frames, qkv_weight, bias_rows, in_weight, down_weight, head_weight, in_bias, mp_size, bits
):
    local_rows, width = frames.shape
    row_total = local_rows * mp_size
    peers = mp_size - 1
    levels = max(bits, 1)
    anywhere = pl.BlockSpec(memory_space=pl.ANY)
    return pl.pallas_call(
        partial(gather_kernel, bits),
        out_shape=(
            jax.ShapeDtypeStruct((row_total, width), BF16),
            jax.ShapeDtypeStruct((3, row_total, qkv_weight.shape[2]), BF16),
            jax.ShapeDtypeStruct((mp_size,) + in_weight.shape, BF16),
            jax.ShapeDtypeStruct((mp_size,) + down_weight.shape, BF16),
            jax.ShapeDtypeStruct((mp_size,) + head_weight.shape, BF16),
            jax.ShapeDtypeStruct((mp_size,) + in_bias.shape, BF16),
        ),
        in_specs=[whole()] * 3 + [anywhere] * 4,
        out_specs=(whole(), whole()) + (anywhere,) * 4,
        scratch_shapes=[
            pltpu.SemaphoreType.DMA((4,)),
            pltpu.SemaphoreType.DMA((peers,)),
            pltpu.SemaphoreType.DMA((peers,)),
            pltpu.SemaphoreType.DMA((peers,)),
            pltpu.SemaphoreType.DMA((peers,)),
            pltpu.SemaphoreType.DMA((3, peers)),
            pltpu.SemaphoreType.DMA((3, peers)),
            pltpu.SemaphoreType.DMA((3, levels, peers)),
            pltpu.SemaphoreType.DMA((3, levels, peers)),
        ],
        compiler_params=pltpu.CompilerParams(
            collective_id=0, has_side_effects=True, vmem_limit_bytes=VMEM_BYTES
        ),
        cost_estimate=pl.CostEstimate(
            flops=6 * row_total * width * qkv_weight.shape[2],
            bytes_accessed=32 * 1024 * 1024,
            transcendentals=0,
        ),
        name="gather_inputs",
    )(frames, qkv_weight, bias_rows, in_weight, down_weight, head_weight, in_bias)


def trade_kernel(pieces, arrived, own_sem, send_sems, recv_sems):
    mp_size = pieces.shape[0]
    me = lax.axis_index("mp")
    enter(0, me, mp_size, 0)
    copies = []
    for offset in range(1, mp_size):
        target = lax.rem(me + offset, mp_size)
        copies.append(
            send(
                pieces.at[target],
                arrived.at[me],
                (send_sems, recv_sems),
                offset - 1,
                {"mp": target},
            )
        )
    for copy in copies:
        copy.start()
    own = pltpu.make_async_copy(pieces.at[me], arrived.at[me], own_sem)
    own.start()
    own.wait()
    for copy in copies:
        copy.wait()


def trade_heads(pieces):
    peers = pieces.shape[0] - 1
    anywhere = pl.BlockSpec(memory_space=pl.ANY)
    return pl.pallas_call(
        trade_kernel,
        out_shape=jax.ShapeDtypeStruct(pieces.shape, pieces.dtype),
        in_specs=[anywhere],
        out_specs=anywhere,
        scratch_shapes=[
            pltpu.SemaphoreType.DMA,
            pltpu.SemaphoreType.DMA((peers,)),
            pltpu.SemaphoreType.DMA((peers,)),
        ],
        compiler_params=pltpu.CompilerParams(collective_id=1, has_side_effects=True),
        name="trade_heads",
    )(pieces)


def norm_rows(inputs, norm_gain, norm_shift):
    row_mean = jnp.mean(inputs, axis=-1, keepdims=True)
    centred = inputs - row_mean
    variance = jnp.mean(centred * centred, axis=-1, keepdims=True)
    inv_std = lax.rsqrt(variance + 1e-05)
    normed = centred * inv_std
    return (normed * norm_gain + norm_shift, normed, inv_std)


def norm_back(cotangent, normed, inv_std, norm_gain):
    scaled = cotangent * norm_gain
    adjusted = (
        scaled
        - jnp.mean(scaled, axis=-1, keepdims=True)
        - normed * jnp.mean(scaled * normed, axis=-1, keepdims=True)
    )
    return (adjusted * inv_std, jnp.sum(cotangent * normed, axis=0), jnp.sum(cotangent, axis=0))


def ring_perm(size, offset):
    return [(place, (place + offset) % size) for place in range(size)]


def exchange(pieces):
    size = lax.axis_size("mp")
    me = lax.axis_index("mp")
    own = lax.dynamic_index_in_dim(pieces, me, 0, keepdims=True)
    gathered = lax.dynamic_update_slice_in_dim(pieces, own, me, 0)
    for offset in range(1, size):
        piece = lax.dynamic_index_in_dim(pieces, (me + offset) % size, 0, keepdims=True)
        arrived = lax.ppermute(piece, "mp", ring_perm(size, offset))
        gathered = lax.dynamic_update_slice_in_dim(
            gathered, arrived, (me + size - offset) % size, 0
        )
    return gathered


def dp_groups():
    total = lax.axis_size("dp")
    size = min(8, total)
    groups = [list(range(start, start + size)) for start in range(0, total, size)]
    return (size, groups)


def on_device(
    frames,
    segment_ids,
    qkv_weight,
    q_bias,
    v_bias,
    out_weight,
    out_bias,
    ff_in_weight,
    ff_in_bias,
    ff_out_weight,
    ff_out_bias,
    norm_gain,
    norm_shift,
    out_grad,
):
    local_rows, width = frames.shape
    mp_size = lax.axis_size("mp")
    group, groups = dp_groups()
    place = lax.axis_index("dp") % group
    head_cols = qkv_weight.shape[3]
    head_total = head_cols // HEAD_DIM
    units = ff_in_weight.shape[2]

    bits = group_bits(lax.axis_size("dp"))
    bias_rows = jnp.stack([q_bias[0], jnp.zeros_like(q_bias[0]), v_bias[0]]).astype(F32)
    input_all, qkv_low, in_all, down_all, out_all, in_bias_all = gather_inputs(
        frames,
        qkv_weight[0],
        bias_rows,
        ff_in_weight[0].T,
        ff_out_weight[0],
        out_weight[0],
        jnp.broadcast_to(ff_in_bias, (16, units)),
        mp_size,
        bits,
    )
    in_rows = in_all.reshape(-1, width)
    down_all = down_all.reshape(-1, width)
    out_all = out_all.reshape(-1, width)
    in_bias_all = in_bias_all[:, 0].reshape(-1).astype(F32)

    qkv_rows, qkv_low = lax.optimization_barrier((qkv_weight[0], qkv_low))
    qkv_rows = (
        qkv_rows.reshape(3, width, head_total, HEAD_DIM).transpose(2, 0, 3, 1)
    ).reshape(-1, width)
    share = qkv_rows.shape[0] // group
    part = lax.dynamic_slice_in_dim(qkv_rows, place * share, share, 0)
    part = lax.all_gather(part, "mp", axis=0)
    qkv_all = lax.all_gather(part, "dp", axis=0, axis_index_groups=groups)
    qkv_all = qkv_all.transpose(1, 0, 2, 3).reshape(-1, width)

    seg_row = segment_ids.reshape(TILES // STEP, 1, STEP * TILE)
    seg_col = jnp.broadcast_to(segment_ids[:, None], (ROW_LEN, 128))
    limits = tile_limits(segment_ids)
    heads_out, out_cols, log_total = attend(limits, seg_row, seg_col, qkv_low)
    heads_low = trade_heads(heads_out.reshape(mp_size, local_rows, head_cols))
    heads_low = heads_low.transpose(1, 0, 2).reshape(local_rows, width)

    gains = norm_gain[0].astype(F32)
    shifts = norm_shift[0].astype(F32)
    residual = frames.astype(F32) + (dot(heads_low, out_all) + out_bias[0].astype(F32))
    mid, normed_mid, inv_std_mid = norm_rows(residual, gains[0], shifts[0])
    mid_low = mid.astype(BF16)
    pre_act = dot_rows(mid_low, in_rows) + in_bias_all
    unit_cdf = 0.5 * (1.0 + lax.erf(pre_act * 0.5**0.5))
    hidden = (pre_act * unit_cdf).astype(BF16)
    slope = unit_cdf + pre_act * jnp.exp(-0.5 * pre_act * pre_act) * (2.0 * jnp.pi) ** (-0.5)
    summed = mid + (dot(hidden, down_all) + ff_out_bias[0].astype(F32))
    block_out, normed_out, inv_std_out = norm_rows(summed, gains[1], shifts[1])

    sum_grad, gain_out_grad, shift_out_grad = norm_back(
        out_grad.astype(F32), normed_out, inv_std_out, gains[1]
    )
    ffn_grad_low = sum_grad.astype(BF16)
    down_bias_grad = jnp.sum(ffn_grad_low, axis=0, dtype=F32)
    pre_grad_low = (dot_rows(ffn_grad_low, down_all) * slope).astype(BF16)
    in_bias_grad = jnp.sum(pre_grad_low, axis=0, dtype=F32)
    mid_grad = sum_grad + dot(pre_grad_low, in_rows)
    resid_grad, gain_mid_grad, shift_mid_grad = norm_back(
        mid_grad, normed_mid, inv_std_mid, gains[0]
    )
    attn_grad_low = resid_grad.astype(BF16)
    head_bias_grad = jnp.sum(attn_grad_low, axis=0, dtype=F32)
    heads_grad_low = dot_rows(attn_grad_low, out_all).astype(BF16)
    heads_grad = exchange(
        heads_grad_low.reshape(local_rows, mp_size, head_cols).transpose(1, 0, 2)
    ).reshape(-1, head_cols)

    grad_rows = jnp.concatenate(
        [
            dot_cols(heads_low, attn_grad_low).astype(BF16).reshape(mp_size, head_cols, width),
            dot_cols(pre_grad_low, mid_low).astype(BF16).reshape(mp_size, units, width),
            dot_cols(hidden, ffn_grad_low).astype(BF16).reshape(mp_size, units, width),
        ],
        axis=1,
    )
    grad_rows = grad_rows.reshape(mp_size * lax.axis_size("dp"), -1, width)
    grad_sum = lax.psum_scatter(grad_rows, ("mp", "dp"), scatter_dimension=0, tiled=False)
    grad_sum = lax.all_gather(
        grad_sum, "dp", axis=0, tiled=True
    ).astype(F32)
    ends = [0, head_cols, head_cols + units, head_cols + 2 * units]
    out_weight_grad = grad_sum[: ends[1]][None]
    in_weight_grad = grad_sum[ends[1] : ends[2]].T[None]
    down_weight_grad = grad_sum[ends[2] : ends[3]][None]

    stream_grad = resid_grad
    weight_sums = []
    bias_sums = []
    qkv_blocks = qkv_all.reshape(mp_size, head_total, 3 * HEAD_DIM, width)
    for head in range(head_total):
        qkv_grad = attend_back(
            head, seg_row, seg_col, qkv_low, out_cols, log_total, heads_grad
        )
        arrived = exchange(qkv_grad.reshape(mp_size, local_rows, 3 * HEAD_DIM))
        for source in range(mp_size):
            stream_grad = stream_grad + dot(arrived[source], qkv_blocks[source, head])
        weight_sums.append(dot_cols(input_all, qkv_grad))
        bias_sums.append(jnp.sum(qkv_grad, axis=0, dtype=F32))
    weight_sums = lax.psum(jnp.stack(weight_sums).astype(BF16), "dp").astype(F32)
    qkv_weight_grad = (
        weight_sums.reshape(head_total, width, 3, HEAD_DIM)
        .transpose(2, 1, 0, 3)
        .reshape(1, 3, width, head_cols)
    )
    bias_sums = lax.psum(jnp.stack(bias_sums), "dp").reshape(head_total, 3, HEAD_DIM)
    query_bias_grad = bias_sums[:, 0].reshape(1, head_cols)
    value_bias_grad = bias_sums[:, 2].reshape(1, head_cols)

    gain_grad, shift_grad, head_bias_grad, down_bias_grad, in_bias_grad = lax.psum(
        (
            jnp.stack([gain_mid_grad, gain_out_grad])[None],
            jnp.stack([shift_mid_grad, shift_out_grad])[None],
            head_bias_grad[None],
            down_bias_grad[None],
            in_bias_grad,
        ),
        ("dp", "mp"),
    )
    in_bias_grad = lax.dynamic_slice_in_dim(
        in_bias_grad, lax.axis_index("mp") * units, units, 0
    )[None]
    return (
        block_out,
        stream_grad,
        qkv_weight_grad,
        query_bias_grad,
        value_bias_grad,
        out_weight_grad,
        head_bias_grad,
        in_weight_grad,
        in_bias_grad,
        down_weight_grad,
        down_bias_grad,
        gain_grad,
        shift_grad,
    )


def solution(mesh):
    return jax.shard_map(
        on_device,
        mesh=mesh,
        in_specs=(
            P(("dp", "mp"), None),
            P("dp"),
            P(None, None, None, "mp"),
            P(None, "mp"),
            P(None, "mp"),
            P(None, "mp", None),
            P(),
            P(None, None, "mp"),
            P(None, "mp"),
            P(None, "mp", None),
            P(),
            P(),
            P(),
            P(("dp", "mp"), None),
        ),
        out_specs=(
            P(("dp", "mp"), None),
            P(("dp", "mp"), None),
            P(None, None, None, "mp"),
            P(None, "mp"),
            P(None, "mp"),
            P(None, "mp", None),
            P(),
            P(None, None, "mp"),
            P(None, "mp"),
            P(None, "mp", None),
            P(),
            P(),
            P(),
        ),
        check_vma=False,
    )
```

```python
from functools import partial

import jax
import jax.numpy as jnp
from jax import lax
from jax.experimental import pallas as pl
from jax.experimental.pallas import tpu as pltpu
from jax.sharding import PartitionSpec as P

HEAD_DIM = 64
ROW_LEN = 2304
BLOCK = 768
BLOCKS = ROW_LEN // BLOCK
EXTRA = 16
SCALE = HEAD_DIM ** (-0.5)
MASKED = -1e30
F32 = jnp.float32
BF16 = jnp.bfloat16
VMEM_BYTES = 56 * 1024 * 1024


def dot_rows(left, right):
    return lax.dot_general(left, right, (((1,), (1,)), ((), ())), preferred_element_type=F32)


def dot_cols(left, right):
    return lax.dot_general(left, right, (((0,), (0,)), ((), ())), preferred_element_type=F32)


def dot(left, right):
    return jnp.dot(left, right, preferred_element_type=F32)


def block_rows(number):
    return pl.ds(pl.multiple_of(number * BLOCK, BLOCK), BLOCK)


def as_pieces(row):
    high = row.astype(BF16).astype(F32)
    middle = (row - high).astype(BF16).astype(F32)
    last = row - high - middle
    place = lax.broadcasted_iota(jnp.int32, (EXTRA, row.shape[1]), 0)
    pieces = jnp.where(place == 0, high, jnp.where(place == 1, middle, jnp.where(place == 2, last, 0.0)))
    return pieces.astype(BF16)


def ones_columns(rows):
    place = lax.broadcasted_iota(jnp.int32, (rows, EXTRA), 1)
    return jnp.where(place < 3, 1.0, 0.0).astype(BF16)


def attend_kernel(
    seg_row, seg_col, qkv, out, out_cols, log_total, key_cols, value_buf, query_buf, peak_buf, out_buf
):
    head_total = qkv.shape[2] // HEAD_DIM
    lane = lax.broadcasted_iota(jnp.int32, (BLOCK, EXTRA), 1)
    place = lax.broadcasted_iota(jnp.int32, (EXTRA, BLOCK), 0)
    for head in range(head_total):
        cols = slice(head * HEAD_DIM, (head + 1) * HEAD_DIM)
        key_peak = jnp.zeros((1, BLOCK), F32)
        for step in range(BLOCKS):
            rows = slice(step * BLOCK, (step + 1) * BLOCK)
            keys = qkv[1, rows, cols].astype(F32).T
            key_peak = jnp.maximum(key_peak, jnp.sum(keys * keys, axis=0, keepdims=True))
            key_cols[step, :HEAD_DIM] = keys.astype(BF16)
            key_cols[step, HEAD_DIM:] = jnp.where(place == 0, 1.0, 0.0).astype(BF16)
            value_buf[step, :, :HEAD_DIM] = qkv[2, rows, cols]
            value_buf[step, :, HEAD_DIM:] = jnp.where(lane == 0, 1.0, 0.0).astype(BF16)
        key_peak = jnp.max(key_peak, axis=1, keepdims=True)

        def query_block(number, _):
            rows = block_rows(number)
            queries = qkv[0, rows, cols].astype(F32) * SCALE
            length = jnp.sum(queries * queries, axis=1, keepdims=True)
            bound = jnp.sqrt(length * key_peak).astype(BF16).astype(F32)
            query_buf[:, :HEAD_DIM] = queries.astype(BF16)
            query_buf[:, HEAD_DIM:] = jnp.where(lane == 0, -bound, 0.0).astype(BF16)

            def scores_of(step):
                same = jnp.concatenate([seg_col[rows]] * (BLOCK // 128), axis=1) == seg_row[step]
                scores = dot(query_buf[...], key_cols[step])
                return jnp.where(same, scores, MASKED)

            def mix(step, mixed):
                return mixed + dot(jnp.exp(scores_of(step)).astype(BF16), value_buf[step])

            def store(mixed, shift):
                total = mixed[:, HEAD_DIM : HEAD_DIM + 1]
                mixed = mixed[:, :HEAD_DIM] / total
                logs = jnp.broadcast_to(shift + jnp.log(total), (BLOCK, HEAD_DIM))
                both = jnp.concatenate([mixed, logs], axis=1).T
                out_cols[head, number] = both[:HEAD_DIM]
                log_total[head, number] = both[HEAD_DIM : HEAD_DIM + 1]
                out_buf[rows, cols] = mixed.astype(BF16)

            empty = jnp.zeros((BLOCK, HEAD_DIM + EXTRA), F32)
            mixed = lax.fori_loop(0, BLOCKS, mix, empty)
            store(mixed, bound)

            @pl.when(jnp.min(mixed[:, HEAD_DIM : HEAD_DIM + 1]) < 2.0**-64)
            def _():
                def top(step, peak):
                    return jnp.maximum(peak, jnp.max(scores_of(step), axis=1, keepdims=True))

                peak_buf[...] = lax.fori_loop(0, BLOCKS, top, jnp.full((BLOCK, 1), MASKED, F32))

                def mix_again(step, mixed):
                    soft = jnp.exp(scores_of(step) - peak_buf[...])
                    return mixed + dot(soft.astype(BF16), value_buf[step])

                store(lax.fori_loop(0, BLOCKS, mix_again, empty), bound + peak_buf[...])

            return 0

        lax.fori_loop(0, BLOCKS, query_block, 0)
    half = out.shape[1]
    width = head_total * HEAD_DIM
    for chunk in range(out.shape[0]):
        for side in range(2):
            start = (2 * chunk + side) * half
            out[chunk, :, side * width : (side + 1) * width] = out_buf[start : start + half]


def whole(memory_space=pltpu.VMEM):
    return pl.BlockSpec(memory_space=memory_space)


def attend(seg_row, seg_col, qkv_low, chunks):
    head_total = qkv_low.shape[2] // HEAD_DIM
    half = ROW_LEN // chunks // 2
    return pl.pallas_call(
        attend_kernel,
        out_shape=(
            jax.ShapeDtypeStruct((chunks, half, 2 * head_total * HEAD_DIM), BF16),
            jax.ShapeDtypeStruct((head_total, BLOCKS, HEAD_DIM, BLOCK), F32),
            jax.ShapeDtypeStruct((head_total, BLOCKS, 1, BLOCK), F32),
        ),
        in_specs=[whole()] * 3,
        out_specs=(whole(), whole(), whole()),
        scratch_shapes=[
            pltpu.VMEM((BLOCKS, HEAD_DIM + EXTRA, BLOCK), BF16),
            pltpu.VMEM((BLOCKS, BLOCK, HEAD_DIM + EXTRA), BF16),
            pltpu.VMEM((BLOCK, HEAD_DIM + EXTRA), BF16),
            pltpu.VMEM((BLOCK, 1), F32),
            pltpu.VMEM((ROW_LEN, head_total * HEAD_DIM), BF16),
        ],
        compiler_params=pltpu.CompilerParams(vmem_limit_bytes=VMEM_BYTES),
        cost_estimate=pl.CostEstimate(
            flops=16 * head_total * ROW_LEN * ROW_LEN * HEAD_DIM,
            bytes_accessed=8 * ROW_LEN * 256 * 3,
            transcendentals=head_total * ROW_LEN * ROW_LEN,
        ),
        name="attend",
    )(seg_row, seg_col, qkv_low)


MESH = pl.DeviceIdType.MESH


def group_bits(dp_size):
    return min(3, dp_size.bit_length() - 1)


def place_in(dp_index, order):
    slot = 0
    for at, bit in enumerate(order):
        slot = slot + (dp_index // 2**bit) % 2 * 2**at
    return slot


def partner_of(dp_index, bit):
    return dp_index + (1 - 2 * ((dp_index // 2**bit) % 2)) * 2**bit


def enter(dp_index, mp_index, mp_size, bits):
    barrier = pltpu.get_barrier_semaphore()
    for offset in range(1, mp_size):
        pl.semaphore_signal(
            barrier, device_id={"mp": lax.rem(mp_index + offset, mp_size)}, device_id_type=MESH
        )
    for bit in range(bits):
        pl.semaphore_signal(
            barrier, device_id={"dp": partner_of(dp_index, bit)}, device_id_type=MESH
        )
    pl.semaphore_wait(barrier, mp_size - 1 + bits)


def send(src, dst, sems, at, device_id):
    return pltpu.make_async_remote_copy(
        src_ref=src,
        dst_ref=dst,
        send_sem=sems[0].at[at],
        recv_sem=sems[1].at[at],
        device_id=device_id,
        device_id_type=MESH,
    )


def gather_orders(bits):
    if bits == 3:
        return ((1, 2, 0), (2, 1, 0), (1, 2))
    return (tuple(range(bits)),) * 3


def gather_kernel(
    bits,
    frames,
    qkv_weight,
    bias_rows,
    in_weight,
    down_weight,
    head_weight,
    in_bias,
    input_all,
    qkv_low,
    in_all,
    down_all,
    head_all,
    bias_all,
    own_sems,
    frame_send,
    frame_recv,
    bias_send,
    bias_recv,
    first_send,
    first_recv,
    later_send,
    later_recv,
):
    mp_size = in_all.shape[0]
    me = lax.axis_index("mp")
    dp_index = lax.axis_index("dp")
    local_rows = frames.shape[0]
    orders = gather_orders(bits)
    shares = (in_weight, down_weight, head_weight)
    wholes = (in_all, down_all, head_all)
    enter(dp_index, me, mp_size, bits)

    def slots(which, level):
        order = orders[which]
        count = shares[which].shape[0] // 2 ** len(order)
        start = place_in(dp_index, order) // 2**level * 2**level
        return pl.ds(pl.multiple_of(start * count, 16), count * 2**level)

    def first_copy(which, offset):
        rows = slots(which, 0)
        return send(
            shares[which].at[rows],
            wholes[which].at[me, rows],
            (first_send, first_recv),
            (which, offset - 1),
            {"mp": lax.rem(me + offset, mp_size)},
        )

    def later_copy(which, level, offset):
        rows = slots(which, level)
        held = wholes[which].at[lax.rem(me + mp_size - offset, mp_size), rows]
        return send(
            held,
            held,
            (later_send, later_recv),
            (which, level, offset - 1),
            {"dp": partner_of(dp_index, orders[which][level])},
        )

    def frame_rows(index):
        return pl.ds(pl.multiple_of(index * local_rows, local_rows), local_rows)

    def frame_copy(offset):
        return send(
            frames,
            input_all.at[frame_rows(me)],
            (frame_send, frame_recv),
            offset - 1,
            {"mp": lax.rem(me + offset, mp_size)},
        )

    def bias_copy(offset):
        return send(
            in_bias,
            bias_all.at[me],
            (bias_send, bias_recv),
            offset - 1,
            {"mp": lax.rem(me + offset, mp_size)},
        )

    def project(index):
        rows = frame_rows(index)
        inputs = input_all[rows]
        for part in range(3):
            products = dot(inputs, qkv_weight[part]) + bias_rows[part : part + 1]
            qkv_low[part, rows] = products.astype(BF16)

    offsets = range(1, mp_size)
    for which in range(3):
        for offset in offsets:
            first_copy(which, offset).start()
    for offset in offsets:
        bias_copy(offset).start()
    own = [
        pltpu.make_async_copy(shares[which], wholes[which].at[me], own_sems.at[which])
        for which in range(3)
    ]
    own.append(pltpu.make_async_copy(in_bias, bias_all.at[me], own_sems.at[3]))
    for copy in own:
        copy.start()
    input_all[frame_rows(me)] = frames[...]
    project(me)
    for which in range(3):
        for offset in offsets:
            first_copy(which, offset).wait_send()
    for offset in offsets:
        frame_copy(offset).start()

    waited = 0
    for level in range(bits + 1):
        for which in range(3):
            depth = len(orders[which])
            for offset in offsets:
                if level == 0:
                    first_copy(which, offset).wait_recv()
                elif level <= depth:
                    later_copy(which, level - 1, offset).wait_recv()
                if level < depth:
                    later_copy(which, level, offset).start()
        if level > 0 and waited < mp_size - 1:
            waited += 1
            frame_copy(waited).wait_recv()
            project(lax.rem(me + mp_size - waited, mp_size))
    while waited < mp_size - 1:
        waited += 1
        frame_copy(waited).wait_recv()
        project(lax.rem(me + mp_size - waited, mp_size))
    for offset in offsets:
        bias_copy(offset).wait_recv()
        bias_copy(offset).wait_send()
        frame_copy(offset).wait_send()
        for which in range(3):
            for level in range(len(orders[which])):
                later_copy(which, level, offset).wait_send()
    for copy in own:
        copy.wait()


def gather_inputs(
    frames, qkv_weight, bias_rows, in_weight, down_weight, head_weight, in_bias, mp_size, bits
):
    local_rows, width = frames.shape
    row_total = local_rows * mp_size
    peers = mp_size - 1
    levels = max(bits, 1)
    anywhere = pl.BlockSpec(memory_space=pl.ANY)
    return pl.pallas_call(
        partial(gather_kernel, bits),
        out_shape=(
            jax.ShapeDtypeStruct((row_total, width), BF16),
            jax.ShapeDtypeStruct((3, row_total, qkv_weight.shape[2]), BF16),
            jax.ShapeDtypeStruct((mp_size,) + in_weight.shape, BF16),
            jax.ShapeDtypeStruct((mp_size,) + down_weight.shape, BF16),
            jax.ShapeDtypeStruct((mp_size,) + head_weight.shape, BF16),
            jax.ShapeDtypeStruct((mp_size,) + in_bias.shape, BF16),
        ),
        in_specs=[whole()] * 3 + [anywhere] * 4,
        out_specs=(whole(), whole()) + (anywhere,) * 4,
        scratch_shapes=[
            pltpu.SemaphoreType.DMA((4,)),
            pltpu.SemaphoreType.DMA((peers,)),
            pltpu.SemaphoreType.DMA((peers,)),
            pltpu.SemaphoreType.DMA((peers,)),
            pltpu.SemaphoreType.DMA((peers,)),
            pltpu.SemaphoreType.DMA((3, peers)),
            pltpu.SemaphoreType.DMA((3, peers)),
            pltpu.SemaphoreType.DMA((3, levels, peers)),
            pltpu.SemaphoreType.DMA((3, levels, peers)),
        ],
        compiler_params=pltpu.CompilerParams(
            collective_id=0, has_side_effects=True, vmem_limit_bytes=VMEM_BYTES
        ),
        cost_estimate=pl.CostEstimate(
            flops=6 * row_total * width * qkv_weight.shape[2],
            bytes_accessed=32 * 1024 * 1024,
            transcendentals=0,
        ),
        name="gather_inputs",
    )(frames, qkv_weight, bias_rows, in_weight, down_weight, head_weight, in_bias)


def trade_kernel(pieces, arrived, own_sem, send_sems, recv_sems):
    mp_size = pieces.shape[0]
    me = lax.axis_index("mp")
    enter(0, me, mp_size, 0)
    copies = []
    for offset in range(1, mp_size):
        target = lax.rem(me + offset, mp_size)
        copies.append(
            send(
                pieces.at[target],
                arrived.at[me],
                (send_sems, recv_sems),
                offset - 1,
                {"mp": target},
            )
        )
    for copy in copies:
        copy.start()
    own = pltpu.make_async_copy(pieces.at[me], arrived.at[me], own_sem)
    own.start()
    own.wait()
    for copy in copies:
        copy.wait()


def trade_heads(pieces):
    peers = pieces.shape[0] - 1
    anywhere = pl.BlockSpec(memory_space=pl.ANY)
    return pl.pallas_call(
        trade_kernel,
        out_shape=jax.ShapeDtypeStruct(pieces.shape, pieces.dtype),
        in_specs=[anywhere],
        out_specs=anywhere,
        scratch_shapes=[
            pltpu.SemaphoreType.DMA,
            pltpu.SemaphoreType.DMA((peers,)),
            pltpu.SemaphoreType.DMA((peers,)),
        ],
        compiler_params=pltpu.CompilerParams(collective_id=1, has_side_effects=True),
        name="trade_heads",
    )(pieces)


def reduce_orders(bits):
    if bits == 3:
        return ((0, 1, 2), (0, 2, 1), (0, 1, 2))
    return (tuple(range(bits)),) * 3


def back_kernel(
    bits,
    seg_row,
    seg_col,
    qkv,
    out_cols,
    log_total,
    grads_out,
    in_grads,
    down_grads,
    head_grads,
    traded,
    qkv_grad,
    in_sum,
    down_sum,
    head_sum,
    grads_in,
    grads,
    key_buf,
    key_cols,
    value_buf,
    query_sum,
    key_sum,
    value_sum,
    staged,
    kept,
    taken,
    last,
    keep_sems,
    grads_own,
    grads_send,
    grads_recv,
    traded_own,
    traded_send,
    traded_recv,
    level_send,
    level_recv,
    last_send,
    last_recv,
):
    head_total, mp_size = grads_out.shape[1], grads_out.shape[0]
    half = grads_out.shape[2]
    me = lax.axis_index("mp")
    dp_index = lax.axis_index("dp")
    peers = range(1, mp_size)
    orders = reduce_orders(bits)
    partials = (in_grads, down_grads, head_grads)
    sums = (in_sum, down_sum, head_sum)
    arrays = range(3)

    def target(offset):
        return lax.rem(me + offset, mp_size)

    def bit_of(which, level):
        return (dp_index // 2 ** orders[which][level]) % 2


    def level_copy(which, level):
        count = 2 ** (bits - 1 - level)
        other = (1 - bit_of(which, level)) * count
        source = partials[which] if level == 0 else taken[which][level - 1]
        return send(
            source.at[:, pl.ds(other, count)],
            taken[which][level],
            (level_send, level_recv),
            (which, level),
            {"dp": partner_of(dp_index, orders[which][level])},
        )

    def keep_copy(which):
        count = 2 ** (bits - 1)
        return pltpu.make_async_copy(
            partials[which].at[:, pl.ds(bit_of(which, 0) * count, count)],
            kept[which],
            keep_sems.at[which],
        )

    def last_copy(which, offset):
        return send(
            taken[which][bits - 1].at[target(offset)],
            last[which].at[offset - 1],
            (last_send, last_recv),
            (which, offset - 1),
            {"mp": target(offset)},
        )

    def add_level(which, level):
        level_copy(which, level).wait_recv()
        count = 2 ** (bits - 1 - level)
        if level == 0:
            keep_copy(which).wait()
        start = bit_of(which, level) * count
        into = taken[which][level]

        def add(at, _):
            for slot in range(count):
                if level == 0:
                    mine = kept[which][at, slot]
                else:
                    mine = taken[which][level - 1][at, start + slot]
                into[at, slot] = (into[at, slot].astype(F32) + mine.astype(F32)).astype(BF16)
            return 0

        lax.fori_loop(0, mp_size, add, 0)
        if level + 1 < bits:
            level_copy(which, level + 1).start()
        else:
            for offset in peers:
                last_copy(which, offset).start()

    def finish_sum(which):
        total = taken[which][bits - 1][me, 0].astype(F32)
        for offset in peers:
            last_copy(which, offset).wait_recv()
            total = total + last[which][offset - 1, 0].astype(F32)
        sums[which][...] = total.astype(BF16)


    def grads_copy(head, offset):
        return send(
            grads_out.at[target(offset), head],
            grads_in.at[head, me],
            (grads_send, grads_recv),
            (head, offset - 1),
            {"mp": target(offset)},
        )

    def grads_own_copy(head):
        return pltpu.make_async_copy(
            grads_out.at[me, head], grads_in.at[head, me], grads_own.at[head]
        )

    def traded_copy(head, offset):
        return send(
            staged.at[head, target(offset)],
            traded.at[head, me],
            (traded_send, traded_recv),
            (head, offset - 1),
            {"mp": target(offset)},
        )

    def traded_own_copy(head):
        return pltpu.make_async_copy(
            staged.at[head, me], traded.at[head, me], traded_own.at[head]
        )

    def prepare(head):
        cols = slice(head * HEAD_DIM, (head + 1) * HEAD_DIM)
        key_buf[:, :HEAD_DIM] = qkv[1, :, cols]
        key_buf[:, HEAD_DIM:] = ones_columns(ROW_LEN)
        value_buf[:, :HEAD_DIM] = qkv[2, :, cols]
        value_buf[:, HEAD_DIM:] = ones_columns(ROW_LEN)
        for step in range(BLOCKS):
            key_cols[step] = qkv[1, step * BLOCK : (step + 1) * BLOCK, cols].T
        key_sum[...] = jnp.zeros_like(key_sum)
        value_sum[...] = jnp.zeros_like(value_sum)

    def take_grads(head):
        grads_own_copy(head).wait()
        for offset in peers:
            grads_copy(head, offset).wait_recv()
        for chunk in range(mp_size):
            for side in range(2):
                start = (2 * chunk + side) * half
                grads[start : start + half] = grads_in[
                    head, chunk, :, side * HEAD_DIM : (side + 1) * HEAD_DIM
                ]

    def attend_back(head, events):
        cols = slice(head * HEAD_DIM, (head + 1) * HEAD_DIM)

        def query_block(number, _):
            rows = block_rows(number)
            queries = qkv[0, rows, cols] * SCALE
            grad_rows = grads[rows]
            seg_query = seg_row[number]
            grad_cols = grad_rows.astype(F32).T
            row_dot = jnp.sum(grad_cols * out_cols[head, number], axis=0, keepdims=True)
            grad_cols = jnp.concatenate([grad_cols.astype(BF16), as_pieces(-row_dot)], axis=0)
            query_cols = jnp.concatenate(
                [queries.astype(F32).T.astype(BF16), as_pieces(-log_total[head, number])], axis=0
            )

            def step_back(step, query_grad):
                key_rows = block_rows(step)
                same = jnp.concatenate([seg_col[key_rows]] * (BLOCK // 128), axis=1) == seg_query
                scores = dot(key_buf[key_rows], query_cols)
                soft = jnp.exp(jnp.where(same, scores, MASKED))
                soft_grad = dot(value_buf[key_rows], grad_cols)
                score_grad = (soft * soft_grad).astype(BF16)
                value_sum[key_rows] += dot(soft.astype(BF16), grad_rows)
                key_sum[key_rows] += dot(score_grad, queries)
                return query_grad + dot(key_cols[step], score_grad)

            query_grad = lax.fori_loop(0, BLOCKS, step_back, jnp.zeros((HEAD_DIM, BLOCK), F32))
            query_sum[rows] = (query_grad * SCALE).T
            for at, event in events.items():
                pl.when(number == at)(event)
            return 0

        lax.fori_loop(0, BLOCKS, query_block, 0)

    def give_grads(head):
        for part, total in enumerate((query_sum, key_sum, value_sum)):
            qkv_grad[head, :, part * HEAD_DIM : (part + 1) * HEAD_DIM] = total[...].astype(BF16)
            for chunk in range(mp_size):
                for side in range(2):
                    start = (2 * chunk + side) * half
                    staged[head, chunk, part, :, side * HEAD_DIM : (side + 1) * HEAD_DIM] = total[
                        start : start + half
                    ].astype(BF16)
        for offset in peers:
            traded_copy(head, offset).start()
        traded_own_copy(head).start()

    def advance(level):
        def event():
            for which in arrays:
                add_level(which, level)

        return event

    enter(dp_index, me, mp_size, bits)
    for offset in peers:
        grads_copy(0, offset).start()
    for which in arrays:
        level_copy(which, 0).start()
        keep_copy(which).start()
    for head in range(head_total):
        grads_own_copy(head).start()
    due = {0: (0, 1), 1: (head_total - 1, 0), 2: (head_total, 0)}
    for head in range(head_total):
        prepare(head)
        take_grads(head)
        if head == 0:
            for later in range(1, head_total):
                for offset in peers:
                    grads_copy(later, offset).start()
        attend_back(
            head,
            {at: advance(level) for level, (turn, at) in due.items() if turn == head and level < bits},
        )
        give_grads(head)
    for level, (turn, _) in due.items():
        if turn == head_total and level < bits:
            advance(level)()
    for which in arrays:
        finish_sum(which)
        for offset in peers:
            last_copy(which, offset).wait_send()
        for level in range(bits):
            level_copy(which, level).wait_send()
    for head in range(head_total):
        traded_own_copy(head).wait()
        for offset in peers:
            grads_copy(head, offset).wait_send()
            traded_copy(head, offset).wait()


def back(seg_row, seg_col, qkv_low, out_cols, log_total, grads_out, partials, bits):
    mp_size, head_total, half, lanes = grads_out.shape
    peers = mp_size - 1
    anywhere = pl.BlockSpec(memory_space=pl.ANY)
    shapes = [partial_sum.shape for partial_sum in partials]
    blocks = [shape[2:] for shape in shapes]
    return pl.pallas_call(
        partial(back_kernel, bits),
        out_shape=(
            jax.ShapeDtypeStruct((head_total, mp_size, 3, half, lanes), BF16),
            jax.ShapeDtypeStruct((head_total, ROW_LEN, 3 * HEAD_DIM), BF16),
        )
        + tuple(jax.ShapeDtypeStruct(block, BF16) for block in blocks),
        in_specs=[whole()] * 5 + [anywhere] * 4,
        out_specs=(anywhere,) + (whole(),) * 4,
        scratch_shapes=[
            pltpu.VMEM((head_total, mp_size, half, lanes), BF16),
            pltpu.VMEM((ROW_LEN, HEAD_DIM), BF16),
            pltpu.VMEM((ROW_LEN, HEAD_DIM + EXTRA), BF16),
            pltpu.VMEM((BLOCKS, HEAD_DIM, BLOCK), BF16),
            pltpu.VMEM((ROW_LEN, HEAD_DIM + EXTRA), BF16),
            pltpu.VMEM((ROW_LEN, HEAD_DIM), F32),
            pltpu.VMEM((ROW_LEN, HEAD_DIM), F32),
            pltpu.VMEM((ROW_LEN, HEAD_DIM), F32),
            pltpu.VMEM((head_total, mp_size, 3, half, lanes), BF16),
            [pltpu.VMEM((mp_size, 2 ** (bits - 1)) + block, BF16) for block in blocks],
            [
                [
                    pltpu.VMEM((mp_size, 2 ** (bits - 1 - level)) + block, BF16)
                    for level in range(bits)
                ]
                for block in blocks
            ],
            [pltpu.VMEM((peers, 1) + block, BF16) for block in blocks],
            pltpu.SemaphoreType.DMA((3,)),
            pltpu.SemaphoreType.DMA((head_total,)),
            pltpu.SemaphoreType.DMA((head_total, peers)),
            pltpu.SemaphoreType.DMA((head_total, peers)),
            pltpu.SemaphoreType.DMA((head_total,)),
            pltpu.SemaphoreType.DMA((head_total, peers)),
            pltpu.SemaphoreType.DMA((head_total, peers)),
            pltpu.SemaphoreType.DMA((3, bits)),
            pltpu.SemaphoreType.DMA((3, bits)),
            pltpu.SemaphoreType.DMA((3, peers)),
            pltpu.SemaphoreType.DMA((3, peers)),
        ],
        compiler_params=pltpu.CompilerParams(
            collective_id=2, has_side_effects=True, vmem_limit_bytes=VMEM_BYTES
        ),
        cost_estimate=pl.CostEstimate(
            flops=40 * head_total * ROW_LEN * ROW_LEN * HEAD_DIM,
            bytes_accessed=64 * 1024 * 1024,
            transcendentals=head_total * ROW_LEN * ROW_LEN,
        ),
        name="back",
    )(seg_row, seg_col, qkv_low, out_cols, log_total, grads_out, *partials)


def norm_rows(inputs, norm_gain, norm_shift):
    row_mean = jnp.mean(inputs, axis=-1, keepdims=True)
    centred = inputs - row_mean
    variance = jnp.mean(centred * centred, axis=-1, keepdims=True)
    inv_std = lax.rsqrt(variance + 1e-05)
    normed = centred * inv_std
    return (normed * norm_gain + norm_shift, normed, inv_std)


def norm_back(cotangent, normed, inv_std, norm_gain):
    scaled = cotangent * norm_gain
    adjusted = (
        scaled
        - jnp.mean(scaled, axis=-1, keepdims=True)
        - normed * jnp.mean(scaled * normed, axis=-1, keepdims=True)
    )
    return (adjusted * inv_std, jnp.sum(cotangent * normed, axis=0), jnp.sum(cotangent, axis=0))


def dp_groups():
    total = lax.axis_size("dp")
    size = min(8, total)
    groups = [list(range(start, start + size)) for start in range(0, total, size)]
    return (size, groups)


def on_device(
    frames,
    segment_ids,
    qkv_weight,
    q_bias,
    v_bias,
    out_weight,
    out_bias,
    ff_in_weight,
    ff_in_bias,
    ff_out_weight,
    ff_out_bias,
    norm_gain,
    norm_shift,
    out_grad,
):
    local_rows, width = frames.shape
    mp_size = lax.axis_size("mp")
    group, groups = dp_groups()
    place = lax.axis_index("dp") % group
    head_cols = qkv_weight.shape[3]
    head_total = head_cols // HEAD_DIM
    units = ff_in_weight.shape[2]

    bits = group_bits(lax.axis_size("dp"))
    bias_rows = jnp.stack([q_bias[0], jnp.zeros_like(q_bias[0]), v_bias[0]]).astype(F32)
    input_all, qkv_low, in_all, down_all, out_all, in_bias_all = gather_inputs(
        frames,
        qkv_weight[0],
        bias_rows,
        ff_in_weight[0].T,
        ff_out_weight[0],
        out_weight[0],
        jnp.broadcast_to(ff_in_bias, (16, units)),
        mp_size,
        bits,
    )
    in_rows = in_all.reshape(-1, width)
    down_all = down_all.reshape(-1, width)
    out_all = out_all.reshape(-1, width)
    in_bias_all = in_bias_all[:, 0].reshape(-1).astype(F32)

    qkv_rows, qkv_low = lax.optimization_barrier((qkv_weight[0], qkv_low))
    qkv_rows = (
        qkv_rows.reshape(3, width, head_total, HEAD_DIM).transpose(2, 0, 3, 1)
    ).reshape(-1, width)
    share = qkv_rows.shape[0] // group
    part = lax.dynamic_slice_in_dim(qkv_rows, place * share, share, 0)
    part = lax.all_gather(part, "mp", axis=0)
    qkv_all = lax.all_gather(part, "dp", axis=0, axis_index_groups=groups)
    qkv_all = qkv_all.transpose(1, 0, 2, 3).reshape(-1, width)

    seg_row = segment_ids.reshape(BLOCKS, 1, BLOCK)
    seg_col = jnp.broadcast_to(segment_ids[:, None], (ROW_LEN, 128))
    heads_out, out_cols, log_total = attend(seg_row, seg_col, qkv_low, mp_size)
    heads_low = trade_heads(heads_out).reshape(mp_size, local_rows // 2, 2, head_cols)
    heads_low = heads_low.transpose(2, 1, 0, 3).reshape(local_rows, width)

    gains = norm_gain[0].astype(F32)
    shifts = norm_shift[0].astype(F32)
    residual = frames.astype(F32) + (dot(heads_low, out_all) + out_bias[0].astype(F32))
    mid, normed_mid, inv_std_mid = norm_rows(residual, gains[0], shifts[0])
    mid_low = mid.astype(BF16)
    pre_act = dot_rows(mid_low, in_rows) + in_bias_all
    unit_cdf = 0.5 * (1.0 + lax.erf(pre_act * 0.5**0.5))
    hidden = (pre_act * unit_cdf).astype(BF16)
    slope = unit_cdf + pre_act * jnp.exp(-0.5 * pre_act * pre_act) * (2.0 * jnp.pi) ** (-0.5)
    summed = mid + (dot(hidden, down_all) + ff_out_bias[0].astype(F32))
    block_out, normed_out, inv_std_out = norm_rows(summed, gains[1], shifts[1])

    sum_grad, gain_out_grad, shift_out_grad = norm_back(
        out_grad.astype(F32), normed_out, inv_std_out, gains[1]
    )
    ffn_grad_low = sum_grad.astype(BF16)
    down_bias_grad = jnp.sum(ffn_grad_low, axis=0, dtype=F32)
    pre_grad_low = (dot_rows(ffn_grad_low, down_all) * slope).astype(BF16)
    in_bias_grad = jnp.sum(pre_grad_low, axis=0, dtype=F32)
    mid_grad = sum_grad + dot(pre_grad_low, in_rows)
    resid_grad, gain_mid_grad, shift_mid_grad = norm_back(
        mid_grad, normed_mid, inv_std_mid, gains[0]
    )
    attn_grad_low = resid_grad.astype(BF16)
    head_bias_grad = jnp.sum(attn_grad_low, axis=0, dtype=F32)
    heads_grad_low = dot_rows(attn_grad_low, out_all).astype(BF16)
    heads_grad = heads_grad_low.reshape(2, local_rows // 2, mp_size, head_total, HEAD_DIM)
    heads_grad = heads_grad.transpose(2, 3, 1, 0, 4).reshape(
        mp_size, head_total, local_rows // 2, 2 * HEAD_DIM
    )

    slots = 2**bits
    partials = [
        dot_cols(left, right).astype(BF16).reshape(mp_size, slots, -1, width)
        for left, right in (
            (pre_grad_low, mid_low),
            (hidden, ffn_grad_low),
            (heads_low, attn_grad_low),
        )
    ]
    head_rows = partials[2].shape[2]
    partials[2] = jnp.pad(partials[2], ((0, 0), (0, 0), (0, -head_rows % 16), (0, 0)))

    traded, qkv_grad, *grad_sums = back(
        seg_row, seg_col, qkv_low, out_cols, log_total, heads_grad, partials, bits
    )
    grad_sums = jnp.concatenate(grad_sums)
    if len(groups) > 1:
        across = [list(range(at, lax.axis_size("dp"), group)) for at in range(group)]
        grad_sums = lax.psum(grad_sums, "dp", axis_index_groups=across)
    share = [block.shape[2] for block in partials]
    grad_sums = lax.all_gather(grad_sums, "dp", axis=0, axis_index_groups=groups).astype(F32)
    grad_sums = grad_sums.reshape((2,) * bits + grad_sums.shape[1:])

    def unscramble(order, start, stop, rows):
        axes = tuple(bits - 1 - bit for bit in order)
        slices = grad_sums.transpose(axes + (bits, bits + 1))[..., start:stop, :]
        return slices.reshape(slots, stop - start, width)[:, :rows].reshape(1, -1, width)

    orders = reduce_orders(bits)
    in_weight_grad = unscramble(orders[0], 0, share[0], share[0]).transpose(0, 2, 1)
    down_weight_grad = unscramble(orders[1], share[0], share[0] + share[1], share[1])
    out_weight_grad = unscramble(orders[2], share[0] + share[1], sum(share), head_rows)

    traded = traded.reshape(head_total, mp_size, 3, local_rows // 2, 2, HEAD_DIM)
    traded = traded.transpose(4, 3, 1, 0, 2, 5).reshape(local_rows, -1)
    stream_grad = resid_grad + dot(traded, qkv_all)
    weight_sums = jnp.einsum("td,hte->hde", input_all, qkv_grad, preferred_element_type=F32)
    weight_sums = lax.psum(weight_sums.astype(BF16), "dp").astype(F32)
    qkv_weight_grad = (
        weight_sums.reshape(head_total, width, 3, HEAD_DIM)
        .transpose(2, 1, 0, 3)
        .reshape(1, 3, width, head_cols)
    )
    bias_sums = lax.psum(jnp.sum(qkv_grad, axis=1, dtype=F32), "dp")
    bias_sums = bias_sums.reshape(head_total, 3, HEAD_DIM)
    query_bias_grad = bias_sums[:, 0].reshape(1, head_cols)
    value_bias_grad = bias_sums[:, 2].reshape(1, head_cols)

    gain_grad, shift_grad, head_bias_grad, down_bias_grad, in_bias_grad = lax.psum(
        (
            jnp.stack([gain_mid_grad, gain_out_grad])[None],
            jnp.stack([shift_mid_grad, shift_out_grad])[None],
            head_bias_grad[None],
            down_bias_grad[None],
            in_bias_grad,
        ),
        ("dp", "mp"),
    )
    in_bias_grad = lax.dynamic_slice_in_dim(
        in_bias_grad, lax.axis_index("mp") * units, units, 0
    )[None]
    return (
        block_out,
        stream_grad,
        qkv_weight_grad,
        query_bias_grad,
        value_bias_grad,
        out_weight_grad,
        head_bias_grad,
        in_weight_grad,
        in_bias_grad,
        down_weight_grad,
        down_bias_grad,
        gain_grad,
        shift_grad,
    )


def solution(mesh):
    return jax.shard_map(
        on_device,
        mesh=mesh,
        in_specs=(
            P(("dp", "mp"), None),
            P("dp"),
            P(None, None, None, "mp"),
            P(None, "mp"),
            P(None, "mp"),
            P(None, "mp", None),
            P(),
            P(None, None, "mp"),
            P(None, "mp"),
            P(None, "mp", None),
            P(),
            P(),
            P(),
            P(("dp", "mp"), None),
        ),
        out_specs=(
            P(("dp", "mp"), None),
            P(("dp", "mp"), None),
            P(None, None, None, "mp"),
            P(None, "mp"),
            P(None, "mp"),
            P(None, "mp", None),
            P(),
            P(None, None, "mp"),
            P(None, "mp"),
            P(None, "mp", None),
            P(),
            P(),
            P(),
        ),
        check_vma=False,
    )
```

```python
from functools import partial

import jax
import jax.numpy as jnp
from jax import lax
from jax.experimental import pallas as pl
from jax.experimental.pallas import tpu as pltpu
from jax.sharding import PartitionSpec as P

HEAD_DIM = 64
ROW_LEN = 2304
BLOCK = 768
BLOCKS = ROW_LEN // BLOCK
EXTRA = 16
SCALE = HEAD_DIM ** (-0.5)
MASKED = -1e30
F32 = jnp.float32
BF16 = jnp.bfloat16
VMEM_BYTES = 56 * 1024 * 1024


def dot_rows(left, right):
    return lax.dot_general(left, right, (((1,), (1,)), ((), ())), preferred_element_type=F32)


def dot_cols(left, right):
    return lax.dot_general(left, right, (((0,), (0,)), ((), ())), preferred_element_type=F32)


def dot(left, right):
    return jnp.dot(left, right, preferred_element_type=F32)


def block_rows(number):
    return pl.ds(pl.multiple_of(number * BLOCK, BLOCK), BLOCK)


def as_pieces(row):
    high = row.astype(BF16).astype(F32)
    middle = (row - high).astype(BF16).astype(F32)
    last = row - high - middle
    place = lax.broadcasted_iota(jnp.int32, (EXTRA, row.shape[1]), 0)
    pieces = jnp.where(place == 0, high, jnp.where(place == 1, middle, jnp.where(place == 2, last, 0.0)))
    return pieces.astype(BF16)


def ones_columns(rows):
    place = lax.broadcasted_iota(jnp.int32, (rows, EXTRA), 1)
    return jnp.where(place < 3, 1.0, 0.0).astype(BF16)


def attend_kernel(
    seg_row, seg_col, qkv, out, out_cols, log_total, key_cols, value_buf, query_buf, peak_buf, out_buf
):
    head_total = qkv.shape[2] // HEAD_DIM
    lane = lax.broadcasted_iota(jnp.int32, (BLOCK, EXTRA), 1)
    place = lax.broadcasted_iota(jnp.int32, (EXTRA, BLOCK), 0)
    for head in range(head_total):
        cols = slice(head * HEAD_DIM, (head + 1) * HEAD_DIM)
        key_peak = jnp.zeros((1, BLOCK), F32)
        for step in range(BLOCKS):
            rows = slice(step * BLOCK, (step + 1) * BLOCK)
            keys = qkv[1, rows, cols].astype(F32).T
            key_peak = jnp.maximum(key_peak, jnp.sum(keys * keys, axis=0, keepdims=True))
            key_cols[step, :HEAD_DIM] = keys.astype(BF16)
            key_cols[step, HEAD_DIM:] = jnp.where(place == 0, 1.0, 0.0).astype(BF16)
            value_buf[step, :, :HEAD_DIM] = qkv[2, rows, cols]
            value_buf[step, :, HEAD_DIM:] = jnp.where(lane == 0, 1.0, 0.0).astype(BF16)
        key_peak = jnp.max(key_peak, axis=1, keepdims=True)

        def query_block(number, _):
            rows = block_rows(number)
            queries = qkv[0, rows, cols].astype(F32) * SCALE
            length = jnp.sum(queries * queries, axis=1, keepdims=True)
            bound = jnp.sqrt(length * key_peak).astype(BF16).astype(F32)
            query_buf[:, :HEAD_DIM] = queries.astype(BF16)
            query_buf[:, HEAD_DIM:] = jnp.where(lane == 0, -bound, 0.0).astype(BF16)

            def scores_of(step):
                same = jnp.concatenate([seg_col[rows]] * (BLOCK // 128), axis=1) == seg_row[step]
                scores = dot(query_buf[...], key_cols[step])
                return jnp.where(same, scores, MASKED)

            def mix(step, mixed):
                return mixed + dot(jnp.exp(scores_of(step)).astype(BF16), value_buf[step])

            def store(mixed, shift):
                total = mixed[:, HEAD_DIM : HEAD_DIM + 1]
                mixed = mixed[:, :HEAD_DIM] / total
                logs = jnp.broadcast_to(shift + jnp.log(total), (BLOCK, HEAD_DIM))
                both = jnp.concatenate([mixed, logs], axis=1).T
                out_cols[head, number] = both[:HEAD_DIM]
                log_total[head, number] = both[HEAD_DIM : HEAD_DIM + 1]
                out_buf[rows, cols] = mixed.astype(BF16)

            empty = jnp.zeros((BLOCK, HEAD_DIM + EXTRA), F32)
            mixed = lax.fori_loop(0, BLOCKS, mix, empty)
            store(mixed, bound)

            @pl.when(jnp.min(mixed[:, HEAD_DIM : HEAD_DIM + 1]) < 2.0**-64)
            def _():
                def top(step, peak):
                    return jnp.maximum(peak, jnp.max(scores_of(step), axis=1, keepdims=True))

                peak_buf[...] = lax.fori_loop(0, BLOCKS, top, jnp.full((BLOCK, 1), MASKED, F32))

                def mix_again(step, mixed):
                    soft = jnp.exp(scores_of(step) - peak_buf[...])
                    return mixed + dot(soft.astype(BF16), value_buf[step])

                store(lax.fori_loop(0, BLOCKS, mix_again, empty), bound + peak_buf[...])

            return 0

        lax.fori_loop(0, BLOCKS, query_block, 0)
    half = out.shape[1]
    width = head_total * HEAD_DIM
    for chunk in range(out.shape[0]):
        for side in range(2):
            start = (2 * chunk + side) * half
            out[chunk, :, side * width : (side + 1) * width] = out_buf[start : start + half]


def whole(memory_space=pltpu.VMEM):
    return pl.BlockSpec(memory_space=memory_space)


def attend(seg_row, seg_col, qkv_low, chunks):
    head_total = qkv_low.shape[2] // HEAD_DIM
    half = ROW_LEN // chunks // 2
    return pl.pallas_call(
        attend_kernel,
        out_shape=(
            jax.ShapeDtypeStruct((chunks, half, 2 * head_total * HEAD_DIM), BF16),
            jax.ShapeDtypeStruct((head_total, BLOCKS, HEAD_DIM, BLOCK), F32),
            jax.ShapeDtypeStruct((head_total, BLOCKS, 1, BLOCK), F32),
        ),
        in_specs=[whole()] * 3,
        out_specs=(whole(), whole(), whole()),
        scratch_shapes=[
            pltpu.VMEM((BLOCKS, HEAD_DIM + EXTRA, BLOCK), BF16),
            pltpu.VMEM((BLOCKS, BLOCK, HEAD_DIM + EXTRA), BF16),
            pltpu.VMEM((BLOCK, HEAD_DIM + EXTRA), BF16),
            pltpu.VMEM((BLOCK, 1), F32),
            pltpu.VMEM((ROW_LEN, head_total * HEAD_DIM), BF16),
        ],
        compiler_params=pltpu.CompilerParams(vmem_limit_bytes=VMEM_BYTES),
        cost_estimate=pl.CostEstimate(
            flops=16 * head_total * ROW_LEN * ROW_LEN * HEAD_DIM,
            bytes_accessed=8 * ROW_LEN * 256 * 3,
            transcendentals=head_total * ROW_LEN * ROW_LEN,
        ),
        name="attend",
    )(seg_row, seg_col, qkv_low)


MESH = pl.DeviceIdType.MESH


def group_bits(dp_size):
    return min(3, dp_size.bit_length() - 1)


def place_in(dp_index, order):
    slot = 0
    for at, bit in enumerate(order):
        slot = slot + (dp_index // 2**bit) % 2 * 2**at
    return slot


def partner_of(dp_index, bit):
    return dp_index + (1 - 2 * ((dp_index // 2**bit) % 2)) * 2**bit


def enter(dp_index, mp_index, mp_size, bits):
    barrier = pltpu.get_barrier_semaphore()
    for offset in range(1, mp_size):
        pl.semaphore_signal(
            barrier, device_id={"mp": lax.rem(mp_index + offset, mp_size)}, device_id_type=MESH
        )
    for bit in range(bits):
        pl.semaphore_signal(
            barrier, device_id={"dp": partner_of(dp_index, bit)}, device_id_type=MESH
        )
    pl.semaphore_wait(barrier, mp_size - 1 + bits)


def send(src, dst, sems, at, device_id):
    return pltpu.make_async_remote_copy(
        src_ref=src,
        dst_ref=dst,
        send_sem=sems[0].at[at],
        recv_sem=sems[1].at[at],
        device_id=device_id,
        device_id_type=MESH,
    )


def gather_orders(bits):
    if bits == 3:
        return ((1, 2, 0), (2, 1, 0), (1, 2, 0), (2, 1, 0))
    return (tuple(range(bits)),) * 4


SIDES = (1, -1)


def inside(index, size):
    return jnp.logical_and(index >= 0, index < size)


def gather_kernel(
    bits,
    frames,
    qkv_weight,
    bias_rows,
    in_weight,
    down_weight,
    other_weight,
    in_bias,
    input_all,
    qkv_low,
    in_all,
    down_all,
    other_all,
    bias_all,
    own_sems,
    frame_send,
    frame_recv,
    bias_send,
    bias_recv,
    first_send,
    first_recv,
    later_send,
    later_recv,
):
    mp_size = in_all.shape[0]
    me = lax.axis_index("mp")
    dp_index = lax.axis_index("dp")
    local_rows = frames.shape[0]
    orders = gather_orders(bits)
    middle = other_weight.shape[0] // 2
    parts = (
        (in_weight, in_all, 0, in_weight.shape[0]),
        (down_weight, down_all, 0, down_weight.shape[0]),
        (other_weight, other_all, 0, middle),
        (other_weight, other_all, middle, middle),
    )
    hops = range(mp_size - 1)
    ways = [(side, hop) for hop in hops for side in (0, 1)]
    enter(dp_index, me, mp_size, bits)

    def chunk_sent(side, hop):
        return me - SIDES[side] * hop

    def wrapped(index):
        return lax.rem(index + mp_size, mp_size)

    def if_sent(side, hop):
        there = inside(me + SIDES[side], mp_size)
        return pl.when(jnp.logical_and(there, inside(chunk_sent(side, hop), mp_size)))

    def if_taken(side, hop):
        return pl.when(inside(chunk_sent(side, hop + 1), mp_size))

    def neighbour(side):
        return {"mp": wrapped(me + SIDES[side])}

    def slots(which, level):
        count = parts[which][3] // 2**bits
        start = place_in(dp_index, orders[which]) // 2**level * 2**level
        return pl.ds(pl.multiple_of(parts[which][2] + start * count, 16), count * 2**level)

    def first_copy(which, side, hop):
        rows = slots(which, 0)
        place = parts[which][1].at[wrapped(chunk_sent(side, hop)), rows]
        source = parts[which][0].at[rows] if hop == 0 else place
        return send(source, place, (first_send, first_recv), (which, side, hop), neighbour(side))

    def later_copy(which, level, side, hop):
        held = parts[which][1].at[wrapped(chunk_sent(side, hop + 1)), slots(which, level)]
        partner = {"dp": partner_of(dp_index, orders[which][level])}
        return send(held, held, (later_send, later_recv), (which, level, side, hop), partner)

    def frame_rows(index):
        return pl.ds(pl.multiple_of(wrapped(index) * local_rows, local_rows), local_rows)

    def frame_copy(side, hop):
        place = input_all.at[frame_rows(chunk_sent(side, hop))]
        source = frames if hop == 0 else place
        return send(source, place, (frame_send, frame_recv), (side, hop), neighbour(side))

    def bias_copy(side, hop):
        place = bias_all.at[wrapped(chunk_sent(side, hop))]
        source = in_bias if hop == 0 else place
        return send(source, place, (bias_send, bias_recv), (side, hop), neighbour(side))

    def project(index):
        rows = frame_rows(index)
        inputs = input_all[rows]
        for part in range(3):
            products = dot(inputs, qkv_weight[part]) + bias_rows[part : part + 1]
            qkv_low[part, rows] = products.astype(BF16)

    def start_slices(side, hop):
        for which in range(4):
            first_copy(which, side, hop).start()
        bias_copy(side, hop).start()

    own = [
        pltpu.make_async_copy(shard, gathered.at[me], own_sems.at[at])
        for at, (shard, gathered) in enumerate(
            (
                (in_weight, in_all),
                (down_weight, down_all),
                (other_weight, other_all),
                (in_bias, bias_all),
            )
        )
    ]
    for side in (0, 1):
        if_sent(side, 0)(partial(start_slices, side, 0))
    for copy in own:
        copy.start()
    input_all[frame_rows(me)] = frames[...]
    project(me)

    def take_slices(side, hop):
        for which in range(4):
            first_copy(which, side, hop).wait_recv()
        bias_copy(side, hop).wait_recv()
        if hop + 1 < mp_size - 1:
            if_sent(side, hop + 1)(partial(start_slices, side, hop + 1))
        if bits:
            for which in range(4):
                later_copy(which, 0, side, hop).start()

    def sent_slices(side, hop):
        for which in range(4):
            first_copy(which, side, hop).wait_send()
        bias_copy(side, hop).wait_send()

    for side, hop in ways:
        if_taken(side, hop)(partial(take_slices, side, hop))
    for side, hop in ways:
        if_sent(side, hop)(partial(sent_slices, side, hop))
    for side in (0, 1):
        if_sent(side, 0)(lambda side=side: frame_copy(side, 0).start())

    def take_frames(side, hop):
        frame_copy(side, hop).wait_recv()
        if hop + 1 < mp_size - 1:
            if_sent(side, hop + 1)(lambda: frame_copy(side, hop + 1).start())

    def project_taken(side, hop):
        project(chunk_sent(side, hop + 1))

    def trade_slices(level, side, hop):
        for which in range(4):
            later_copy(which, level, side, hop).wait_recv()
            if level + 1 < bits:
                later_copy(which, level + 1, side, hop).start()

    for level in range(max(bits, mp_size - 1)):
        if level < bits:
            for side, hop in ways:
                if_taken(side, hop)(partial(trade_slices, level, side, hop))
        if level < mp_size - 1:
            for side in (0, 1):
                if_taken(side, level)(partial(take_frames, side, level))
            for side in (0, 1):
                if_taken(side, level)(partial(project_taken, side, level))

    def sent_rest(side, hop):
        frame_copy(side, hop).wait_send()

    def sent_later(side, hop):
        for which in range(4):
            for level in range(bits):
                later_copy(which, level, side, hop).wait_send()

    for side, hop in ways:
        if_sent(side, hop)(partial(sent_rest, side, hop))
        if_taken(side, hop)(partial(sent_later, side, hop))
    for copy in own:
        copy.wait()


def gather_inputs(frames, qkv_weight, bias_rows, weights, in_bias, mp_size, bits):
    local_rows, width = frames.shape
    row_total = local_rows * mp_size
    peers = mp_size - 1
    levels = max(bits, 1)
    anywhere = pl.BlockSpec(memory_space=pl.ANY)
    return pl.pallas_call(
        partial(gather_kernel, bits),
        out_shape=(
            jax.ShapeDtypeStruct((row_total, width), BF16),
            jax.ShapeDtypeStruct((3, row_total, qkv_weight.shape[2]), BF16),
        )
        + tuple(
            jax.ShapeDtypeStruct((mp_size,) + array.shape, BF16) for array in (*weights, in_bias)
        ),
        in_specs=[whole()] * 3 + [anywhere] * 4,
        out_specs=(whole(), whole()) + (anywhere,) * 4,
        scratch_shapes=[
            pltpu.SemaphoreType.DMA((4,)),
            pltpu.SemaphoreType.DMA((2, peers)),
            pltpu.SemaphoreType.DMA((2, peers)),
            pltpu.SemaphoreType.DMA((2, peers)),
            pltpu.SemaphoreType.DMA((2, peers)),
            pltpu.SemaphoreType.DMA((4, 2, peers)),
            pltpu.SemaphoreType.DMA((4, 2, peers)),
            pltpu.SemaphoreType.DMA((4, levels, 2, peers)),
            pltpu.SemaphoreType.DMA((4, levels, 2, peers)),
        ],
        compiler_params=pltpu.CompilerParams(
            collective_id=0, has_side_effects=True, vmem_limit_bytes=VMEM_BYTES
        ),
        cost_estimate=pl.CostEstimate(
            flops=6 * row_total * width * qkv_weight.shape[2],
            bytes_accessed=32 * 1024 * 1024,
            transcendentals=0,
        ),
        name="gather_inputs",
    )(frames, qkv_weight, bias_rows, *weights, in_bias)


def trade_kernel(pieces, arrived, own_sem, send_sems, recv_sems):
    mp_size = pieces.shape[0]
    me = lax.axis_index("mp")
    enter(0, me, mp_size, 0)
    copies = []
    for offset in range(1, mp_size):
        target = lax.rem(me + offset, mp_size)
        copies.append(
            send(
                pieces.at[target],
                arrived.at[me],
                (send_sems, recv_sems),
                offset - 1,
                {"mp": target},
            )
        )
    for copy in copies:
        copy.start()
    own = pltpu.make_async_copy(pieces.at[me], arrived.at[me], own_sem)
    own.start()
    own.wait()
    for copy in copies:
        copy.wait()


def trade_heads(pieces):
    peers = pieces.shape[0] - 1
    anywhere = pl.BlockSpec(memory_space=pl.ANY)
    return pl.pallas_call(
        trade_kernel,
        out_shape=jax.ShapeDtypeStruct(pieces.shape, pieces.dtype),
        in_specs=[anywhere],
        out_specs=anywhere,
        scratch_shapes=[
            pltpu.SemaphoreType.DMA,
            pltpu.SemaphoreType.DMA((peers,)),
            pltpu.SemaphoreType.DMA((peers,)),
        ],
        compiler_params=pltpu.CompilerParams(collective_id=1, has_side_effects=True),
        name="trade_heads",
    )(pieces)


def reduce_orders(bits):
    if bits == 3:
        return ((0, 1, 2), (0, 2, 1), (0, 1, 2))
    return (tuple(range(bits)),) * 3


def back_kernel(
    bits,
    seg_row,
    seg_col,
    qkv,
    out_cols,
    log_total,
    grads_out,
    in_grads,
    down_grads,
    head_grads,
    input_all,
    vector,
    traded,
    in_sum,
    down_sum,
    head_sum,
    proj_sum,
    vector_sum,
    bias_sum,
    grads_in,
    grads,
    qkv_grad,
    key_buf,
    key_cols,
    value_buf,
    query_sum,
    key_sum,
    value_sum,
    staged,
    kept,
    taken,
    last,
    proj,
    proj_taken,
    proj_all,
    proj_rows,
    vectors,
    vectors_taken,
    vectors_all,
    biases,
    biases_taken,
    keep_sems,
    grads_own,
    grads_send,
    grads_recv,
    traded_own,
    traded_send,
    traded_recv,
    level_send,
    level_recv,
    last_send,
    last_recv,
    back_send,
    back_recv,
    proj_send,
    proj_recv,
    vector_send,
    vector_recv,
    vector_last_send,
    vector_last_recv,
    bias_send,
    bias_recv,
):
    head_total, mp_size = grads_out.shape[1], grads_out.shape[0]
    half = grads_out.shape[2]
    me = lax.axis_index("mp")
    dp_index = lax.axis_index("dp")
    peers = range(1, mp_size)
    orders = reduce_orders(bits)
    partials = (in_grads, down_grads, head_grads)
    sums = (in_sum, down_sum, head_sum)
    arrays = range(3)

    def target(offset):
        return lax.rem(me + offset, mp_size)

    def bit_of(which, level):
        return (dp_index // 2 ** orders[which][level]) % 2


    def level_copy(which, level):
        count = 2 ** (bits - 1 - level)
        other = (1 - bit_of(which, level)) * count
        source = partials[which] if level == 0 else taken[which][level - 1]
        return send(
            source.at[:, pl.ds(other, count)],
            taken[which][level],
            (level_send, level_recv),
            (which, level),
            {"dp": partner_of(dp_index, orders[which][level])},
        )

    def keep_copy(which):
        count = 2 ** (bits - 1)
        return pltpu.make_async_copy(
            partials[which].at[:, pl.ds(bit_of(which, 0) * count, count)],
            kept[which],
            keep_sems.at[which],
        )

    def last_copy(which, offset):
        return send(
            taken[which][bits - 1].at[target(offset)],
            last[which].at[offset - 1],
            (last_send, last_recv),
            (which, offset - 1),
            {"mp": target(offset)},
        )

    def add_level(which, level):
        level_copy(which, level).wait_recv()
        count = 2 ** (bits - 1 - level)
        if level == 0:
            keep_copy(which).wait()
        start = bit_of(which, level) * count
        into = taken[which][level]

        def add(at, _):
            for slot in range(count):
                if level == 0:
                    mine = kept[which][at, slot]
                else:
                    mine = taken[which][level - 1][at, start + slot]
                into[at, slot] = (into[at, slot].astype(F32) + mine.astype(F32)).astype(BF16)
            return 0

        lax.fori_loop(0, mp_size, add, 0)
        if level + 1 < bits:
            level_copy(which, level + 1).start()
        else:
            for offset in peers:
                last_copy(which, offset).start()

    def slot_of(order):
        return place_in(dp_index, order[::-1])

    def held_slots(order, level):
        count = 2 ** (bits - 1 - level)
        return pl.ds(slot_of(order) // count * count, count)

    def spread_copy(which, level):
        held = sums[which].at[held_slots(orders[which], level)]
        partner = {"dp": partner_of(dp_index, orders[which][level])}
        return send(held, held, (back_send, back_recv), (which, level), partner)

    def finish_sum(which):
        total = taken[which][bits - 1][me, 0].astype(F32)
        for offset in peers:
            last_copy(which, offset).wait_recv()
            total = total + last[which][offset - 1, 0].astype(F32)
        sums[which][slot_of(orders[which])] = total.astype(BF16)
        spread_copy(which, bits - 1).start()

    def spread(level):
        for which in arrays:
            spread_copy(which, level).wait_recv()
            if level:
                spread_copy(which, level - 1).start()


    def proj_copy(head, level):
        count = 2 ** (bits - 1 - level)
        other = (1 - bit_of(0, level)) * count
        source = proj[head] if level == 0 else proj_taken[head][level - 1]
        return send(
            source.at[pl.ds(other, count)],
            proj_taken[head][level],
            (proj_send, proj_recv),
            (0, head, level),
            {"dp": partner_of(dp_index, orders[0][level])},
        )

    def proj_spread_copy(head, level):
        held = proj_all[head].at[held_slots(orders[0], level)]
        partner = {"dp": partner_of(dp_index, orders[0][level])}
        return send(held, held, (proj_send, proj_recv), (1, head, level), partner)

    def add_proj(head, level):
        proj_copy(head, level).wait_recv()
        count = 2 ** (bits - 1 - level)
        start = bit_of(0, level) * count
        into = proj_taken[head][level]
        for slot in range(count):
            mine = proj[head][start + slot] if level == 0 else proj_taken[head][level - 1][start + slot]
            into[slot] = (into[slot].astype(F32) + mine.astype(F32)).astype(BF16)
        if level + 1 < bits:
            proj_copy(head, level + 1).start()
        else:
            proj_all[head][slot_of(orders[0])] = into[0]
            proj_spread_copy(head, level).start()

    def spread_proj(head, level):
        proj_spread_copy(head, level).wait_recv()
        if level:
            proj_spread_copy(head, level - 1).start()

    def finish_proj(head):
        cols = slice(head * HEAD_DIM, (head + 1) * HEAD_DIM)
        slot_rows = proj_all[head].shape[1]
        for slot in range(2**bits):
            proj_rows[slot * slot_rows : (slot + 1) * slot_rows] = proj_all[head][slot].astype(F32)
        for part in range(3):
            columns = proj_rows[part * HEAD_DIM : (part + 1) * HEAD_DIM].T
            proj_sum[part, :, cols] = columns.astype(BF16)


    def vector_copy(level):
        return send(
            vectors[level],
            vectors_taken[level],
            (vector_send, vector_recv),
            level,
            {"dp": partner_of(dp_index, level)},
        )

    def vector_last_copy(offset):
        return send(
            vectors[bits],
            vectors_all.at[me],
            (vector_last_send, vector_last_recv),
            offset - 1,
            {"mp": target(offset)},
        )

    def add_vector(level):
        vector_copy(level).wait_recv()
        vectors[level + 1][...] = vectors[level][...] + vectors_taken[level][...]
        if level + 1 < bits:
            vector_copy(level + 1).start()
        else:
            vectors_all[me] = vectors[bits][...]
            for offset in peers:
                vector_last_copy(offset).start()

    def finish_vector():
        for offset in peers:
            vector_last_copy(offset).wait_recv()
        total = vectors_all[0]
        for index in peers:
            total = total + vectors_all[index]
        vector_sum[...] = total

    def bias_copy(level):
        return send(
            biases[level],
            biases_taken[level],
            (bias_send, bias_recv),
            level,
            {"dp": partner_of(dp_index, level)},
        )

    def add_bias(level):
        bias_copy(level).wait_recv()
        biases[level + 1][...] = biases[level][...] + biases_taken[level][...]
        if level + 1 < bits:
            bias_copy(level + 1).start()
        else:
            bias_sum[...] = biases[bits][...]


    def grads_copy(head, offset):
        return send(
            grads_out.at[target(offset), head],
            grads_in.at[head, me],
            (grads_send, grads_recv),
            (head, offset - 1),
            {"mp": target(offset)},
        )

    def grads_own_copy(head):
        return pltpu.make_async_copy(
            grads_out.at[me, head], grads_in.at[head, me], grads_own.at[head]
        )

    def traded_copy(head, offset):
        return send(
            staged.at[head, target(offset)],
            traded.at[head, me],
            (traded_send, traded_recv),
            (head, offset - 1),
            {"mp": target(offset)},
        )

    def traded_own_copy(head):
        return pltpu.make_async_copy(
            staged.at[head, me], traded.at[head, me], traded_own.at[head]
        )

    def prepare(head):
        cols = slice(head * HEAD_DIM, (head + 1) * HEAD_DIM)
        key_buf[:, :HEAD_DIM] = qkv[1, :, cols]
        key_buf[:, HEAD_DIM:] = ones_columns(ROW_LEN)
        value_buf[:, :HEAD_DIM] = qkv[2, :, cols]
        value_buf[:, HEAD_DIM:] = ones_columns(ROW_LEN)
        for step in range(BLOCKS):
            key_cols[step] = qkv[1, step * BLOCK : (step + 1) * BLOCK, cols].T
        key_sum[...] = jnp.zeros_like(key_sum)
        value_sum[...] = jnp.zeros_like(value_sum)

    def take_grads(head):
        grads_own_copy(head).wait()
        for offset in peers:
            grads_copy(head, offset).wait_recv()
        for chunk in range(mp_size):
            for side in range(2):
                start = (2 * chunk + side) * half
                grads[start : start + half] = grads_in[
                    head, chunk, :, side * HEAD_DIM : (side + 1) * HEAD_DIM
                ]

    def attend_back(head, events):
        cols = slice(head * HEAD_DIM, (head + 1) * HEAD_DIM)

        def query_block(number, _):
            rows = block_rows(number)
            queries = qkv[0, rows, cols] * SCALE
            grad_rows = grads[rows]
            seg_query = seg_row[number]
            grad_cols = grad_rows.astype(F32).T
            row_dot = jnp.sum(grad_cols * out_cols[head, number], axis=0, keepdims=True)
            grad_cols = jnp.concatenate([grad_cols.astype(BF16), as_pieces(-row_dot)], axis=0)
            query_cols = jnp.concatenate(
                [queries.astype(F32).T.astype(BF16), as_pieces(-log_total[head, number])], axis=0
            )

            def step_back(step, query_grad):
                key_rows = block_rows(step)
                same = jnp.concatenate([seg_col[key_rows]] * (BLOCK // 128), axis=1) == seg_query
                scores = dot(key_buf[key_rows], query_cols)
                soft = jnp.exp(jnp.where(same, scores, MASKED))
                soft_grad = dot(value_buf[key_rows], grad_cols)
                score_grad = (soft * soft_grad).astype(BF16)
                value_sum[key_rows] += dot(soft.astype(BF16), grad_rows)
                key_sum[key_rows] += dot(score_grad, queries)
                return query_grad + dot(key_cols[step], score_grad)

            query_grad = lax.fori_loop(0, BLOCKS, step_back, jnp.zeros((HEAD_DIM, BLOCK), F32))
            query_sum[rows] = (query_grad * SCALE).T
            for at, acts in events.items():

                @pl.when(number == at)
                def _():
                    for act in acts:
                        act()

            return 0

        lax.fori_loop(0, BLOCKS, query_block, 0)

    def give_grads(head):
        for part, total in enumerate((query_sum, key_sum, value_sum)):
            low = total[...].astype(BF16)
            qkv_grad[:, part * HEAD_DIM : (part + 1) * HEAD_DIM] = low
            if part != 1:
                cols = slice(head * HEAD_DIM, (head + 1) * HEAD_DIM)
                sum_low = jnp.sum(low.astype(F32), axis=0, keepdims=True)
                biases[0][part : part + 1, cols] = sum_low
            for chunk in range(mp_size):
                for side in range(2):
                    start = (2 * chunk + side) * half
                    staged[head, chunk, part, :, side * HEAD_DIM : (side + 1) * HEAD_DIM] = total[
                        start : start + half
                    ].astype(BF16)

    def start_trade(head):
        for offset in peers:
            traded_copy(head, offset).start()
        traded_own_copy(head).start()

    def start_proj(head):
        products = dot_cols(qkv_grad[...], input_all[...])
        slot_rows = proj[head].shape[1]
        for slot in range(2**bits):
            proj[head][slot] = products[slot * slot_rows : (slot + 1) * slot_rows].astype(BF16)
        proj_copy(head, 0).start()

    def advance(level):
        for which in arrays:
            add_level(which, level)

    events = {}

    def due(head, number, act, *which):
        events.setdefault((head, number), []).append(partial(act, *which))

    levels = list(range(bits))
    for level, when in zip(levels, ((0, 1), (1, 2), (2, 1))):
        due(*when, advance, level)
    for level, when in zip(levels, ((0, 0), (0, 1), (0, 2))):
        due(*when, add_vector, level)
    due(1, 0, finish_vector)
    for at, level in enumerate(levels):
        due(1, at, add_proj, 0, level)
    for at, level in enumerate(levels[::-1]):
        due(2, at, spread_proj, 0, level)
    for at, level in enumerate(levels):
        due(2, at, add_proj, 1, level)

    enter(dp_index, me, mp_size, bits)
    for offset in peers:
        grads_copy(0, offset).start()
    vectors[0][...] = vector[...]
    vector_copy(0).start()
    for which in arrays:
        level_copy(which, 0).start()
        keep_copy(which).start()
    for head in range(head_total):
        grads_own_copy(head).start()
    biases[0][...] = jnp.zeros_like(biases[0])
    for head in range(head_total):
        prepare(head)
        take_grads(head)
        if head == 0:
            for later in range(1, head_total):
                for offset in peers:
                    grads_copy(later, offset).start()
        attend_back(head, {number: acts for (turn, number), acts in events.items() if turn == head})
        give_grads(head)
        if head + 1 < head_total:
            start_trade(head)
        start_proj(head)
    final = head_total - 1
    bias_copy(0).start()
    for which in arrays:
        for offset in peers:
            last_copy(which, offset).wait_send()
    start_trade(final)
    for level in levels:
        add_proj(final, level)
        add_bias(level)
    for which in arrays:
        finish_sum(which)
    for level in levels[::-1]:
        spread_proj(final, level)
        spread_proj(final - 1, level)
        spread(level)
    for head in range(head_total):
        finish_proj(head)
        traded_own_copy(head).wait()
        for offset in peers:
            grads_copy(head, offset).wait_send()
            traded_copy(head, offset).wait()
        for level in levels:
            proj_copy(head, level).wait_send()
            proj_spread_copy(head, level).wait_send()
    for level in levels:
        vector_copy(level).wait_send()
        bias_copy(level).wait_send()
        for which in arrays:
            level_copy(which, level).wait_send()
            spread_copy(which, level).wait_send()
    for offset in peers:
        vector_last_copy(offset).wait_send()


def back(
    seg_row, seg_col, qkv_low, out_cols, log_total, grads_out, partials, input_all, vector, bits
):
    mp_size, head_total, half, lanes = grads_out.shape
    peers = mp_size - 1
    slots = 2**bits
    width = input_all.shape[1]
    anywhere = pl.BlockSpec(memory_space=pl.ANY)
    blocks = [partial_sum.shape[2:] for partial_sum in partials]
    proj_block = (3 * HEAD_DIM // slots, width)
    bias_block = (8, 2 * 128)

    def halves(shape, dtype, lead=()):
        return [pltpu.VMEM(lead + (slots >> (level + 1),) + shape, dtype) for level in range(bits)]

    def sems(*shapes):
        return [pltpu.SemaphoreType.DMA(shape) for shape in shapes for _ in range(2)]

    return pl.pallas_call(
        partial(back_kernel, bits),
        out_shape=(jax.ShapeDtypeStruct((head_total, mp_size, 3, half, lanes), BF16),)
        + tuple(jax.ShapeDtypeStruct((slots,) + block, BF16) for block in blocks)
        + (
            jax.ShapeDtypeStruct((3, width, head_total * HEAD_DIM), BF16),
            jax.ShapeDtypeStruct(vector.shape, F32),
            jax.ShapeDtypeStruct(bias_block, F32),
        ),
        in_specs=[whole()] * 5 + [anywhere] * 4 + [whole()] * 2,
        out_specs=(anywhere,) + (whole(),) * 6,
        scratch_shapes=[
            pltpu.VMEM((head_total, mp_size, half, lanes), BF16),
            pltpu.VMEM((ROW_LEN, HEAD_DIM), BF16),
            pltpu.VMEM((ROW_LEN, 3 * HEAD_DIM), BF16),
            pltpu.VMEM((ROW_LEN, HEAD_DIM + EXTRA), BF16),
            pltpu.VMEM((BLOCKS, HEAD_DIM, BLOCK), BF16),
            pltpu.VMEM((ROW_LEN, HEAD_DIM + EXTRA), BF16),
            pltpu.VMEM((ROW_LEN, HEAD_DIM), F32),
            pltpu.VMEM((ROW_LEN, HEAD_DIM), F32),
            pltpu.VMEM((ROW_LEN, HEAD_DIM), F32),
            pltpu.VMEM((head_total, mp_size, 3, half, lanes), BF16),
            [pltpu.VMEM((mp_size, slots // 2) + block, BF16) for block in blocks],
            [halves(block, BF16, (mp_size,)) for block in blocks],
            [pltpu.VMEM((peers, 1) + block, BF16) for block in blocks],
            [pltpu.VMEM((slots,) + proj_block, BF16) for _ in range(head_total)],
            [halves(proj_block, BF16) for _ in range(head_total)],
            [pltpu.VMEM((slots,) + proj_block, BF16) for _ in range(head_total)],
            pltpu.VMEM((3 * HEAD_DIM, width), F32),
            [pltpu.VMEM(vector.shape, F32) for _ in range(bits + 1)],
            [pltpu.VMEM(vector.shape, F32) for _ in range(bits)],
            pltpu.VMEM((mp_size,) + vector.shape, F32),
            [pltpu.VMEM(bias_block, F32) for _ in range(bits + 1)],
            [pltpu.VMEM(bias_block, F32) for _ in range(bits)],
            pltpu.SemaphoreType.DMA((3,)),
            pltpu.SemaphoreType.DMA((head_total,)),
            *sems((head_total, peers)),
            pltpu.SemaphoreType.DMA((head_total,)),
            *sems(
                (head_total, peers),
                (3, bits),
                (3, peers),
                (3, bits),
                (2, head_total, bits),
                (bits,),
                (peers,),
                (bits,),
            ),
        ],
        compiler_params=pltpu.CompilerParams(
            collective_id=2, has_side_effects=True, vmem_limit_bytes=VMEM_BYTES
        ),
        cost_estimate=pl.CostEstimate(
            flops=40 * head_total * ROW_LEN * ROW_LEN * HEAD_DIM,
            bytes_accessed=64 * 1024 * 1024,
            transcendentals=head_total * ROW_LEN * ROW_LEN,
        ),
        name="back",
    )(
        seg_row,
        seg_col,
        qkv_low,
        out_cols,
        log_total,
        grads_out,
        *partials,
        input_all,
        vector,
    )


def norm_rows(inputs, norm_gain, norm_shift):
    row_mean = jnp.mean(inputs, axis=-1, keepdims=True)
    centred = inputs - row_mean
    variance = jnp.mean(centred * centred, axis=-1, keepdims=True)
    inv_std = lax.rsqrt(variance + 1e-05)
    normed = centred * inv_std
    return (normed * norm_gain + norm_shift, normed, inv_std)


def norm_back(cotangent, normed, inv_std, norm_gain):
    scaled = cotangent * norm_gain
    adjusted = (
        scaled
        - jnp.mean(scaled, axis=-1, keepdims=True)
        - normed * jnp.mean(scaled * normed, axis=-1, keepdims=True)
    )
    return (adjusted * inv_std, jnp.sum(cotangent * normed, axis=0), jnp.sum(cotangent, axis=0))


def dp_groups():
    total = lax.axis_size("dp")
    size = min(8, total)
    groups = [list(range(start, start + size)) for start in range(0, total, size)]
    return (size, groups)


def on_device(
    frames,
    segment_ids,
    qkv_weight,
    q_bias,
    v_bias,
    out_weight,
    out_bias,
    ff_in_weight,
    ff_in_bias,
    ff_out_weight,
    ff_out_bias,
    norm_gain,
    norm_shift,
    out_grad,
):
    local_rows, width = frames.shape
    mp_size = lax.axis_size("mp")
    group, groups = dp_groups()
    head_cols = qkv_weight.shape[3]
    head_total = head_cols // HEAD_DIM
    units = ff_in_weight.shape[2]

    bits = group_bits(lax.axis_size("dp"))
    bias_rows = jnp.stack([q_bias[0], jnp.zeros_like(q_bias[0]), v_bias[0]]).astype(F32)
    qkv_rows = (
        qkv_weight[0].reshape(3, width, head_total, HEAD_DIM).transpose(2, 0, 3, 1)
    ).reshape(-1, width)
    input_all, qkv_low, in_all, down_all, other_all, in_bias_all = gather_inputs(
        frames,
        qkv_weight[0],
        bias_rows,
        (ff_in_weight[0].T, ff_out_weight[0], jnp.concatenate([out_weight[0], qkv_rows])),
        jnp.broadcast_to(ff_in_bias, (16, units)),
        mp_size,
        bits,
    )
    in_rows = in_all.reshape(-1, width)
    down_all = down_all.reshape(-1, width)
    out_all = other_all[:, :head_cols].reshape(-1, width)
    qkv_all = other_all[:, head_cols:].reshape(-1, width)
    in_bias_all = in_bias_all[:, 0].reshape(-1).astype(F32)

    seg_row = segment_ids.reshape(BLOCKS, 1, BLOCK)
    seg_col = jnp.broadcast_to(segment_ids[:, None], (ROW_LEN, 128))
    heads_out, out_cols, log_total = attend(seg_row, seg_col, qkv_low, mp_size)
    heads_low = trade_heads(heads_out).reshape(mp_size, local_rows // 2, 2, head_cols)
    heads_low = heads_low.transpose(2, 1, 0, 3).reshape(local_rows, width)

    gains = norm_gain[0].astype(F32)
    shifts = norm_shift[0].astype(F32)
    residual = frames.astype(F32) + (dot(heads_low, out_all) + out_bias[0].astype(F32))
    mid, normed_mid, inv_std_mid = norm_rows(residual, gains[0], shifts[0])
    mid_low = mid.astype(BF16)
    pre_act = dot_rows(mid_low, in_rows) + in_bias_all
    unit_cdf = 0.5 * (1.0 + lax.erf(pre_act * 0.5**0.5))
    hidden = (pre_act * unit_cdf).astype(BF16)
    slope = unit_cdf + pre_act * jnp.exp(-0.5 * pre_act * pre_act) * (2.0 * jnp.pi) ** (-0.5)
    summed = mid + (dot(hidden, down_all) + ff_out_bias[0].astype(F32))
    block_out, normed_out, inv_std_out = norm_rows(summed, gains[1], shifts[1])

    sum_grad, gain_out_grad, shift_out_grad = norm_back(
        out_grad.astype(F32), normed_out, inv_std_out, gains[1]
    )
    ffn_grad_low = sum_grad.astype(BF16)
    down_bias_grad = jnp.sum(ffn_grad_low, axis=0, dtype=F32)
    pre_grad_low = (dot_rows(ffn_grad_low, down_all) * slope).astype(BF16)
    in_bias_grad = jnp.sum(pre_grad_low, axis=0, dtype=F32)
    mid_grad = sum_grad + dot(pre_grad_low, in_rows)
    resid_grad, gain_mid_grad, shift_mid_grad = norm_back(
        mid_grad, normed_mid, inv_std_mid, gains[0]
    )
    attn_grad_low = resid_grad.astype(BF16)
    head_bias_grad = jnp.sum(attn_grad_low, axis=0, dtype=F32)
    heads_grad_low = dot_rows(attn_grad_low, out_all).astype(BF16)
    heads_grad = heads_grad_low.reshape(2, local_rows // 2, mp_size, head_total, HEAD_DIM)
    heads_grad = heads_grad.transpose(2, 3, 1, 0, 4).reshape(
        mp_size, head_total, local_rows // 2, 2 * HEAD_DIM
    )

    slots = 2**bits
    partials = [
        dot_cols(left, right).astype(BF16).reshape(mp_size, slots, -1, width)
        for left, right in (
            (pre_grad_low, mid_low),
            (hidden, ffn_grad_low),
            (heads_low, attn_grad_low),
        )
    ]
    head_rows = partials[2].shape[2]
    partials[2] = jnp.pad(partials[2], ((0, 0), (0, 0), (0, -head_rows % 16), (0, 0)))

    vector = jnp.concatenate(
        [
            gain_mid_grad[None],
            gain_out_grad[None],
            shift_mid_grad[None],
            shift_out_grad[None],
            head_bias_grad[None],
            down_bias_grad[None],
            in_bias_grad.reshape(mp_size, units),
        ]
    )
    vector = jnp.pad(vector, ((0, -vector.shape[0] % 8), (0, 0)))
    traded, *summed = back(
        seg_row,
        seg_col,
        qkv_low,
        out_cols,
        log_total,
        heads_grad,
        partials,
        input_all,
        vector,
        bits,
    )
    summed = [array.astype(F32) for array in summed]
    if len(groups) > 1:
        across = [list(range(at, lax.axis_size("dp"), group)) for at in range(group)]
        summed = lax.psum(summed, "dp", axis_index_groups=across)
    in_sum, down_sum, head_sum, proj_sum, vector_sum, bias_sum = summed
    in_weight_grad = in_sum.reshape(units, width).T[None]
    down_weight_grad = down_sum.reshape(1, units, width)
    out_weight_grad = head_sum[:, :head_rows].reshape(1, head_cols, width)
    qkv_weight_grad = proj_sum[None]
    query_bias_grad = bias_sum[:1, :head_cols]
    value_bias_grad = bias_sum[2:3, :head_cols]
    gain_grad = vector_sum[None, 0:2]
    shift_grad = vector_sum[None, 2:4]
    head_bias_grad = vector_sum[4:5]
    down_bias_grad = vector_sum[5:6]
    in_bias_grad = lax.dynamic_slice_in_dim(vector_sum, 6 + lax.axis_index("mp"), 1, 0)

    traded = traded.reshape(head_total, mp_size, 3, local_rows // 2, 2, HEAD_DIM)
    traded = traded.transpose(4, 3, 1, 0, 2, 5).reshape(local_rows, -1)
    stream_grad = resid_grad + dot(traded, qkv_all)
    return (
        block_out,
        stream_grad,
        qkv_weight_grad,
        query_bias_grad,
        value_bias_grad,
        out_weight_grad,
        head_bias_grad,
        in_weight_grad,
        in_bias_grad,
        down_weight_grad,
        down_bias_grad,
        gain_grad,
        shift_grad,
    )


def solution(mesh):
    return jax.shard_map(
        on_device,
        mesh=mesh,
        in_specs=(
            P(("dp", "mp"), None),
            P("dp"),
            P(None, None, None, "mp"),
            P(None, "mp"),
            P(None, "mp"),
            P(None, "mp", None),
            P(),
            P(None, None, "mp"),
            P(None, "mp"),
            P(None, "mp", None),
            P(),
            P(),
            P(),
            P(("dp", "mp"), None),
        ),
        out_specs=(
            P(("dp", "mp"), None),
            P(("dp", "mp"), None),
            P(None, None, None, "mp"),
            P(None, "mp"),
            P(None, "mp"),
            P(None, "mp", None),
            P(),
            P(None, None, "mp"),
            P(None, "mp"),
            P(None, "mp", None),
            P(),
            P(),
            P(),
        ),
        check_vma=False,
    )
```

```python
from functools import partial

import jax
import jax.numpy as jnp
from jax import lax
from jax.experimental import pallas as pl
from jax.experimental.pallas import tpu as pltpu
from jax.sharding import PartitionSpec as P

HEAD_DIM = 64
ROW_LEN = 2304
BLOCK = 768
BLOCKS = ROW_LEN // BLOCK
EXTRA = 16
SCALE = HEAD_DIM ** (-0.5)
MASKED = -1e30
F32 = jnp.float32
BF16 = jnp.bfloat16
VMEM_BYTES = 56 * 1024 * 1024


def dot_rows(left, right):
    return lax.dot_general(left, right, (((1,), (1,)), ((), ())), preferred_element_type=F32)


def dot_cols(left, right):
    return lax.dot_general(left, right, (((0,), (0,)), ((), ())), preferred_element_type=F32)


def dot(left, right):
    return jnp.dot(left, right, preferred_element_type=F32)


def block_rows(number):
    return pl.ds(pl.multiple_of(number * BLOCK, BLOCK), BLOCK)


def as_pieces(row):
    high = row.astype(BF16).astype(F32)
    middle = (row - high).astype(BF16).astype(F32)
    last = row - high - middle
    place = lax.broadcasted_iota(jnp.int32, (EXTRA, row.shape[1]), 0)
    pieces = jnp.where(place == 0, high, jnp.where(place == 1, middle, jnp.where(place == 2, last, 0.0)))
    return pieces.astype(BF16)


def ones_columns(rows):
    place = lax.broadcasted_iota(jnp.int32, (rows, EXTRA), 1)
    return jnp.where(place < 3, 1.0, 0.0).astype(BF16)


def whole(memory_space=pltpu.VMEM):
    return pl.BlockSpec(memory_space=memory_space)


MESH = pl.DeviceIdType.MESH


def group_bits(dp_size):
    return min(3, dp_size.bit_length() - 1)


def place_in(dp_index, order):
    slot = 0
    for at, bit in enumerate(order):
        slot = slot + (dp_index // 2**bit) % 2 * 2**at
    return slot


def partner_of(dp_index, bit):
    return dp_index + (1 - 2 * ((dp_index // 2**bit) % 2)) * 2**bit


def enter(dp_index, mp_index, mp_size, bits):
    barrier = pltpu.get_barrier_semaphore()
    for offset in range(1, mp_size):
        pl.semaphore_signal(
            barrier, device_id={"mp": lax.rem(mp_index + offset, mp_size)}, device_id_type=MESH
        )
    for bit in range(bits):
        pl.semaphore_signal(
            barrier, device_id={"dp": partner_of(dp_index, bit)}, device_id_type=MESH
        )
    pl.semaphore_wait(barrier, mp_size - 1 + bits)


def send(src, dst, sems, at, device_id):
    return pltpu.make_async_remote_copy(
        src_ref=src,
        dst_ref=dst,
        send_sem=sems[0].at[at],
        recv_sem=sems[1].at[at],
        device_id=device_id,
        device_id_type=MESH,
    )


def gather_orders(bits):
    if bits == 3:
        return ((1, 2, 0), (2, 1, 0), (1, 2, 0), (2, 1, 0))
    return (tuple(range(bits)),) * 4


SIDES = (1, -1)


def inside(index, size):
    return jnp.logical_and(index >= 0, index < size)


def front_kernel(
    bits,
    frames,
    qkv_weight,
    bias_rows,
    seg_row,
    seg_col,
    in_weight,
    down_weight,
    out_weight,
    in_bias,
    input_all,
    qkv_low,
    in_all,
    down_all,
    other_all,
    bias_all,
    out_cols,
    log_total,
    heads_low,
    key_cols,
    value_buf,
    out_buf,
    staged,
    heads_in,
    own_sems,
    frame_send,
    frame_recv,
    bias_send,
    bias_recv,
    first_send,
    first_recv,
    later_send,
    later_recv,
    heads_own,
    heads_send,
    heads_recv,
):
    mp_size = in_all.shape[0]
    me = lax.axis_index("mp")
    dp_index = lax.axis_index("dp")
    local_rows = frames.shape[0]
    half = local_rows // 2
    head_total = out_cols.shape[0]
    orders = gather_orders(bits)
    head_rows = out_weight.shape[0]
    other_rows = other_all.shape[1]
    middle = other_rows // 2
    parts = (
        (in_weight, in_all, 0, in_weight.shape[0]),
        (down_weight, down_all, 0, down_weight.shape[0]),
        (other_all.at[me], other_all, 0, middle),
        (other_all.at[me], other_all, middle, middle),
    )
    hops = range(mp_size - 1)
    ways = [(side, hop) for hop in hops for side in (0, 1)]
    enter(dp_index, me, mp_size, bits)

    def chunk_sent(side, hop):
        return me - SIDES[side] * hop

    def wrapped(index):
        return lax.rem(index + mp_size, mp_size)

    def sends(side, hop):
        there = inside(me + SIDES[side], mp_size)
        return jnp.logical_and(there, inside(chunk_sent(side, hop), mp_size))

    def takes(side, hop):
        return inside(chunk_sent(side, hop + 1), mp_size)

    def if_sent(side, hop):
        return pl.when(sends(side, hop))

    def if_taken(side, hop):
        return pl.when(takes(side, hop))

    def neighbour(side):
        return {"mp": wrapped(me + SIDES[side])}

    def slots(which, level):
        count = parts[which][3] // 2**bits
        start = place_in(dp_index, orders[which]) // 2**level * 2**level
        return pl.ds(pl.multiple_of(parts[which][2] + start * count, 16), count * 2**level)

    def first_copy(which, side, hop):
        rows = slots(which, 0)
        place = parts[which][1].at[wrapped(chunk_sent(side, hop)), rows]
        source = parts[which][0].at[rows] if hop == 0 else place
        return send(source, place, (first_send, first_recv), (which, side, hop), neighbour(side))

    def later_copy(which, level, side, hop):
        held = parts[which][1].at[wrapped(chunk_sent(side, hop + 1)), slots(which, level)]
        partner = {"dp": partner_of(dp_index, orders[which][level])}
        return send(held, held, (later_send, later_recv), (which, level, side, hop), partner)

    def frame_rows(index):
        return pl.ds(pl.multiple_of(wrapped(index) * local_rows, local_rows), local_rows)

    def frame_copy(side, hop):
        place = input_all.at[frame_rows(chunk_sent(side, hop))]
        source = frames if hop == 0 else place
        return send(source, place, (frame_send, frame_recv), (side, hop), neighbour(side))

    def bias_copy(side, hop):
        place = bias_all.at[wrapped(chunk_sent(side, hop))]
        source = in_bias if hop == 0 else place
        return send(source, place, (bias_send, bias_recv), (side, hop), neighbour(side))

    def project(index):
        rows = frame_rows(index)
        inputs = input_all[rows]
        for part in range(3):
            products = dot_rows(inputs, qkv_weight[part]) + bias_rows[part : part + 1]
            qkv_low[part, rows] = products.astype(BF16)

    def start_slices(side, hop):
        for which in range(4):
            first_copy(which, side, hop).start()
        bias_copy(side, hop).start()

    def take_slices(side, hop):
        for which in range(4):
            first_copy(which, side, hop).wait_recv()
        bias_copy(side, hop).wait_recv()
        if hop + 1 < mp_size - 1:
            if_sent(side, hop + 1)(partial(start_slices, side, hop + 1))
        if bits:
            for which in range(4):
                later_copy(which, 0, side, hop).start()

    def trade_slices(level, side, hop):
        for which in range(4):
            later_copy(which, level, side, hop).wait_recv()
            if level + 1 < bits:
                later_copy(which, level + 1, side, hop).start()

    def take_hop(hop):
        for side in (0, 1):
            if_taken(side, hop)(partial(take_slices, side, hop))

    def trade_hop(level, hop):
        if level < bits:
            for side in (0, 1):
                if_taken(side, hop)(partial(trade_slices, level, side, hop))


    for side in (0, 1):
        if_sent(side, 0)(lambda side=side: frame_copy(side, 0).start())
    qkv_rows = [
        pltpu.make_async_copy(
            qkv_weight.at[part],
            other_all.at[me, pl.ds(head_rows * (part + 1), head_rows)],
            own_sems.at[part],
        )
        for part in range(3)
    ]
    own = [
        pltpu.make_async_copy(shard, gathered, own_sems.at[3 + at])
        for at, (shard, gathered) in enumerate(
            (
                (out_weight, other_all.at[me, pl.ds(0, head_rows)]),
                (in_weight, in_all.at[me]),
                (down_weight, down_all.at[me]),
                (in_bias, bias_all.at[me]),
            )
        )
    ]
    for copy in qkv_rows + own:
        copy.start()
    input_all[frame_rows(me)] = frames[...]
    project(me)
    for copy in qkv_rows + own:
        copy.wait()

    def take_frames(side, hop):
        frame_copy(side, hop).wait_recv()
        if hop + 1 < mp_size - 1:
            if_sent(side, hop + 1)(lambda: frame_copy(side, hop + 1).start())

    def project_taken(side, hop):
        project(chunk_sent(side, hop + 1))

    for hop in hops:
        for side in (0, 1):
            if_taken(side, hop)(partial(take_frames, side, hop))
        for side in (0, 1):
            free = sends(side, hop)
            if hop + 1 < mp_size - 1:
                free = jnp.logical_and(free, jnp.logical_not(sends(side, hop + 1)))
            pl.when(free)(partial(start_slices, side, 0))
        for side in (0, 1):
            if_taken(side, hop)(partial(project_taken, side, hop))

    events = {}

    def due(at, act, *which):
        events.setdefault((at // BLOCKS, at % BLOCKS), []).append(partial(act, *which))

    schedule = (
        (1, take_hop, 0),
        (3, take_hop, 1),
        (4, trade_hop, 0, 0),
        (6, take_hop, 2),
        (6, trade_hop, 0, 1),
        (7, trade_hop, 1, 0),
    )
    for entry in schedule:
        if entry[-1] < mp_size - 1:
            due(*entry)

    def attend(head):
        cols = slice(head * HEAD_DIM, (head + 1) * HEAD_DIM)
        lane = lax.broadcasted_iota(jnp.int32, (BLOCK, EXTRA), 1)
        for step in range(BLOCKS):
            rows = slice(step * BLOCK, (step + 1) * BLOCK)
            key_cols[step] = qkv_low[1, rows, cols].T
            value_buf[step, :, :HEAD_DIM] = qkv_low[2, rows, cols]
            value_buf[step, :, HEAD_DIM:] = jnp.where(lane == 0, 1.0, 0.0).astype(BF16)

        def query_block(number, _):
            rows = block_rows(number)
            queries = qkv_low[0, rows, cols] * SCALE

            def mix(step, carry):
                peak, mixed = carry
                same = jnp.concatenate([seg_col[rows]] * (BLOCK // 128), axis=1) == seg_row[step]
                scores = jnp.where(same, dot(queries, key_cols[step]), MASKED)
                higher = jnp.maximum(peak, jnp.max(scores, axis=1, keepdims=True))
                soft = jnp.exp(scores - higher).astype(BF16)
                return higher, mixed * jnp.exp(peak - higher) + dot(soft, value_buf[step])

            start = (
                jnp.full((BLOCK, 1), MASKED, F32),
                jnp.zeros((BLOCK, HEAD_DIM + EXTRA), F32),
            )
            peak, mixed = lax.fori_loop(0, BLOCKS, mix, start)
            total = mixed[:, HEAD_DIM : HEAD_DIM + 1]
            mixed = mixed[:, :HEAD_DIM] / total
            logs = jnp.broadcast_to(peak + jnp.log(total), (BLOCK, HEAD_DIM))
            both = jnp.concatenate([mixed, logs], axis=1).T
            out_cols[head, number] = both[:HEAD_DIM]
            log_total[head, number] = both[HEAD_DIM : HEAD_DIM + 1]
            out_buf[rows] = mixed.astype(BF16)
            for at in range(BLOCKS):
                if (head, at) in events:

                    @pl.when(number == at)
                    def _():
                        for act in events[(head, at)]:
                            act()

            return 0

        lax.fori_loop(0, BLOCKS, query_block, 0)

    def heads_copy(head, offset):
        return send(
            staged.at[head, wrapped(me + offset)],
            heads_in.at[head, me],
            (heads_send, heads_recv),
            (head, offset - 1),
            {"mp": wrapped(me + offset)},
        )

    def heads_own_copy(head):
        return pltpu.make_async_copy(
            staged.at[head, me], heads_in.at[head, me], heads_own.at[head]
        )

    peers = range(1, mp_size)
    for head in range(head_total):
        attend(head)
        for chunk in range(mp_size):
            for side in range(2):
                start = (2 * chunk + side) * half
                staged[head, chunk, :, side * HEAD_DIM : (side + 1) * HEAD_DIM] = out_buf[
                    start : start + half
                ]
        for offset in peers:
            heads_copy(head, offset).start()
        heads_own_copy(head).start()

    for level in range(bits):
        for hop in hops:
            if (level, hop) not in ((0, 0), (0, 1), (1, 0)):
                trade_hop(level, hop)
    for head in range(head_total):
        heads_own_copy(head).wait()
        for offset in peers:
            heads_copy(head, offset).wait_recv()
        for chunk in range(mp_size):
            for side in range(2):
                at = (chunk * head_total + head) * HEAD_DIM
                heads_low[side * half : (side + 1) * half, at : at + HEAD_DIM] = heads_in[
                    head, chunk, :, side * HEAD_DIM : (side + 1) * HEAD_DIM
                ]
        for offset in peers:
            heads_copy(head, offset).wait_send()

    def sent_all(side, hop):
        frame_copy(side, hop).wait_send()
        bias_copy(side, hop).wait_send()
        for which in range(4):
            first_copy(which, side, hop).wait_send()

    def sent_later(side, hop):
        for which in range(4):
            for level in range(bits):
                later_copy(which, level, side, hop).wait_send()

    for side, hop in ways:
        if_sent(side, hop)(partial(sent_all, side, hop))
        if_taken(side, hop)(partial(sent_later, side, hop))


def front(frames, qkv_weight, bias_rows, seg_row, seg_col, weights, in_bias, mp_size, bits):
    local_rows, width = frames.shape
    head_cols = qkv_weight.shape[1]
    head_total = head_cols // HEAD_DIM
    peers = mp_size - 1
    levels = max(bits, 1)
    anywhere = pl.BlockSpec(memory_space=pl.ANY)
    in_weight, down_weight, out_weight = weights

    def sems(*shapes):
        return [pltpu.SemaphoreType.DMA(shape) for shape in shapes for _ in range(2)]

    piece = (head_total, mp_size, local_rows // 2, 2 * HEAD_DIM)
    return pl.pallas_call(
        partial(front_kernel, bits),
        out_shape=(
            jax.ShapeDtypeStruct((ROW_LEN, width), BF16),
            jax.ShapeDtypeStruct((3, ROW_LEN, head_cols), BF16),
            jax.ShapeDtypeStruct((mp_size,) + in_weight.shape, BF16),
            jax.ShapeDtypeStruct((mp_size,) + down_weight.shape, BF16),
            jax.ShapeDtypeStruct((mp_size, 4 * head_cols, width), BF16),
            jax.ShapeDtypeStruct((mp_size,) + in_bias.shape, BF16),
            jax.ShapeDtypeStruct((head_total, BLOCKS, HEAD_DIM, BLOCK), F32),
            jax.ShapeDtypeStruct((head_total, BLOCKS, 1, BLOCK), F32),
            jax.ShapeDtypeStruct((local_rows, width), BF16),
        ),
        in_specs=[whole()] * 5 + [anywhere] * 4,
        out_specs=(whole(), whole()) + (anywhere,) * 4 + (whole(),) * 3,
        scratch_shapes=[
            pltpu.VMEM((BLOCKS, HEAD_DIM, BLOCK), BF16),
            pltpu.VMEM((BLOCKS, BLOCK, HEAD_DIM + EXTRA), BF16),
            pltpu.VMEM((ROW_LEN, HEAD_DIM), BF16),
            pltpu.VMEM(piece, BF16),
            pltpu.VMEM(piece, BF16),
            pltpu.SemaphoreType.DMA((7,)),
            *sems((2, peers), (2, peers), (4, 2, peers), (4, levels, 2, peers)),
            pltpu.SemaphoreType.DMA((head_total,)),
            *sems((head_total, peers)),
        ],
        compiler_params=pltpu.CompilerParams(
            collective_id=0, has_side_effects=True, vmem_limit_bytes=VMEM_BYTES
        ),
        cost_estimate=pl.CostEstimate(
            flops=16 * head_total * ROW_LEN * ROW_LEN * HEAD_DIM,
            bytes_accessed=32 * 1024 * 1024,
            transcendentals=head_total * ROW_LEN * ROW_LEN,
        ),
        name="front",
    )(frames, qkv_weight, bias_rows, seg_row, seg_col, in_weight, down_weight, out_weight, in_bias)


def reduce_orders(bits):
    if bits == 3:
        return ((0, 1, 2), (0, 2, 1), (0, 1, 2))
    return (tuple(range(bits)),) * 3


def back_kernel(
    bits,
    seg_row,
    seg_col,
    qkv,
    out_cols,
    log_total,
    grads_out,
    in_grads,
    down_grads,
    head_grads,
    input_all,
    vector,
    traded,
    in_sum,
    down_sum,
    head_sum,
    proj_sum,
    vector_sum,
    bias_sum,
    grads_in,
    grads,
    qkv_grad,
    key_buf,
    key_cols,
    value_buf,
    query_sum,
    key_sum,
    value_sum,
    staged,
    kept,
    taken,
    last,
    proj,
    proj_taken,
    proj_all,
    proj_rows,
    vectors,
    vectors_taken,
    vectors_all,
    biases,
    biases_taken,
    keep_sems,
    grads_own,
    grads_send,
    grads_recv,
    traded_own,
    traded_send,
    traded_recv,
    level_send,
    level_recv,
    last_send,
    last_recv,
    back_send,
    back_recv,
    proj_send,
    proj_recv,
    vector_send,
    vector_recv,
    vector_last_send,
    vector_last_recv,
    bias_send,
    bias_recv,
):
    head_total, mp_size = grads_out.shape[1], grads_out.shape[0]
    half = grads_out.shape[2]
    me = lax.axis_index("mp")
    dp_index = lax.axis_index("dp")
    peers = range(1, mp_size)
    orders = reduce_orders(bits)
    partials = (in_grads, down_grads, head_grads)
    sums = (in_sum, down_sum, head_sum)
    arrays = range(3)

    def target(offset):
        return lax.rem(me + offset, mp_size)

    def bit_of(which, level):
        return (dp_index // 2 ** orders[which][level]) % 2


    def level_copy(which, level):
        count = 2 ** (bits - 1 - level)
        other = (1 - bit_of(which, level)) * count
        source = partials[which] if level == 0 else taken[which][level - 1]
        return send(
            source.at[:, pl.ds(other, count)],
            taken[which][level],
            (level_send, level_recv),
            (which, level),
            {"dp": partner_of(dp_index, orders[which][level])},
        )

    def keep_copy(which):
        count = 2 ** (bits - 1)
        return pltpu.make_async_copy(
            partials[which].at[:, pl.ds(bit_of(which, 0) * count, count)],
            kept[which],
            keep_sems.at[which],
        )

    def last_copy(which, offset):
        return send(
            taken[which][bits - 1].at[target(offset)],
            last[which].at[offset - 1],
            (last_send, last_recv),
            (which, offset - 1),
            {"mp": target(offset)},
        )

    def add_level(which, level):
        level_copy(which, level).wait_recv()
        count = 2 ** (bits - 1 - level)
        if level == 0:
            keep_copy(which).wait()
        start = bit_of(which, level) * count
        into = taken[which][level]

        def add(at, _):
            for slot in range(count):
                if level == 0:
                    mine = kept[which][at, slot]
                else:
                    mine = taken[which][level - 1][at, start + slot]
                into[at, slot] = (into[at, slot].astype(F32) + mine.astype(F32)).astype(BF16)
            return 0

        lax.fori_loop(0, mp_size, add, 0)
        if level + 1 < bits:
            level_copy(which, level + 1).start()
        else:
            for offset in peers:
                last_copy(which, offset).start()

    def slot_of(order):
        return place_in(dp_index, order[::-1])

    def held_slots(order, level):
        count = 2 ** (bits - 1 - level)
        return pl.ds(slot_of(order) // count * count, count)

    def spread_copy(which, level):
        held = sums[which].at[held_slots(orders[which], level)]
        partner = {"dp": partner_of(dp_index, orders[which][level])}
        return send(held, held, (back_send, back_recv), (which, level), partner)

    def finish_sum(which):
        total = taken[which][bits - 1][me, 0].astype(F32)
        for offset in peers:
            last_copy(which, offset).wait_recv()
            total = total + last[which][offset - 1, 0].astype(F32)
        sums[which][slot_of(orders[which])] = total.astype(BF16)
        spread_copy(which, bits - 1).start()

    def spread(level):
        for which in arrays:
            spread_copy(which, level).wait_recv()
            if level:
                spread_copy(which, level - 1).start()


    def proj_copy(head, level):
        count = 2 ** (bits - 1 - level)
        other = (1 - bit_of(0, level)) * count
        source = proj[head] if level == 0 else proj_taken[head][level - 1]
        return send(
            source.at[pl.ds(other, count)],
            proj_taken[head][level],
            (proj_send, proj_recv),
            (0, head, level),
            {"dp": partner_of(dp_index, orders[0][level])},
        )

    def proj_spread_copy(head, level):
        held = proj_all[head].at[held_slots(orders[0], level)]
        partner = {"dp": partner_of(dp_index, orders[0][level])}
        return send(held, held, (proj_send, proj_recv), (1, head, level), partner)

    def add_proj(head, level):
        proj_copy(head, level).wait_recv()
        count = 2 ** (bits - 1 - level)
        start = bit_of(0, level) * count
        into = proj_taken[head][level]
        for slot in range(count):
            mine = proj[head][start + slot] if level == 0 else proj_taken[head][level - 1][start + slot]
            into[slot] = (into[slot].astype(F32) + mine.astype(F32)).astype(BF16)
        if level + 1 < bits:
            proj_copy(head, level + 1).start()
        else:
            proj_all[head][slot_of(orders[0])] = into[0]
            proj_spread_copy(head, level).start()

    def spread_proj(head, level):
        proj_spread_copy(head, level).wait_recv()
        if level:
            proj_spread_copy(head, level - 1).start()

    def finish_proj(head):
        cols = slice(head * HEAD_DIM, (head + 1) * HEAD_DIM)
        slot_rows = proj_all[head].shape[1]
        for slot in range(2**bits):
            proj_rows[slot * slot_rows : (slot + 1) * slot_rows] = proj_all[head][slot].astype(F32)
        for part in range(3):
            rows = proj_rows[part * HEAD_DIM : (part + 1) * HEAD_DIM]
            proj_sum[part, cols] = rows.astype(BF16)


    def vector_copy(level):
        return send(
            vectors[level],
            vectors_taken[level],
            (vector_send, vector_recv),
            level,
            {"dp": partner_of(dp_index, level)},
        )

    def vector_last_copy(offset):
        return send(
            vectors[bits],
            vectors_all.at[me],
            (vector_last_send, vector_last_recv),
            offset - 1,
            {"mp": target(offset)},
        )

    def add_vector(level):
        vector_copy(level).wait_recv()
        vectors[level + 1][...] = vectors[level][...] + vectors_taken[level][...]
        if level + 1 < bits:
            vector_copy(level + 1).start()
        else:
            vectors_all[me] = vectors[bits][...]
            for offset in peers:
                vector_last_copy(offset).start()

    def finish_vector():
        for offset in peers:
            vector_last_copy(offset).wait_recv()
        total = vectors_all[0]
        for index in peers:
            total = total + vectors_all[index]
        vector_sum[...] = total

    def bias_copy(level):
        return send(
            biases[level],
            biases_taken[level],
            (bias_send, bias_recv),
            level,
            {"dp": partner_of(dp_index, level)},
        )

    def add_bias(level):
        bias_copy(level).wait_recv()
        biases[level + 1][...] = biases[level][...] + biases_taken[level][...]
        if level + 1 < bits:
            bias_copy(level + 1).start()
        else:
            bias_sum[...] = biases[bits][...]


    def grads_copy(head, offset):
        return send(
            grads_out.at[target(offset), head],
            grads_in.at[head, me],
            (grads_send, grads_recv),
            (head, offset - 1),
            {"mp": target(offset)},
        )

    def grads_own_copy(head):
        return pltpu.make_async_copy(
            grads_out.at[me, head], grads_in.at[head, me], grads_own.at[head]
        )

    def traded_copy(head, offset):
        return send(
            staged.at[head, target(offset)],
            traded.at[head, me],
            (traded_send, traded_recv),
            (head, offset - 1),
            {"mp": target(offset)},
        )

    def traded_own_copy(head):
        return pltpu.make_async_copy(
            staged.at[head, me], traded.at[head, me], traded_own.at[head]
        )

    def prepare(head):
        cols = slice(head * HEAD_DIM, (head + 1) * HEAD_DIM)
        key_buf[:, :HEAD_DIM] = qkv[1, :, cols]
        key_buf[:, HEAD_DIM:] = ones_columns(ROW_LEN)
        value_buf[:, :HEAD_DIM] = qkv[2, :, cols]
        value_buf[:, HEAD_DIM:] = ones_columns(ROW_LEN)
        for step in range(BLOCKS):
            key_cols[step] = qkv[1, step * BLOCK : (step + 1) * BLOCK, cols].T
        key_sum[...] = jnp.zeros_like(key_sum)
        value_sum[...] = jnp.zeros_like(value_sum)

    def take_grads(head):
        grads_own_copy(head).wait()
        for offset in peers:
            grads_copy(head, offset).wait_recv()
        for chunk in range(mp_size):
            for side in range(2):
                start = (2 * chunk + side) * half
                grads[start : start + half] = grads_in[
                    head, chunk, :, side * HEAD_DIM : (side + 1) * HEAD_DIM
                ]

    def attend_back(head, events):
        cols = slice(head * HEAD_DIM, (head + 1) * HEAD_DIM)

        def query_block(number, _):
            rows = block_rows(number)
            queries = qkv[0, rows, cols] * SCALE
            grad_rows = grads[rows]
            seg_query = seg_row[number]
            grad_cols = grad_rows.astype(F32).T
            row_dot = jnp.sum(grad_cols * out_cols[head, number], axis=0, keepdims=True)
            grad_cols = jnp.concatenate([grad_cols.astype(BF16), as_pieces(-row_dot)], axis=0)
            query_cols = jnp.concatenate(
                [queries.astype(F32).T.astype(BF16), as_pieces(-log_total[head, number])], axis=0
            )

            def step_back(step, query_grad):
                key_rows = block_rows(step)
                same = jnp.concatenate([seg_col[key_rows]] * (BLOCK // 128), axis=1) == seg_query
                scores = dot(key_buf[key_rows], query_cols)
                soft = jnp.exp(jnp.where(same, scores, MASKED))
                soft_grad = dot(value_buf[key_rows], grad_cols)
                score_grad = (soft * soft_grad).astype(BF16)
                value_sum[key_rows] += dot(soft.astype(BF16), grad_rows)
                key_sum[key_rows] += dot(score_grad, queries)
                return query_grad + dot(key_cols[step], score_grad)

            query_grad = lax.fori_loop(0, BLOCKS, step_back, jnp.zeros((HEAD_DIM, BLOCK), F32))
            query_sum[rows] = (query_grad * SCALE).T
            for at, acts in events.items():

                @pl.when(number == at)
                def _():
                    for act in acts:
                        act()

            return 0

        lax.fori_loop(0, BLOCKS, query_block, 0)

    def give_grads(head):
        for part, total in enumerate((query_sum, key_sum, value_sum)):
            low = total[...].astype(BF16)
            qkv_grad[:, part * HEAD_DIM : (part + 1) * HEAD_DIM] = low
            if part != 1:
                cols = slice(head * HEAD_DIM, (head + 1) * HEAD_DIM)
                sum_low = jnp.sum(low.astype(F32), axis=0, keepdims=True)
                biases[0][part : part + 1, cols] = sum_low
            for chunk in range(mp_size):
                for side in range(2):
                    start = (2 * chunk + side) * half
                    staged[head, chunk, part, :, side * HEAD_DIM : (side + 1) * HEAD_DIM] = total[
                        start : start + half
                    ].astype(BF16)

    def start_trade(head):
        for offset in peers:
            traded_copy(head, offset).start()
        traded_own_copy(head).start()

    def start_proj(head):
        products = dot_cols(qkv_grad[...], input_all[...])
        slot_rows = proj[head].shape[1]
        for slot in range(2**bits):
            proj[head][slot] = products[slot * slot_rows : (slot + 1) * slot_rows].astype(BF16)
        proj_copy(head, 0).start()

    def advance(level):
        for which in arrays:
            add_level(which, level)

    events = {}

    def due(head, number, act, *which):
        events.setdefault((head, number), []).append(partial(act, *which))

    levels = list(range(bits))
    for level, when in zip(levels, ((0, 1), (1, 2), (2, 1))):
        due(*when, advance, level)
    for level, when in zip(levels, ((0, 0), (0, 1), (0, 2))):
        due(*when, add_vector, level)
    due(1, 0, finish_vector)
    for at, level in enumerate(levels):
        due(1, at, add_proj, 0, level)
    for at, level in enumerate(levels[::-1]):
        due(2, at, spread_proj, 0, level)
    for at, level in enumerate(levels):
        due(2, at, add_proj, 1, level)

    enter(dp_index, me, mp_size, bits)
    for offset in peers:
        grads_copy(0, offset).start()
    vectors[0][...] = vector[...]
    vector_copy(0).start()
    for which in arrays:
        level_copy(which, 0).start()
        keep_copy(which).start()
    for head in range(head_total):
        grads_own_copy(head).start()
    biases[0][...] = jnp.zeros_like(biases[0])
    for head in range(head_total):
        prepare(head)
        take_grads(head)
        if head == 0:
            for later in range(1, head_total):
                for offset in peers:
                    grads_copy(later, offset).start()
        attend_back(head, {number: acts for (turn, number), acts in events.items() if turn == head})
        give_grads(head)
        if head + 1 < head_total:
            start_trade(head)
        start_proj(head)
    final = head_total - 1
    bias_copy(0).start()
    for which in arrays:
        for offset in peers:
            last_copy(which, offset).wait_send()
    start_trade(final)
    for level in levels:
        add_proj(final, level)
        add_bias(level)
    for which in arrays:
        finish_sum(which)
    for level in levels[::-1]:
        spread_proj(final, level)
        spread_proj(final - 1, level)
        spread(level)
    for head in range(head_total):
        finish_proj(head)
        traded_own_copy(head).wait()
        for offset in peers:
            grads_copy(head, offset).wait_send()
            traded_copy(head, offset).wait()
        for level in levels:
            proj_copy(head, level).wait_send()
            proj_spread_copy(head, level).wait_send()
    for level in levels:
        vector_copy(level).wait_send()
        bias_copy(level).wait_send()
        for which in arrays:
            level_copy(which, level).wait_send()
            spread_copy(which, level).wait_send()
    for offset in peers:
        vector_last_copy(offset).wait_send()


def back(
    seg_row, seg_col, qkv_low, out_cols, log_total, grads_out, partials, input_all, vector, bits
):
    mp_size, head_total, half, lanes = grads_out.shape
    peers = mp_size - 1
    slots = 2**bits
    width = input_all.shape[1]
    anywhere = pl.BlockSpec(memory_space=pl.ANY)
    blocks = [partial_sum.shape[2:] for partial_sum in partials]
    proj_block = (3 * HEAD_DIM // slots, width)
    bias_block = (8, 2 * 128)

    def halves(shape, dtype, lead=()):
        return [pltpu.VMEM(lead + (slots >> (level + 1),) + shape, dtype) for level in range(bits)]

    def sems(*shapes):
        return [pltpu.SemaphoreType.DMA(shape) for shape in shapes for _ in range(2)]

    return pl.pallas_call(
        partial(back_kernel, bits),
        out_shape=(jax.ShapeDtypeStruct((head_total, mp_size, 3, half, lanes), BF16),)
        + tuple(jax.ShapeDtypeStruct((slots,) + block, BF16) for block in blocks)
        + (
            jax.ShapeDtypeStruct((3, head_total * HEAD_DIM, width), BF16),
            jax.ShapeDtypeStruct(vector.shape, F32),
            jax.ShapeDtypeStruct(bias_block, F32),
        ),
        in_specs=[whole()] * 5 + [anywhere] * 4 + [whole()] * 2,
        out_specs=(anywhere,) + (whole(),) * 6,
        scratch_shapes=[
            pltpu.VMEM((head_total, mp_size, half, lanes), BF16),
            pltpu.VMEM((ROW_LEN, HEAD_DIM), BF16),
            pltpu.VMEM((ROW_LEN, 3 * HEAD_DIM), BF16),
            pltpu.VMEM((ROW_LEN, HEAD_DIM + EXTRA), BF16),
            pltpu.VMEM((BLOCKS, HEAD_DIM, BLOCK), BF16),
            pltpu.VMEM((ROW_LEN, HEAD_DIM + EXTRA), BF16),
            pltpu.VMEM((ROW_LEN, HEAD_DIM), F32),
            pltpu.VMEM((ROW_LEN, HEAD_DIM), F32),
            pltpu.VMEM((ROW_LEN, HEAD_DIM), F32),
            pltpu.VMEM((head_total, mp_size, 3, half, lanes), BF16),
            [pltpu.VMEM((mp_size, slots // 2) + block, BF16) for block in blocks],
            [halves(block, BF16, (mp_size,)) for block in blocks],
            [pltpu.VMEM((peers, 1) + block, BF16) for block in blocks],
            [pltpu.VMEM((slots,) + proj_block, BF16) for _ in range(head_total)],
            [halves(proj_block, BF16) for _ in range(head_total)],
            [pltpu.VMEM((slots,) + proj_block, BF16) for _ in range(head_total)],
            pltpu.VMEM((3 * HEAD_DIM, width), F32),
            [pltpu.VMEM(vector.shape, F32) for _ in range(bits + 1)],
            [pltpu.VMEM(vector.shape, F32) for _ in range(bits)],
            pltpu.VMEM((mp_size,) + vector.shape, F32),
            [pltpu.VMEM(bias_block, F32) for _ in range(bits + 1)],
            [pltpu.VMEM(bias_block, F32) for _ in range(bits)],
            pltpu.SemaphoreType.DMA((3,)),
            pltpu.SemaphoreType.DMA((head_total,)),
            *sems((head_total, peers)),
            pltpu.SemaphoreType.DMA((head_total,)),
            *sems(
                (head_total, peers),
                (3, bits),
                (3, peers),
                (3, bits),
                (2, head_total, bits),
                (bits,),
                (peers,),
                (bits,),
            ),
        ],
        compiler_params=pltpu.CompilerParams(
            collective_id=2, has_side_effects=True, vmem_limit_bytes=VMEM_BYTES
        ),
        cost_estimate=pl.CostEstimate(
            flops=40 * head_total * ROW_LEN * ROW_LEN * HEAD_DIM,
            bytes_accessed=64 * 1024 * 1024,
            transcendentals=head_total * ROW_LEN * ROW_LEN,
        ),
        name="back",
    )(
        seg_row,
        seg_col,
        qkv_low,
        out_cols,
        log_total,
        grads_out,
        *partials,
        input_all,
        vector,
    )


def norm_rows(inputs, norm_gain, norm_shift):
    row_mean = jnp.mean(inputs, axis=-1, keepdims=True)
    centred = inputs - row_mean
    variance = jnp.mean(centred * centred, axis=-1, keepdims=True)
    inv_std = lax.rsqrt(variance + 1e-05)
    normed = centred * inv_std
    return (normed * norm_gain + norm_shift, normed, inv_std)


def norm_back(cotangent, normed, inv_std, norm_gain):
    scaled = cotangent * norm_gain
    adjusted = (
        scaled
        - jnp.mean(scaled, axis=-1, keepdims=True)
        - normed * jnp.mean(scaled * normed, axis=-1, keepdims=True)
    )
    return adjusted * inv_std


def sum_rows(array):
    return jnp.sum(array.astype(F32), axis=0, keepdims=True)


def middle_kernel(
    frames,
    heads_low,
    out_grad,
    in_bias,
    out_bias,
    down_bias,
    norm_gain,
    norm_shift,
    in_all,
    down_all,
    other_all,
    block_out,
    resid_grad,
    grads_out,
    vector,
    in_grads,
    down_grads,
    head_grads,
    in_buf,
    down_buf,
    out_buf,
    hidden,
    slope,
    pre_grad,
    mid_buf,
    normed_buf,
    normed_out,
    low_buf,
    grad_buf,
    given,
    in_sems,
    down_sems,
    out_sems,
    given_sems,
):
    mp_size, units, width = down_all.shape
    head_cols = width // mp_size
    local_rows = frames.shape[0]
    half = local_rows // 2
    slots = in_grads.shape[1]
    out_copies = [
        pltpu.make_async_copy(
            other_all.at[index, pl.ds(0, head_cols)],
            out_buf.at[pl.ds(index * head_cols, head_cols)],
            out_sems.at[index],
        )
        for index in range(mp_size)
    ]

    def in_copy(index):
        return pltpu.make_async_copy(in_all.at[index], in_buf.at[index], in_sems.at[index])

    def down_copy(index):
        return pltpu.make_async_copy(down_all.at[index], down_buf.at[index], down_sems.at[index])

    for copy in out_copies:
        copy.start()
    for index in range(mp_size):
        in_copy(index).start()
        down_copy(index).start()
    vector[...] = jnp.zeros_like(vector)
    gains = norm_gain[...].astype(F32)
    shifts = norm_shift[...].astype(F32)

    for copy in out_copies:
        copy.wait()
    branch = dot(heads_low[...], out_buf[...]) + out_bias[...].astype(F32)
    mid, normed, inv_mid = norm_rows(frames[...].astype(F32) + branch, gains[:1], shifts[:1])
    mid_buf[...] = mid + down_bias[...].astype(F32)
    normed_buf[...] = normed
    low_buf[...] = mid.astype(BF16)

    def feed(index, _):
        in_copy(index).wait()
        pre_act = dot(low_buf[...], in_buf[index]) + in_bias[index, 0:1].astype(F32)
        unit_cdf = 0.5 * (1.0 + lax.erf(pre_act * 0.5**0.5))
        bell = jnp.exp(-0.5 * pre_act * pre_act) * (2.0 * jnp.pi) ** (-0.5)
        slope[index] = unit_cdf + pre_act * bell
        hidden[index] = (pre_act * unit_cdf).astype(BF16)
        down_copy(index).wait()
        mid_buf[...] += dot(hidden[index], down_buf[index])
        return 0

    lax.fori_loop(0, mp_size, feed, 0)
    output, normed, inv_out = norm_rows(mid_buf[...], gains[1:], shifts[1:])
    block_out[...] = output
    normed_out[...] = normed

    cotangent = out_grad[...].astype(F32)
    vector[1:2] = sum_rows(cotangent * normed_out[...])
    vector[3:4] = sum_rows(cotangent)
    sum_grad = norm_back(cotangent, normed_out[...], inv_out, gains[1:])
    mid_buf[...] = sum_grad
    grad_buf[...] = sum_grad.astype(BF16)
    vector[5:6] = sum_rows(grad_buf[...])

    def feed_back(index, _):
        pre = dot_rows(grad_buf[...], down_buf[index]) * slope[index]
        pre_grad[index] = pre.astype(BF16)
        vector[pl.ds(8 + index, 1)] = sum_rows(pre_grad[index])
        mid_buf[...] += dot_rows(pre_grad[index], in_buf[index])
        return 0

    lax.fori_loop(0, mp_size, feed_back, 0)
    mid_grad = mid_buf[...]
    vector[0:1] = sum_rows(mid_grad * normed_buf[...])
    vector[2:3] = sum_rows(mid_grad)
    resid = norm_back(mid_grad, normed_buf[...], inv_mid, gains[:1])
    resid_grad[...] = resid
    attn_grad = resid.astype(BF16)
    vector[4:5] = sum_rows(attn_grad)
    heads_grad = dot_rows(attn_grad, out_buf[...]).astype(BF16)
    for index in range(mp_size):
        for head in range(head_cols // HEAD_DIM):
            at = index * head_cols + head * HEAD_DIM
            for side in range(2):
                grads_out[index, head, :, side * HEAD_DIM : (side + 1) * HEAD_DIM] = heads_grad[
                    side * half : (side + 1) * half, at : at + HEAD_DIM
                ]

    products = dot_cols(heads_low[...], attn_grad).astype(BF16)
    rows = head_cols // slots
    for index in range(mp_size):
        for slot in range(slots):
            start = index * head_cols + slot * rows
            head_grads[index, slot, :rows] = products[start : start + rows]
            if rows < head_grads.shape[2]:
                head_grads[index, slot, rows:] = jnp.zeros(
                    (head_grads.shape[2] - rows, width), BF16
                )
    normed_low = low_buf[...].T

    def given_copy(which, index):
        return pltpu.make_async_copy(
            given.at[which, index % 2],
            (in_grads, down_grads)[which].at[index],
            given_sems.at[which, index % 2],
        )

    for index in range(mp_size):
        for which in range(2):
            if index >= 2:
                given_copy(which, index - 2).wait()
            if which == 0:
                result = dot(normed_low, pre_grad[index])
            else:
                result = dot_cols(hidden[index], grad_buf[...])
            share = result.shape[0] // slots
            for slot in range(slots):
                given[which, index % 2, slot] = result[slot * share : (slot + 1) * share].astype(BF16)
            given_copy(which, index).start()
    for index in range(max(mp_size - 2, 0), mp_size):
        for which in range(2):
            given_copy(which, index).wait()


def middle(frames, heads_low, out_grad, in_bias, small, in_all, down_all, other_all, slots):
    local_rows, width = frames.shape
    mp_size, units = down_all.shape[:2]
    head_cols = width // mp_size
    head_rows = head_cols // slots
    anywhere = pl.BlockSpec(memory_space=pl.ANY)
    rows = jax.ShapeDtypeStruct((local_rows, width), F32)
    gradient = jax.ShapeDtypeStruct((mp_size, slots, units // slots, width), BF16)
    return pl.pallas_call(
        middle_kernel,
        out_shape=(
            rows,
            rows,
            jax.ShapeDtypeStruct(
                (mp_size, head_cols // HEAD_DIM, local_rows // 2, 2 * HEAD_DIM), BF16
            ),
            jax.ShapeDtypeStruct((8 + -(-mp_size // 8) * 8, width), F32),
            gradient,
            gradient,
            jax.ShapeDtypeStruct((mp_size, slots, -(-head_rows // 16) * 16, width), BF16),
        ),
        in_specs=[whole()] * 8 + [anywhere] * 3,
        out_specs=(whole(),) * 4 + (anywhere,) * 2 + (whole(),),
        scratch_shapes=[
            pltpu.VMEM((mp_size, width, units), BF16),
            pltpu.VMEM((mp_size, units, width), BF16),
            pltpu.VMEM((width, width), BF16),
            pltpu.VMEM((mp_size, local_rows, units), BF16),
            pltpu.VMEM((mp_size, local_rows, units), F32),
            pltpu.VMEM((mp_size, local_rows, units), BF16),
            pltpu.VMEM((local_rows, width), F32),
            pltpu.VMEM((local_rows, width), F32),
            pltpu.VMEM((local_rows, width), F32),
            pltpu.VMEM((local_rows, width), BF16),
            pltpu.VMEM((local_rows, width), BF16),
            pltpu.VMEM((2, 2, slots, units // slots, width), BF16),
            pltpu.SemaphoreType.DMA((mp_size,)),
            pltpu.SemaphoreType.DMA((mp_size,)),
            pltpu.SemaphoreType.DMA((mp_size,)),
            pltpu.SemaphoreType.DMA((2, 2)),
        ],
        compiler_params=pltpu.CompilerParams(vmem_limit_bytes=VMEM_BYTES),
        cost_estimate=pl.CostEstimate(
            flops=12 * local_rows * width * (mp_size * units + width // 2),
            bytes_accessed=40 * 1024 * 1024,
            transcendentals=2 * local_rows * mp_size * units,
        ),
        name="middle",
    )(frames, heads_low, out_grad, in_bias, *small, in_all, down_all, other_all)


def finish_kernel(
    traded,
    other_all,
    resid_grad,
    in_sum,
    down_sum,
    head_sum,
    proj_sum,
    stream_grad,
    in_grad,
    down_grad,
    out_grad,
    proj_grad,
    columns,
    weight_buf,
    sems,
):
    head_total, mp_size = traded.shape[:2]
    half = traded.shape[3]
    head_cols = head_total * HEAD_DIM
    copies = [
        pltpu.make_async_copy(
            other_all.at[index, pl.ds(head_cols, 3 * head_cols)],
            weight_buf.at[index],
            sems.at[index],
        )
        for index in range(mp_size)
    ]
    for copy in copies:
        copy.start()
    for sums, grad in ((in_sum, in_grad), (down_sum, down_grad), (head_sum, out_grad)):
        rows = grad.shape[0] // sums.shape[0]
        for slot in range(sums.shape[0]):
            grad[slot * rows : (slot + 1) * rows] = sums[slot, :rows].astype(F32)
    proj_grad[...] = proj_sum[...].astype(F32)
    stream_grad[...] = resid_grad[...]
    for index in range(mp_size):
        for head in range(head_total):
            for part in range(3):
                at = part * head_cols + head * HEAD_DIM
                for side in range(2):
                    columns[side * half : (side + 1) * half, at : at + HEAD_DIM] = traded[
                        head, index, part, :, side * HEAD_DIM : (side + 1) * HEAD_DIM
                    ]
        copies[index].wait()
        stream_grad[...] += dot(columns[...], weight_buf[index])


def finish(traded, other_all, resid_grad, in_sum, down_sum, head_sum, proj_sum):
    head_total, mp_size = traded.shape[:2]
    head_cols = head_total * HEAD_DIM
    local_rows, width = resid_grad.shape
    units = in_sum.shape[0] * in_sum.shape[1]
    anywhere = pl.BlockSpec(memory_space=pl.ANY)
    return pl.pallas_call(
        finish_kernel,
        out_shape=(
            jax.ShapeDtypeStruct((local_rows, width), F32),
            jax.ShapeDtypeStruct((units, width), F32),
            jax.ShapeDtypeStruct((units, width), F32),
            jax.ShapeDtypeStruct((head_cols, width), F32),
            jax.ShapeDtypeStruct((3, head_cols, width), F32),
        ),
        in_specs=[whole(), anywhere] + [whole()] * 5,
        out_specs=(whole(),) * 5,
        scratch_shapes=[
            pltpu.VMEM((local_rows, 3 * head_cols), BF16),
            pltpu.VMEM((mp_size, 3 * head_cols, width), BF16),
            pltpu.SemaphoreType.DMA((mp_size,)),
        ],
        compiler_params=pltpu.CompilerParams(vmem_limit_bytes=VMEM_BYTES),
        cost_estimate=pl.CostEstimate(
            flops=6 * local_rows * width * width, bytes_accessed=24 * 1024 * 1024, transcendentals=0
        ),
        name="finish",
    )(traded, other_all, resid_grad, in_sum, down_sum, head_sum, proj_sum)


def dp_groups():
    total = lax.axis_size("dp")
    size = min(8, total)
    groups = [list(range(start, start + size)) for start in range(0, total, size)]
    return (size, groups)


def on_device(
    frames,
    segment_ids,
    qkv_weight,
    q_bias,
    v_bias,
    out_weight,
    out_bias,
    ff_in_weight,
    ff_in_bias,
    ff_out_weight,
    ff_out_bias,
    norm_gain,
    norm_shift,
    out_grad,
):
    local_rows, width = frames.shape
    mp_size = lax.axis_size("mp")
    group, groups = dp_groups()
    bits = group_bits(lax.axis_size("dp"))
    slots = 2**bits
    head_cols = qkv_weight.shape[3]
    units = ff_in_weight.shape[2]

    bias_rows = jnp.stack([q_bias[0], jnp.zeros_like(q_bias[0]), v_bias[0]]).astype(F32)
    seg_row = segment_ids.reshape(BLOCKS, 1, BLOCK)
    seg_col = jnp.broadcast_to(segment_ids[:, None], (ROW_LEN, 128))
    (
        input_all,
        qkv_low,
        in_all,
        down_all,
        other_all,
        in_bias_all,
        out_cols,
        log_total,
        heads_low,
    ) = front(
        frames,
        qkv_weight[0].transpose(0, 2, 1),
        bias_rows,
        seg_row,
        seg_col,
        (ff_in_weight[0], ff_out_weight[0], out_weight[0]),
        jnp.broadcast_to(ff_in_bias, (16, units)),
        mp_size,
        bits,
    )
    block_out, resid_grad, grads_out, vector, *partials = middle(
        frames,
        heads_low,
        out_grad,
        in_bias_all,
        (out_bias, ff_out_bias, norm_gain[0], norm_shift[0]),
        in_all,
        down_all,
        other_all,
        slots,
    )
    traded, *summed = back(
        seg_row,
        seg_col,
        qkv_low,
        out_cols,
        log_total,
        grads_out,
        partials,
        input_all,
        vector,
        bits,
    )
    if len(groups) > 1:
        across = [list(range(at, lax.axis_size("dp"), group)) for at in range(group)]
        summed = lax.psum(summed, "dp", axis_index_groups=across)
    *weight_sums, vector_sum, bias_sum = summed
    stream_grad, in_weight_grad, down_weight_grad, out_weight_grad, proj_grad = finish(
        traded, other_all, resid_grad, *weight_sums
    )
    in_weight_grad = in_weight_grad[None]
    down_weight_grad = down_weight_grad[None]
    out_weight_grad = out_weight_grad[None]
    qkv_weight_grad = proj_grad.transpose(0, 2, 1)[None]
    query_bias_grad = bias_sum[:1, :head_cols]
    value_bias_grad = bias_sum[2:3, :head_cols]
    gain_grad = vector_sum[None, 0:2]
    shift_grad = vector_sum[None, 2:4]
    head_bias_grad = vector_sum[4:5]
    down_bias_grad = vector_sum[5:6]
    in_bias_grad = lax.dynamic_slice_in_dim(vector_sum, 8 + lax.axis_index("mp"), 1, 0)
    return (
        block_out,
        stream_grad,
        qkv_weight_grad,
        query_bias_grad,
        value_bias_grad,
        out_weight_grad,
        head_bias_grad,
        in_weight_grad,
        in_bias_grad,
        down_weight_grad,
        down_bias_grad,
        gain_grad,
        shift_grad,
    )


def solution(mesh):
    return jax.shard_map(
        on_device,
        mesh=mesh,
        in_specs=(
            P(("dp", "mp"), None),
            P("dp"),
            P(None, None, None, "mp"),
            P(None, "mp"),
            P(None, "mp"),
            P(None, "mp", None),
            P(),
            P(None, None, "mp"),
            P(None, "mp"),
            P(None, "mp", None),
            P(),
            P(),
            P(),
            P(("dp", "mp"), None),
        ),
        out_specs=(
            P(("dp", "mp"), None),
            P(("dp", "mp"), None),
            P(None, None, None, "mp"),
            P(None, "mp"),
            P(None, "mp"),
            P(None, "mp", None),
            P(),
            P(None, None, "mp"),
            P(None, "mp"),
            P(None, "mp", None),
            P(),
            P(),
            P(),
        ),
        check_vma=False,
    )
```

```python
from functools import partial

import jax
import jax.numpy as jnp
from jax import lax
from jax.experimental import pallas as pl
from jax.experimental.pallas import tpu as pltpu
from jax.sharding import PartitionSpec as P

HEAD_DIM = 64
ROW_LEN = 2304
BLOCK = 768
BLOCKS = ROW_LEN // BLOCK
EXTRA = 16
SCALE = HEAD_DIM ** (-0.5)
MASKED = -1e30
F32 = jnp.float32
BF16 = jnp.bfloat16
VMEM_BYTES = 56 * 1024 * 1024


def dot_rows(left, right):
    return lax.dot_general(left, right, (((1,), (1,)), ((), ())), preferred_element_type=F32)


def dot_cols(left, right):
    return lax.dot_general(left, right, (((0,), (0,)), ((), ())), preferred_element_type=F32)


def dot(left, right):
    return jnp.dot(left, right, preferred_element_type=F32)


def block_rows(number):
    return pl.ds(pl.multiple_of(number * BLOCK, BLOCK), BLOCK)


def as_pieces(row):
    high = row.astype(BF16).astype(F32)
    middle = (row - high).astype(BF16).astype(F32)
    last = row - high - middle
    place = lax.broadcasted_iota(jnp.int32, (EXTRA, row.shape[1]), 0)
    pieces = jnp.where(place == 0, high, jnp.where(place == 1, middle, jnp.where(place == 2, last, 0.0)))
    return pieces.astype(BF16)


def ones_columns(rows):
    place = lax.broadcasted_iota(jnp.int32, (rows, EXTRA), 1)
    return jnp.where(place < 3, 1.0, 0.0).astype(BF16)


def whole(memory_space=pltpu.VMEM):
    return pl.BlockSpec(memory_space=memory_space)


MESH = pl.DeviceIdType.MESH


def group_bits(dp_size):
    return min(3, dp_size.bit_length() - 1)


def place_in(dp_index, order):
    slot = 0
    for at, bit in enumerate(order):
        slot = slot + (dp_index // 2**bit) % 2 * 2**at
    return slot


def partner_of(dp_index, bit):
    return dp_index + (1 - 2 * ((dp_index // 2**bit) % 2)) * 2**bit


def enter(dp_index, mp_index, mp_size, bits):
    barrier = pltpu.get_barrier_semaphore()
    for offset in range(1, mp_size):
        pl.semaphore_signal(
            barrier, device_id={"mp": lax.rem(mp_index + offset, mp_size)}, device_id_type=MESH
        )
    for bit in range(bits):
        pl.semaphore_signal(
            barrier, device_id={"dp": partner_of(dp_index, bit)}, device_id_type=MESH
        )
    pl.semaphore_wait(barrier, mp_size - 1 + bits)


def send(src, dst, sems, at, device_id):
    return pltpu.make_async_remote_copy(
        src_ref=src,
        dst_ref=dst,
        send_sem=sems[0].at[at],
        recv_sem=sems[1].at[at],
        device_id=device_id,
        device_id_type=MESH,
    )


def gather_orders(bits):
    if bits == 3:
        return ((1, 2, 0), (2, 1, 0), (1, 2), (1, 2, 0))
    return (tuple(range(bits)),) * 4


SIDES = (1, -1)


def inside(index, size):
    return jnp.logical_and(index >= 0, index < size)


class Line:
    def __init__(self, mp_size, me):
        self.size = mp_size
        self.me = me
        self.hops = range(mp_size - 1)
        self.ways = [(side, hop) for hop in self.hops for side in (0, 1)]

    def wrapped(self, index):
        return lax.rem(index + self.size, self.size)

    def chunk(self, side, hop):
        return self.me - SIDES[side] * hop

    def place(self, side, hop):
        return self.wrapped(self.chunk(side, hop))

    def sends(self, side, hop):
        there = inside(self.me + SIDES[side], self.size)
        return jnp.logical_and(there, inside(self.chunk(side, hop), self.size))

    def if_sent(self, side, hop):
        return pl.when(self.sends(side, hop))

    def if_taken(self, side, hop):
        return pl.when(inside(self.chunk(side, hop + 1), self.size))

    def neighbour(self, side):
        return {"mp": self.wrapped(self.me + SIDES[side])}


def front_kernel(
    bits,
    frames,
    qkv_weight,
    bias_rows,
    seg_row,
    seg_col,
    in_weight,
    down_weight,
    out_weight,
    in_bias,
    input_all,
    qkv_low,
    in_all,
    down_all,
    out_all,
    bias_all,
    out_cols,
    log_total,
    heads_low,
    key_cols,
    value_buf,
    out_buf,
    staged,
    heads_in,
    own_sems,
    frame_send,
    frame_recv,
    bias_send,
    bias_recv,
    first_send,
    first_recv,
    later_send,
    later_recv,
    heads_own,
    heads_send,
    heads_recv,
):
    mp_size = in_all.shape[0]
    me = lax.axis_index("mp")
    dp_index = lax.axis_index("dp")
    local_rows = frames.shape[0]
    half = local_rows // 2
    head_total = out_cols.shape[0]
    orders = gather_orders(bits)[:3]
    parts = ((in_weight, in_all), (down_weight, down_all), (out_weight, out_all))
    line = Line(mp_size, me)
    hops, ways, wrapped = line.hops, line.ways, line.wrapped
    enter(dp_index, me, mp_size, bits)

    def slots(which, level):
        count = parts[which][0].shape[0] // 2 ** len(orders[which])
        start = place_in(dp_index, orders[which]) // 2**level * 2**level
        return pl.ds(pl.multiple_of(start * count, 16), count * 2**level)

    def first_copy(which, side, hop):
        rows = slots(which, 0)
        place = parts[which][1].at[line.place(side, hop), rows]
        source = parts[which][0].at[rows] if hop == 0 else place
        sems = (first_send, first_recv)
        return send(source, place, sems, (which, side, hop), line.neighbour(side))

    def later_copy(which, level, side, hop):
        held = parts[which][1].at[line.place(side, hop + 1), slots(which, level)]
        partner = {"dp": partner_of(dp_index, orders[which][level])}
        return send(held, held, (later_send, later_recv), (which, level, side, hop), partner)

    def frame_rows(index):
        return pl.ds(pl.multiple_of(wrapped(index) * local_rows, local_rows), local_rows)

    def frame_copy(side, hop):
        place = input_all.at[frame_rows(line.chunk(side, hop))]
        source = frames if hop == 0 else place
        return send(source, place, (frame_send, frame_recv), (side, hop), line.neighbour(side))

    def bias_copy(side, hop):
        place = bias_all.at[line.place(side, hop)]
        source = in_bias if hop == 0 else place
        return send(source, place, (bias_send, bias_recv), (side, hop), line.neighbour(side))

    def project(index):
        rows = frame_rows(index)
        inputs = input_all[rows]
        for part in range(3):
            products = dot_rows(inputs, qkv_weight[part]) + bias_rows[part : part + 1]
            qkv_low[part, rows] = products.astype(BF16)

    def start_slices(side, hop):
        for which in range(3):
            first_copy(which, side, hop).start()
        bias_copy(side, hop).start()

    def take_slices(side, hop):
        for which in range(3):
            first_copy(which, side, hop).wait_recv()
        bias_copy(side, hop).wait_recv()
        if hop + 1 < mp_size - 1:
            line.if_sent(side, hop + 1)(partial(start_slices, side, hop + 1))
        for which in range(3):
            if orders[which]:
                later_copy(which, 0, side, hop).start()

    def trade_slices(level, side, hop):
        for which in range(3):
            if level < len(orders[which]):
                later_copy(which, level, side, hop).wait_recv()
            if level + 1 < len(orders[which]):
                later_copy(which, level + 1, side, hop).start()

    def take_hop(hop):
        for side in (0, 1):
            line.if_taken(side, hop)(partial(take_slices, side, hop))

    def trade_hop(level, hop):
        for side in (0, 1):
            line.if_taken(side, hop)(partial(trade_slices, level, side, hop))


    for side in (0, 1):
        line.if_sent(side, 0)(lambda side=side: frame_copy(side, 0).start())
    own = [
        pltpu.make_async_copy(shard, gathered.at[me], own_sems.at[at])
        for at, (shard, gathered) in enumerate(parts + ((in_bias, bias_all),))
    ]
    for copy in own:
        copy.start()
    input_all[frame_rows(me)] = frames[...]
    project(me)

    def take_frames(side, hop):
        frame_copy(side, hop).wait_recv()
        if hop + 1 < mp_size - 1:
            line.if_sent(side, hop + 1)(lambda: frame_copy(side, hop + 1).start())

    def project_taken(side, hop):
        project(line.chunk(side, hop + 1))

    for hop in hops:
        for side in (0, 1):
            line.if_taken(side, hop)(partial(take_frames, side, hop))
        for side in (0, 1):
            free = line.sends(side, hop)
            if hop + 1 < mp_size - 1:
                free = jnp.logical_and(free, jnp.logical_not(line.sends(side, hop + 1)))
            pl.when(free)(partial(start_slices, side, 0))
        for side in (0, 1):
            line.if_taken(side, hop)(partial(project_taken, side, hop))

    schedule = (
        (3, take_hop, 0),
        (7, trade_hop, 0, 0),
        (9, take_hop, 1),
        (12, trade_hop, 0, 1),
        (14, trade_hop, 1, 0),
        (15, take_hop, 2),
        (18, trade_hop, 0, 2),
        (20, trade_hop, 1, 1),
        (26, trade_hop, 1, 2),
    )
    events = {}
    done = set()
    for at, act, *which in schedule:
        if which[-1] in hops and (act is take_hop or which[0] < bits):
            events.setdefault(at, []).append(partial(act, *which))
            done.add((act, *which))

    def attend(head):
        cols = slice(head * HEAD_DIM, (head + 1) * HEAD_DIM)
        lane = lax.broadcasted_iota(jnp.int32, (BLOCK, EXTRA), 1)
        for step in range(BLOCKS):
            rows = slice(step * BLOCK, (step + 1) * BLOCK)
            key_cols[step] = qkv_low[1, rows, cols].T
            value_buf[step, :, :HEAD_DIM] = qkv_low[2, rows, cols]
            value_buf[step, :, HEAD_DIM:] = jnp.where(lane == 0, 1.0, 0.0).astype(BF16)

        def query_block(number, _):
            rows = block_rows(number)
            queries = qkv_low[0, rows, cols] * SCALE

            def mix(step, carry):
                peak, mixed = carry
                same = jnp.concatenate([seg_col[rows]] * (BLOCK // 128), axis=1) == seg_row[step]
                scores = jnp.where(same, dot(queries, key_cols[step]), MASKED)
                higher = jnp.maximum(peak, jnp.max(scores, axis=1, keepdims=True))
                soft = jnp.exp(scores - higher).astype(BF16)
                mixed = mixed * jnp.exp(peak - higher) + dot(soft, value_buf[step])
                for at in range(head * BLOCKS**2, (head + 1) * BLOCKS**2):
                    if at in events:

                        @pl.when(number * BLOCKS + step == at - head * BLOCKS**2)
                        def _():
                            for act in events[at]:
                                act()

                return higher, mixed

            start = (
                jnp.full((BLOCK, 1), MASKED, F32),
                jnp.zeros((BLOCK, HEAD_DIM + EXTRA), F32),
            )
            peak, mixed = lax.fori_loop(0, BLOCKS, mix, start)
            total = mixed[:, HEAD_DIM : HEAD_DIM + 1]
            mixed = mixed[:, :HEAD_DIM] / total
            logs = jnp.broadcast_to(peak + jnp.log(total), (BLOCK, HEAD_DIM))
            both = jnp.concatenate([mixed, logs], axis=1).T
            out_cols[head, number] = both[:HEAD_DIM]
            log_total[head, number] = both[HEAD_DIM : HEAD_DIM + 1]
            out_buf[rows] = mixed.astype(BF16)
            return 0

        lax.fori_loop(0, BLOCKS, query_block, 0)

    def heads_copy(head, offset):
        return send(
            staged.at[head, wrapped(me + offset)],
            heads_in.at[head, me],
            (heads_send, heads_recv),
            (head, offset - 1),
            {"mp": wrapped(me + offset)},
        )

    def heads_own_copy(head):
        return pltpu.make_async_copy(
            staged.at[head, me], heads_in.at[head, me], heads_own.at[head]
        )

    peers = range(1, mp_size)
    for head in range(head_total):
        attend(head)
        for chunk in range(mp_size):
            for side in range(2):
                start = (2 * chunk + side) * half
                staged[head, chunk, :, side * HEAD_DIM : (side + 1) * HEAD_DIM] = out_buf[
                    start : start + half
                ]
        for offset in peers:
            heads_copy(head, offset).start()
        heads_own_copy(head).start()

    for hop in hops:
        if (take_hop, hop) not in done:
            take_hop(hop)
    for level in range(bits):
        for hop in hops:
            if (trade_hop, level, hop) not in done:
                trade_hop(level, hop)
    for head in range(head_total):
        heads_own_copy(head).wait()
        for offset in peers:
            heads_copy(head, offset).wait_recv()
        for chunk in range(mp_size):
            for side in range(2):
                at = (chunk * head_total + head) * HEAD_DIM
                heads_low[side * half : (side + 1) * half, at : at + HEAD_DIM] = heads_in[
                    head, chunk, :, side * HEAD_DIM : (side + 1) * HEAD_DIM
                ]
        for offset in peers:
            heads_copy(head, offset).wait_send()

    def sent_all(side, hop):
        frame_copy(side, hop).wait_send()
        bias_copy(side, hop).wait_send()
        for which in range(3):
            first_copy(which, side, hop).wait_send()

    def sent_later(side, hop):
        for which in range(3):
            for level in range(len(orders[which])):
                later_copy(which, level, side, hop).wait_send()

    for side, hop in ways:
        line.if_sent(side, hop)(partial(sent_all, side, hop))
        line.if_taken(side, hop)(partial(sent_later, side, hop))
    for copy in own:
        copy.wait()


def front(frames, qkv_weight, bias_rows, seg_row, seg_col, weights, in_bias, mp_size, bits):
    local_rows, width = frames.shape
    head_cols = qkv_weight.shape[1]
    head_total = head_cols // HEAD_DIM
    peers = mp_size - 1
    levels = max(bits, 1)
    anywhere = pl.BlockSpec(memory_space=pl.ANY)
    in_weight, down_weight, out_weight = weights

    def sems(*shapes):
        return [pltpu.SemaphoreType.DMA(shape) for shape in shapes for _ in range(2)]

    piece = (head_total, mp_size, local_rows // 2, 2 * HEAD_DIM)
    return pl.pallas_call(
        partial(front_kernel, bits),
        out_shape=(
            jax.ShapeDtypeStruct((ROW_LEN, width), BF16),
            jax.ShapeDtypeStruct((3, ROW_LEN, head_cols), BF16),
            jax.ShapeDtypeStruct((mp_size,) + in_weight.shape, BF16),
            jax.ShapeDtypeStruct((mp_size,) + down_weight.shape, BF16),
            jax.ShapeDtypeStruct((mp_size,) + out_weight.shape, BF16),
            jax.ShapeDtypeStruct((mp_size,) + in_bias.shape, BF16),
            jax.ShapeDtypeStruct((head_total, BLOCKS, HEAD_DIM, BLOCK), F32),
            jax.ShapeDtypeStruct((head_total, BLOCKS, 1, BLOCK), F32),
            jax.ShapeDtypeStruct((local_rows, width), BF16),
        ),
        in_specs=[whole()] * 5 + [anywhere] * 4,
        out_specs=(whole(), whole()) + (anywhere,) * 4 + (whole(),) * 3,
        scratch_shapes=[
            pltpu.VMEM((BLOCKS, HEAD_DIM, BLOCK), BF16),
            pltpu.VMEM((BLOCKS, BLOCK, HEAD_DIM + EXTRA), BF16),
            pltpu.VMEM((ROW_LEN, HEAD_DIM), BF16),
            pltpu.VMEM(piece, BF16),
            pltpu.VMEM(piece, BF16),
            pltpu.SemaphoreType.DMA((4,)),
            *sems((2, peers), (2, peers), (3, 2, peers), (3, levels, 2, peers)),
            pltpu.SemaphoreType.DMA((head_total,)),
            *sems((head_total, peers)),
        ],
        compiler_params=pltpu.CompilerParams(
            collective_id=0, has_side_effects=True, vmem_limit_bytes=VMEM_BYTES
        ),
        cost_estimate=pl.CostEstimate(
            flops=16 * head_total * ROW_LEN * ROW_LEN * HEAD_DIM,
            bytes_accessed=32 * 1024 * 1024,
            transcendentals=head_total * ROW_LEN * ROW_LEN,
        ),
        name="front",
    )(frames, qkv_weight, bias_rows, seg_row, seg_col, in_weight, down_weight, out_weight, in_bias)


def reduce_orders(bits):
    if bits == 3:
        return ((0, 1, 2), (0, 2, 1), (0, 1, 2))
    return (tuple(range(bits)),) * 3


def back_kernel(
    bits,
    seg_row,
    seg_col,
    qkv,
    out_cols,
    log_total,
    grads_out,
    in_grads,
    down_grads,
    head_grads,
    input_all,
    vector,
    traded,
    in_sum,
    down_sum,
    head_sum,
    proj_sum,
    vector_sum,
    bias_sum,
    grads_in,
    grads,
    qkv_grad,
    key_buf,
    key_cols,
    value_buf,
    query_sum,
    key_sum,
    value_sum,
    staged,
    kept,
    taken,
    last,
    proj,
    proj_taken,
    proj_all,
    proj_rows,
    vectors,
    vectors_taken,
    vectors_all,
    biases,
    biases_taken,
    keep_sems,
    grads_own,
    grads_send,
    grads_recv,
    traded_own,
    traded_send,
    traded_recv,
    level_send,
    level_recv,
    last_send,
    last_recv,
    back_send,
    back_recv,
    proj_send,
    proj_recv,
    vector_send,
    vector_recv,
    vector_last_send,
    vector_last_recv,
    bias_send,
    bias_recv,
):
    head_total, mp_size = grads_out.shape[1], grads_out.shape[0]
    half = grads_out.shape[2]
    me = lax.axis_index("mp")
    dp_index = lax.axis_index("dp")
    peers = range(1, mp_size)
    orders = reduce_orders(bits)
    partials = (in_grads, down_grads, head_grads)
    sums = (in_sum, down_sum, head_sum)
    arrays = range(3)

    def target(offset):
        return lax.rem(me + offset, mp_size)

    def bit_of(which, level):
        return (dp_index // 2 ** orders[which][level]) % 2


    def level_copy(which, level):
        count = 2 ** (bits - 1 - level)
        other = (1 - bit_of(which, level)) * count
        source = partials[which] if level == 0 else taken[which][level - 1]
        return send(
            source.at[:, pl.ds(other, count)],
            taken[which][level],
            (level_send, level_recv),
            (which, level),
            {"dp": partner_of(dp_index, orders[which][level])},
        )

    def keep_copy(which):
        count = 2 ** (bits - 1)
        return pltpu.make_async_copy(
            partials[which].at[:, pl.ds(bit_of(which, 0) * count, count)],
            kept[which],
            keep_sems.at[which],
        )

    def last_copy(which, offset):
        return send(
            taken[which][bits - 1].at[target(offset)],
            last[which].at[offset - 1],
            (last_send, last_recv),
            (which, offset - 1),
            {"mp": target(offset)},
        )

    def add_level(which, level):
        level_copy(which, level).wait_recv()
        count = 2 ** (bits - 1 - level)
        if level == 0:
            keep_copy(which).wait()
        start = bit_of(which, level) * count
        into = taken[which][level]

        def add(at, _):
            for slot in range(count):
                if level == 0:
                    mine = kept[which][at, slot]
                else:
                    mine = taken[which][level - 1][at, start + slot]
                into[at, slot] = (into[at, slot].astype(F32) + mine.astype(F32)).astype(BF16)
            return 0

        lax.fori_loop(0, mp_size, add, 0)
        if level + 1 < bits:
            level_copy(which, level + 1).start()
        else:
            for offset in peers:
                last_copy(which, offset).start()

    def slot_of(order):
        return place_in(dp_index, order[::-1])

    def held_slots(order, level):
        count = 2 ** (bits - 1 - level)
        return pl.ds(slot_of(order) // count * count, count)

    def spread_copy(which, level):
        held = sums[which].at[held_slots(orders[which], level)]
        partner = {"dp": partner_of(dp_index, orders[which][level])}
        return send(held, held, (back_send, back_recv), (which, level), partner)

    def finish_sum(which):
        total = taken[which][bits - 1][me, 0].astype(F32)
        for offset in peers:
            last_copy(which, offset).wait_recv()
            total = total + last[which][offset - 1, 0].astype(F32)
        sums[which][slot_of(orders[which])] = total.astype(BF16)
        spread_copy(which, bits - 1).start()

    def spread(level):
        for which in arrays:
            spread_copy(which, level).wait_recv()
            if level:
                spread_copy(which, level - 1).start()


    def proj_copy(head, level):
        count = 2 ** (bits - 1 - level)
        other = (1 - bit_of(0, level)) * count
        source = proj[head] if level == 0 else proj_taken[head][level - 1]
        return send(
            source.at[pl.ds(other, count)],
            proj_taken[head][level],
            (proj_send, proj_recv),
            (0, head, level),
            {"dp": partner_of(dp_index, orders[0][level])},
        )

    def proj_spread_copy(head, level):
        held = proj_all[head].at[held_slots(orders[0], level)]
        partner = {"dp": partner_of(dp_index, orders[0][level])}
        return send(held, held, (proj_send, proj_recv), (1, head, level), partner)

    def add_proj(head, level):
        proj_copy(head, level).wait_recv()
        count = 2 ** (bits - 1 - level)
        start = bit_of(0, level) * count
        into = proj_taken[head][level]
        for slot in range(count):
            mine = proj[head][start + slot] if level == 0 else proj_taken[head][level - 1][start + slot]
            into[slot] = (into[slot].astype(F32) + mine.astype(F32)).astype(BF16)
        if level + 1 < bits:
            proj_copy(head, level + 1).start()
        else:
            proj_all[head][slot_of(orders[0])] = into[0]
            proj_spread_copy(head, level).start()

    def spread_proj(head, level):
        proj_spread_copy(head, level).wait_recv()
        if level:
            proj_spread_copy(head, level - 1).start()

    def finish_proj(head):
        cols = slice(head * HEAD_DIM, (head + 1) * HEAD_DIM)
        slot_rows = proj_all[head].shape[1]
        for slot in range(2**bits):
            proj_rows[slot * slot_rows : (slot + 1) * slot_rows] = proj_all[head][slot].astype(F32)
        for part in range(3):
            rows = proj_rows[part * HEAD_DIM : (part + 1) * HEAD_DIM]
            proj_sum[part, cols] = rows.astype(BF16)


    def vector_copy(level):
        return send(
            vectors[level],
            vectors_taken[level],
            (vector_send, vector_recv),
            level,
            {"dp": partner_of(dp_index, level)},
        )

    def vector_last_copy(offset):
        return send(
            vectors[bits],
            vectors_all.at[me],
            (vector_last_send, vector_last_recv),
            offset - 1,
            {"mp": target(offset)},
        )

    def add_vector(level):
        vector_copy(level).wait_recv()
        vectors[level + 1][...] = vectors[level][...] + vectors_taken[level][...]
        if level + 1 < bits:
            vector_copy(level + 1).start()
        else:
            vectors_all[me] = vectors[bits][...]
            for offset in peers:
                vector_last_copy(offset).start()

    def finish_vector():
        for offset in peers:
            vector_last_copy(offset).wait_recv()
        total = vectors_all[0]
        for index in peers:
            total = total + vectors_all[index]
        vector_sum[...] = total

    def bias_copy(level):
        return send(
            biases[level],
            biases_taken[level],
            (bias_send, bias_recv),
            level,
            {"dp": partner_of(dp_index, level)},
        )

    def add_bias(level):
        bias_copy(level).wait_recv()
        biases[level + 1][...] = biases[level][...] + biases_taken[level][...]
        if level + 1 < bits:
            bias_copy(level + 1).start()
        else:
            bias_sum[...] = biases[bits][...]


    def grads_copy(head, offset):
        return send(
            grads_out.at[target(offset), head],
            grads_in.at[head, me],
            (grads_send, grads_recv),
            (head, offset - 1),
            {"mp": target(offset)},
        )

    def grads_own_copy(head):
        return pltpu.make_async_copy(
            grads_out.at[me, head], grads_in.at[head, me], grads_own.at[head]
        )

    def traded_copy(head, offset):
        return send(
            staged.at[head, target(offset)],
            traded.at[head, me],
            (traded_send, traded_recv),
            (head, offset - 1),
            {"mp": target(offset)},
        )

    def traded_own_copy(head):
        return pltpu.make_async_copy(
            staged.at[head, me], traded.at[head, me], traded_own.at[head]
        )

    def prepare(head):
        cols = slice(head * HEAD_DIM, (head + 1) * HEAD_DIM)
        key_buf[:, :HEAD_DIM] = qkv[1, :, cols]
        key_buf[:, HEAD_DIM:] = ones_columns(ROW_LEN)
        value_buf[:, :HEAD_DIM] = qkv[2, :, cols]
        value_buf[:, HEAD_DIM:] = ones_columns(ROW_LEN)
        for step in range(BLOCKS):
            key_cols[step] = qkv[1, step * BLOCK : (step + 1) * BLOCK, cols].T
        key_sum[...] = jnp.zeros_like(key_sum)
        value_sum[...] = jnp.zeros_like(value_sum)

    def take_grads(head):
        grads_own_copy(head).wait()
        for offset in peers:
            grads_copy(head, offset).wait_recv()
        for chunk in range(mp_size):
            for side in range(2):
                start = (2 * chunk + side) * half
                grads[start : start + half] = grads_in[
                    head, chunk, :, side * HEAD_DIM : (side + 1) * HEAD_DIM
                ]

    def attend_back(head, events):
        cols = slice(head * HEAD_DIM, (head + 1) * HEAD_DIM)

        def query_block(number, _):
            rows = block_rows(number)
            queries = qkv[0, rows, cols] * SCALE
            grad_rows = grads[rows]
            seg_query = seg_row[number]
            grad_cols = grad_rows.astype(F32).T
            row_dot = jnp.sum(grad_cols * out_cols[head, number], axis=0, keepdims=True)
            grad_cols = jnp.concatenate([grad_cols.astype(BF16), as_pieces(-row_dot)], axis=0)
            query_cols = jnp.concatenate(
                [queries.astype(F32).T.astype(BF16), as_pieces(-log_total[head, number])], axis=0
            )

            def step_back(step, query_grad):
                key_rows = block_rows(step)
                same = jnp.concatenate([seg_col[key_rows]] * (BLOCK // 128), axis=1) == seg_query
                scores = dot(key_buf[key_rows], query_cols)
                soft = jnp.exp(jnp.where(same, scores, MASKED))
                soft_grad = dot(value_buf[key_rows], grad_cols)
                score_grad = (soft * soft_grad).astype(BF16)
                value_sum[key_rows] += dot(soft.astype(BF16), grad_rows)
                key_sum[key_rows] += dot(score_grad, queries)
                return query_grad + dot(key_cols[step], score_grad)

            query_grad = lax.fori_loop(0, BLOCKS, step_back, jnp.zeros((HEAD_DIM, BLOCK), F32))
            query_sum[rows] = (query_grad * SCALE).T
            for at, acts in events.items():

                @pl.when(number == at)
                def _():
                    for act in acts:
                        act()

            return 0

        lax.fori_loop(0, BLOCKS, query_block, 0)

    def give_grads(head):
        for part, total in enumerate((query_sum, key_sum, value_sum)):
            low = total[...].astype(BF16)
            qkv_grad[:, part * HEAD_DIM : (part + 1) * HEAD_DIM] = low
            if part != 1:
                cols = slice(head * HEAD_DIM, (head + 1) * HEAD_DIM)
                sum_low = jnp.sum(low.astype(F32), axis=0, keepdims=True)
                biases[0][part : part + 1, cols] = sum_low
            for chunk in range(mp_size):
                for side in range(2):
                    start = (2 * chunk + side) * half
                    staged[head, chunk, part, :, side * HEAD_DIM : (side + 1) * HEAD_DIM] = total[
                        start : start + half
                    ].astype(BF16)

    def start_trade(head):
        for offset in peers:
            traded_copy(head, offset).start()
        traded_own_copy(head).start()

    def start_proj(head):
        products = dot_cols(qkv_grad[...], input_all[...])
        slot_rows = proj[head].shape[1]
        for slot in range(2**bits):
            proj[head][slot] = products[slot * slot_rows : (slot + 1) * slot_rows].astype(BF16)
        proj_copy(head, 0).start()

    def advance(level):
        for which in arrays:
            add_level(which, level)

    events = {}

    def due(head, number, act, *which):
        events.setdefault((head, number), []).append(partial(act, *which))

    levels = list(range(bits))
    for level, when in zip(levels, ((0, 1), (1, 2), (2, 1))):
        due(*when, advance, level)
    for level, when in zip(levels, ((0, 0), (0, 1), (0, 2))):
        due(*when, add_vector, level)
    due(1, 0, finish_vector)
    for at, level in enumerate(levels):
        due(1, at, add_proj, 0, level)
    for at, level in enumerate(levels[::-1]):
        due(2, at, spread_proj, 0, level)
    for at, level in enumerate(levels):
        due(2, at, add_proj, 1, level)

    enter(dp_index, me, mp_size, bits)
    for offset in peers:
        grads_copy(0, offset).start()
    vectors[0][...] = vector[...]
    vector_copy(0).start()
    for which in arrays:
        level_copy(which, 0).start()
        keep_copy(which).start()
    for head in range(head_total):
        grads_own_copy(head).start()
    biases[0][...] = jnp.zeros_like(biases[0])
    for head in range(head_total):
        prepare(head)
        take_grads(head)
        if head == 0:
            for later in range(1, head_total):
                for offset in peers:
                    grads_copy(later, offset).start()
        attend_back(head, {number: acts for (turn, number), acts in events.items() if turn == head})
        give_grads(head)
        if head + 1 < head_total:
            start_trade(head)
        start_proj(head)
    final = head_total - 1
    bias_copy(0).start()
    for which in arrays:
        for offset in peers:
            last_copy(which, offset).wait_send()
    start_trade(final)
    for level in levels:
        add_proj(final, level)
        add_bias(level)
    for which in arrays:
        finish_sum(which)
    for level in levels[::-1]:
        spread_proj(final, level)
        spread_proj(final - 1, level)
        spread(level)
    for head in range(head_total):
        finish_proj(head)
        traded_own_copy(head).wait()
        for offset in peers:
            grads_copy(head, offset).wait_send()
            traded_copy(head, offset).wait()
        for level in levels:
            proj_copy(head, level).wait_send()
            proj_spread_copy(head, level).wait_send()
    for level in levels:
        vector_copy(level).wait_send()
        bias_copy(level).wait_send()
        for which in arrays:
            level_copy(which, level).wait_send()
            spread_copy(which, level).wait_send()
    for offset in peers:
        vector_last_copy(offset).wait_send()


def back(
    seg_row, seg_col, qkv_low, out_cols, log_total, grads_out, partials, input_all, vector, bits
):
    mp_size, head_total, half, lanes = grads_out.shape
    peers = mp_size - 1
    slots = 2**bits
    width = input_all.shape[1]
    anywhere = pl.BlockSpec(memory_space=pl.ANY)
    blocks = [partial_sum.shape[2:] for partial_sum in partials]
    proj_block = (3 * HEAD_DIM // slots, width)
    bias_block = (8, 2 * 128)

    def halves(shape, dtype, lead=()):
        return [pltpu.VMEM(lead + (slots >> (level + 1),) + shape, dtype) for level in range(bits)]

    def sems(*shapes):
        return [pltpu.SemaphoreType.DMA(shape) for shape in shapes for _ in range(2)]

    return pl.pallas_call(
        partial(back_kernel, bits),
        out_shape=(jax.ShapeDtypeStruct((head_total, mp_size, 3, half, lanes), BF16),)
        + tuple(jax.ShapeDtypeStruct((slots,) + block, BF16) for block in blocks)
        + (
            jax.ShapeDtypeStruct((3, head_total * HEAD_DIM, width), BF16),
            jax.ShapeDtypeStruct(vector.shape, F32),
            jax.ShapeDtypeStruct(bias_block, F32),
        ),
        in_specs=[whole()] * 5 + [anywhere] * 4 + [whole()] * 2,
        out_specs=(anywhere,) + (whole(),) * 6,
        scratch_shapes=[
            pltpu.VMEM((head_total, mp_size, half, lanes), BF16),
            pltpu.VMEM((ROW_LEN, HEAD_DIM), BF16),
            pltpu.VMEM((ROW_LEN, 3 * HEAD_DIM), BF16),
            pltpu.VMEM((ROW_LEN, HEAD_DIM + EXTRA), BF16),
            pltpu.VMEM((BLOCKS, HEAD_DIM, BLOCK), BF16),
            pltpu.VMEM((ROW_LEN, HEAD_DIM + EXTRA), BF16),
            pltpu.VMEM((ROW_LEN, HEAD_DIM), F32),
            pltpu.VMEM((ROW_LEN, HEAD_DIM), F32),
            pltpu.VMEM((ROW_LEN, HEAD_DIM), F32),
            pltpu.VMEM((head_total, mp_size, 3, half, lanes), BF16),
            [pltpu.VMEM((mp_size, slots // 2) + block, BF16) for block in blocks],
            [halves(block, BF16, (mp_size,)) for block in blocks],
            [pltpu.VMEM((peers, 1) + block, BF16) for block in blocks],
            [pltpu.VMEM((slots,) + proj_block, BF16) for _ in range(head_total)],
            [halves(proj_block, BF16) for _ in range(head_total)],
            [pltpu.VMEM((slots,) + proj_block, BF16) for _ in range(head_total)],
            pltpu.VMEM((3 * HEAD_DIM, width), F32),
            [pltpu.VMEM(vector.shape, F32) for _ in range(bits + 1)],
            [pltpu.VMEM(vector.shape, F32) for _ in range(bits)],
            pltpu.VMEM((mp_size,) + vector.shape, F32),
            [pltpu.VMEM(bias_block, F32) for _ in range(bits + 1)],
            [pltpu.VMEM(bias_block, F32) for _ in range(bits)],
            pltpu.SemaphoreType.DMA((3,)),
            pltpu.SemaphoreType.DMA((head_total,)),
            *sems((head_total, peers)),
            pltpu.SemaphoreType.DMA((head_total,)),
            *sems(
                (head_total, peers),
                (3, bits),
                (3, peers),
                (3, bits),
                (2, head_total, bits),
                (bits,),
                (peers,),
                (bits,),
            ),
        ],
        compiler_params=pltpu.CompilerParams(
            collective_id=2, has_side_effects=True, vmem_limit_bytes=VMEM_BYTES
        ),
        cost_estimate=pl.CostEstimate(
            flops=40 * head_total * ROW_LEN * ROW_LEN * HEAD_DIM,
            bytes_accessed=64 * 1024 * 1024,
            transcendentals=head_total * ROW_LEN * ROW_LEN,
        ),
        name="back",
    )(
        seg_row,
        seg_col,
        qkv_low,
        out_cols,
        log_total,
        grads_out,
        *partials,
        input_all,
        vector,
    )


def norm_rows(inputs, norm_gain, norm_shift):
    row_mean = jnp.mean(inputs, axis=-1, keepdims=True)
    centred = inputs - row_mean
    variance = jnp.mean(centred * centred, axis=-1, keepdims=True)
    inv_std = lax.rsqrt(variance + 1e-05)
    normed = centred * inv_std
    return (normed * norm_gain + norm_shift, normed, inv_std)


def norm_back(cotangent, normed, inv_std, norm_gain):
    scaled = cotangent * norm_gain
    adjusted = (
        scaled
        - jnp.mean(scaled, axis=-1, keepdims=True)
        - normed * jnp.mean(scaled * normed, axis=-1, keepdims=True)
    )
    return adjusted * inv_std


def sum_rows(array):
    return jnp.sum(array.astype(F32), axis=0, keepdims=True)


def middle_kernel(
    bits,
    frames,
    heads_low,
    out_grad,
    in_bias,
    out_bias,
    down_bias,
    norm_gain,
    norm_shift,
    in_all,
    down_all,
    out_all,
    proj_weight,
    block_out,
    resid_grad,
    grads_out,
    vector,
    in_grads,
    down_grads,
    head_grads,
    proj_all,
    in_buf,
    down_buf,
    out_buf,
    hidden,
    slope,
    pre_grad,
    mid_buf,
    normed_buf,
    normed_out,
    low_buf,
    grad_buf,
    given,
    in_sems,
    down_sems,
    out_sems,
    given_sems,
    proj_own,
    proj_send,
    proj_recv,
    trade_send,
    trade_recv,
):
    mp_size, units, width = down_all.shape
    head_cols = width // mp_size
    local_rows = frames.shape[0]
    half = local_rows // 2
    slots = in_grads.shape[1]
    out_copies = [
        pltpu.make_async_copy(
            out_all.at[index],
            out_buf.at[pl.ds(index * head_cols, head_cols)],
            out_sems.at[index],
        )
        for index in range(mp_size)
    ]

    def in_copy(index):
        return pltpu.make_async_copy(in_all.at[index], in_buf.at[index], in_sems.at[index])

    def down_copy(index):
        return pltpu.make_async_copy(down_all.at[index], down_buf.at[index], down_sems.at[index])

    me = lax.axis_index("mp")
    dp_index = lax.axis_index("dp")
    line = Line(mp_size, me)
    order = gather_orders(bits)[3]
    own_slot = place_in(dp_index, order)

    def proj_copy(side, hop):
        place = proj_all.at[line.place(side, hop), pl.ds(own_slot, 1)]
        source = proj_weight.at[pl.ds(own_slot, 1)] if hop == 0 else place
        return send(source, place, (proj_send, proj_recv), (side, hop), line.neighbour(side))

    def trade_copy(level, side, hop):
        held = pl.ds(own_slot // 2**level * 2**level, 2**level)
        place = proj_all.at[line.place(side, hop + 1), held]
        partner = {"dp": partner_of(dp_index, order[level])}
        return send(place, place, (trade_send, trade_recv), (level, side, hop), partner)

    def take_proj(side, hop):
        proj_copy(side, hop).wait_recv()
        if hop + 1 < mp_size - 1:
            line.if_sent(side, hop + 1)(lambda: proj_copy(side, hop + 1).start())
        if bits:
            trade_copy(0, side, hop).start()

    def trade_proj(level, side, hop):
        trade_copy(level, side, hop).wait_recv()
        if level + 1 < bits:
            trade_copy(level + 1, side, hop).start()

    def both_sides(act, *which):
        for side in (0, 1):
            line.if_taken(side, which[-1])(partial(act, *which[:-1], side, which[-1]))

    schedule = (
        (0, take_proj, 0),
        (1, take_proj, 1),
        (2, take_proj, 2),
        (2, trade_proj, 0, 0),
        (3, trade_proj, 0, 1),
        (3, trade_proj, 0, 2),
        (4, trade_proj, 1, 0),
        (6, trade_proj, 1, 1),
        (8, trade_proj, 1, 2),
    )
    done = set()

    def at_point(point, offset=0, index=None):
        for at, act, *which in schedule:
            if which[-1] not in line.hops or (act is trade_proj and which[0] >= bits):
                continue
            if index is None and at == point:
                both_sides(act, *which)
                done.add((act, *which))
            if index is not None and offset <= at < offset + mp_size:
                pl.when(index == at - offset)(partial(both_sides, act, *which))
                done.add((act, *which))

    enter(dp_index, me, mp_size, bits)
    for side in (0, 1):
        line.if_sent(side, 0)(lambda side=side: proj_copy(side, 0).start())
    own = pltpu.make_async_copy(proj_weight, proj_all.at[me], proj_own)
    own.start()
    for copy in out_copies:
        copy.start()
    for index in range(mp_size):
        in_copy(index).start()
        down_copy(index).start()
    vector[...] = jnp.zeros_like(vector)
    gains = norm_gain[...].astype(F32)
    shifts = norm_shift[...].astype(F32)

    for copy in out_copies:
        copy.wait()
    branch = dot(heads_low[...], out_buf[...]) + out_bias[...].astype(F32)
    mid, normed, inv_mid = norm_rows(frames[...].astype(F32) + branch, gains[:1], shifts[:1])
    mid_buf[...] = mid + down_bias[...].astype(F32)
    normed_buf[...] = normed
    low_buf[...] = mid.astype(BF16)
    at_point(0)

    def feed(index, _):
        in_copy(index).wait()
        pre_act = dot(low_buf[...], in_buf[index]) + in_bias[index, 0:1].astype(F32)
        unit_cdf = 0.5 * (1.0 + lax.erf(pre_act * 0.5**0.5))
        bell = jnp.exp(-0.5 * pre_act * pre_act) * (2.0 * jnp.pi) ** (-0.5)
        slope[index] = unit_cdf + pre_act * bell
        hidden[index] = (pre_act * unit_cdf).astype(BF16)
        down_copy(index).wait()
        mid_buf[...] += dot(hidden[index], down_buf[index])
        at_point(None, 1, index)
        return 0

    lax.fori_loop(0, mp_size, feed, 0)
    output, normed, inv_out = norm_rows(mid_buf[...], gains[1:], shifts[1:])
    block_out[...] = output
    normed_out[...] = normed

    cotangent = out_grad[...].astype(F32)
    vector[1:2] = sum_rows(cotangent * normed_out[...])
    vector[3:4] = sum_rows(cotangent)
    sum_grad = norm_back(cotangent, normed_out[...], inv_out, gains[1:])
    mid_buf[...] = sum_grad
    grad_buf[...] = sum_grad.astype(BF16)
    vector[5:6] = sum_rows(grad_buf[...])

    def feed_back(index, _):
        pre = dot_rows(grad_buf[...], down_buf[index]) * slope[index]
        pre_grad[index] = pre.astype(BF16)
        vector[pl.ds(8 + index, 1)] = sum_rows(pre_grad[index])
        mid_buf[...] += dot_rows(pre_grad[index], in_buf[index])
        at_point(None, 1 + mp_size, index)
        return 0

    lax.fori_loop(0, mp_size, feed_back, 0)
    mid_grad = mid_buf[...]
    vector[0:1] = sum_rows(mid_grad * normed_buf[...])
    vector[2:3] = sum_rows(mid_grad)
    resid = norm_back(mid_grad, normed_buf[...], inv_mid, gains[:1])
    resid_grad[...] = resid
    attn_grad = resid.astype(BF16)
    vector[4:5] = sum_rows(attn_grad)
    heads_grad = dot_rows(attn_grad, out_buf[...]).astype(BF16)
    for index in range(mp_size):
        for head in range(head_cols // HEAD_DIM):
            at = index * head_cols + head * HEAD_DIM
            for side in range(2):
                grads_out[index, head, :, side * HEAD_DIM : (side + 1) * HEAD_DIM] = heads_grad[
                    side * half : (side + 1) * half, at : at + HEAD_DIM
                ]

    products = dot_cols(heads_low[...], attn_grad).astype(BF16)
    rows = head_cols // slots
    for index in range(mp_size):
        for slot in range(slots):
            start = index * head_cols + slot * rows
            head_grads[index, slot, :rows] = products[start : start + rows]
            if rows < head_grads.shape[2]:
                head_grads[index, slot, rows:] = jnp.zeros(
                    (head_grads.shape[2] - rows, width), BF16
                )
    normed_low = low_buf[...].T

    def given_copy(which, index):
        return pltpu.make_async_copy(
            given.at[which, index % 2],
            (in_grads, down_grads)[which].at[index],
            given_sems.at[which, index % 2],
        )

    for index in range(mp_size):
        for which in range(2):
            if index >= 2:
                given_copy(which, index - 2).wait()
            if which == 0:
                result = dot(normed_low, pre_grad[index])
            else:
                result = dot_cols(hidden[index], grad_buf[...])
            share = result.shape[0] // slots
            for slot in range(slots):
                given[which, index % 2, slot] = result[slot * share : (slot + 1) * share].astype(BF16)
            given_copy(which, index).start()
    for index in range(max(mp_size - 2, 0), mp_size):
        for which in range(2):
            given_copy(which, index).wait()
    for hop in line.hops:
        if (take_proj, hop) not in done:
            both_sides(take_proj, hop)
    for level in range(bits):
        for hop in line.hops:
            if (trade_proj, level, hop) not in done:
                both_sides(trade_proj, level, hop)

    def sent_trades(side, hop):
        for level in range(bits):
            trade_copy(level, side, hop).wait_send()

    for side, hop in line.ways:
        line.if_sent(side, hop)(lambda side=side, hop=hop: proj_copy(side, hop).wait_send())
        line.if_taken(side, hop)(partial(sent_trades, side, hop))
    own.wait()


def middle(frames, heads_low, out_grad, in_bias, small, weights, proj_weight, bits):
    local_rows, width = frames.shape
    mp_size, units = weights[1].shape[:2]
    slots = 2**bits
    peers = mp_size - 1
    head_cols = width // mp_size
    head_rows = head_cols // slots
    anywhere = pl.BlockSpec(memory_space=pl.ANY)
    rows = jax.ShapeDtypeStruct((local_rows, width), F32)
    gradient = jax.ShapeDtypeStruct((mp_size, slots, units // slots, width), BF16)
    return pl.pallas_call(
        partial(middle_kernel, bits),
        out_shape=(
            rows,
            rows,
            jax.ShapeDtypeStruct(
                (mp_size, head_cols // HEAD_DIM, local_rows // 2, 2 * HEAD_DIM), BF16
            ),
            jax.ShapeDtypeStruct((8 + -(-mp_size // 8) * 8, width), F32),
            gradient,
            gradient,
            jax.ShapeDtypeStruct((mp_size, slots, -(-head_rows // 16) * 16, width), BF16),
            jax.ShapeDtypeStruct((mp_size,) + proj_weight.shape, BF16),
        ),
        in_specs=[whole()] * 8 + [anywhere] * 4,
        out_specs=(whole(),) * 4 + (anywhere,) * 2 + (whole(), anywhere),
        scratch_shapes=[
            pltpu.VMEM((mp_size, width, units), BF16),
            pltpu.VMEM((mp_size, units, width), BF16),
            pltpu.VMEM((width, width), BF16),
            pltpu.VMEM((mp_size, local_rows, units), BF16),
            pltpu.VMEM((mp_size, local_rows, units), F32),
            pltpu.VMEM((mp_size, local_rows, units), BF16),
            pltpu.VMEM((local_rows, width), F32),
            pltpu.VMEM((local_rows, width), F32),
            pltpu.VMEM((local_rows, width), F32),
            pltpu.VMEM((local_rows, width), BF16),
            pltpu.VMEM((local_rows, width), BF16),
            pltpu.VMEM((2, 2, slots, units // slots, width), BF16),
            pltpu.SemaphoreType.DMA((mp_size,)),
            pltpu.SemaphoreType.DMA((mp_size,)),
            pltpu.SemaphoreType.DMA((mp_size,)),
            pltpu.SemaphoreType.DMA((2, 2)),
            pltpu.SemaphoreType.DMA,
            pltpu.SemaphoreType.DMA((2, peers)),
            pltpu.SemaphoreType.DMA((2, peers)),
            pltpu.SemaphoreType.DMA((max(bits, 1), 2, peers)),
            pltpu.SemaphoreType.DMA((max(bits, 1), 2, peers)),
        ],
        compiler_params=pltpu.CompilerParams(
            collective_id=1, has_side_effects=True, vmem_limit_bytes=VMEM_BYTES
        ),
        cost_estimate=pl.CostEstimate(
            flops=12 * local_rows * width * (mp_size * units + width // 2),
            bytes_accessed=40 * 1024 * 1024,
            transcendentals=2 * local_rows * mp_size * units,
        ),
        name="middle",
    )(frames, heads_low, out_grad, in_bias, *small, *weights, proj_weight)


def finish_kernel(
    traded,
    proj_all,
    resid_grad,
    in_sum,
    down_sum,
    head_sum,
    proj_sum,
    stream_grad,
    in_grad,
    down_grad,
    out_grad,
    proj_grad,
    columns,
    weight_buf,
    sems,
):
    head_total, mp_size = traded.shape[:2]
    half = traded.shape[3]
    head_cols = head_total * HEAD_DIM
    copies = [
        pltpu.make_async_copy(
            proj_all.at[index],
            weight_buf.at[index],
            sems.at[index],
        )
        for index in range(mp_size)
    ]
    for copy in copies:
        copy.start()
    for sums, grad in ((in_sum, in_grad), (down_sum, down_grad), (head_sum, out_grad)):
        rows = grad.shape[0] // sums.shape[0]
        for slot in range(sums.shape[0]):
            grad[slot * rows : (slot + 1) * rows] = sums[slot, :rows].astype(F32)
    proj_grad[...] = proj_sum[...].astype(F32)
    stream_grad[...] = resid_grad[...]
    for index in range(mp_size):
        for head in range(head_total):
            for part in range(3):
                at = part * head_cols + head * HEAD_DIM
                for side in range(2):
                    columns[side * half : (side + 1) * half, at : at + HEAD_DIM] = traded[
                        head, index, part, :, side * HEAD_DIM : (side + 1) * HEAD_DIM
                    ]
        copies[index].wait()
        stream_grad[...] += dot(columns[...], weight_buf[index])


def finish(traded, proj_all, resid_grad, in_sum, down_sum, head_sum, proj_sum):
    head_total, mp_size = traded.shape[:2]
    head_cols = head_total * HEAD_DIM
    local_rows, width = resid_grad.shape
    units = in_sum.shape[0] * in_sum.shape[1]
    anywhere = pl.BlockSpec(memory_space=pl.ANY)
    return pl.pallas_call(
        finish_kernel,
        out_shape=(
            jax.ShapeDtypeStruct((local_rows, width), F32),
            jax.ShapeDtypeStruct((units, width), F32),
            jax.ShapeDtypeStruct((units, width), F32),
            jax.ShapeDtypeStruct((head_cols, width), F32),
            jax.ShapeDtypeStruct((3, head_cols, width), F32),
        ),
        in_specs=[whole(), anywhere] + [whole()] * 5,
        out_specs=(whole(),) * 5,
        scratch_shapes=[
            pltpu.VMEM((local_rows, 3 * head_cols), BF16),
            pltpu.VMEM((mp_size, 3 * head_cols, width), BF16),
            pltpu.SemaphoreType.DMA((mp_size,)),
        ],
        compiler_params=pltpu.CompilerParams(vmem_limit_bytes=VMEM_BYTES),
        cost_estimate=pl.CostEstimate(
            flops=6 * local_rows * width * width, bytes_accessed=24 * 1024 * 1024, transcendentals=0
        ),
        name="finish",
    )(traded, proj_all, resid_grad, in_sum, down_sum, head_sum, proj_sum)


def dp_groups():
    total = lax.axis_size("dp")
    size = min(8, total)
    groups = [list(range(start, start + size)) for start in range(0, total, size)]
    return (size, groups)


def on_device(
    frames,
    segment_ids,
    qkv_weight,
    q_bias,
    v_bias,
    out_weight,
    out_bias,
    ff_in_weight,
    ff_in_bias,
    ff_out_weight,
    ff_out_bias,
    norm_gain,
    norm_shift,
    out_grad,
):
    local_rows, width = frames.shape
    mp_size = lax.axis_size("mp")
    group, groups = dp_groups()
    bits = group_bits(lax.axis_size("dp"))
    slots = 2**bits
    head_cols = qkv_weight.shape[3]
    units = ff_in_weight.shape[2]

    proj_weight = qkv_weight[0].transpose(0, 2, 1)
    bias_rows = jnp.stack([q_bias[0], jnp.zeros_like(q_bias[0]), v_bias[0]]).astype(F32)
    seg_row = segment_ids.reshape(BLOCKS, 1, BLOCK)
    seg_col = jnp.broadcast_to(segment_ids[:, None], (ROW_LEN, 128))
    (
        input_all,
        qkv_low,
        in_all,
        down_all,
        out_all,
        in_bias_all,
        out_cols,
        log_total,
        heads_low,
    ) = front(
        frames,
        proj_weight,
        bias_rows,
        seg_row,
        seg_col,
        (ff_in_weight[0], ff_out_weight[0], out_weight[0]),
        jnp.broadcast_to(ff_in_bias, (16, units)),
        mp_size,
        bits,
    )
    block_out, resid_grad, grads_out, vector, *partials, proj_all = middle(
        frames,
        heads_low,
        out_grad,
        in_bias_all,
        (out_bias, ff_out_bias, norm_gain[0], norm_shift[0]),
        (in_all, down_all, out_all),
        proj_weight.reshape(slots, -1, width),
        bits,
    )
    traded, *summed = back(
        seg_row,
        seg_col,
        qkv_low,
        out_cols,
        log_total,
        grads_out,
        partials,
        input_all,
        vector,
        bits,
    )
    if len(groups) > 1:
        across = [list(range(at, lax.axis_size("dp"), group)) for at in range(group)]
        summed = lax.psum(summed, "dp", axis_index_groups=across)
    *weight_sums, vector_sum, bias_sum = summed
    stream_grad, in_weight_grad, down_weight_grad, out_weight_grad, proj_grad = finish(
        traded, proj_all.reshape(mp_size, -1, width), resid_grad, *weight_sums
    )
    in_weight_grad = in_weight_grad[None]
    down_weight_grad = down_weight_grad[None]
    out_weight_grad = out_weight_grad[None]
    qkv_weight_grad = proj_grad.transpose(0, 2, 1)[None]
    query_bias_grad = bias_sum[:1, :head_cols]
    value_bias_grad = bias_sum[2:3, :head_cols]
    gain_grad = vector_sum[None, 0:2]
    shift_grad = vector_sum[None, 2:4]
    head_bias_grad = vector_sum[4:5]
    down_bias_grad = vector_sum[5:6]
    in_bias_grad = lax.dynamic_slice_in_dim(vector_sum, 8 + lax.axis_index("mp"), 1, 0)
    return (
        block_out,
        stream_grad,
        qkv_weight_grad,
        query_bias_grad,
        value_bias_grad,
        out_weight_grad,
        head_bias_grad,
        in_weight_grad,
        in_bias_grad,
        down_weight_grad,
        down_bias_grad,
        gain_grad,
        shift_grad,
    )


def solution(mesh):
    return jax.shard_map(
        on_device,
        mesh=mesh,
        in_specs=(
            P(("dp", "mp"), None),
            P("dp"),
            P(None, None, None, "mp"),
            P(None, "mp"),
            P(None, "mp"),
            P(None, "mp", None),
            P(),
            P(None, None, "mp"),
            P(None, "mp"),
            P(None, "mp", None),
            P(),
            P(),
            P(),
            P(("dp", "mp"), None),
        ),
        out_specs=(
            P(("dp", "mp"), None),
            P(("dp", "mp"), None),
            P(None, None, None, "mp"),
            P(None, "mp"),
            P(None, "mp"),
            P(None, "mp", None),
            P(),
            P(None, None, "mp"),
            P(None, "mp"),
            P(None, "mp", None),
            P(),
            P(),
            P(),
        ),
        check_vma=False,
    )
```

```python
import itertools
from functools import partial

import jax
import jax.numpy as jnp
from jax import lax
from jax.experimental import pallas as pl
from jax.experimental.pallas import tpu as pltpu
from jax.sharding import PartitionSpec as P

HEAD_DIM = 64
ROW_LEN = 2304
BLOCK = 768
BLOCKS = ROW_LEN // BLOCK
EXTRA = 16
SCALE = HEAD_DIM ** (-0.5)
MASKED = -1e30
F32 = jnp.float32
BF16 = jnp.bfloat16
VMEM_BYTES = 56 * 1024 * 1024


def dot_rows(left, right):
    return lax.dot_general(left, right, (((1,), (1,)), ((), ())), preferred_element_type=F32)


def dot_cols(left, right):
    return lax.dot_general(left, right, (((0,), (0,)), ((), ())), preferred_element_type=F32)


def dot(left, right):
    return jnp.dot(left, right, preferred_element_type=F32)


def block_rows(number):
    return pl.ds(pl.multiple_of(number * BLOCK, BLOCK), BLOCK)


def as_pieces(row):
    high = row.astype(BF16).astype(F32)
    middle = (row - high).astype(BF16).astype(F32)
    last = row - high - middle
    place = lax.broadcasted_iota(jnp.int32, (EXTRA, row.shape[1]), 0)
    pieces = jnp.where(place == 0, high, jnp.where(place == 1, middle, jnp.where(place == 2, last, 0.0)))
    return pieces.astype(BF16)


def ones_columns(rows):
    place = lax.broadcasted_iota(jnp.int32, (rows, EXTRA), 1)
    return jnp.where(place < 3, 1.0, 0.0).astype(BF16)


def whole(memory_space=pltpu.VMEM):
    return pl.BlockSpec(memory_space=memory_space)


MESH = pl.DeviceIdType.MESH


def group_bits(dp_size):
    return min(3, dp_size.bit_length() - 1)


def place_in(dp_index, order):
    slot = 0
    for at, bit in enumerate(order):
        slot = slot + (dp_index // 2**bit) % 2 * 2**at
    return slot


def partner_of(dp_index, bit):
    return dp_index + (1 - 2 * ((dp_index // 2**bit) % 2)) * 2**bit


def enter(dp_index, mp_index, mp_size, bits):
    barrier = pltpu.get_barrier_semaphore()
    for offset in range(1, mp_size):
        pl.semaphore_signal(
            barrier, device_id={"mp": lax.rem(mp_index + offset, mp_size)}, device_id_type=MESH
        )
    for bit in range(bits):
        pl.semaphore_signal(
            barrier, device_id={"dp": partner_of(dp_index, bit)}, device_id_type=MESH
        )
    pl.semaphore_wait(barrier, mp_size - 1 + bits)


def send(src, dst, sems, at, device_id):
    return pltpu.make_async_remote_copy(
        src_ref=src,
        dst_ref=dst,
        send_sem=sems[0].at[at],
        recv_sem=sems[1].at[at],
        device_id=device_id,
        device_id_type=MESH,
    )


def gather_orders(bits):
    if bits == 3:
        return ((1, 2, 0), (2, 1, 0), (1, 2), (1, 2, 0))
    return (tuple(range(bits)),) * 4


SIDES = (1, -1)


def inside(index, size):
    return jnp.logical_and(index >= 0, index < size)


class Line:
    def __init__(self, mp_size, me):
        self.size = mp_size
        self.me = me
        self.hops = range(mp_size - 1)
        self.ways = [(side, hop) for hop in self.hops for side in (0, 1)]

    def wrapped(self, index):
        return lax.rem(index + self.size, self.size)

    def chunk(self, side, hop):
        return self.me - SIDES[side] * hop

    def place(self, side, hop):
        return self.wrapped(self.chunk(side, hop))

    def sends(self, side, hop):
        there = inside(self.me + SIDES[side], self.size)
        return jnp.logical_and(there, inside(self.chunk(side, hop), self.size))

    def if_sent(self, side, hop):
        return pl.when(self.sends(side, hop))

    def if_taken(self, side, hop):
        return pl.when(inside(self.chunk(side, hop + 1), self.size))

    def neighbour(self, side):
        return {"mp": self.wrapped(self.me + SIDES[side])}


def front_kernel(
    bits,
    frames,
    qkv_weight,
    q_bias,
    v_bias,
    seg_row,
    in_weight,
    down_weight,
    out_weight,
    in_bias,
    input_all,
    qkv_low,
    in_all,
    down_all,
    out_all,
    bias_all,
    seg_col,
    out_cols,
    log_total,
    heads_low,
    bias_buf,
    key_cols,
    value_buf,
    out_buf,
    staged,
    heads_in,
    own_sems,
    frame_send,
    frame_recv,
    bias_send,
    bias_recv,
    first_send,
    first_recv,
    later_send,
    later_recv,
    heads_own,
    heads_send,
    heads_recv,
):
    mp_size = in_all.shape[0]
    me = lax.axis_index("mp")
    dp_index = lax.axis_index("dp")
    local_rows = frames.shape[0]
    half = local_rows // 2
    head_total = out_cols.shape[0]
    orders = gather_orders(bits)[:3]
    parts = ((in_weight, in_all), (down_weight, down_all), (out_weight, out_all))
    line = Line(mp_size, me)
    hops, ways, wrapped = line.hops, line.ways, line.wrapped
    enter(dp_index, me, mp_size, bits)

    def slots(which, level):
        count = parts[which][0].shape[0] // 2 ** len(orders[which])
        start = place_in(dp_index, orders[which]) // 2**level * 2**level
        return pl.ds(pl.multiple_of(start * count, 16), count * 2**level)

    def first_copy(which, side, hop):
        rows = slots(which, 0)
        place = parts[which][1].at[line.place(side, hop), rows]
        source = parts[which][0].at[rows] if hop == 0 else place
        sems = (first_send, first_recv)
        return send(source, place, sems, (which, side, hop), line.neighbour(side))

    def later_copy(which, level, side, hop):
        held = parts[which][1].at[line.place(side, hop + 1), slots(which, level)]
        partner = {"dp": partner_of(dp_index, orders[which][level])}
        return send(held, held, (later_send, later_recv), (which, level, side, hop), partner)

    def frame_rows(index):
        return pl.ds(pl.multiple_of(wrapped(index) * local_rows, local_rows), local_rows)

    def frame_copy(side, hop):
        place = input_all.at[frame_rows(line.chunk(side, hop))]
        source = frames if hop == 0 else place
        return send(source, place, (frame_send, frame_recv), (side, hop), line.neighbour(side))

    def bias_copy(side, hop):
        place = bias_all.at[line.place(side, hop)]
        source = bias_buf if hop == 0 else place
        return send(source, place, (bias_send, bias_recv), (side, hop), line.neighbour(side))

    def project(index):
        rows = frame_rows(index)
        inputs = input_all[rows]
        for part, bias in enumerate((q_bias, None, v_bias)):
            products = dot_rows(inputs, qkv_weight[part])
            if bias is not None:
                products = products + bias[...].astype(F32)
            qkv_low[part, rows] = products.astype(BF16)

    def start_slices(side, hop):
        for which in range(3):
            first_copy(which, side, hop).start()
        bias_copy(side, hop).start()

    def take_slices(side, hop):
        for which in range(3):
            first_copy(which, side, hop).wait_recv()
        bias_copy(side, hop).wait_recv()
        if 0 < hop < mp_size - 2:
            line.if_sent(side, hop + 1)(partial(start_slices, side, hop + 1))
        for which in range(3):
            if orders[which]:
                later_copy(which, 0, side, hop).start()

    def trade_slices(level, side, hop):
        for which in range(3):
            if level < len(orders[which]):
                later_copy(which, level, side, hop).wait_recv()
            if level + 1 < len(orders[which]):
                later_copy(which, level + 1, side, hop).start()

    def take_hop(hop):
        for side in (0, 1):
            line.if_taken(side, hop)(partial(take_slices, side, hop))

    def trade_hop(level, hop):
        for side in (0, 1):
            line.if_taken(side, hop)(partial(trade_slices, level, side, hop))


    bias_buf[...] = jnp.broadcast_to(in_bias[...], bias_buf.shape)
    for side in (0, 1):
        line.if_sent(side, 0)(partial(start_slices, side, 0))
    for side in (0, 1):
        line.if_sent(side, 0)(lambda side=side: frame_copy(side, 0).start())
    own = [
        pltpu.make_async_copy(shard, gathered.at[me], own_sems.at[at])
        for at, (shard, gathered) in enumerate(parts + ((bias_buf, bias_all),))
    ]
    for copy in own:
        copy.start()
    input_all[frame_rows(me)] = frames[...]
    project(me)
    for step in range(BLOCKS):
        ids = jnp.broadcast_to(seg_row[:, step * BLOCK : (step + 1) * BLOCK].astype(F32), (128, BLOCK))
        seg_col[step * BLOCK : (step + 1) * BLOCK] = ids.T.astype(jnp.int32)

    def take_frames(side, hop):
        frame_copy(side, hop).wait_recv()
        if hop + 1 < mp_size - 1:
            line.if_sent(side, hop + 1)(lambda: frame_copy(side, hop + 1).start())

    def project_taken(side, hop):
        project(line.chunk(side, hop + 1))

    for hop in hops:
        for side in (0, 1):
            line.if_taken(side, hop)(partial(take_frames, side, hop))
        if hop == 0:
            take_hop(0)
        elif hop - 1 < bits:
            trade_hop(hop - 1, 0)
        for side in (0, 1):
            free = line.sends(side, hop)
            if hop + 1 < mp_size - 1:
                free = jnp.logical_and(free, jnp.logical_not(line.sends(side, hop + 1)))
            if mp_size > 2:
                passes = jnp.logical_and(free, line.sends(side, 1))
                pl.when(passes)(partial(start_slices, side, 1))
        for side in (0, 1):
            line.if_taken(side, hop)(partial(project_taken, side, hop))

    schedule = (
        (1, take_hop, 1),
        (3, trade_hop, 0, 1),
        (4, take_hop, 2),
        (6, trade_hop, 1, 1),
        (6, trade_hop, 0, 2),
    )
    events = {}
    done = {(take_hop, 0)} | {(trade_hop, hop - 1, 0) for hop in hops if 0 < hop <= bits}
    for at, act, *which in schedule:
        if which[-1] in hops and (act is take_hop or which[0] < bits):
            events.setdefault((at // BLOCKS, at % BLOCKS), []).append(partial(act, *which))
            done.add((act, *which))

    def attend(head):
        cols = slice(head * HEAD_DIM, (head + 1) * HEAD_DIM)
        lane = lax.broadcasted_iota(jnp.int32, (BLOCK, EXTRA), 1)
        for step in range(BLOCKS):
            rows = slice(step * BLOCK, (step + 1) * BLOCK)
            key_cols[step] = qkv_low[1, rows, cols].T
            value_buf[step, :, :HEAD_DIM] = qkv_low[2, rows, cols]
            value_buf[step, :, HEAD_DIM:] = jnp.where(lane == 0, 1.0, 0.0).astype(BF16)

        def query_block(number, _):
            rows = block_rows(number)
            queries = qkv_low[0, rows, cols] * SCALE

            def scores_of(step):
                ids = seg_row[:, step * BLOCK : (step + 1) * BLOCK]
                same = jnp.concatenate([seg_col[rows]] * (BLOCK // 128), axis=1) == ids
                return jnp.where(same, dot(queries, key_cols[step]), MASKED)

            peak = jnp.full((BLOCK, 1), MASKED, F32)
            mixed = jnp.zeros((BLOCK, HEAD_DIM + EXTRA), F32)
            scores = scores_of(0)
            for step in range(BLOCKS):
                ahead = scores_of(step + 1) if step + 1 < BLOCKS else None
                higher = jnp.maximum(peak, jnp.max(scores, axis=1, keepdims=True))
                soft = jnp.exp(scores - higher).astype(BF16)
                mixed = mixed * jnp.exp(peak - higher) + dot(soft, value_buf[step])
                peak, scores = higher, ahead
            total = mixed[:, HEAD_DIM : HEAD_DIM + 1]
            mixed = mixed[:, :HEAD_DIM] / total
            logs = jnp.broadcast_to(peak + jnp.log(total), (BLOCK, HEAD_DIM))
            both = jnp.concatenate([mixed, logs], axis=1).T
            out_cols[head, number] = both[:HEAD_DIM]
            log_total[head, number] = both[HEAD_DIM : HEAD_DIM + 1]
            out_buf[rows] = mixed.astype(BF16)
            for at in range(BLOCKS):
                if (head, at) in events:

                    @pl.when(number == at)
                    def _():
                        for act in events[(head, at)]:
                            act()

            return 0

        lax.fori_loop(0, BLOCKS, query_block, 0)

    def heads_copy(head, offset):
        return send(
            staged.at[head, wrapped(me + offset)],
            heads_in.at[head, me],
            (heads_send, heads_recv),
            (head, offset - 1),
            {"mp": wrapped(me + offset)},
        )

    def heads_own_copy(head):
        return pltpu.make_async_copy(
            staged.at[head, me], heads_in.at[head, me], heads_own.at[head]
        )

    peers = range(1, mp_size)
    for head in range(head_total):
        attend(head)
        for chunk in range(mp_size):
            for side in range(2):
                start = (2 * chunk + side) * half
                staged[head, chunk, :, side * HEAD_DIM : (side + 1) * HEAD_DIM] = out_buf[
                    start : start + half
                ]
        for offset in peers:
            heads_copy(head, offset).start()
        heads_own_copy(head).start()

    for hop in hops:
        if (take_hop, hop) not in done:
            take_hop(hop)
    for level in range(bits):
        for hop in hops:
            if (trade_hop, level, hop) not in done:
                trade_hop(level, hop)
    for head in range(head_total):
        heads_own_copy(head).wait()
        for offset in peers:
            heads_copy(head, offset).wait_recv()
        for chunk in range(mp_size):
            for side in range(2):
                at = (chunk * head_total + head) * HEAD_DIM
                heads_low[side * half : (side + 1) * half, at : at + HEAD_DIM] = heads_in[
                    head, chunk, :, side * HEAD_DIM : (side + 1) * HEAD_DIM
                ]
        for offset in peers:
            heads_copy(head, offset).wait_send()

    def sent_all(side, hop):
        frame_copy(side, hop).wait_send()
        bias_copy(side, hop).wait_send()
        for which in range(3):
            first_copy(which, side, hop).wait_send()

    def sent_later(side, hop):
        for which in range(3):
            for level in range(len(orders[which])):
                later_copy(which, level, side, hop).wait_send()

    for side, hop in ways:
        line.if_sent(side, hop)(partial(sent_all, side, hop))
        line.if_taken(side, hop)(partial(sent_later, side, hop))
    for copy in own:
        copy.wait()


def front(frames, qkv_weight, q_bias, v_bias, seg_row, weights, in_bias, mp_size, bits):
    local_rows, width = frames.shape
    head_cols = qkv_weight.shape[1]
    head_total = head_cols // HEAD_DIM
    peers = mp_size - 1
    levels = max(bits, 1)
    anywhere = pl.BlockSpec(memory_space=pl.ANY)
    in_weight, down_weight, out_weight = weights

    def sems(*shapes):
        return [pltpu.SemaphoreType.DMA(shape) for shape in shapes for _ in range(2)]

    piece = (head_total, mp_size, local_rows // 2, 2 * HEAD_DIM)
    return pl.pallas_call(
        partial(front_kernel, bits),
        out_shape=(
            jax.ShapeDtypeStruct((ROW_LEN, width), BF16),
            jax.ShapeDtypeStruct((3, ROW_LEN, head_cols), BF16),
            jax.ShapeDtypeStruct((mp_size,) + in_weight.shape, BF16),
            jax.ShapeDtypeStruct((mp_size,) + down_weight.shape, BF16),
            jax.ShapeDtypeStruct((mp_size,) + out_weight.shape, BF16),
            jax.ShapeDtypeStruct((mp_size, 16, in_bias.shape[1]), BF16),
            jax.ShapeDtypeStruct((ROW_LEN, 128), jnp.int32),
            jax.ShapeDtypeStruct((head_total, BLOCKS, HEAD_DIM, BLOCK), F32),
            jax.ShapeDtypeStruct((head_total, BLOCKS, 1, BLOCK), F32),
            jax.ShapeDtypeStruct((local_rows, width), BF16),
        ),
        in_specs=[whole()] * 5 + [anywhere] * 3 + [whole()],
        out_specs=(whole(), whole()) + (anywhere,) * 4 + (whole(),) * 4,
        scratch_shapes=[
            pltpu.VMEM((16, in_bias.shape[1]), BF16),
            pltpu.VMEM((BLOCKS, HEAD_DIM, BLOCK), BF16),
            pltpu.VMEM((BLOCKS, BLOCK, HEAD_DIM + EXTRA), BF16),
            pltpu.VMEM((ROW_LEN, HEAD_DIM), BF16),
            pltpu.VMEM(piece, BF16),
            pltpu.VMEM(piece, BF16),
            pltpu.SemaphoreType.DMA((4,)),
            *sems((2, peers), (2, peers), (3, 2, peers), (3, levels, 2, peers)),
            pltpu.SemaphoreType.DMA((head_total,)),
            *sems((head_total, peers)),
        ],
        compiler_params=pltpu.CompilerParams(
            collective_id=0, has_side_effects=True, vmem_limit_bytes=VMEM_BYTES
        ),
        cost_estimate=pl.CostEstimate(
            flops=16 * head_total * ROW_LEN * ROW_LEN * HEAD_DIM,
            bytes_accessed=32 * 1024 * 1024,
            transcendentals=head_total * ROW_LEN * ROW_LEN,
        ),
        name="front",
    )(frames, qkv_weight, q_bias, v_bias, seg_row, in_weight, down_weight, out_weight, in_bias)


def reduce_orders(bits):
    if bits == 3:
        return ((0, 1, 2), (0, 2, 1), (0, 1, 2))
    return (tuple(range(bits)),) * 3


def back_kernel(
    bits,
    seg_row,
    seg_col,
    qkv,
    out_cols,
    log_total,
    grads_out,
    in_grads,
    down_grads,
    head_grads,
    input_all,
    vector,
    traded,
    in_sum,
    down_sum,
    head_sum,
    proj_sum,
    vector_sum,
    bias_sum,
    seg_blocks,
    grads_in,
    grads,
    qkv_grad,
    key_buf,
    key_cols,
    value_buf,
    query_sum,
    key_sum,
    value_sum,
    staged,
    kept,
    taken,
    last,
    proj,
    proj_taken,
    proj_all,
    proj_rows,
    vectors,
    vectors_taken,
    vectors_all,
    biases,
    biases_taken,
    keep_sems,
    grads_own,
    grads_send,
    grads_recv,
    traded_own,
    traded_send,
    traded_recv,
    level_send,
    level_recv,
    last_send,
    last_recv,
    back_send,
    back_recv,
    proj_send,
    proj_recv,
    vector_send,
    vector_recv,
    vector_last_send,
    vector_last_recv,
    bias_send,
    bias_recv,
):
    head_total, mp_size = grads_out.shape[1], grads_out.shape[0]
    half = grads_out.shape[2]
    me = lax.axis_index("mp")
    dp_index = lax.axis_index("dp")
    peers = range(1, mp_size)
    orders = reduce_orders(bits)
    partials = (in_grads, down_grads, head_grads)
    sums = (in_sum, down_sum, head_sum)
    arrays = range(3)

    def target(offset):
        return lax.rem(me + offset, mp_size)

    def bit_of(which, level):
        return (dp_index // 2 ** orders[which][level]) % 2


    def part_of(turn):
        return target(turn + 1)

    def level_copy(which, level, turn):
        count = 2 ** (bits - 1 - level)
        other = (1 - bit_of(which, level)) * count
        part = pl.ds(part_of(turn), 1)
        source = partials[which] if level == 0 else taken[which][level - 1]
        return send(
            source.at[part, pl.ds(other, count)],
            taken[which][level].at[part],
            (level_send, level_recv),
            (which, level, turn),
            {"dp": partner_of(dp_index, orders[which][level])},
        )

    def keep_copy(which):
        count = 2 ** (bits - 1)
        return pltpu.make_async_copy(
            partials[which].at[:, pl.ds(bit_of(which, 0) * count, count)],
            kept[which],
            keep_sems.at[which],
        )

    def last_copy(which, offset):
        return send(
            taken[which][bits - 1].at[target(offset)],
            last[which].at[offset - 1],
            (last_send, last_recv),
            (which, offset - 1),
            {"mp": target(offset)},
        )

    def add_level(which, level, turn):
        level_copy(which, level, turn).wait_recv()
        count = 2 ** (bits - 1 - level)
        if level == 0 and turn == 0:
            keep_copy(which).wait()
        start = bit_of(which, level) * count
        into = taken[which][level]
        part = part_of(turn)
        for slot in range(count):
            if level == 0:
                mine = kept[which][part, slot]
            else:
                mine = taken[which][level - 1][part, start + slot]
            into[part, slot] = (into[part, slot].astype(F32) + mine.astype(F32)).astype(BF16)
        if level + 1 < bits:
            level_copy(which, level + 1, turn).start()
        elif turn + 1 < mp_size:
            last_copy(which, turn + 1).start()

    def slot_of(order):
        return place_in(dp_index, order[::-1])

    def held_slots(order, level):
        count = 2 ** (bits - 1 - level)
        return pl.ds(slot_of(order) // count * count, count)

    def spread_copy(which, level):
        held = sums[which].at[held_slots(orders[which], level)]
        partner = {"dp": partner_of(dp_index, orders[which][level])}
        return send(held, held, (back_send, back_recv), (which, level), partner)

    def finish_sum(which):
        total = taken[which][bits - 1][me, 0].astype(F32)
        for offset in peers:
            last_copy(which, offset).wait_recv()
            total = total + last[which][offset - 1, 0].astype(F32)
        sums[which][slot_of(orders[which])] = total.astype(BF16)
        spread_copy(which, bits - 1).start()

    def spread(level):
        for which in arrays:
            spread_copy(which, level).wait_recv()
            if level:
                spread_copy(which, level - 1).start()


    def proj_copy(head, level):
        count = 2 ** (bits - 1 - level)
        other = (1 - bit_of(0, level)) * count
        source = proj[head] if level == 0 else proj_taken[head][level - 1]
        return send(
            source.at[pl.ds(other, count)],
            proj_taken[head][level],
            (proj_send, proj_recv),
            (0, head, level),
            {"dp": partner_of(dp_index, orders[0][level])},
        )

    def proj_spread_copy(head, level):
        held = proj_all[head].at[held_slots(orders[0], level)]
        partner = {"dp": partner_of(dp_index, orders[0][level])}
        return send(held, held, (proj_send, proj_recv), (1, head, level), partner)

    def add_proj(head, level):
        proj_copy(head, level).wait_recv()
        count = 2 ** (bits - 1 - level)
        start = bit_of(0, level) * count
        into = proj_taken[head][level]
        for slot in range(count):
            mine = proj[head][start + slot] if level == 0 else proj_taken[head][level - 1][start + slot]
            into[slot] = (into[slot].astype(F32) + mine.astype(F32)).astype(BF16)
        if level + 1 < bits:
            proj_copy(head, level + 1).start()
        else:
            proj_all[head][slot_of(orders[0])] = into[0]
            proj_spread_copy(head, level).start()

    def spread_proj(head, level):
        proj_spread_copy(head, level).wait_recv()
        if level:
            proj_spread_copy(head, level - 1).start()

    def finish_proj(head):
        cols = slice(head * HEAD_DIM, (head + 1) * HEAD_DIM)
        slot_rows = proj_all[head].shape[1]
        for slot in range(2**bits):
            proj_rows[slot * slot_rows : (slot + 1) * slot_rows] = proj_all[head][slot].astype(F32)
        for part in range(3):
            rows = proj_rows[part * HEAD_DIM : (part + 1) * HEAD_DIM]
            proj_sum[part, cols] = rows.astype(BF16)


    def vector_copy(level):
        return send(
            vectors[level],
            vectors_taken[level],
            (vector_send, vector_recv),
            level,
            {"dp": partner_of(dp_index, level)},
        )

    def vector_last_copy(offset):
        return send(
            vectors[bits],
            vectors_all.at[me],
            (vector_last_send, vector_last_recv),
            offset - 1,
            {"mp": target(offset)},
        )

    def add_vector(level):
        vector_copy(level).wait_recv()
        vectors[level + 1][...] = vectors[level][...] + vectors_taken[level][...]
        if level + 1 < bits:
            vector_copy(level + 1).start()
        else:
            vectors_all[me] = vectors[bits][...]
            for offset in peers:
                vector_last_copy(offset).start()

    def finish_vector():
        for offset in peers:
            vector_last_copy(offset).wait_recv()
        total = vectors_all[0]
        for index in peers:
            total = total + vectors_all[index]
        vector_sum[...] = total

    def bias_copy(level):
        return send(
            biases[level],
            biases_taken[level],
            (bias_send, bias_recv),
            level,
            {"dp": partner_of(dp_index, level)},
        )

    def add_bias(level):
        bias_copy(level).wait_recv()
        biases[level + 1][...] = biases[level][...] + biases_taken[level][...]
        if level + 1 < bits:
            bias_copy(level + 1).start()
        else:
            bias_sum[...] = biases[bits][...]


    def grads_copy(head, offset):
        return send(
            grads_out.at[target(offset), head],
            grads_in.at[head, me],
            (grads_send, grads_recv),
            (head, offset - 1),
            {"mp": target(offset)},
        )

    def grads_own_copy(head):
        return pltpu.make_async_copy(
            grads_out.at[me, head], grads_in.at[head, me], grads_own.at[head]
        )

    def traded_copy(head, offset):
        return send(
            staged.at[head, target(offset)],
            traded.at[head, me],
            (traded_send, traded_recv),
            (head, offset - 1),
            {"mp": target(offset)},
        )

    def traded_own_copy(head):
        return pltpu.make_async_copy(
            staged.at[head, me], traded.at[head, me], traded_own.at[head]
        )

    def prepare(head):
        cols = slice(head * HEAD_DIM, (head + 1) * HEAD_DIM)
        key_buf[:, :HEAD_DIM] = qkv[1, :, cols]
        key_buf[:, HEAD_DIM:] = ones_columns(ROW_LEN)
        value_buf[:, :HEAD_DIM] = qkv[2, :, cols]
        value_buf[:, HEAD_DIM:] = ones_columns(ROW_LEN)
        for step in range(BLOCKS):
            key_cols[step] = qkv[1, step * BLOCK : (step + 1) * BLOCK, cols].T
        key_sum[...] = jnp.zeros_like(key_sum)
        value_sum[...] = jnp.zeros_like(value_sum)

    def take_grads(head):
        grads_own_copy(head).wait()
        for offset in peers:
            grads_copy(head, offset).wait_recv()
        for chunk in range(mp_size):
            for side in range(2):
                start = (2 * chunk + side) * half
                grads[start : start + half] = grads_in[
                    head, chunk, :, side * HEAD_DIM : (side + 1) * HEAD_DIM
                ]

    def attend_back(head):
        cols = slice(head * HEAD_DIM, (head + 1) * HEAD_DIM)

        def query_block(number, _):
            rows = block_rows(number)
            queries = qkv[0, rows, cols] * SCALE
            grad_rows = grads[rows]
            seg_query = seg_blocks[number]
            grad_cols = grad_rows.astype(F32).T
            row_dot = jnp.sum(grad_cols * out_cols[head, number], axis=0, keepdims=True)
            grad_cols = jnp.concatenate([grad_cols.astype(BF16), as_pieces(-row_dot)], axis=0)
            query_cols = jnp.concatenate(
                [queries.astype(F32).T.astype(BF16), as_pieces(-log_total[head, number])], axis=0
            )

            def step_back(step, query_grad):
                key_rows = block_rows(step)
                same = jnp.concatenate([seg_col[key_rows]] * (BLOCK // 128), axis=1) == seg_query
                scores = dot(key_buf[key_rows], query_cols)
                soft = jnp.exp(jnp.where(same, scores, MASKED))
                soft_grad = dot(value_buf[key_rows], grad_cols)
                score_grad = (soft * soft_grad).astype(BF16)
                value_sum[key_rows] += dot(soft.astype(BF16), grad_rows)
                key_sum[key_rows] += dot(score_grad, queries)
                query_grad = query_grad + dot(key_cols[step], score_grad)
                for at in range(head * BLOCKS**2, (head + 1) * BLOCKS**2):
                    if at in events:

                        @pl.when(number * BLOCKS + step == at - head * BLOCKS**2)
                        def _():
                            for act in events[at]:
                                act()

                return query_grad

            query_grad = lax.fori_loop(0, BLOCKS, step_back, jnp.zeros((HEAD_DIM, BLOCK), F32))
            query_sum[rows] = (query_grad * SCALE).T
            return 0

        lax.fori_loop(0, BLOCKS, query_block, 0)

    def give_grads(head):
        for part, total in enumerate((query_sum, key_sum, value_sum)):
            low = total[...].astype(BF16)
            qkv_grad[:, part * HEAD_DIM : (part + 1) * HEAD_DIM] = low
            if part != 1:
                cols = slice(head * HEAD_DIM, (head + 1) * HEAD_DIM)
                sum_low = jnp.sum(low.astype(F32), axis=0, keepdims=True)
                biases[0][part : part + 1, cols] = sum_low
            for chunk in range(mp_size):
                for side in range(2):
                    start = (2 * chunk + side) * half
                    staged[head, chunk, part, :, side * HEAD_DIM : (side + 1) * HEAD_DIM] = total[
                        start : start + half
                    ].astype(BF16)

    def start_trade(head):
        for offset in peers:
            traded_copy(head, offset).start()
        traded_own_copy(head).start()

    def start_proj(head):
        products = dot_cols(qkv_grad[...], input_all[...])
        slot_rows = proj[head].shape[1]
        for slot in range(2**bits):
            proj[head][slot] = products[slot * slot_rows : (slot + 1) * slot_rows].astype(BF16)
        proj_copy(head, 0).start()

    def advance(level, turn):
        for which in arrays:
            add_level(which, level, turn)

    events = {}
    levels = list(range(bits))
    turns = range(mp_size)
    schedule = [
        *zip((1, 3, 5), itertools.repeat(add_vector), levels),
        (9, finish_vector),
        *zip((11, 13, 15), itertools.repeat(add_proj), itertools.repeat(0), levels),
        *zip((17, 19, 21), itertools.repeat(spread_proj), itertools.repeat(0), levels[::-1]),
        *zip((20, 22, 24), itertools.repeat(add_proj), itertools.repeat(1), levels),
    ]
    for level, when in zip(levels, ((2, 8, 12, 18), (6, 11, 16, 22), (9, 14, 19, 25))):
        schedule += zip(when, itertools.repeat(advance), itertools.repeat(level), turns)
    for at, act, *which in schedule:
        events.setdefault(at, []).append(partial(act, *which))

    enter(dp_index, me, mp_size, bits)
    for offset in peers:
        grads_copy(0, offset).start()
    vectors[0][...] = vector[...]
    vector_copy(0).start()
    for turn in turns:
        for which in arrays:
            level_copy(which, 0, turn).start()
    for which in arrays:
        keep_copy(which).start()
    for head in range(head_total):
        grads_own_copy(head).start()
    biases[0][...] = jnp.zeros_like(biases[0])
    for step in range(BLOCKS):
        seg_blocks[step] = seg_row[:, step * BLOCK : (step + 1) * BLOCK]
    final = head_total - 1
    for head in range(head_total):
        prepare(head)
        take_grads(head)
        if head == 0:
            for later in range(1, head_total):
                for offset in peers:
                    grads_copy(later, offset).start()
        attend_back(head)
        give_grads(head)
        start_trade(head)
        if head == final:
            for which in arrays:
                finish_sum(which)
        start_proj(head)
    bias_copy(0).start()
    for level in levels:
        add_proj(final, level)
        add_bias(level)
        spread(bits - 1 - level)
        spread_proj(final - 1, bits - 1 - level)
    for level in levels[::-1]:
        spread_proj(final, level)
    for head in range(head_total):
        finish_proj(head)
        traded_own_copy(head).wait()
        for offset in peers:
            grads_copy(head, offset).wait_send()
            traded_copy(head, offset).wait()
        for level in levels:
            proj_copy(head, level).wait_send()
            proj_spread_copy(head, level).wait_send()
    for level in levels:
        vector_copy(level).wait_send()
        bias_copy(level).wait_send()
        for which in arrays:
            spread_copy(which, level).wait_send()
            for turn in turns:
                level_copy(which, level, turn).wait_send()
    for offset in peers:
        vector_last_copy(offset).wait_send()
        for which in arrays:
            last_copy(which, offset).wait_send()


def back(
    seg_row, seg_col, qkv_low, out_cols, log_total, grads_out, partials, input_all, vector, bits
):
    mp_size, head_total, half, lanes = grads_out.shape
    peers = mp_size - 1
    slots = 2**bits
    width = input_all.shape[1]
    anywhere = pl.BlockSpec(memory_space=pl.ANY)
    blocks = [partial_sum.shape[2:] for partial_sum in partials]
    proj_block = (3 * HEAD_DIM // slots, width)
    bias_block = (8, 2 * 128)

    def halves(shape, dtype, lead=()):
        return [pltpu.VMEM(lead + (slots >> (level + 1),) + shape, dtype) for level in range(bits)]

    def sems(*shapes):
        return [pltpu.SemaphoreType.DMA(shape) for shape in shapes for _ in range(2)]

    return pl.pallas_call(
        partial(back_kernel, bits),
        out_shape=(jax.ShapeDtypeStruct((head_total, mp_size, 3, half, lanes), BF16),)
        + tuple(jax.ShapeDtypeStruct((slots,) + block, BF16) for block in blocks)
        + (
            jax.ShapeDtypeStruct((3, head_total * HEAD_DIM, width), BF16),
            jax.ShapeDtypeStruct(vector.shape, F32),
            jax.ShapeDtypeStruct(bias_block, F32),
        ),
        in_specs=[whole()] * 5 + [anywhere] * 4 + [whole()] * 2,
        out_specs=(anywhere,) + (whole(),) * 6,
        scratch_shapes=[
            pltpu.VMEM((BLOCKS, 1, BLOCK), jnp.int32),
            pltpu.VMEM((head_total, mp_size, half, lanes), BF16),
            pltpu.VMEM((ROW_LEN, HEAD_DIM), BF16),
            pltpu.VMEM((ROW_LEN, 3 * HEAD_DIM), BF16),
            pltpu.VMEM((ROW_LEN, HEAD_DIM + EXTRA), BF16),
            pltpu.VMEM((BLOCKS, HEAD_DIM, BLOCK), BF16),
            pltpu.VMEM((ROW_LEN, HEAD_DIM + EXTRA), BF16),
            pltpu.VMEM((ROW_LEN, HEAD_DIM), F32),
            pltpu.VMEM((ROW_LEN, HEAD_DIM), F32),
            pltpu.VMEM((ROW_LEN, HEAD_DIM), F32),
            pltpu.VMEM((head_total, mp_size, 3, half, lanes), BF16),
            [pltpu.VMEM((mp_size, slots // 2) + block, BF16) for block in blocks],
            [halves(block, BF16, (mp_size,)) for block in blocks],
            [pltpu.VMEM((peers, 1) + block, BF16) for block in blocks],
            [pltpu.VMEM((slots,) + proj_block, BF16) for _ in range(head_total)],
            [halves(proj_block, BF16) for _ in range(head_total)],
            [pltpu.VMEM((slots,) + proj_block, BF16) for _ in range(head_total)],
            pltpu.VMEM((3 * HEAD_DIM, width), F32),
            [pltpu.VMEM(vector.shape, F32) for _ in range(bits + 1)],
            [pltpu.VMEM(vector.shape, F32) for _ in range(bits)],
            pltpu.VMEM((mp_size,) + vector.shape, F32),
            [pltpu.VMEM(bias_block, F32) for _ in range(bits + 1)],
            [pltpu.VMEM(bias_block, F32) for _ in range(bits)],
            pltpu.SemaphoreType.DMA((3,)),
            pltpu.SemaphoreType.DMA((head_total,)),
            *sems((head_total, peers)),
            pltpu.SemaphoreType.DMA((head_total,)),
            *sems(
                (head_total, peers),
                (3, bits, mp_size),
                (3, peers),
                (3, bits),
                (2, head_total, bits),
                (bits,),
                (peers,),
                (bits,),
            ),
        ],
        compiler_params=pltpu.CompilerParams(
            collective_id=2, has_side_effects=True, vmem_limit_bytes=VMEM_BYTES
        ),
        cost_estimate=pl.CostEstimate(
            flops=40 * head_total * ROW_LEN * ROW_LEN * HEAD_DIM,
            bytes_accessed=64 * 1024 * 1024,
            transcendentals=head_total * ROW_LEN * ROW_LEN,
        ),
        name="back",
    )(
        seg_row,
        seg_col,
        qkv_low,
        out_cols,
        log_total,
        grads_out,
        *partials,
        input_all,
        vector,
    )


def norm_rows(inputs, norm_gain, norm_shift):
    row_mean = jnp.mean(inputs, axis=-1, keepdims=True)
    centred = inputs - row_mean
    variance = jnp.mean(centred * centred, axis=-1, keepdims=True)
    inv_std = lax.rsqrt(variance + 1e-05)
    normed = centred * inv_std
    return (normed * norm_gain + norm_shift, normed, inv_std)


def norm_back(cotangent, normed, inv_std, norm_gain):
    scaled = cotangent * norm_gain
    adjusted = (
        scaled
        - jnp.mean(scaled, axis=-1, keepdims=True)
        - normed * jnp.mean(scaled * normed, axis=-1, keepdims=True)
    )
    return adjusted * inv_std


def sum_rows(array):
    return jnp.sum(array.astype(F32), axis=0, keepdims=True)


def middle_kernel(
    bits,
    frames,
    heads_low,
    out_grad,
    in_bias,
    out_bias,
    down_bias,
    norm_gain,
    norm_shift,
    in_all,
    down_all,
    out_all,
    proj_weight,
    block_out,
    resid_grad,
    grads_out,
    vector,
    in_grads,
    down_grads,
    head_grads,
    proj_all,
    in_buf,
    down_buf,
    out_buf,
    hidden,
    slope,
    pre_grad,
    mid_buf,
    normed_buf,
    normed_out,
    low_buf,
    grad_buf,
    given,
    in_sems,
    down_sems,
    out_sems,
    given_sems,
    proj_own,
    proj_send,
    proj_recv,
    trade_send,
    trade_recv,
):
    mp_size, units, width = down_all.shape
    head_cols = width // mp_size
    local_rows = frames.shape[0]
    half = local_rows // 2
    slots = in_grads.shape[1]
    out_copies = [
        pltpu.make_async_copy(
            out_all.at[index],
            out_buf.at[pl.ds(index * head_cols, head_cols)],
            out_sems.at[index],
        )
        for index in range(mp_size)
    ]

    def in_copy(index):
        return pltpu.make_async_copy(in_all.at[index], in_buf.at[index], in_sems.at[index])

    def down_copy(index):
        return pltpu.make_async_copy(down_all.at[index], down_buf.at[index], down_sems.at[index])

    me = lax.axis_index("mp")
    dp_index = lax.axis_index("dp")
    line = Line(mp_size, me)
    order = gather_orders(bits)[3]
    own_slot = place_in(dp_index, order)

    def proj_copy(side, hop):
        place = proj_all.at[line.place(side, hop), pl.ds(own_slot, 1)]
        source = proj_weight.at[pl.ds(own_slot, 1)] if hop == 0 else place
        return send(source, place, (proj_send, proj_recv), (side, hop), line.neighbour(side))

    def trade_copy(level, side, hop):
        held = pl.ds(own_slot // 2**level * 2**level, 2**level)
        place = proj_all.at[line.place(side, hop + 1), held]
        partner = {"dp": partner_of(dp_index, order[level])}
        return send(place, place, (trade_send, trade_recv), (level, side, hop), partner)

    def take_proj(side, hop):
        proj_copy(side, hop).wait_recv()
        if hop + 1 < mp_size - 1:
            line.if_sent(side, hop + 1)(lambda: proj_copy(side, hop + 1).start())
        if bits:
            trade_copy(0, side, hop).start()

    def trade_proj(level, side, hop):
        trade_copy(level, side, hop).wait_recv()
        if level + 1 < bits:
            trade_copy(level + 1, side, hop).start()

    def both_sides(act, *which):
        for side in (0, 1):
            line.if_taken(side, which[-1])(partial(act, *which[:-1], side, which[-1]))

    schedule = (
        (0, take_proj, 0),
        (1, take_proj, 1),
        (2, take_proj, 2),
        (2, trade_proj, 0, 0),
        (3, trade_proj, 0, 1),
        (3, trade_proj, 0, 2),
        (4, trade_proj, 1, 0),
        (6, trade_proj, 1, 1),
        (8, trade_proj, 1, 2),
    )
    done = set()

    def at_point(point, offset=0, index=None):
        for at, act, *which in schedule:
            if which[-1] not in line.hops or (act is trade_proj and which[0] >= bits):
                continue
            if index is None and at == point:
                both_sides(act, *which)
                done.add((act, *which))
            if index is not None and offset <= at < offset + mp_size:
                pl.when(index == at - offset)(partial(both_sides, act, *which))
                done.add((act, *which))

    enter(dp_index, me, mp_size, bits)
    for side in (0, 1):
        line.if_sent(side, 0)(lambda side=side: proj_copy(side, 0).start())
    own = pltpu.make_async_copy(proj_weight, proj_all.at[me], proj_own)
    own.start()
    for copy in out_copies:
        copy.start()
    for index in range(mp_size):
        in_copy(index).start()
        down_copy(index).start()
    vector[...] = jnp.zeros_like(vector)
    gains = norm_gain[...].astype(F32)
    shifts = norm_shift[...].astype(F32)

    for copy in out_copies:
        copy.wait()
    branch = dot(heads_low[...], out_buf[...]) + out_bias[...].astype(F32)
    mid, normed, inv_mid = norm_rows(frames[...].astype(F32) + branch, gains[:1], shifts[:1])
    mid_buf[...] = mid + down_bias[...].astype(F32)
    normed_buf[...] = normed
    low_buf[...] = mid.astype(BF16)
    at_point(0)

    def feed(index, _):
        in_copy(index).wait()
        pre_act = dot(low_buf[...], in_buf[index]) + in_bias[index, 0:1].astype(F32)
        unit_cdf = 0.5 * (1.0 + lax.erf(pre_act * 0.5**0.5))
        bell = jnp.exp(-0.5 * pre_act * pre_act) * (2.0 * jnp.pi) ** (-0.5)
        slope[index] = unit_cdf + pre_act * bell
        hidden[index] = (pre_act * unit_cdf).astype(BF16)
        down_copy(index).wait()
        mid_buf[...] += dot(hidden[index], down_buf[index])
        at_point(None, 1, index)
        return 0

    lax.fori_loop(0, mp_size, feed, 0)
    output, normed, inv_out = norm_rows(mid_buf[...], gains[1:], shifts[1:])
    block_out[...] = output
    normed_out[...] = normed

    cotangent = out_grad[...].astype(F32)
    vector[1:2] = sum_rows(cotangent * normed_out[...])
    vector[3:4] = sum_rows(cotangent)
    sum_grad = norm_back(cotangent, normed_out[...], inv_out, gains[1:])
    mid_buf[...] = sum_grad
    grad_buf[...] = sum_grad.astype(BF16)
    vector[5:6] = sum_rows(grad_buf[...])

    def feed_back(index, _):
        pre = dot_rows(grad_buf[...], down_buf[index]) * slope[index]
        pre_grad[index] = pre.astype(BF16)
        vector[pl.ds(8 + index, 1)] = sum_rows(pre_grad[index])
        mid_buf[...] += dot_rows(pre_grad[index], in_buf[index])
        at_point(None, 1 + mp_size, index)
        return 0

    lax.fori_loop(0, mp_size, feed_back, 0)
    mid_grad = mid_buf[...]
    vector[0:1] = sum_rows(mid_grad * normed_buf[...])
    vector[2:3] = sum_rows(mid_grad)
    resid = norm_back(mid_grad, normed_buf[...], inv_mid, gains[:1])
    resid_grad[...] = resid
    attn_grad = resid.astype(BF16)
    vector[4:5] = sum_rows(attn_grad)
    heads_grad = dot_rows(attn_grad, out_buf[...]).astype(BF16)
    for index in range(mp_size):
        for head in range(head_cols // HEAD_DIM):
            at = index * head_cols + head * HEAD_DIM
            for side in range(2):
                grads_out[index, head, :, side * HEAD_DIM : (side + 1) * HEAD_DIM] = heads_grad[
                    side * half : (side + 1) * half, at : at + HEAD_DIM
                ]

    products = dot_cols(heads_low[...], attn_grad).astype(BF16)
    rows = head_cols // slots
    for index in range(mp_size):
        for slot in range(slots):
            start = index * head_cols + slot * rows
            head_grads[index, slot, :rows] = products[start : start + rows]
            if rows < head_grads.shape[2]:
                head_grads[index, slot, rows:] = jnp.zeros(
                    (head_grads.shape[2] - rows, width), BF16
                )
    normed_low = low_buf[...].T

    def given_copy(which, index):
        return pltpu.make_async_copy(
            given.at[which, index % 2],
            (in_grads, down_grads)[which].at[index],
            given_sems.at[which, index % 2],
        )

    for index in range(mp_size):
        for which in range(2):
            if index >= 2:
                given_copy(which, index - 2).wait()
            if which == 0:
                result = dot(normed_low, pre_grad[index])
            else:
                result = dot_cols(hidden[index], grad_buf[...])
            share = result.shape[0] // slots
            for slot in range(slots):
                given[which, index % 2, slot] = result[slot * share : (slot + 1) * share].astype(BF16)
            given_copy(which, index).start()
    for index in range(max(mp_size - 2, 0), mp_size):
        for which in range(2):
            given_copy(which, index).wait()
    for hop in line.hops:
        if (take_proj, hop) not in done:
            both_sides(take_proj, hop)
    for level in range(bits):
        for hop in line.hops:
            if (trade_proj, level, hop) not in done:
                both_sides(trade_proj, level, hop)

    def sent_trades(side, hop):
        for level in range(bits):
            trade_copy(level, side, hop).wait_send()

    for side, hop in line.ways:
        line.if_sent(side, hop)(lambda side=side, hop=hop: proj_copy(side, hop).wait_send())
        line.if_taken(side, hop)(partial(sent_trades, side, hop))
    own.wait()


def middle(frames, heads_low, out_grad, in_bias, small, weights, proj_weight, bits):
    local_rows, width = frames.shape
    mp_size, units = weights[1].shape[:2]
    slots = 2**bits
    peers = mp_size - 1
    head_cols = width // mp_size
    head_rows = head_cols // slots
    anywhere = pl.BlockSpec(memory_space=pl.ANY)
    rows = jax.ShapeDtypeStruct((local_rows, width), F32)
    gradient = jax.ShapeDtypeStruct((mp_size, slots, units // slots, width), BF16)
    return pl.pallas_call(
        partial(middle_kernel, bits),
        out_shape=(
            rows,
            rows,
            jax.ShapeDtypeStruct(
                (mp_size, head_cols // HEAD_DIM, local_rows // 2, 2 * HEAD_DIM), BF16
            ),
            jax.ShapeDtypeStruct((8 + -(-mp_size // 8) * 8, width), F32),
            gradient,
            gradient,
            jax.ShapeDtypeStruct((mp_size, slots, -(-head_rows // 16) * 16, width), BF16),
            jax.ShapeDtypeStruct((mp_size,) + proj_weight.shape, BF16),
        ),
        in_specs=[whole()] * 8 + [anywhere] * 4,
        out_specs=(whole(),) * 4 + (anywhere,) * 2 + (whole(), anywhere),
        scratch_shapes=[
            pltpu.VMEM((mp_size, width, units), BF16),
            pltpu.VMEM((mp_size, units, width), BF16),
            pltpu.VMEM((width, width), BF16),
            pltpu.VMEM((mp_size, local_rows, units), BF16),
            pltpu.VMEM((mp_size, local_rows, units), F32),
            pltpu.VMEM((mp_size, local_rows, units), BF16),
            pltpu.VMEM((local_rows, width), F32),
            pltpu.VMEM((local_rows, width), F32),
            pltpu.VMEM((local_rows, width), F32),
            pltpu.VMEM((local_rows, width), BF16),
            pltpu.VMEM((local_rows, width), BF16),
            pltpu.VMEM((2, 2, slots, units // slots, width), BF16),
            pltpu.SemaphoreType.DMA((mp_size,)),
            pltpu.SemaphoreType.DMA((mp_size,)),
            pltpu.SemaphoreType.DMA((mp_size,)),
            pltpu.SemaphoreType.DMA((2, 2)),
            pltpu.SemaphoreType.DMA,
            pltpu.SemaphoreType.DMA((2, peers)),
            pltpu.SemaphoreType.DMA((2, peers)),
            pltpu.SemaphoreType.DMA((max(bits, 1), 2, peers)),
            pltpu.SemaphoreType.DMA((max(bits, 1), 2, peers)),
        ],
        compiler_params=pltpu.CompilerParams(
            collective_id=1, has_side_effects=True, vmem_limit_bytes=VMEM_BYTES
        ),
        cost_estimate=pl.CostEstimate(
            flops=12 * local_rows * width * (mp_size * units + width // 2),
            bytes_accessed=40 * 1024 * 1024,
            transcendentals=2 * local_rows * mp_size * units,
        ),
        name="middle",
    )(frames, heads_low, out_grad, in_bias, *small, *weights, proj_weight)


def finish_kernel(
    traded,
    proj_all,
    resid_grad,
    in_sum,
    down_sum,
    head_sum,
    proj_sum,
    vector_sum,
    bias_sum,
    stream_grad,
    in_grad,
    down_grad,
    out_grad,
    proj_grad,
    query_bias_grad,
    value_bias_grad,
    out_bias_grad,
    in_bias_grad,
    down_bias_grad,
    gain_grad,
    shift_grad,
    columns,
    weight_buf,
    sems,
):
    head_total, mp_size = traded.shape[:2]
    half = traded.shape[3]
    head_cols = head_total * HEAD_DIM
    copies = [
        pltpu.make_async_copy(
            proj_all.at[index],
            weight_buf.at[index],
            sems.at[index],
        )
        for index in range(mp_size)
    ]
    for copy in copies:
        copy.start()
    for sums, grad in ((in_sum, in_grad), (down_sum, down_grad), (head_sum, out_grad)):
        rows = grad.shape[0] // sums.shape[0]
        for slot in range(sums.shape[0]):
            grad[slot * rows : (slot + 1) * rows] = sums[slot, :rows].astype(F32)
    proj_grad[...] = proj_sum[...].astype(F32)
    query_bias_grad[...] = bias_sum[0:1, :head_cols]
    value_bias_grad[...] = bias_sum[2:3, :head_cols]
    gain_grad[...] = vector_sum[0:2]
    shift_grad[...] = vector_sum[2:4]
    out_bias_grad[...] = vector_sum[4:5]
    down_bias_grad[...] = vector_sum[5:6]
    in_bias_grad[...] = vector_sum[pl.ds(8 + lax.axis_index("mp"), 1)]
    stream_grad[...] = resid_grad[...]
    for index in range(mp_size):
        for head in range(head_total):
            for part in range(3):
                at = part * head_cols + head * HEAD_DIM
                for side in range(2):
                    columns[side * half : (side + 1) * half, at : at + HEAD_DIM] = traded[
                        head, index, part, :, side * HEAD_DIM : (side + 1) * HEAD_DIM
                    ]
        copies[index].wait()
        stream_grad[...] += dot(columns[...], weight_buf[index])


def finish(traded, proj_all, resid_grad, sums):
    head_total, mp_size = traded.shape[:2]
    head_cols = head_total * HEAD_DIM
    local_rows, width = resid_grad.shape
    units = sums[0].shape[0] * sums[0].shape[1]
    row = jax.ShapeDtypeStruct((1, width), F32)
    head_row = jax.ShapeDtypeStruct((1, head_cols), F32)
    anywhere = pl.BlockSpec(memory_space=pl.ANY)
    return pl.pallas_call(
        finish_kernel,
        out_shape=(
            jax.ShapeDtypeStruct((local_rows, width), F32),
            jax.ShapeDtypeStruct((units, width), F32),
            jax.ShapeDtypeStruct((units, width), F32),
            jax.ShapeDtypeStruct((head_cols, width), F32),
            jax.ShapeDtypeStruct((3, head_cols, width), F32),
            head_row,
            head_row,
            row,
            jax.ShapeDtypeStruct((1, units), F32),
            row,
            jax.ShapeDtypeStruct((2, width), F32),
            jax.ShapeDtypeStruct((2, width), F32),
        ),
        in_specs=[whole(), anywhere] + [whole()] * 7,
        out_specs=(whole(),) * 12,
        scratch_shapes=[
            pltpu.VMEM((local_rows, 3 * head_cols), BF16),
            pltpu.VMEM((mp_size, 3 * head_cols, width), BF16),
            pltpu.SemaphoreType.DMA((mp_size,)),
        ],
        compiler_params=pltpu.CompilerParams(vmem_limit_bytes=VMEM_BYTES),
        cost_estimate=pl.CostEstimate(
            flops=6 * local_rows * width * width, bytes_accessed=24 * 1024 * 1024, transcendentals=0
        ),
        name="finish",
    )(traded, proj_all, resid_grad, *sums)


def dp_groups():
    total = lax.axis_size("dp")
    size = min(8, total)
    groups = [list(range(start, start + size)) for start in range(0, total, size)]
    return (size, groups)


def on_device(
    frames,
    segment_ids,
    qkv_weight,
    q_bias,
    v_bias,
    out_weight,
    out_bias,
    ff_in_weight,
    ff_in_bias,
    ff_out_weight,
    ff_out_bias,
    norm_gain,
    norm_shift,
    out_grad,
):
    local_rows, width = frames.shape
    mp_size = lax.axis_size("mp")
    group, groups = dp_groups()
    bits = group_bits(lax.axis_size("dp"))
    slots = 2**bits

    proj_weight = qkv_weight[0].transpose(0, 2, 1)
    seg_row = segment_ids.reshape(1, ROW_LEN)
    (
        input_all,
        qkv_low,
        in_all,
        down_all,
        out_all,
        in_bias_all,
        seg_col,
        out_cols,
        log_total,
        heads_low,
    ) = front(
        frames,
        proj_weight,
        q_bias,
        v_bias,
        seg_row,
        (ff_in_weight[0], ff_out_weight[0], out_weight[0]),
        ff_in_bias,
        mp_size,
        bits,
    )
    block_out, resid_grad, grads_out, vector, *partials, proj_all = middle(
        frames,
        heads_low,
        out_grad,
        in_bias_all,
        (out_bias, ff_out_bias, norm_gain[0], norm_shift[0]),
        (in_all, down_all, out_all),
        proj_weight.reshape(slots, -1, width),
        bits,
    )
    traded, *summed = back(
        seg_row,
        seg_col,
        qkv_low,
        out_cols,
        log_total,
        grads_out,
        partials,
        input_all,
        vector,
        bits,
    )
    if len(groups) > 1:
        across = [list(range(at, lax.axis_size("dp"), group)) for at in range(group)]
        summed = lax.psum(summed, "dp", axis_index_groups=across)
    (
        stream_grad,
        in_weight_grad,
        down_weight_grad,
        out_weight_grad,
        proj_grad,
        query_bias_grad,
        value_bias_grad,
        head_bias_grad,
        in_bias_grad,
        down_bias_grad,
        gain_grad,
        shift_grad,
    ) = finish(traded, proj_all.reshape(mp_size, -1, width), resid_grad, summed)
    return (
        block_out,
        stream_grad,
        proj_grad.transpose(0, 2, 1)[None],
        query_bias_grad,
        value_bias_grad,
        out_weight_grad[None],
        head_bias_grad,
        in_weight_grad[None],
        in_bias_grad,
        down_weight_grad[None],
        down_bias_grad,
        gain_grad[None],
        shift_grad[None],
    )


def solution(mesh):
    return jax.shard_map(
        on_device,
        mesh=mesh,
        in_specs=(
            P(("dp", "mp"), None),
            P("dp"),
            P(None, None, None, "mp"),
            P(None, "mp"),
            P(None, "mp"),
            P(None, "mp", None),
            P(),
            P(None, None, "mp"),
            P(None, "mp"),
            P(None, "mp", None),
            P(),
            P(),
            P(),
            P(("dp", "mp"), None),
        ),
        out_specs=(
            P(("dp", "mp"), None),
            P(("dp", "mp"), None),
            P(None, None, None, "mp"),
            P(None, "mp"),
            P(None, "mp"),
            P(None, "mp", None),
            P(),
            P(None, None, "mp"),
            P(None, "mp"),
            P(None, "mp", None),
            P(),
            P(),
            P(),
        ),
        check_vma=False,
    )
```

```python
import itertools
from functools import partial

import jax
import jax.numpy as jnp
from jax import lax
from jax.experimental import pallas as pl
from jax.experimental.pallas import tpu as pltpu
from jax.sharding import PartitionSpec as P

HEAD_DIM = 64
ROW_LEN = 2304
BLOCK = 768
BLOCKS = ROW_LEN // BLOCK
EXTRA = 16
SCALE = HEAD_DIM ** (-0.5)
MASKED = -1e30
F32 = jnp.float32
BF16 = jnp.bfloat16
VMEM_BYTES = 56 * 1024 * 1024
REAR_VMEM_BYTES = 63 * 1024 * 1024


def dot_rows(left, right):
    return lax.dot_general(left, right, (((1,), (1,)), ((), ())), preferred_element_type=F32)


def dot_cols(left, right):
    return lax.dot_general(left, right, (((0,), (0,)), ((), ())), preferred_element_type=F32)


def dot(left, right):
    return jnp.dot(left, right, preferred_element_type=F32)


def block_rows(number):
    return pl.ds(pl.multiple_of(number * BLOCK, BLOCK), BLOCK)


def as_pieces(row):
    high = row.astype(BF16).astype(F32)
    middle = (row - high).astype(BF16).astype(F32)
    last = row - high - middle
    place = lax.broadcasted_iota(jnp.int32, (EXTRA, row.shape[1]), 0)
    pieces = jnp.where(place == 0, high, jnp.where(place == 1, middle, jnp.where(place == 2, last, 0.0)))
    return pieces.astype(BF16)


def ones_columns(rows):
    place = lax.broadcasted_iota(jnp.int32, (rows, EXTRA), 1)
    return jnp.where(place < 3, 1.0, 0.0).astype(BF16)


def whole(memory_space=pltpu.VMEM):
    return pl.BlockSpec(memory_space=memory_space)


MESH = pl.DeviceIdType.MESH


def group_bits(dp_size):
    return min(3, dp_size.bit_length() - 1)


def place_in(dp_index, order):
    slot = 0
    for at, bit in enumerate(order):
        slot = slot + (dp_index // 2**bit) % 2 * 2**at
    return slot


def partner_of(dp_index, bit):
    return dp_index + (1 - 2 * ((dp_index // 2**bit) % 2)) * 2**bit


def enter(dp_index, mp_index, mp_size, bits):
    barrier = pltpu.get_barrier_semaphore()
    for offset in range(1, mp_size):
        pl.semaphore_signal(
            barrier, device_id={"mp": lax.rem(mp_index + offset, mp_size)}, device_id_type=MESH
        )
    for bit in range(bits):
        pl.semaphore_signal(
            barrier, device_id={"dp": partner_of(dp_index, bit)}, device_id_type=MESH
        )
    pl.semaphore_wait(barrier, mp_size - 1 + bits)


def send(src, dst, sems, at, device_id):
    return pltpu.make_async_remote_copy(
        src_ref=src,
        dst_ref=dst,
        send_sem=sems[0].at[at],
        recv_sem=sems[1].at[at],
        device_id=device_id,
        device_id_type=MESH,
    )


def gather_orders(bits):
    if bits == 3:
        return ((1, 2, 0), (2, 1, 0), (1, 2), (1, 2, 0))
    return (tuple(range(bits)),) * 4


SIDES = (1, -1)


def inside(index, size):
    return jnp.logical_and(index >= 0, index < size)


class Line:
    def __init__(self, mp_size, me):
        self.size = mp_size
        self.me = me
        self.hops = range(mp_size - 1)
        self.ways = [(side, hop) for hop in self.hops for side in (0, 1)]

    def wrapped(self, index):
        return lax.rem(index + self.size, self.size)

    def chunk(self, side, hop):
        return self.me - SIDES[side] * hop

    def place(self, side, hop):
        return self.wrapped(self.chunk(side, hop))

    def sends(self, side, hop):
        there = inside(self.me + SIDES[side], self.size)
        return jnp.logical_and(there, inside(self.chunk(side, hop), self.size))

    def if_sent(self, side, hop):
        return pl.when(self.sends(side, hop))

    def if_taken(self, side, hop):
        return pl.when(inside(self.chunk(side, hop + 1), self.size))

    def neighbour(self, side):
        return {"mp": self.wrapped(self.me + SIDES[side])}


def front_kernel(
    bits,
    frames,
    qkv_weight,
    q_bias,
    v_bias,
    seg_row,
    in_weight,
    down_weight,
    out_weight,
    in_bias,
    input_all,
    qkv_low,
    in_all,
    down_all,
    out_all,
    bias_all,
    seg_col,
    out_cols,
    log_total,
    heads_low,
    bias_buf,
    key_cols,
    value_buf,
    out_buf,
    staged,
    heads_in,
    own_sems,
    frame_send,
    frame_recv,
    bias_send,
    bias_recv,
    first_send,
    first_recv,
    later_send,
    later_recv,
    heads_own,
    heads_send,
    heads_recv,
):
    mp_size = in_all.shape[0]
    me = lax.axis_index("mp")
    dp_index = lax.axis_index("dp")
    local_rows = frames.shape[0]
    half = local_rows // 2
    head_total = out_cols.shape[0]
    orders = gather_orders(bits)[:3]
    parts = ((in_weight, in_all), (down_weight, down_all), (out_weight, out_all))
    line = Line(mp_size, me)
    hops, ways, wrapped = line.hops, line.ways, line.wrapped
    enter(dp_index, me, mp_size, bits)

    def slots(which, level):
        count = parts[which][0].shape[0] // 2 ** len(orders[which])
        start = place_in(dp_index, orders[which]) // 2**level * 2**level
        return pl.ds(pl.multiple_of(start * count, 16), count * 2**level)

    def first_copy(which, side, hop):
        rows = slots(which, 0)
        place = parts[which][1].at[line.place(side, hop), rows]
        source = parts[which][0].at[rows] if hop == 0 else place
        sems = (first_send, first_recv)
        return send(source, place, sems, (which, side, hop), line.neighbour(side))

    def later_copy(which, level, side, hop):
        held = parts[which][1].at[line.place(side, hop + 1), slots(which, level)]
        partner = {"dp": partner_of(dp_index, orders[which][level])}
        return send(held, held, (later_send, later_recv), (which, level, side, hop), partner)

    def frame_rows(index):
        return pl.ds(pl.multiple_of(wrapped(index) * local_rows, local_rows), local_rows)

    def frame_copy(side, hop):
        place = input_all.at[frame_rows(line.chunk(side, hop))]
        source = frames if hop == 0 else place
        return send(source, place, (frame_send, frame_recv), (side, hop), line.neighbour(side))

    def bias_copy(side, hop):
        place = bias_all.at[line.place(side, hop)]
        source = bias_buf if hop == 0 else place
        return send(source, place, (bias_send, bias_recv), (side, hop), line.neighbour(side))

    def project(index):
        rows = frame_rows(index)
        inputs = input_all[rows]
        for part, bias in enumerate((q_bias, None, v_bias)):
            products = dot_rows(inputs, qkv_weight[part])
            if bias is not None:
                products = products + bias[...].astype(F32)
            qkv_low[part, rows] = products.astype(BF16)

    def start_slices(side, hop):
        for which in range(3):
            first_copy(which, side, hop).start()
        bias_copy(side, hop).start()

    def take_slices(side, hop):
        for which in range(3):
            first_copy(which, side, hop).wait_recv()
        bias_copy(side, hop).wait_recv()
        if 0 < hop < mp_size - 2:
            line.if_sent(side, hop + 1)(partial(start_slices, side, hop + 1))
        for which in range(3):
            if orders[which]:
                later_copy(which, 0, side, hop).start()

    def trade_slices(level, side, hop):
        for which in range(3):
            if level < len(orders[which]):
                later_copy(which, level, side, hop).wait_recv()
            if level + 1 < len(orders[which]):
                later_copy(which, level + 1, side, hop).start()

    def take_hop(hop):
        for side in (0, 1):
            line.if_taken(side, hop)(partial(take_slices, side, hop))

    def trade_hop(level, hop):
        for side in (0, 1):
            line.if_taken(side, hop)(partial(trade_slices, level, side, hop))


    bias_buf[...] = jnp.broadcast_to(in_bias[...], bias_buf.shape)
    for side in (0, 1):
        line.if_sent(side, 0)(partial(start_slices, side, 0))
    for side in (0, 1):
        line.if_sent(side, 0)(lambda side=side: frame_copy(side, 0).start())
    own = [
        pltpu.make_async_copy(shard, gathered.at[me], own_sems.at[at])
        for at, (shard, gathered) in enumerate(parts + ((bias_buf, bias_all),))
    ]
    for copy in own:
        copy.start()
    input_all[frame_rows(me)] = frames[...]
    project(me)
    for step in range(BLOCKS):
        ids = jnp.broadcast_to(seg_row[:, step * BLOCK : (step + 1) * BLOCK].astype(F32), (128, BLOCK))
        seg_col[step * BLOCK : (step + 1) * BLOCK] = ids.T.astype(jnp.int32)

    def take_frames(side, hop):
        frame_copy(side, hop).wait_recv()
        if hop + 1 < mp_size - 1:
            line.if_sent(side, hop + 1)(lambda: frame_copy(side, hop + 1).start())

    def project_taken(side, hop):
        project(line.chunk(side, hop + 1))

    for hop in hops:
        for side in (0, 1):
            line.if_taken(side, hop)(partial(take_frames, side, hop))
        if hop == 0:
            take_hop(0)
        elif hop - 1 < bits:
            trade_hop(hop - 1, 0)
        for side in (0, 1):
            free = line.sends(side, hop)
            if hop + 1 < mp_size - 1:
                free = jnp.logical_and(free, jnp.logical_not(line.sends(side, hop + 1)))
            if mp_size > 2:
                passes = jnp.logical_and(free, line.sends(side, 1))
                pl.when(passes)(partial(start_slices, side, 1))
        for side in (0, 1):
            line.if_taken(side, hop)(partial(project_taken, side, hop))

    schedule = (
        (1, take_hop, 1),
        (3, trade_hop, 0, 1),
        (4, take_hop, 2),
        (6, trade_hop, 1, 1),
        (6, trade_hop, 0, 2),
    )
    events = {}
    done = {(take_hop, 0)} | {(trade_hop, hop - 1, 0) for hop in hops if 0 < hop <= bits}
    for at, act, *which in schedule:
        if which[-1] in hops and (act is take_hop or which[0] < bits):
            events.setdefault((at // BLOCKS, at % BLOCKS), []).append(partial(act, *which))
            done.add((act, *which))

    def attend(head):
        cols = slice(head * HEAD_DIM, (head + 1) * HEAD_DIM)
        lane = lax.broadcasted_iota(jnp.int32, (BLOCK, EXTRA), 1)
        for step in range(BLOCKS):
            rows = slice(step * BLOCK, (step + 1) * BLOCK)
            key_cols[step] = qkv_low[1, rows, cols].T
            value_buf[step, :, :HEAD_DIM] = qkv_low[2, rows, cols]
            value_buf[step, :, HEAD_DIM:] = jnp.where(lane == 0, 1.0, 0.0).astype(BF16)

        def query_block(number, _):
            rows = block_rows(number)
            queries = qkv_low[0, rows, cols] * SCALE

            def scores_of(step):
                ids = seg_row[:, step * BLOCK : (step + 1) * BLOCK]
                same = jnp.concatenate([seg_col[rows]] * (BLOCK // 128), axis=1) == ids
                return jnp.where(same, dot(queries, key_cols[step]), MASKED)

            peak = jnp.full((BLOCK, 1), MASKED, F32)
            mixed = jnp.zeros((BLOCK, HEAD_DIM + EXTRA), F32)
            scores = scores_of(0)
            for step in range(BLOCKS):
                ahead = scores_of(step + 1) if step + 1 < BLOCKS else None
                higher = jnp.maximum(peak, jnp.max(scores, axis=1, keepdims=True))
                soft = jnp.exp(scores - higher).astype(BF16)
                mixed = mixed * jnp.exp(peak - higher) + dot(soft, value_buf[step])
                peak, scores = higher, ahead
            total = mixed[:, HEAD_DIM : HEAD_DIM + 1]
            mixed = mixed[:, :HEAD_DIM] / total
            logs = jnp.broadcast_to(peak + jnp.log(total), (BLOCK, HEAD_DIM))
            both = jnp.concatenate([mixed, logs], axis=1).T
            out_cols[head, number] = both[:HEAD_DIM]
            log_total[head, number] = both[HEAD_DIM : HEAD_DIM + 1]
            out_buf[rows] = mixed.astype(BF16)
            for at in range(BLOCKS):
                if (head, at) in events:

                    @pl.when(number == at)
                    def _():
                        for act in events[(head, at)]:
                            act()

            return 0

        lax.fori_loop(0, BLOCKS, query_block, 0)

    def heads_copy(head, offset):
        return send(
            staged.at[head, wrapped(me + offset)],
            heads_in.at[head, me],
            (heads_send, heads_recv),
            (head, offset - 1),
            {"mp": wrapped(me + offset)},
        )

    def heads_own_copy(head):
        return pltpu.make_async_copy(
            staged.at[head, me], heads_in.at[head, me], heads_own.at[head]
        )

    peers = range(1, mp_size)
    for head in range(head_total):
        attend(head)
        for chunk in range(mp_size):
            for side in range(2):
                start = (2 * chunk + side) * half
                staged[head, chunk, :, side * HEAD_DIM : (side + 1) * HEAD_DIM] = out_buf[
                    start : start + half
                ]
        for offset in peers:
            heads_copy(head, offset).start()
        heads_own_copy(head).start()

    for hop in hops:
        if (take_hop, hop) not in done:
            take_hop(hop)
    for level in range(bits):
        for hop in hops:
            if (trade_hop, level, hop) not in done:
                trade_hop(level, hop)
    for head in range(head_total):
        heads_own_copy(head).wait()
        for offset in peers:
            heads_copy(head, offset).wait_recv()
        for chunk in range(mp_size):
            for side in range(2):
                at = (chunk * head_total + head) * HEAD_DIM
                heads_low[side * half : (side + 1) * half, at : at + HEAD_DIM] = heads_in[
                    head, chunk, :, side * HEAD_DIM : (side + 1) * HEAD_DIM
                ]
        for offset in peers:
            heads_copy(head, offset).wait_send()

    def sent_all(side, hop):
        frame_copy(side, hop).wait_send()
        bias_copy(side, hop).wait_send()
        for which in range(3):
            first_copy(which, side, hop).wait_send()

    def sent_later(side, hop):
        for which in range(3):
            for level in range(len(orders[which])):
                later_copy(which, level, side, hop).wait_send()

    for side, hop in ways:
        line.if_sent(side, hop)(partial(sent_all, side, hop))
        line.if_taken(side, hop)(partial(sent_later, side, hop))
    for copy in own:
        copy.wait()


def front(frames, qkv_weight, q_bias, v_bias, seg_row, weights, in_bias, mp_size, bits):
    local_rows, width = frames.shape
    head_cols = qkv_weight.shape[1]
    head_total = head_cols // HEAD_DIM
    peers = mp_size - 1
    levels = max(bits, 1)
    anywhere = pl.BlockSpec(memory_space=pl.ANY)
    in_weight, down_weight, out_weight = weights

    def sems(*shapes):
        return [pltpu.SemaphoreType.DMA(shape) for shape in shapes for _ in range(2)]

    piece = (head_total, mp_size, local_rows // 2, 2 * HEAD_DIM)
    return pl.pallas_call(
        partial(front_kernel, bits),
        out_shape=(
            jax.ShapeDtypeStruct((ROW_LEN, width), BF16),
            jax.ShapeDtypeStruct((3, ROW_LEN, head_cols), BF16),
            jax.ShapeDtypeStruct((mp_size,) + in_weight.shape, BF16),
            jax.ShapeDtypeStruct((mp_size,) + down_weight.shape, BF16),
            jax.ShapeDtypeStruct((mp_size,) + out_weight.shape, BF16),
            jax.ShapeDtypeStruct((mp_size, 16, in_bias.shape[1]), BF16),
            jax.ShapeDtypeStruct((ROW_LEN, 128), jnp.int32),
            jax.ShapeDtypeStruct((head_total, BLOCKS, HEAD_DIM, BLOCK), F32),
            jax.ShapeDtypeStruct((head_total, BLOCKS, 1, BLOCK), F32),
            jax.ShapeDtypeStruct((local_rows, width), BF16),
        ),
        in_specs=[whole()] * 5 + [anywhere] * 3 + [whole()],
        out_specs=(whole(), whole()) + (anywhere,) * 4 + (whole(),) * 4,
        scratch_shapes=[
            pltpu.VMEM((16, in_bias.shape[1]), BF16),
            pltpu.VMEM((BLOCKS, HEAD_DIM, BLOCK), BF16),
            pltpu.VMEM((BLOCKS, BLOCK, HEAD_DIM + EXTRA), BF16),
            pltpu.VMEM((ROW_LEN, HEAD_DIM), BF16),
            pltpu.VMEM(piece, BF16),
            pltpu.VMEM(piece, BF16),
            pltpu.SemaphoreType.DMA((4,)),
            *sems((2, peers), (2, peers), (3, 2, peers), (3, levels, 2, peers)),
            pltpu.SemaphoreType.DMA((head_total,)),
            *sems((head_total, peers)),
        ],
        compiler_params=pltpu.CompilerParams(
            collective_id=0, has_side_effects=True, vmem_limit_bytes=VMEM_BYTES
        ),
        cost_estimate=pl.CostEstimate(
            flops=16 * head_total * ROW_LEN * ROW_LEN * HEAD_DIM,
            bytes_accessed=32 * 1024 * 1024,
            transcendentals=head_total * ROW_LEN * ROW_LEN,
        ),
        name="front",
    )(frames, qkv_weight, q_bias, v_bias, seg_row, in_weight, down_weight, out_weight, in_bias)


def reduce_orders(bits):
    if bits == 3:
        return ((0, 1, 2), (0, 2, 1), (0, 1, 2))
    return (tuple(range(bits)),) * 3


def norm_rows(inputs, norm_gain, norm_shift):
    row_mean = jnp.mean(inputs, axis=-1, keepdims=True)
    centred = inputs - row_mean
    variance = jnp.mean(centred * centred, axis=-1, keepdims=True)
    inv_std = lax.rsqrt(variance + 1e-05)
    normed = centred * inv_std
    return (normed * norm_gain + norm_shift, normed, inv_std)


def norm_back(cotangent, normed, inv_std, norm_gain):
    scaled = cotangent * norm_gain
    adjusted = (
        scaled
        - jnp.mean(scaled, axis=-1, keepdims=True)
        - normed * jnp.mean(scaled * normed, axis=-1, keepdims=True)
    )
    return adjusted * inv_std


def sum_rows(array):
    return jnp.sum(array.astype(F32), axis=0, keepdims=True)


def rear_kernel(
    bits,
    seg_row,
    in_bias,
    out_bias,
    down_bias,
    norm_gain,
    norm_shift,
    frames,
    heads_low,
    out_grad,
    in_all,
    down_all,
    out_all,
    proj_weight,
    qkv_source,
    out_source,
    log_source,
    seg_source,
    input_source,
    block_out,
    resid_grad,
    in_grads,
    down_grads,
    head_grads,
    proj_all,
    traded,
    in_sum,
    down_sum,
    head_sum,
    proj_sum,
    vector_sum,
    bias_sum,
    grads_out,
    grads_in,
    kept,
    taken,
    last,
    proj,
    proj_taken,
    proj_slots,
    vectors,
    vectors_taken,
    vectors_all,
    biases,
    biases_taken,
    load_sems,
    in_sems,
    down_sems,
    out_sems,
    given_sems,
    head_sem,
    store_sems,
    attention_sems,
    weight_own,
    weight_send,
    weight_recv,
    weight_trade_send,
    weight_trade_recv,
    keep_sems,
    grads_own,
    grads_send,
    grads_recv,
    traded_own,
    traded_send,
    traded_recv,
    level_send,
    level_recv,
    last_send,
    last_recv,
    back_send,
    back_recv,
    proj_send,
    proj_recv,
    vector_send,
    vector_recv,
    vector_last_send,
    vector_last_recv,
    bias_send,
    bias_recv,
):
    mp_size, units, width = down_all.shape
    head_total = grads_out.shape[1]
    half = grads_out.shape[2]
    head_cols = width // mp_size
    slots = 2**bits
    me = lax.axis_index("mp")
    dp_index = lax.axis_index("dp")
    peers = range(1, mp_size)
    turns = range(mp_size)
    levels = list(range(bits))
    orders = reduce_orders(bits)
    partials = (in_grads, down_grads, head_grads)
    sums = (in_sum, down_sum, head_sum)
    arrays = range(3)
    vector = vectors[0]

    def target(offset):
        return lax.rem(me + offset, mp_size)

    def bit_of(which, level):
        return (dp_index // 2 ** orders[which][level]) % 2


    def part_of(turn):
        return target(turn + 1)

    def level_copy(which, level, turn):
        count = 2 ** (bits - 1 - level)
        other = (1 - bit_of(which, level)) * count
        part = pl.ds(part_of(turn), 1)
        source = partials[which] if level == 0 else taken[which][level - 1]
        return send(
            source.at[part, pl.ds(other, count)],
            taken[which][level].at[part],
            (level_send, level_recv),
            (which, level, turn),
            {"dp": partner_of(dp_index, orders[which][level])},
        )

    def keep_copy(which, turn):
        count = 2 ** (bits - 1)
        return pltpu.make_async_copy(
            partials[which].at[part_of(turn), pl.ds(bit_of(which, 0) * count, count)],
            kept[which].at[turn % 2],
            keep_sems.at[which, turn % 2],
        )

    def last_copy(which, offset):
        return send(
            taken[which][bits - 1].at[target(offset)],
            last[which].at[offset - 1],
            (last_send, last_recv),
            (which, offset - 1),
            {"mp": target(offset)},
        )

    def add_level(which, level, turn):
        level_copy(which, level, turn).wait_recv()
        count = 2 ** (bits - 1 - level)
        if level == 0:
            keep_copy(which, turn).wait()
        start = bit_of(which, level) * count
        into = taken[which][level]
        part = part_of(turn)
        for slot in range(count):
            if level == 0:
                mine = kept[which][turn % 2, slot]
            else:
                mine = taken[which][level - 1][part, start + slot]
            into[part, slot] = (into[part, slot].astype(F32) + mine.astype(F32)).astype(BF16)
        if level == 0 and turn + 2 < mp_size:
            keep_copy(which, turn + 2).start()
        if level + 1 < bits:
            level_copy(which, level + 1, turn).start()
        elif turn + 1 < mp_size:
            last_copy(which, turn + 1).start()

    def offer(which, turn):
        level_copy(which, 0, turn).start()
        if turn < 2:
            keep_copy(which, turn).start()

    def slot_of(order):
        return place_in(dp_index, order[::-1])

    def held_slots(order, level):
        count = 2 ** (bits - 1 - level)
        return pl.ds(slot_of(order) // count * count, count)

    def spread_copy(which, level):
        held = sums[which].at[held_slots(orders[which], level)]
        partner = {"dp": partner_of(dp_index, orders[which][level])}
        return send(held, held, (back_send, back_recv), (which, level), partner)

    def finish_sum(which):
        total = taken[which][bits - 1][me, 0].astype(F32)
        for offset in peers:
            last_copy(which, offset).wait_recv()
            total = total + last[which][offset - 1, 0].astype(F32)
        sums[which][slot_of(orders[which])] = total.astype(BF16)
        spread_copy(which, bits - 1).start()

    def spread(which, level):
        spread_copy(which, level).wait_recv()
        if level:
            spread_copy(which, level - 1).start()


    def proj_copy(head, level):
        count = 2 ** (bits - 1 - level)
        other = (1 - bit_of(0, level)) * count
        source = proj[head] if level == 0 else proj_taken[head][level - 1]
        return send(
            source.at[pl.ds(other, count)],
            proj_taken[head][level],
            (proj_send, proj_recv),
            (0, head, level),
            {"dp": partner_of(dp_index, orders[0][level])},
        )

    def proj_spread_copy(head, level):
        held = proj_slots[head].at[held_slots(orders[0], level)]
        partner = {"dp": partner_of(dp_index, orders[0][level])}
        return send(held, held, (proj_send, proj_recv), (1, head, level), partner)

    def add_proj(head, level):
        proj_copy(head, level).wait_recv()
        count = 2 ** (bits - 1 - level)
        start = bit_of(0, level) * count
        into = proj_taken[head][level]
        for slot in range(count):
            mine = proj[head][start + slot] if level == 0 else proj_taken[head][level - 1][start + slot]
            into[slot] = (into[slot].astype(F32) + mine.astype(F32)).astype(BF16)
        if level + 1 < bits:
            proj_copy(head, level + 1).start()
        else:
            proj_slots[head][slot_of(orders[0])] = into[0]
            proj_spread_copy(head, level).start()

    def spread_proj(head, level):
        proj_spread_copy(head, level).wait_recv()
        if level:
            proj_spread_copy(head, level - 1).start()


    def vector_copy(level):
        return send(
            vectors[level],
            vectors_taken[level],
            (vector_send, vector_recv),
            level,
            {"dp": partner_of(dp_index, level)},
        )

    def vector_last_copy(offset):
        return send(
            vectors[bits],
            vectors_all.at[me],
            (vector_last_send, vector_last_recv),
            offset - 1,
            {"mp": target(offset)},
        )

    def add_vector(level):
        vector_copy(level).wait_recv()
        vectors[level + 1][...] = vectors[level][...] + vectors_taken[level][...]
        if level + 1 < bits:
            vector_copy(level + 1).start()
        else:
            vectors_all[me] = vectors[bits][...]
            for offset in peers:
                vector_last_copy(offset).start()

    def finish_vector():
        for offset in peers:
            vector_last_copy(offset).wait_recv()
        total = vectors_all[0]
        for index in peers:
            total = total + vectors_all[index]
        vector_sum[...] = total

    def bias_copy(level):
        return send(
            biases[level],
            biases_taken[level],
            (bias_send, bias_recv),
            level,
            {"dp": partner_of(dp_index, level)},
        )

    def add_bias(level):
        bias_copy(level).wait_recv()
        biases[level + 1][...] = biases[level][...] + biases_taken[level][...]
        if level + 1 < bits:
            bias_copy(level + 1).start()
        else:
            bias_sum[...] = biases[bits][...]


    def grads_copy(head, offset):
        return send(
            grads_out.at[target(offset), head],
            grads_in.at[head, me],
            (grads_send, grads_recv),
            (head, offset - 1),
            {"mp": target(offset)},
        )

    def grads_own_copy(head):
        return pltpu.make_async_copy(
            grads_out.at[me, head], grads_in.at[head, me], grads_own.at[head]
        )

    line = Line(mp_size, me)
    order = gather_orders(bits)[3]
    own_slot = place_in(dp_index, order)

    def weight_copy(side, hop):
        place = proj_all.at[line.place(side, hop), pl.ds(own_slot, 1)]
        source = proj_weight.at[pl.ds(own_slot, 1)] if hop == 0 else place
        return send(source, place, (weight_send, weight_recv), (side, hop), line.neighbour(side))

    def weight_trade_copy(level, side, hop):
        held = pl.ds(own_slot // 2**level * 2**level, 2**level)
        place = proj_all.at[line.place(side, hop + 1), held]
        partner = {"dp": partner_of(dp_index, order[level])}
        return send(place, place, (weight_trade_send, weight_trade_recv), (level, side, hop), partner)

    def take_weight(side, hop):
        weight_copy(side, hop).wait_recv()
        if hop + 1 < mp_size - 1:
            line.if_sent(side, hop + 1)(lambda: weight_copy(side, hop + 1).start())
        if bits:
            weight_trade_copy(0, side, hop).start()

    def trade_weight(level, side, hop):
        weight_trade_copy(level, side, hop).wait_recv()
        if level + 1 < bits:
            weight_trade_copy(level + 1, side, hop).start()

    def both_sides(act, *which):
        for side in (0, 1):
            line.if_taken(side, which[-1])(partial(act, *which[:-1], side, which[-1]))

    schedule = (
        (0, take_weight, 0),
        (1, take_weight, 1),
        (2, take_weight, 2),
        (2, trade_weight, 0, 0),
        (3, trade_weight, 0, 1),
        (3, trade_weight, 0, 2),
        (4, trade_weight, 1, 0),
        (6, trade_weight, 1, 1),
        (8, trade_weight, 1, 2),
    )
    done = set()

    def at_point(point, index=None):
        for at, act, *which in schedule:
            if which[-1] not in line.hops or (act is trade_weight and which[0] >= bits):
                continue
            if index is None and at == point:
                both_sides(act, *which)
                done.add((act, *which))
            if index is not None and point <= at < point + mp_size:
                pl.when(index == at - point)(partial(both_sides, act, *which))
                done.add((act, *which))

    def dense_phase(
        frames_buf,
        heads_buf,
        cotangent_buf,
        in_buf,
        down_buf,
        out_buf,
        hidden,
        slope,
        mid_buf,
        normed_buf,
        store_buf,
        low_buf,
        grad_buf,
        given,
        head_buf,
    ):
        loads = [
            pltpu.make_async_copy(source, into, load_sems.at[at])
            for at, (source, into) in enumerate(
                ((frames, frames_buf), (heads_low, heads_buf), (out_grad, cotangent_buf))
            )
        ]
        out_copies = [
            pltpu.make_async_copy(
                out_all.at[index],
                out_buf.at[pl.ds(index * head_cols, head_cols)],
                out_sems.at[index],
            )
            for index in range(mp_size)
        ]

        def in_copy(index):
            return pltpu.make_async_copy(in_all.at[index], in_buf.at[index], in_sems.at[index])

        def down_copy(index):
            return pltpu.make_async_copy(
                down_all.at[index], down_buf.at[index], down_sems.at[index]
            )

        def given_copy(which, turn):
            return pltpu.make_async_copy(
                given.at[turn % 2], partials[which].at[part_of(turn)], given_sems.at[turn % 2]
            )

        def store_copy(at):
            return pltpu.make_async_copy(
                store_buf, (block_out, resid_grad)[at], store_sems.at[at]
            )

        for copy in loads + out_copies:
            copy.start()
        for index in range(mp_size):
            in_copy(index).start()
            down_copy(index).start()
        enter(dp_index, me, mp_size, bits)
        for side in (0, 1):
            line.if_sent(side, 0)(lambda side=side: weight_copy(side, 0).start())
        weight_own_copy.start()
        vector[...] = jnp.zeros_like(vector)
        gains = norm_gain[...].astype(F32)
        shifts = norm_shift[...].astype(F32)
        both = [slice(side * half, (side + 1) * half) for side in range(2)]

        for copy in loads + out_copies:
            copy.wait()
        branch = dot(heads_buf[...], out_buf[...]) + out_bias[...].astype(F32)
        mid, normed, inv_mid = norm_rows(
            frames_buf[...].astype(F32) + branch, gains[:1], shifts[:1]
        )
        mid_buf[...] = mid + down_bias[...].astype(F32)
        normed_buf[...] = normed
        low_buf[...] = mid.astype(BF16)
        at_point(0)

        def feed(index, _):
            in_copy(index).wait()
            down_copy(index).wait()
            for rows in both:
                pre_act = dot(low_buf[rows], in_buf[index]) + in_bias[index, 0:1].astype(F32)
                unit_cdf = 0.5 * (1.0 + lax.erf(pre_act * 0.5**0.5))
                bell = jnp.exp(-0.5 * pre_act * pre_act) * (2.0 * jnp.pi) ** (-0.5)
                slope[index, rows] = (unit_cdf + pre_act * bell).astype(BF16)
                hidden[index, rows] = (pre_act * unit_cdf).astype(BF16)
                mid_buf[rows] += dot(hidden[index, rows], down_buf[index])
            at_point(1, index)
            return 0

        lax.fori_loop(0, mp_size, feed, 0)
        output, normed, inv_out = norm_rows(mid_buf[...], gains[1:], shifts[1:])
        store_buf[...] = output
        store_copy(0).start()

        cotangent = cotangent_buf[...].astype(F32)
        vector[1:2] = sum_rows(cotangent * normed)
        vector[3:4] = sum_rows(cotangent)
        sum_grad = norm_back(cotangent, normed, inv_out, gains[1:])
        mid_buf[...] = sum_grad
        grad_buf[...] = sum_grad.astype(BF16)
        vector[5:6] = sum_rows(grad_buf[...])

        def give(which, turn, result):
            if turn >= 2:
                offer_given(which, turn - 2)
            share = result.shape[0] // slots
            for slot in range(slots):
                given[turn % 2, slot] = result[slot * share : (slot + 1) * share].astype(BF16)
            given_copy(which, turn).start()

        def offer_given(which, turn):
            given_copy(which, turn).wait()
            offer(which, turn)

        for turn in turns:
            index = part_of(turn)
            give(1, turn, dot_cols(hidden[index], grad_buf[...]))
            pre = dot_rows(grad_buf[...], down_buf[index]) * slope[index].astype(F32)
            hidden[index] = pre.astype(BF16)
            vector[pl.ds(8 + index, 1)] = sum_rows(hidden[index])
            mid_buf[...] += dot_rows(hidden[index], in_buf[index])
            at_point(1 + mp_size + turn)
        for turn in turns[-2:]:
            offer_given(1, turn)
        mid_grad = mid_buf[...]
        vector[0:1] = sum_rows(mid_grad * normed_buf[...])
        vector[2:3] = sum_rows(mid_grad)
        resid = norm_back(mid_grad, normed_buf[...], inv_mid, gains[:1])
        store_copy(0).wait()
        store_buf[...] = resid
        store_copy(1).start()
        attn_grad = resid.astype(BF16)
        grad_buf[...] = attn_grad
        vector[4:5] = sum_rows(attn_grad)
        heads_grad = dot_rows(attn_grad, out_buf[...]).astype(BF16)
        for head in range(head_total):
            for index in range(mp_size):
                at = index * head_cols + head * HEAD_DIM
                for side in range(2):
                    grads_out[index, head, :, side * HEAD_DIM : (side + 1) * HEAD_DIM] = (
                        heads_grad[both[side], at : at + HEAD_DIM]
                    )
            if head == 0:
                for offset in peers:
                    grads_copy(0, offset).start()
        for head in range(head_total):
            grads_own_copy(head).start()
        vector_copy(0).start()

        products = dot_cols(heads_buf[...], grad_buf[...]).astype(BF16)
        rows = head_cols // slots
        for index in range(mp_size):
            for slot in range(slots):
                start = index * head_cols + slot * rows
                head_buf[index, slot, :rows] = products[start : start + rows]
                if rows < head_buf.shape[2]:
                    head_buf[index, slot, rows:] = jnp.zeros(
                        (head_buf.shape[2] - rows, width), BF16
                    )
        head_copy = pltpu.make_async_copy(head_buf, head_grads, head_sem)
        head_copy.start()
        normed_low = low_buf[...].T
        for turn in turns:
            give(0, turn, dot(normed_low, hidden[part_of(turn)]))
            if turn == 0:
                head_copy.wait()
                for at in turns:
                    offer(2, at)
                for later in range(1, head_total):
                    for offset in peers:
                        grads_copy(later, offset).start()
        for turn in turns[-2:]:
            offer_given(0, turn)
        store_copy(1).wait()

    weight_own_copy = pltpu.make_async_copy(proj_weight, proj_all.at[me], weight_own)
    rows_low = pltpu.VMEM((2 * half, width), BF16)
    rows_full = pltpu.VMEM((2 * half, width), F32)
    pl.run_scoped(
        dense_phase,
        rows_low,
        rows_low,
        rows_low,
        pltpu.VMEM((mp_size, width, units), BF16),
        pltpu.VMEM((mp_size, units, width), BF16),
        pltpu.VMEM((width, width), BF16),
        pltpu.VMEM((mp_size, 2 * half, units), BF16),
        pltpu.VMEM((mp_size, 2 * half, units), BF16),
        rows_full,
        rows_full,
        rows_full,
        rows_low,
        rows_low,
        pltpu.VMEM((2, slots, units // slots, width), BF16),
        pltpu.VMEM(head_grads.shape, BF16),
    )

    def attention_phase(
        qkv,
        out_cols,
        log_total,
        seg_col,
        input_all,
        staged,
        qkv_grad,
        seg_blocks,
        grads,
        key_buf,
        key_cols,
        value_buf,
        query_sum,
        key_sum,
        value_sum,
        proj_rows,
    ):
        def traded_copy(head, offset):
            return send(
                staged.at[head, target(offset)],
                traded.at[head, me],
                (traded_send, traded_recv),
                (head, offset - 1),
                {"mp": target(offset)},
            )

        def traded_own_copy(head):
            return pltpu.make_async_copy(
                staged.at[head, me], traded.at[head, me], traded_own.at[head]
            )

        def prepare(head):
            cols = slice(head * HEAD_DIM, (head + 1) * HEAD_DIM)
            key_buf[:, :HEAD_DIM] = qkv[1, :, cols]
            key_buf[:, HEAD_DIM:] = ones_columns(ROW_LEN)
            value_buf[:, :HEAD_DIM] = qkv[2, :, cols]
            value_buf[:, HEAD_DIM:] = ones_columns(ROW_LEN)
            for step in range(BLOCKS):
                key_cols[step] = qkv[1, step * BLOCK : (step + 1) * BLOCK, cols].T
            key_sum[...] = jnp.zeros_like(key_sum)
            value_sum[...] = jnp.zeros_like(value_sum)

        def take_grads(head):
            grads_own_copy(head).wait()
            for offset in peers:
                grads_copy(head, offset).wait_recv()
            for chunk in range(mp_size):
                for side in range(2):
                    start = (2 * chunk + side) * half
                    grads[start : start + half] = grads_in[
                        head, chunk, :, side * HEAD_DIM : (side + 1) * HEAD_DIM
                    ]

        def attend_back(head):
            cols = slice(head * HEAD_DIM, (head + 1) * HEAD_DIM)

            def query_block(number, _):
                rows = block_rows(number)
                queries = qkv[0, rows, cols] * SCALE
                grad_rows = grads[rows]
                seg_query = seg_blocks[number]
                grad_cols = grad_rows.astype(F32).T
                row_dot = jnp.sum(grad_cols * out_cols[head, number], axis=0, keepdims=True)
                grad_cols = jnp.concatenate([grad_cols.astype(BF16), as_pieces(-row_dot)], axis=0)
                query_cols = jnp.concatenate(
                    [queries.astype(F32).T.astype(BF16), as_pieces(-log_total[head, number])], axis=0
                )

                def step_back(step, query_grad):
                    key_rows = block_rows(step)
                    same = jnp.concatenate([seg_col[key_rows]] * (BLOCK // 128), axis=1) == seg_query
                    scores = dot(key_buf[key_rows], query_cols)
                    soft = jnp.exp(jnp.where(same, scores, MASKED))
                    soft_grad = dot(value_buf[key_rows], grad_cols)
                    score_grad = (soft * soft_grad).astype(BF16)
                    value_sum[key_rows] += dot(soft.astype(BF16), grad_rows)
                    key_sum[key_rows] += dot(score_grad, queries)
                    query_grad = query_grad + dot(key_cols[step], score_grad)
                    for at in range(head * BLOCKS**2, (head + 1) * BLOCKS**2):
                        if at in events:

                            @pl.when(number * BLOCKS + step == at - head * BLOCKS**2)
                            def _():
                                for act in events[at]:
                                    act()

                    return query_grad

                query_grad = lax.fori_loop(0, BLOCKS, step_back, jnp.zeros((HEAD_DIM, BLOCK), F32))
                query_sum[rows] = (query_grad * SCALE).T
                return 0

            lax.fori_loop(0, BLOCKS, query_block, 0)

        def give_grads(head):
            for part, total in enumerate((query_sum, key_sum, value_sum)):
                low = total[...].astype(BF16)
                qkv_grad[:, part * HEAD_DIM : (part + 1) * HEAD_DIM] = low
                if part != 1:
                    cols = slice(head * HEAD_DIM, (head + 1) * HEAD_DIM)
                    sum_low = jnp.sum(low.astype(F32), axis=0, keepdims=True)
                    biases[0][part : part + 1, cols] = sum_low
                for chunk in range(mp_size):
                    for side in range(2):
                        start = (2 * chunk + side) * half
                        staged[head, chunk, part, :, side * HEAD_DIM : (side + 1) * HEAD_DIM] = total[
                            start : start + half
                        ].astype(BF16)

        def start_trade(head):
            for offset in peers:
                traded_copy(head, offset).start()
            traded_own_copy(head).start()

        def start_proj(head):
            products = dot_cols(qkv_grad[...], input_all[...])
            slot_rows = proj[head].shape[1]
            for slot in range(2**bits):
                proj[head][slot] = products[slot * slot_rows : (slot + 1) * slot_rows].astype(BF16)
            proj_copy(head, 0).start()

        def finish_proj(head):
            cols = slice(head * HEAD_DIM, (head + 1) * HEAD_DIM)
            slot_rows = proj_slots[head].shape[1]
            for slot in range(2**bits):
                proj_rows[slot * slot_rows : (slot + 1) * slot_rows] = proj_slots[head][slot].astype(F32)
            for part in range(3):
                rows = proj_rows[part * HEAD_DIM : (part + 1) * HEAD_DIM]
                proj_sum[part, cols] = rows.astype(BF16)

        events = {}
        rest = []

        def due(at, act, *which):
            events.setdefault(at, []).append(partial(act, *which))

        for at, level in zip((1, 2, 3), levels):
            due(at, add_vector, level)
        due(5, finish_vector)
        for head, adds, spreads in ((0, (10, 12, 14), (15, 17, 19)), (1, (19, 21, 23), (24, 25, 26))):
            for at, level in zip(adds, levels):
                due(at, add_proj, head, level)
            for at, level in zip(spreads, levels[::-1]):
                due(at, spread_proj, head, level)
        times = {
            1: ((0, 0, 1, 1), (4, 7, 9, 10), (6, 9, 11, 12)),
            2: ((4, 4, 4, 4), (7, 7, 7, 7), (9, 9, 9, 9)),
            0: ((6, 8, 10, 12), (9, 11, 14, 16), (11, 13, 16, 18)),
        }
        ends = {1: (20, 22, 24, 26), 2: (20, 22, 24, 26), 0: (24, None, None, None)}
        for which in times:
            for level, when in zip(levels, times[which]):
                for turn, at in zip(turns, when):
                    due(at, add_level, which, level, turn)
            due(ends[which][0], finish_sum, which)
            for level, at in zip(levels[::-1], ends[which][1:]):
                if at is None:
                    rest.append((which, level))
                else:
                    due(at, spread, which, level)

        copies = [
            pltpu.make_async_copy(source, into, attention_sems.at[at])
            for at, (source, into) in enumerate(
                (
                    (qkv_source, qkv),
                    (seg_source, seg_col),
                    (log_source, log_total),
                    (out_source, out_cols),
                    (input_source, input_all),
                )
            )
        ]
        for copy in copies:
            copy.start()
        biases[0][...] = jnp.zeros_like(biases[0])
        for step in range(BLOCKS):
            seg_blocks[step] = seg_row[:, step * BLOCK : (step + 1) * BLOCK]
        final = head_total - 1
        copies[0].wait()
        for head in range(head_total):
            prepare(head)
            take_grads(head)
            if head == 0:
                for copy in copies[1:4]:
                    copy.wait()
            attend_back(head)
            give_grads(head)
            start_trade(head)
            if head == 0:
                copies[4].wait()
            start_proj(head)
        bias_copy(0).start()
        for level in levels:
            add_proj(final, level)
            add_bias(level)
            if rest:
                spread(*rest.pop(0))
        for each in rest:
            spread(*each)
        for level in levels[::-1]:
            spread_proj(final, level)
        for head in range(head_total):
            finish_proj(head)
            traded_own_copy(head).wait()
            for offset in peers:
                traded_copy(head, offset).wait()

    pl.run_scoped(
        attention_phase,
        pltpu.VMEM(qkv_source.shape, BF16),
        pltpu.VMEM(out_source.shape, F32),
        pltpu.VMEM(log_source.shape, F32),
        pltpu.VMEM(seg_source.shape, jnp.int32),
        pltpu.VMEM(input_source.shape, BF16),
        pltpu.VMEM((head_total, mp_size, 3, half, 2 * HEAD_DIM), BF16),
        pltpu.VMEM((ROW_LEN, 3 * HEAD_DIM), BF16),
        pltpu.VMEM((BLOCKS, 1, BLOCK), jnp.int32),
        pltpu.VMEM((ROW_LEN, HEAD_DIM), BF16),
        pltpu.VMEM((ROW_LEN, HEAD_DIM + EXTRA), BF16),
        pltpu.VMEM((BLOCKS, HEAD_DIM, BLOCK), BF16),
        pltpu.VMEM((ROW_LEN, HEAD_DIM + EXTRA), BF16),
        pltpu.VMEM((ROW_LEN, HEAD_DIM), F32),
        pltpu.VMEM((ROW_LEN, HEAD_DIM), F32),
        pltpu.VMEM((ROW_LEN, HEAD_DIM), F32),
        pltpu.VMEM((3 * HEAD_DIM, width), F32),
    )

    for hop in line.hops:
        if (take_weight, hop) not in done:
            both_sides(take_weight, hop)
    for level in levels:
        for hop in line.hops:
            if (trade_weight, level, hop) not in done:
                both_sides(trade_weight, level, hop)

    def sent_trades(side, hop):
        for level in levels:
            weight_trade_copy(level, side, hop).wait_send()

    for side, hop in line.ways:
        line.if_sent(side, hop)(lambda side=side, hop=hop: weight_copy(side, hop).wait_send())
        line.if_taken(side, hop)(partial(sent_trades, side, hop))
    weight_own_copy.wait()
    for head in range(head_total):
        for offset in peers:
            grads_copy(head, offset).wait_send()
        for level in levels:
            proj_copy(head, level).wait_send()
            proj_spread_copy(head, level).wait_send()
    for level in levels:
        vector_copy(level).wait_send()
        bias_copy(level).wait_send()
        for which in arrays:
            spread_copy(which, level).wait_send()
            for turn in turns:
                level_copy(which, level, turn).wait_send()
    for offset in peers:
        vector_last_copy(offset).wait_send()
        for which in arrays:
            last_copy(which, offset).wait_send()


def rear(frames, heads_low, out_grad, seg_row, in_bias, small, weights, proj_weight, saved, bits):
    local_rows, width = frames.shape
    qkv_low, out_cols = saved[:2]
    mp_size, units = weights[1].shape[:2]
    head_total = out_cols.shape[0]
    half, lanes = local_rows // 2, 2 * HEAD_DIM
    peers = mp_size - 1
    slots = 2**bits
    head_rows = -(-width // mp_size // slots // 16) * 16
    anywhere = pl.BlockSpec(memory_space=pl.ANY)
    blocks = [(width // slots, units), (units // slots, width), (head_rows, width)]
    proj_block = (3 * HEAD_DIM // slots, width)
    bias_block = (8, 2 * 128)
    vector_block = (8 + -(-mp_size // 8) * 8, width)

    def halves(shape, lead=()):
        return [pltpu.VMEM(lead + (slots >> (level + 1),) + shape, BF16) for level in range(bits)]

    def sems(*shapes):
        return [pltpu.SemaphoreType.DMA(shape) for shape in shapes for _ in range(2)]

    piece = pltpu.VMEM((mp_size, head_total, half, lanes), BF16)
    return pl.pallas_call(
        partial(rear_kernel, bits),
        out_shape=(
            jax.ShapeDtypeStruct((local_rows, width), F32),
            jax.ShapeDtypeStruct((local_rows, width), F32),
            *(jax.ShapeDtypeStruct((mp_size, slots) + block, BF16) for block in blocks),
            jax.ShapeDtypeStruct((mp_size,) + proj_weight.shape, BF16),
            jax.ShapeDtypeStruct((head_total, mp_size, 3, half, lanes), BF16),
            *(jax.ShapeDtypeStruct((slots,) + block, BF16) for block in blocks),
            jax.ShapeDtypeStruct((3, head_total * HEAD_DIM, width), BF16),
            jax.ShapeDtypeStruct(vector_block, F32),
            jax.ShapeDtypeStruct(bias_block, F32),
        ),
        in_specs=[whole()] * 6 + [anywhere] * 12,
        out_specs=(anywhere,) * 7 + (whole(),) * 6,
        scratch_shapes=[
            piece,
            pltpu.VMEM((head_total, mp_size, half, lanes), BF16),
            [pltpu.VMEM((2, slots // 2) + block, BF16) for block in blocks],
            [halves(block, (mp_size,)) for block in blocks],
            [pltpu.VMEM((peers, 1) + block, BF16) for block in blocks],
            [pltpu.VMEM((slots,) + proj_block, BF16) for _ in range(head_total)],
            [halves(proj_block) for _ in range(head_total)],
            [pltpu.VMEM((slots,) + proj_block, BF16) for _ in range(head_total)],
            [pltpu.VMEM(vector_block, F32) for _ in range(bits + 1)],
            [pltpu.VMEM(vector_block, F32) for _ in range(bits)],
            pltpu.VMEM((mp_size,) + vector_block, F32),
            [pltpu.VMEM(bias_block, F32) for _ in range(bits + 1)],
            [pltpu.VMEM(bias_block, F32) for _ in range(bits)],
            pltpu.SemaphoreType.DMA((3,)),
            pltpu.SemaphoreType.DMA((mp_size,)),
            pltpu.SemaphoreType.DMA((mp_size,)),
            pltpu.SemaphoreType.DMA((mp_size,)),
            pltpu.SemaphoreType.DMA((2,)),
            pltpu.SemaphoreType.DMA,
            pltpu.SemaphoreType.DMA((2,)),
            pltpu.SemaphoreType.DMA((5,)),
            pltpu.SemaphoreType.DMA,
            *sems((2, peers), (max(bits, 1), 2, peers)),
            pltpu.SemaphoreType.DMA((3, 2)),
            pltpu.SemaphoreType.DMA((head_total,)),
            *sems((head_total, peers)),
            pltpu.SemaphoreType.DMA((head_total,)),
            *sems(
                (head_total, peers),
                (3, bits, mp_size),
                (3, peers),
                (3, bits),
                (2, head_total, bits),
                (bits,),
                (peers,),
                (bits,),
            ),
        ],
        compiler_params=pltpu.CompilerParams(
            collective_id=1, has_side_effects=True, vmem_limit_bytes=REAR_VMEM_BYTES
        ),
        cost_estimate=pl.CostEstimate(
            flops=40 * head_total * ROW_LEN * ROW_LEN * HEAD_DIM,
            bytes_accessed=96 * 1024 * 1024,
            transcendentals=head_total * ROW_LEN * ROW_LEN,
        ),
        name="rear",
    )(seg_row, in_bias, *small, frames, heads_low, out_grad, *weights, proj_weight, *saved)


def finish_kernel(
    traded,
    proj_all,
    resid_grad,
    in_sum,
    down_sum,
    head_sum,
    proj_sum,
    vector_sum,
    bias_sum,
    stream_grad,
    in_grad,
    down_grad,
    out_grad,
    proj_grad,
    query_bias_grad,
    value_bias_grad,
    out_bias_grad,
    in_bias_grad,
    down_bias_grad,
    gain_grad,
    shift_grad,
    columns,
    weight_buf,
    sems,
):
    head_total, mp_size = traded.shape[:2]
    half = traded.shape[3]
    head_cols = head_total * HEAD_DIM
    copies = [
        pltpu.make_async_copy(
            proj_all.at[index],
            weight_buf.at[index],
            sems.at[index],
        )
        for index in range(mp_size)
    ]
    for copy in copies:
        copy.start()
    for sums, grad in ((in_sum, in_grad), (down_sum, down_grad), (head_sum, out_grad)):
        rows = grad.shape[0] // sums.shape[0]
        for slot in range(sums.shape[0]):
            grad[slot * rows : (slot + 1) * rows] = sums[slot, :rows].astype(F32)
    proj_grad[...] = proj_sum[...].astype(F32)
    query_bias_grad[...] = bias_sum[0:1, :head_cols]
    value_bias_grad[...] = bias_sum[2:3, :head_cols]
    gain_grad[...] = vector_sum[0:2]
    shift_grad[...] = vector_sum[2:4]
    out_bias_grad[...] = vector_sum[4:5]
    down_bias_grad[...] = vector_sum[5:6]
    in_bias_grad[...] = vector_sum[pl.ds(8 + lax.axis_index("mp"), 1)]
    stream_grad[...] = resid_grad[...]
    for index in range(mp_size):
        for head in range(head_total):
            for part in range(3):
                at = part * head_cols + head * HEAD_DIM
                for side in range(2):
                    columns[side * half : (side + 1) * half, at : at + HEAD_DIM] = traded[
                        head, index, part, :, side * HEAD_DIM : (side + 1) * HEAD_DIM
                    ]
        copies[index].wait()
        stream_grad[...] += dot(columns[...], weight_buf[index])


def finish(traded, proj_all, resid_grad, sums):
    head_total, mp_size = traded.shape[:2]
    head_cols = head_total * HEAD_DIM
    local_rows, width = resid_grad.shape
    units = sums[0].shape[0] * sums[0].shape[1]
    row = jax.ShapeDtypeStruct((1, width), F32)
    head_row = jax.ShapeDtypeStruct((1, head_cols), F32)
    anywhere = pl.BlockSpec(memory_space=pl.ANY)
    return pl.pallas_call(
        finish_kernel,
        out_shape=(
            jax.ShapeDtypeStruct((local_rows, width), F32),
            jax.ShapeDtypeStruct((units, width), F32),
            jax.ShapeDtypeStruct((units, width), F32),
            jax.ShapeDtypeStruct((head_cols, width), F32),
            jax.ShapeDtypeStruct((3, head_cols, width), F32),
            head_row,
            head_row,
            row,
            jax.ShapeDtypeStruct((1, units), F32),
            row,
            jax.ShapeDtypeStruct((2, width), F32),
            jax.ShapeDtypeStruct((2, width), F32),
        ),
        in_specs=[whole(), anywhere] + [whole()] * 7,
        out_specs=(whole(),) * 12,
        scratch_shapes=[
            pltpu.VMEM((local_rows, 3 * head_cols), BF16),
            pltpu.VMEM((mp_size, 3 * head_cols, width), BF16),
            pltpu.SemaphoreType.DMA((mp_size,)),
        ],
        compiler_params=pltpu.CompilerParams(vmem_limit_bytes=VMEM_BYTES),
        cost_estimate=pl.CostEstimate(
            flops=6 * local_rows * width * width, bytes_accessed=24 * 1024 * 1024, transcendentals=0
        ),
        name="finish",
    )(traded, proj_all, resid_grad, *sums)


def dp_groups():
    total = lax.axis_size("dp")
    size = min(8, total)
    groups = [list(range(start, start + size)) for start in range(0, total, size)]
    return (size, groups)


def on_device(
    frames,
    segment_ids,
    qkv_weight,
    q_bias,
    v_bias,
    out_weight,
    out_bias,
    ff_in_weight,
    ff_in_bias,
    ff_out_weight,
    ff_out_bias,
    norm_gain,
    norm_shift,
    out_grad,
):
    local_rows, width = frames.shape
    mp_size = lax.axis_size("mp")
    group, groups = dp_groups()
    bits = group_bits(lax.axis_size("dp"))
    slots = 2**bits

    proj_weight = qkv_weight[0].transpose(0, 2, 1)
    seg_row = segment_ids.reshape(1, ROW_LEN)
    (
        input_all,
        qkv_low,
        in_all,
        down_all,
        out_all,
        in_bias_all,
        seg_col,
        out_cols,
        log_total,
        heads_low,
    ) = front(
        frames,
        proj_weight,
        q_bias,
        v_bias,
        seg_row,
        (ff_in_weight[0], ff_out_weight[0], out_weight[0]),
        ff_in_bias,
        mp_size,
        bits,
    )
    block_out, resid_grad, _, _, _, proj_all, traded, *summed = rear(
        frames,
        heads_low,
        out_grad,
        seg_row,
        in_bias_all,
        (out_bias, ff_out_bias, norm_gain[0], norm_shift[0]),
        (in_all, down_all, out_all),
        proj_weight.reshape(slots, -1, width),
        (qkv_low, out_cols, log_total, seg_col, input_all),
        bits,
    )
    if len(groups) > 1:
        across = [list(range(at, lax.axis_size("dp"), group)) for at in range(group)]
        summed = lax.psum(summed, "dp", axis_index_groups=across)
    (
        stream_grad,
        in_weight_grad,
        down_weight_grad,
        out_weight_grad,
        proj_grad,
        query_bias_grad,
        value_bias_grad,
        head_bias_grad,
        in_bias_grad,
        down_bias_grad,
        gain_grad,
        shift_grad,
    ) = finish(traded, proj_all.reshape(mp_size, -1, width), resid_grad, summed)
    return (
        block_out,
        stream_grad,
        proj_grad.transpose(0, 2, 1)[None],
        query_bias_grad,
        value_bias_grad,
        out_weight_grad[None],
        head_bias_grad,
        in_weight_grad[None],
        in_bias_grad,
        down_weight_grad[None],
        down_bias_grad,
        gain_grad[None],
        shift_grad[None],
    )


def solution(mesh):
    return jax.shard_map(
        on_device,
        mesh=mesh,
        in_specs=(
            P(("dp", "mp"), None),
            P("dp"),
            P(None, None, None, "mp"),
            P(None, "mp"),
            P(None, "mp"),
            P(None, "mp", None),
            P(),
            P(None, None, "mp"),
            P(None, "mp"),
            P(None, "mp", None),
            P(),
            P(),
            P(),
            P(("dp", "mp"), None),
        ),
        out_specs=(
            P(("dp", "mp"), None),
            P(("dp", "mp"), None),
            P(None, None, None, "mp"),
            P(None, "mp"),
            P(None, "mp"),
            P(None, "mp", None),
            P(),
            P(None, None, "mp"),
            P(None, "mp"),
            P(None, "mp", None),
            P(),
            P(),
            P(),
        ),
        check_vma=False,
    )
```

```python
import itertools
from functools import partial

import jax
import jax.numpy as jnp
from jax import lax
from jax.experimental import pallas as pl
from jax.experimental.pallas import tpu as pltpu
from jax.sharding import PartitionSpec as P

HEAD_DIM = 64
ROW_LEN = 2304
BLOCK = 768
BLOCKS = ROW_LEN // BLOCK
EXTRA = 16
SCALE = HEAD_DIM ** (-0.5)
MASKED = -1e30
F32 = jnp.float32
BF16 = jnp.bfloat16
VMEM_BYTES = 56 * 1024 * 1024
REAR_VMEM_BYTES = 63 * 1024 * 1024


def dot_rows(left, right):
    return lax.dot_general(left, right, (((1,), (1,)), ((), ())), preferred_element_type=F32)


def dot_cols(left, right):
    return lax.dot_general(left, right, (((0,), (0,)), ((), ())), preferred_element_type=F32)


def dot(left, right):
    return jnp.dot(left, right, preferred_element_type=F32)


def block_rows(number):
    return pl.ds(pl.multiple_of(number * BLOCK, BLOCK), BLOCK)


def as_pieces(row):
    high = row.astype(BF16).astype(F32)
    middle = (row - high).astype(BF16).astype(F32)
    last = row - high - middle
    place = lax.broadcasted_iota(jnp.int32, (EXTRA, row.shape[1]), 0)
    pieces = jnp.where(place == 0, high, jnp.where(place == 1, middle, jnp.where(place == 2, last, 0.0)))
    return pieces.astype(BF16)


def ones_columns(rows):
    place = lax.broadcasted_iota(jnp.int32, (rows, EXTRA), 1)
    return jnp.where(place < 3, 1.0, 0.0).astype(BF16)


def whole(memory_space=pltpu.VMEM):
    return pl.BlockSpec(memory_space=memory_space)


MESH = pl.DeviceIdType.MESH


def group_bits(dp_size):
    return min(3, dp_size.bit_length() - 1)


def place_in(dp_index, order):
    slot = 0
    for at, bit in enumerate(order):
        slot = slot + (dp_index // 2**bit) % 2 * 2**at
    return slot


def partner_of(dp_index, bit):
    return dp_index + (1 - 2 * ((dp_index // 2**bit) % 2)) * 2**bit


def enter(dp_index, mp_index, mp_size, bits):
    barrier = pltpu.get_barrier_semaphore()
    for offset in range(1, mp_size):
        pl.semaphore_signal(
            barrier, device_id={"mp": lax.rem(mp_index + offset, mp_size)}, device_id_type=MESH
        )
    for bit in range(bits):
        pl.semaphore_signal(
            barrier, device_id={"dp": partner_of(dp_index, bit)}, device_id_type=MESH
        )
    pl.semaphore_wait(barrier, mp_size - 1 + bits)


def send(src, dst, sems, at, device_id):
    return pltpu.make_async_remote_copy(
        src_ref=src,
        dst_ref=dst,
        send_sem=sems[0].at[at],
        recv_sem=sems[1].at[at],
        device_id=device_id,
        device_id_type=MESH,
    )


def gather_orders(bits):
    if bits == 3:
        return ((1, 2, 0), (2, 1, 0), (1, 2), (1, 2, 0))
    return (tuple(range(bits)),) * 4


SIDES = (1, -1)


def inside(index, size):
    return jnp.logical_and(index >= 0, index < size)


class Line:
    def __init__(self, mp_size, me):
        self.size = mp_size
        self.me = me
        self.hops = range(mp_size - 1)
        self.ways = [(side, hop) for hop in self.hops for side in (0, 1)]

    def wrapped(self, index):
        return lax.rem(index + self.size, self.size)

    def chunk(self, side, hop):
        return self.me - SIDES[side] * hop

    def place(self, side, hop):
        return self.wrapped(self.chunk(side, hop))

    def sends(self, side, hop):
        there = inside(self.me + SIDES[side], self.size)
        return jnp.logical_and(there, inside(self.chunk(side, hop), self.size))

    def if_sent(self, side, hop):
        return pl.when(self.sends(side, hop))

    def if_taken(self, side, hop):
        return pl.when(inside(self.chunk(side, hop + 1), self.size))

    def neighbour(self, side):
        return {"mp": self.wrapped(self.me + SIDES[side])}


def front_kernel(
    bits,
    frames,
    qkv_weight,
    q_bias,
    v_bias,
    seg_row,
    in_weight,
    down_weight,
    out_weight,
    in_bias,
    input_all,
    qkv_low,
    in_all,
    down_all,
    out_all,
    bias_all,
    seg_col,
    out_cols,
    log_total,
    heads_low,
    bias_buf,
    key_cols,
    value_buf,
    out_buf,
    staged,
    heads_in,
    own_sems,
    frame_send,
    frame_recv,
    bias_send,
    bias_recv,
    first_send,
    first_recv,
    later_send,
    later_recv,
    heads_own,
    heads_send,
    heads_recv,
):
    mp_size = in_all.shape[0]
    me = lax.axis_index("mp")
    dp_index = lax.axis_index("dp")
    local_rows = frames.shape[0]
    half = local_rows // 2
    head_total = out_cols.shape[0]
    orders = gather_orders(bits)[:3]
    parts = ((in_weight, in_all), (down_weight, down_all), (out_weight, out_all))
    line = Line(mp_size, me)
    hops, ways, wrapped = line.hops, line.ways, line.wrapped
    enter(dp_index, me, mp_size, bits)

    def slots(which, level):
        count = parts[which][0].shape[0] // 2 ** len(orders[which])
        start = place_in(dp_index, orders[which]) // 2**level * 2**level
        return pl.ds(pl.multiple_of(start * count, 16), count * 2**level)

    def first_copy(which, side, hop):
        rows = slots(which, 0)
        place = parts[which][1].at[line.place(side, hop), rows]
        source = parts[which][0].at[rows] if hop == 0 else place
        sems = (first_send, first_recv)
        return send(source, place, sems, (which, side, hop), line.neighbour(side))

    def later_copy(which, level, side, hop):
        held = parts[which][1].at[line.place(side, hop + 1), slots(which, level)]
        partner = {"dp": partner_of(dp_index, orders[which][level])}
        return send(held, held, (later_send, later_recv), (which, level, side, hop), partner)

    def frame_rows(index):
        return pl.ds(pl.multiple_of(wrapped(index) * local_rows, local_rows), local_rows)

    def frame_copy(side, hop):
        place = input_all.at[frame_rows(line.chunk(side, hop))]
        source = frames if hop == 0 else place
        return send(source, place, (frame_send, frame_recv), (side, hop), line.neighbour(side))

    def bias_copy(side, hop):
        place = bias_all.at[line.place(side, hop)]
        source = bias_buf if hop == 0 else place
        return send(source, place, (bias_send, bias_recv), (side, hop), line.neighbour(side))

    def project(index):
        rows = frame_rows(index)
        inputs = input_all[rows]
        for part, bias in enumerate((q_bias, None, v_bias)):
            products = dot_rows(inputs, qkv_weight[part])
            if bias is not None:
                products = products + bias[...].astype(F32)
            qkv_low[part, rows] = products.astype(BF16)

    def start_slices(side, hop):
        for which in range(3):
            first_copy(which, side, hop).start()
        bias_copy(side, hop).start()

    def take_slices(side, hop):
        for which in range(3):
            first_copy(which, side, hop).wait_recv()
        bias_copy(side, hop).wait_recv()
        if 0 < hop < mp_size - 2:
            line.if_sent(side, hop + 1)(partial(start_slices, side, hop + 1))
        for which in range(3):
            if orders[which]:
                later_copy(which, 0, side, hop).start()

    def trade_slices(level, side, hop):
        for which in range(3):
            if level < len(orders[which]):
                later_copy(which, level, side, hop).wait_recv()
            if level + 1 < len(orders[which]):
                later_copy(which, level + 1, side, hop).start()

    def take_hop(hop):
        for side in (0, 1):
            line.if_taken(side, hop)(partial(take_slices, side, hop))

    def trade_hop(level, hop):
        for side in (0, 1):
            line.if_taken(side, hop)(partial(trade_slices, level, side, hop))


    bias_buf[...] = jnp.broadcast_to(in_bias[...], bias_buf.shape)
    for side in (0, 1):
        line.if_sent(side, 0)(partial(start_slices, side, 0))
    for side in (0, 1):
        line.if_sent(side, 0)(lambda side=side: frame_copy(side, 0).start())
    own = [
        pltpu.make_async_copy(shard, gathered.at[me], own_sems.at[at])
        for at, (shard, gathered) in enumerate(parts + ((bias_buf, bias_all),))
    ]
    for copy in own:
        copy.start()
    input_all[frame_rows(me)] = frames[...]
    project(me)
    for step in range(BLOCKS):
        ids = jnp.broadcast_to(seg_row[:, step * BLOCK : (step + 1) * BLOCK].astype(F32), (128, BLOCK))
        seg_col[step * BLOCK : (step + 1) * BLOCK] = ids.T.astype(jnp.int32)

    def take_frames(side, hop):
        frame_copy(side, hop).wait_recv()
        if hop + 1 < mp_size - 1:
            line.if_sent(side, hop + 1)(lambda: frame_copy(side, hop + 1).start())

    def project_taken(side, hop):
        project(line.chunk(side, hop + 1))

    for hop in hops:
        for side in (0, 1):
            line.if_taken(side, hop)(partial(take_frames, side, hop))
        if hop == 0:
            take_hop(0)
        elif hop - 1 < bits:
            trade_hop(hop - 1, 0)
        for side in (0, 1):
            free = line.sends(side, hop)
            if hop + 1 < mp_size - 1:
                free = jnp.logical_and(free, jnp.logical_not(line.sends(side, hop + 1)))
            if mp_size > 2:
                passes = jnp.logical_and(free, line.sends(side, 1))
                pl.when(passes)(partial(start_slices, side, 1))
        for side in (0, 1):
            line.if_taken(side, hop)(partial(project_taken, side, hop))

    schedule = (
        (1, take_hop, 1),
        (3, trade_hop, 0, 1),
        (4, take_hop, 2),
        (6, trade_hop, 1, 1),
        (6, trade_hop, 0, 2),
    )
    events = {}
    done = {(take_hop, 0)} | {(trade_hop, hop - 1, 0) for hop in hops if 0 < hop <= bits}
    for at, act, *which in schedule:
        if which[-1] in hops and (act is take_hop or which[0] < bits):
            events.setdefault((at // BLOCKS, at % BLOCKS), []).append(partial(act, *which))
            done.add((act, *which))

    def attend(head):
        cols = slice(head * HEAD_DIM, (head + 1) * HEAD_DIM)
        lane = lax.broadcasted_iota(jnp.int32, (BLOCK, EXTRA), 1)
        for step in range(BLOCKS):
            rows = slice(step * BLOCK, (step + 1) * BLOCK)
            key_cols[step] = qkv_low[1, rows, cols].T
            value_buf[step, :, :HEAD_DIM] = qkv_low[2, rows, cols]
            value_buf[step, :, HEAD_DIM:] = jnp.where(lane == 0, 1.0, 0.0).astype(BF16)

        def query_block(number, _):
            rows = block_rows(number)
            queries = qkv_low[0, rows, cols] * SCALE

            def scores_of(step):
                ids = seg_row[:, step * BLOCK : (step + 1) * BLOCK]
                same = jnp.concatenate([seg_col[rows]] * (BLOCK // 128), axis=1) == ids
                return jnp.where(same, dot(queries, key_cols[step]), MASKED)

            peak = jnp.full((BLOCK, 1), MASKED, F32)
            mixed = jnp.zeros((BLOCK, HEAD_DIM + EXTRA), F32)
            scores = scores_of(0)
            for step in range(BLOCKS):
                ahead = scores_of(step + 1) if step + 1 < BLOCKS else None
                higher = jnp.maximum(peak, jnp.max(scores, axis=1, keepdims=True))
                soft = jnp.exp(scores - higher).astype(BF16)
                mixed = mixed * jnp.exp(peak - higher) + dot(soft, value_buf[step])
                peak, scores = higher, ahead
            total = mixed[:, HEAD_DIM : HEAD_DIM + 1]
            mixed = mixed[:, :HEAD_DIM] / total
            logs = jnp.broadcast_to(peak + jnp.log(total), (BLOCK, HEAD_DIM))
            both = jnp.concatenate([mixed, logs], axis=1).T
            out_cols[head, number] = both[:HEAD_DIM]
            log_total[head, number] = both[HEAD_DIM : HEAD_DIM + 1]
            out_buf[rows] = mixed.astype(BF16)
            for at in range(BLOCKS):
                if (head, at) in events:

                    @pl.when(number == at)
                    def _():
                        for act in events[(head, at)]:
                            act()

            return 0

        lax.fori_loop(0, BLOCKS, query_block, 0)

    def heads_copy(head, offset):
        return send(
            staged.at[head, wrapped(me + offset)],
            heads_in.at[head, me],
            (heads_send, heads_recv),
            (head, offset - 1),
            {"mp": wrapped(me + offset)},
        )

    def heads_own_copy(head):
        return pltpu.make_async_copy(
            staged.at[head, me], heads_in.at[head, me], heads_own.at[head]
        )

    peers = range(1, mp_size)
    for head in range(head_total):
        attend(head)
        for chunk in range(mp_size):
            for side in range(2):
                start = (2 * chunk + side) * half
                staged[head, chunk, :, side * HEAD_DIM : (side + 1) * HEAD_DIM] = out_buf[
                    start : start + half
                ]
        for offset in peers:
            heads_copy(head, offset).start()
        heads_own_copy(head).start()

    for hop in hops:
        if (take_hop, hop) not in done:
            take_hop(hop)
    for level in range(bits):
        for hop in hops:
            if (trade_hop, level, hop) not in done:
                trade_hop(level, hop)
    for head in range(head_total):
        heads_own_copy(head).wait()
        for offset in peers:
            heads_copy(head, offset).wait_recv()
        for chunk in range(mp_size):
            for side in range(2):
                at = (chunk * head_total + head) * HEAD_DIM
                heads_low[side * half : (side + 1) * half, at : at + HEAD_DIM] = heads_in[
                    head, chunk, :, side * HEAD_DIM : (side + 1) * HEAD_DIM
                ]
        for offset in peers:
            heads_copy(head, offset).wait_send()

    def sent_all(side, hop):
        frame_copy(side, hop).wait_send()
        bias_copy(side, hop).wait_send()
        for which in range(3):
            first_copy(which, side, hop).wait_send()

    def sent_later(side, hop):
        for which in range(3):
            for level in range(len(orders[which])):
                later_copy(which, level, side, hop).wait_send()

    for side, hop in ways:
        line.if_sent(side, hop)(partial(sent_all, side, hop))
        line.if_taken(side, hop)(partial(sent_later, side, hop))
    for copy in own:
        copy.wait()


def front(frames, qkv_weight, q_bias, v_bias, seg_row, weights, in_bias, mp_size, bits):
    local_rows, width = frames.shape
    head_cols = qkv_weight.shape[1]
    head_total = head_cols // HEAD_DIM
    peers = mp_size - 1
    levels = max(bits, 1)
    anywhere = pl.BlockSpec(memory_space=pl.ANY)
    in_weight, down_weight, out_weight = weights

    def sems(*shapes):
        return [pltpu.SemaphoreType.DMA(shape) for shape in shapes for _ in range(2)]

    piece = (head_total, mp_size, local_rows // 2, 2 * HEAD_DIM)
    return pl.pallas_call(
        partial(front_kernel, bits),
        out_shape=(
            jax.ShapeDtypeStruct((ROW_LEN, width), BF16),
            jax.ShapeDtypeStruct((3, ROW_LEN, head_cols), BF16),
            jax.ShapeDtypeStruct((mp_size,) + in_weight.shape, BF16),
            jax.ShapeDtypeStruct((mp_size,) + down_weight.shape, BF16),
            jax.ShapeDtypeStruct((mp_size,) + out_weight.shape, BF16),
            jax.ShapeDtypeStruct((mp_size, 16, in_bias.shape[1]), BF16),
            jax.ShapeDtypeStruct((ROW_LEN, 128), jnp.int32),
            jax.ShapeDtypeStruct((head_total, BLOCKS, HEAD_DIM, BLOCK), F32),
            jax.ShapeDtypeStruct((head_total, BLOCKS, 1, BLOCK), F32),
            jax.ShapeDtypeStruct((local_rows, width), BF16),
        ),
        in_specs=[whole()] * 5 + [anywhere] * 3 + [whole()],
        out_specs=(whole(), whole()) + (anywhere,) * 4 + (whole(),) * 4,
        scratch_shapes=[
            pltpu.VMEM((16, in_bias.shape[1]), BF16),
            pltpu.VMEM((BLOCKS, HEAD_DIM, BLOCK), BF16),
            pltpu.VMEM((BLOCKS, BLOCK, HEAD_DIM + EXTRA), BF16),
            pltpu.VMEM((ROW_LEN, HEAD_DIM), BF16),
            pltpu.VMEM(piece, BF16),
            pltpu.VMEM(piece, BF16),
            pltpu.SemaphoreType.DMA((4,)),
            *sems((2, peers), (2, peers), (3, 2, peers), (3, levels, 2, peers)),
            pltpu.SemaphoreType.DMA((head_total,)),
            *sems((head_total, peers)),
        ],
        compiler_params=pltpu.CompilerParams(
            collective_id=0, has_side_effects=True, vmem_limit_bytes=VMEM_BYTES
        ),
        cost_estimate=pl.CostEstimate(
            flops=16 * head_total * ROW_LEN * ROW_LEN * HEAD_DIM,
            bytes_accessed=32 * 1024 * 1024,
            transcendentals=head_total * ROW_LEN * ROW_LEN,
        ),
        name="front",
    )(frames, qkv_weight, q_bias, v_bias, seg_row, in_weight, down_weight, out_weight, in_bias)


def reduce_orders(bits):
    if bits == 3:
        return ((0, 1, 2), (0, 2, 1), (0, 1, 2))
    return (tuple(range(bits)),) * 3


def norm_rows(inputs, norm_gain, norm_shift):
    row_mean = jnp.mean(inputs, axis=-1, keepdims=True)
    centred = inputs - row_mean
    variance = jnp.mean(centred * centred, axis=-1, keepdims=True)
    inv_std = lax.rsqrt(variance + 1e-05)
    normed = centred * inv_std
    return (normed * norm_gain + norm_shift, normed, inv_std)


def norm_back(cotangent, normed, inv_std, norm_gain):
    scaled = cotangent * norm_gain
    adjusted = (
        scaled
        - jnp.mean(scaled, axis=-1, keepdims=True)
        - normed * jnp.mean(scaled * normed, axis=-1, keepdims=True)
    )
    return adjusted * inv_std


def sum_rows(array):
    return jnp.sum(array.astype(F32), axis=0, keepdims=True)


def rear_kernel(
    bits,
    seg_row,
    in_bias,
    out_bias,
    down_bias,
    norm_gain,
    norm_shift,
    frames,
    heads_low,
    out_grad,
    in_all,
    down_all,
    out_all,
    proj_weight,
    qkv_source,
    out_source,
    log_source,
    seg_source,
    input_source,
    block_out,
    resid_grad,
    in_grads,
    down_grads,
    head_grads,
    proj_all,
    traded,
    in_sum,
    down_sum,
    head_sum,
    proj_sum,
    vector_sum,
    bias_sum,
    grads_out,
    grads_in,
    kept,
    taken,
    last,
    proj,
    proj_taken,
    proj_slots,
    vectors,
    vectors_taken,
    vectors_all,
    biases,
    biases_taken,
    load_sems,
    in_sems,
    down_sems,
    out_sems,
    given_sems,
    head_sem,
    store_sems,
    attention_sems,
    weight_own,
    weight_send,
    weight_recv,
    weight_trade_send,
    weight_trade_recv,
    keep_sems,
    grads_own,
    grads_send,
    grads_recv,
    traded_own,
    traded_send,
    traded_recv,
    level_send,
    level_recv,
    last_send,
    last_recv,
    back_send,
    back_recv,
    proj_send,
    proj_recv,
    vector_send,
    vector_recv,
    vector_last_send,
    vector_last_recv,
    bias_send,
    bias_recv,
):
    mp_size, units, width = down_all.shape
    head_total = grads_out.shape[1]
    half = grads_out.shape[2]
    head_cols = width // mp_size
    slots = 2**bits
    me = lax.axis_index("mp")
    dp_index = lax.axis_index("dp")
    peers = range(1, mp_size)
    turns = range(mp_size)
    levels = list(range(bits))
    orders = reduce_orders(bits)
    partials = (in_grads, down_grads, head_grads)
    sums = (in_sum, down_sum, head_sum)
    arrays = range(3)
    vector = vectors[0]

    def target(offset):
        return lax.rem(me + offset, mp_size)

    def bit_of(which, level):
        return (dp_index // 2 ** orders[which][level]) % 2


    def part_of(turn):
        return target(turn + 1)

    def level_copy(which, level, turn):
        count = 2 ** (bits - 1 - level)
        other = (1 - bit_of(which, level)) * count
        part = pl.ds(part_of(turn), 1)
        source = partials[which] if level == 0 else taken[which][level - 1]
        return send(
            source.at[part, pl.ds(other, count)],
            taken[which][level].at[part],
            (level_send, level_recv),
            (which, level, turn),
            {"dp": partner_of(dp_index, orders[which][level])},
        )

    def keep_copy(which, turn):
        count = 2 ** (bits - 1)
        return pltpu.make_async_copy(
            partials[which].at[part_of(turn), pl.ds(bit_of(which, 0) * count, count)],
            kept[which].at[turn % 2],
            keep_sems.at[which, turn % 2],
        )

    def last_copy(which, offset):
        return send(
            taken[which][bits - 1].at[target(offset)],
            last[which].at[offset - 1],
            (last_send, last_recv),
            (which, offset - 1),
            {"mp": target(offset)},
        )

    def add_level(which, level, turn):
        level_copy(which, level, turn).wait_recv()
        count = 2 ** (bits - 1 - level)
        if level == 0:
            keep_copy(which, turn).wait()
        start = bit_of(which, level) * count
        into = taken[which][level]
        part = part_of(turn)
        for slot in range(count):
            if level == 0:
                mine = kept[which][turn % 2, slot]
            else:
                mine = taken[which][level - 1][part, start + slot]
            into[part, slot] = (into[part, slot].astype(F32) + mine.astype(F32)).astype(BF16)
        if level == 0 and turn + 2 < mp_size:
            keep_copy(which, turn + 2).start()
        if level + 1 < bits:
            level_copy(which, level + 1, turn).start()
        elif turn + 1 < mp_size:
            last_copy(which, turn + 1).start()

    def offer(which, turn):
        level_copy(which, 0, turn).start()
        if turn < 2:
            keep_copy(which, turn).start()

    def slot_of(order):
        return place_in(dp_index, order[::-1])

    def held_slots(order, level):
        count = 2 ** (bits - 1 - level)
        return pl.ds(slot_of(order) // count * count, count)

    def spread_copy(which, level):
        held = sums[which].at[held_slots(orders[which], level)]
        partner = {"dp": partner_of(dp_index, orders[which][level])}
        return send(held, held, (back_send, back_recv), (which, level), partner)

    def finish_sum(which):
        total = taken[which][bits - 1][me, 0].astype(F32)
        for offset in peers:
            last_copy(which, offset).wait_recv()
            total = total + last[which][offset - 1, 0].astype(F32)
        sums[which][slot_of(orders[which])] = total.astype(BF16)
        spread_copy(which, bits - 1).start()

    def spread(which, level):
        spread_copy(which, level).wait_recv()
        if level:
            spread_copy(which, level - 1).start()


    def proj_copy(head, level):
        count = 2 ** (bits - 1 - level)
        other = (1 - bit_of(0, level)) * count
        source = proj[head] if level == 0 else proj_taken[head][level - 1]
        return send(
            source.at[pl.ds(other, count)],
            proj_taken[head][level],
            (proj_send, proj_recv),
            (0, head, level),
            {"dp": partner_of(dp_index, orders[0][level])},
        )

    def proj_spread_copy(head, level):
        held = proj_slots[head].at[held_slots(orders[0], level)]
        partner = {"dp": partner_of(dp_index, orders[0][level])}
        return send(held, held, (proj_send, proj_recv), (1, head, level), partner)

    def add_proj(head, level):
        proj_copy(head, level).wait_recv()
        count = 2 ** (bits - 1 - level)
        start = bit_of(0, level) * count
        into = proj_taken[head][level]
        for slot in range(count):
            mine = proj[head][start + slot] if level == 0 else proj_taken[head][level - 1][start + slot]
            into[slot] = (into[slot].astype(F32) + mine.astype(F32)).astype(BF16)
        if level + 1 < bits:
            proj_copy(head, level + 1).start()
        else:
            proj_slots[head][slot_of(orders[0])] = into[0]
            proj_spread_copy(head, level).start()

    def spread_proj(head, level):
        proj_spread_copy(head, level).wait_recv()
        if level:
            proj_spread_copy(head, level - 1).start()


    def vector_copy(level):
        return send(
            vectors[level],
            vectors_taken[level],
            (vector_send, vector_recv),
            level,
            {"dp": partner_of(dp_index, level)},
        )

    def vector_last_copy(offset):
        return send(
            vectors[bits],
            vectors_all.at[me],
            (vector_last_send, vector_last_recv),
            offset - 1,
            {"mp": target(offset)},
        )

    def add_vector(level):
        vector_copy(level).wait_recv()
        vectors[level + 1][...] = vectors[level][...] + vectors_taken[level][...]
        if level + 1 < bits:
            vector_copy(level + 1).start()
        else:
            vectors_all[me] = vectors[bits][...]
            for offset in peers:
                vector_last_copy(offset).start()

    def finish_vector():
        for offset in peers:
            vector_last_copy(offset).wait_recv()
        total = vectors_all[0]
        for index in peers:
            total = total + vectors_all[index]
        vector_sum[...] = total

    def bias_copy(level):
        return send(
            biases[level],
            biases_taken[level],
            (bias_send, bias_recv),
            level,
            {"dp": partner_of(dp_index, level)},
        )

    def add_bias(level):
        bias_copy(level).wait_recv()
        biases[level + 1][...] = biases[level][...] + biases_taken[level][...]
        if level + 1 < bits:
            bias_copy(level + 1).start()
        else:
            bias_sum[...] = biases[bits][...]


    def grads_copy(head, offset):
        return send(
            grads_out.at[target(offset), head],
            grads_in.at[head, me],
            (grads_send, grads_recv),
            (head, offset - 1),
            {"mp": target(offset)},
        )

    def grads_own_copy(head):
        return pltpu.make_async_copy(
            grads_out.at[me, head], grads_in.at[head, me], grads_own.at[head]
        )

    line = Line(mp_size, me)
    order = gather_orders(bits)[3]
    own_slot = place_in(dp_index, order)

    def weight_copy(side, hop):
        place = proj_all.at[line.place(side, hop), pl.ds(own_slot, 1)]
        source = proj_weight.at[pl.ds(own_slot, 1)] if hop == 0 else place
        return send(source, place, (weight_send, weight_recv), (side, hop), line.neighbour(side))

    def weight_trade_copy(level, side, hop):
        held = pl.ds(own_slot // 2**level * 2**level, 2**level)
        place = proj_all.at[line.place(side, hop + 1), held]
        partner = {"dp": partner_of(dp_index, order[level])}
        return send(place, place, (weight_trade_send, weight_trade_recv), (level, side, hop), partner)

    def take_weight(side, hop):
        weight_copy(side, hop).wait_recv()
        if hop + 1 < mp_size - 1:
            line.if_sent(side, hop + 1)(lambda: weight_copy(side, hop + 1).start())
        if bits:
            weight_trade_copy(0, side, hop).start()

    def trade_weight(level, side, hop):
        weight_trade_copy(level, side, hop).wait_recv()
        if level + 1 < bits:
            weight_trade_copy(level + 1, side, hop).start()

    def both_sides(act, *which):
        for side in (0, 1):
            line.if_taken(side, which[-1])(partial(act, *which[:-1], side, which[-1]))

    schedule = (
        (0, take_weight, 0),
        (1, take_weight, 1),
        (2, take_weight, 2),
        (2, trade_weight, 0, 0),
        (3, trade_weight, 0, 1),
        (3, trade_weight, 0, 2),
        (4, trade_weight, 1, 0),
        (6, trade_weight, 1, 1),
        (8, trade_weight, 1, 2),
    )
    done = set()

    def at_point(point, index=None):
        for at, act, *which in schedule:
            if which[-1] not in line.hops or (act is trade_weight and which[0] >= bits):
                continue
            if index is None and at == point:
                both_sides(act, *which)
                done.add((act, *which))
            if index is not None and point <= at < point + mp_size:
                pl.when(index == at - point)(partial(both_sides, act, *which))
                done.add((act, *which))

    def dense_phase(
        frames_buf,
        heads_buf,
        cotangent_buf,
        in_buf,
        down_buf,
        out_buf,
        hidden,
        slope,
        mid_buf,
        normed_buf,
        store_buf,
        low_buf,
        grad_buf,
        given,
        head_buf,
    ):
        loads = [
            pltpu.make_async_copy(source, into, load_sems.at[at])
            for at, (source, into) in enumerate(
                ((frames, frames_buf), (heads_low, heads_buf), (out_grad, cotangent_buf))
            )
        ]
        out_copies = [
            pltpu.make_async_copy(
                out_all.at[index],
                out_buf.at[pl.ds(index * head_cols, head_cols)],
                out_sems.at[index],
            )
            for index in range(mp_size)
        ]

        def in_copy(index):
            return pltpu.make_async_copy(in_all.at[index], in_buf.at[index], in_sems.at[index])

        def down_copy(index):
            return pltpu.make_async_copy(
                down_all.at[index], down_buf.at[index], down_sems.at[index]
            )

        def given_copy(which, turn):
            return pltpu.make_async_copy(
                given.at[turn % 2], partials[which].at[part_of(turn)], given_sems.at[turn % 2]
            )

        def store_copy(at):
            return pltpu.make_async_copy(
                store_buf, (block_out, resid_grad)[at], store_sems.at[at]
            )

        for copy in loads + out_copies:
            copy.start()
        for index in range(mp_size):
            in_copy(index).start()
            down_copy(index).start()
        enter(dp_index, me, mp_size, bits)
        for side in (0, 1):
            line.if_sent(side, 0)(lambda side=side: weight_copy(side, 0).start())
        weight_own_copy.start()
        vector[...] = jnp.zeros_like(vector)
        gains = norm_gain[...].astype(F32)
        shifts = norm_shift[...].astype(F32)
        both = [slice(side * half, (side + 1) * half) for side in range(2)]

        for copy in loads + out_copies:
            copy.wait()
        branch = dot(heads_buf[...], out_buf[...]) + out_bias[...].astype(F32)
        mid, normed, inv_mid = norm_rows(
            frames_buf[...].astype(F32) + branch, gains[:1], shifts[:1]
        )
        mid_buf[...] = mid + down_bias[...].astype(F32)
        normed_buf[...] = normed
        low_buf[...] = mid.astype(BF16)
        at_point(0)

        def feed(index, _):
            in_copy(index).wait()
            down_copy(index).wait()
            for rows in both:
                pre_act = dot(low_buf[rows], in_buf[index]) + in_bias[index, 0:1].astype(F32)
                unit_cdf = 0.5 * (1.0 + lax.erf(pre_act * 0.5**0.5))
                bell = jnp.exp(-0.5 * pre_act * pre_act) * (2.0 * jnp.pi) ** (-0.5)
                slope[index, rows] = (unit_cdf + pre_act * bell).astype(BF16)
                hidden[index, rows] = (pre_act * unit_cdf).astype(BF16)
                mid_buf[rows] += dot(hidden[index, rows], down_buf[index])
            at_point(1, index)
            return 0

        lax.fori_loop(0, mp_size, feed, 0)
        output, normed, inv_out = norm_rows(mid_buf[...], gains[1:], shifts[1:])
        store_buf[...] = output
        store_copy(0).start()

        cotangent = cotangent_buf[...].astype(F32)
        vector[1:2] = sum_rows(cotangent * normed)
        vector[3:4] = sum_rows(cotangent)
        sum_grad = norm_back(cotangent, normed, inv_out, gains[1:])
        mid_buf[...] = sum_grad
        grad_buf[...] = sum_grad.astype(BF16)
        vector[5:6] = sum_rows(grad_buf[...])

        def give(which, turn, result):
            if turn >= 2:
                offer_given(which, turn - 2)
            share = result.shape[0] // slots
            for slot in range(slots):
                given[turn % 2, slot] = result[slot * share : (slot + 1) * share].astype(BF16)
            given_copy(which, turn).start()

        def offer_given(which, turn):
            given_copy(which, turn).wait()
            offer(which, turn)

        for turn in turns:
            index = part_of(turn)
            give(1, turn, dot_cols(hidden[index], grad_buf[...]))
            pre = dot_rows(grad_buf[...], down_buf[index]) * slope[index].astype(F32)
            hidden[index] = pre.astype(BF16)
            vector[pl.ds(8 + index, 1)] = sum_rows(hidden[index])
            mid_buf[...] += dot_rows(hidden[index], in_buf[index])
            at_point(1 + mp_size + turn)
        for turn in turns[-2:]:
            offer_given(1, turn)
        mid_grad = mid_buf[...]
        vector[0:1] = sum_rows(mid_grad * normed_buf[...])
        vector[2:3] = sum_rows(mid_grad)
        resid = norm_back(mid_grad, normed_buf[...], inv_mid, gains[:1])
        store_copy(0).wait()
        store_buf[...] = resid
        store_copy(1).start()
        attn_grad = resid.astype(BF16)
        grad_buf[...] = attn_grad
        vector[4:5] = sum_rows(attn_grad)
        heads_grad = dot_rows(attn_grad, out_buf[...]).astype(BF16)
        for head in range(head_total):
            for index in range(mp_size):
                at = index * head_cols + head * HEAD_DIM
                for side in range(2):
                    grads_out[index, head, :, side * HEAD_DIM : (side + 1) * HEAD_DIM] = (
                        heads_grad[both[side], at : at + HEAD_DIM]
                    )
            if head == 0:
                for offset in peers:
                    grads_copy(0, offset).start()
        for head in range(head_total):
            grads_own_copy(head).start()
        vector_copy(0).start()

        products = dot_cols(heads_buf[...], grad_buf[...]).astype(BF16)
        rows = head_cols // slots
        for index in range(mp_size):
            for slot in range(slots):
                start = index * head_cols + slot * rows
                head_buf[index, slot, :rows] = products[start : start + rows]
                if rows < head_buf.shape[2]:
                    head_buf[index, slot, rows:] = jnp.zeros(
                        (head_buf.shape[2] - rows, width), BF16
                    )
        head_copy = pltpu.make_async_copy(head_buf, head_grads, head_sem)
        head_copy.start()
        normed_low = low_buf[...].T
        for turn in turns:
            give(0, turn, dot(normed_low, hidden[part_of(turn)]))
            if turn == 0:
                head_copy.wait()
                for at in turns:
                    offer(2, at)
                for later in range(1, head_total):
                    for offset in peers:
                        grads_copy(later, offset).start()
        for turn in turns[-2:]:
            offer_given(0, turn)
        store_copy(1).wait()

    weight_own_copy = pltpu.make_async_copy(proj_weight, proj_all.at[me], weight_own)
    rows_low = pltpu.VMEM((2 * half, width), BF16)
    rows_full = pltpu.VMEM((2 * half, width), F32)
    pl.run_scoped(
        dense_phase,
        rows_low,
        rows_low,
        rows_low,
        pltpu.VMEM((mp_size, width, units), BF16),
        pltpu.VMEM((mp_size, units, width), BF16),
        pltpu.VMEM((width, width), BF16),
        pltpu.VMEM((mp_size, 2 * half, units), BF16),
        pltpu.VMEM((mp_size, 2 * half, units), BF16),
        rows_full,
        rows_full,
        rows_full,
        rows_low,
        rows_low,
        pltpu.VMEM((2, slots, units // slots, width), BF16),
        pltpu.VMEM(head_grads.shape, BF16),
    )

    def attention_phase(
        qkv,
        out_cols,
        log_total,
        seg_col,
        input_all,
        staged,
        qkv_grad,
        seg_blocks,
        grads,
        key_buf,
        key_cols,
        value_buf,
        query_sum,
        key_sum,
        value_sum,
        proj_rows,
    ):
        def traded_copy(head, offset):
            return send(
                staged.at[head, target(offset)],
                traded.at[head, me],
                (traded_send, traded_recv),
                (head, offset - 1),
                {"mp": target(offset)},
            )

        def traded_own_copy(head):
            return pltpu.make_async_copy(
                staged.at[head, me], traded.at[head, me], traded_own.at[head]
            )

        def prepare(head):
            cols = slice(head * HEAD_DIM, (head + 1) * HEAD_DIM)
            key_buf[:, :HEAD_DIM] = qkv[1, :, cols]
            key_buf[:, HEAD_DIM:] = ones_columns(ROW_LEN)
            value_buf[:, :HEAD_DIM] = qkv[2, :, cols]
            value_buf[:, HEAD_DIM:] = ones_columns(ROW_LEN)
            for step in range(BLOCKS):
                key_cols[step] = qkv[1, step * BLOCK : (step + 1) * BLOCK, cols].T
            key_sum[...] = jnp.zeros_like(key_sum)
            value_sum[...] = jnp.zeros_like(value_sum)

        def take_grads(head):
            grads_own_copy(head).wait()
            for offset in peers:
                grads_copy(head, offset).wait_recv()
            for chunk in range(mp_size):
                for side in range(2):
                    start = (2 * chunk + side) * half
                    grads[start : start + half] = grads_in[
                        head, chunk, :, side * HEAD_DIM : (side + 1) * HEAD_DIM
                    ]

        def attend_back(head):
            cols = slice(head * HEAD_DIM, (head + 1) * HEAD_DIM)

            def query_block(number, _):
                rows = block_rows(number)
                queries = qkv[0, rows, cols] * SCALE
                grad_rows = grads[rows]
                seg_query = seg_blocks[number]
                grad_cols = grad_rows.astype(F32).T
                row_dot = jnp.sum(grad_cols * out_cols[head, number], axis=0, keepdims=True)
                grad_cols = jnp.concatenate([grad_cols.astype(BF16), as_pieces(-row_dot)], axis=0)
                query_cols = jnp.concatenate(
                    [queries.astype(F32).T.astype(BF16), as_pieces(-log_total[head, number])], axis=0
                )

                def products_of(step):
                    key_rows = slice(step * BLOCK, (step + 1) * BLOCK)
                    same = (
                        jnp.concatenate([seg_col[key_rows]] * (BLOCK // 128), axis=1) == seg_query
                    )
                    scores = jnp.where(same, dot(key_buf[key_rows], query_cols), MASKED)
                    return scores, dot(value_buf[key_rows], grad_cols)

                query_grad = jnp.zeros((HEAD_DIM, BLOCK), F32)
                ahead = products_of(0)
                for step in range(BLOCKS):
                    scores, soft_grad = ahead
                    if step + 1 < BLOCKS:
                        ahead = products_of(step + 1)
                    key_rows = slice(step * BLOCK, (step + 1) * BLOCK)
                    soft = jnp.exp(scores)
                    score_grad = (soft * soft_grad).astype(BF16)
                    value_sum[key_rows] += dot(soft.astype(BF16), grad_rows)
                    key_sum[key_rows] += dot(score_grad, queries)
                    query_grad = query_grad + dot(key_cols[step], score_grad)
                query_sum[rows] = (query_grad * SCALE).T
                for at in range(head * BLOCKS, (head + 1) * BLOCKS):
                    if at in events:

                        @pl.when(number == at - head * BLOCKS)
                        def _():
                            for act in events[at]:
                                act()

                return 0

            lax.fori_loop(0, BLOCKS, query_block, 0)

        def give_grads(head):
            for part, total in enumerate((query_sum, key_sum, value_sum)):
                low = total[...].astype(BF16)
                qkv_grad[:, part * HEAD_DIM : (part + 1) * HEAD_DIM] = low
                if part != 1:
                    cols = slice(head * HEAD_DIM, (head + 1) * HEAD_DIM)
                    sum_low = jnp.sum(low.astype(F32), axis=0, keepdims=True)
                    biases[0][part : part + 1, cols] = sum_low
                for chunk in range(mp_size):
                    for side in range(2):
                        start = (2 * chunk + side) * half
                        staged[head, chunk, part, :, side * HEAD_DIM : (side + 1) * HEAD_DIM] = total[
                            start : start + half
                        ].astype(BF16)

        def start_trade(head):
            for offset in peers:
                traded_copy(head, offset).start()
            traded_own_copy(head).start()

        def start_proj(head):
            products = dot_cols(qkv_grad[...], input_all[...])
            slot_rows = proj[head].shape[1]
            for slot in range(2**bits):
                proj[head][slot] = products[slot * slot_rows : (slot + 1) * slot_rows].astype(BF16)
            proj_copy(head, 0).start()

        def finish_proj(head):
            cols = slice(head * HEAD_DIM, (head + 1) * HEAD_DIM)
            slot_rows = proj_slots[head].shape[1]
            for slot in range(2**bits):
                proj_rows[slot * slot_rows : (slot + 1) * slot_rows] = proj_slots[head][slot].astype(F32)
            for part in range(3):
                rows = proj_rows[part * HEAD_DIM : (part + 1) * HEAD_DIM]
                proj_sum[part, cols] = rows.astype(BF16)

        events = {}
        rest = []

        def due(at, act, *which):
            if at is None:
                rest.append((act, *which))
            else:
                events.setdefault(at, []).append(partial(act, *which))

        for at, level in zip((0, 1, 2), levels):
            due(at, add_vector, level)
        due(3, finish_vector)
        times = {
            1: ((0, 0, 0, 0), (2, 3, 3, 4), (3, 4, 4, 5)),
            2: ((1, 1, 1, 1), (3, 3, 3, 3), (4, 4, 4, 4)),
            0: ((2, 3, 3, 5), (3, 5, 6, 6), (4, 6, 7, 8)),
        }
        ends = {1: (7, 8, None, None), 2: (7, 8, None, None), 0: (None, None, None, None)}
        for level in levels:
            for which in times:
                for turn, at in zip(turns, times[which][level]):
                    due(at, add_level, which, level, turn)
        for at, level in zip((3, 4, 5), levels):
            due(at, add_proj, 0, level)
        for at, level in zip((6, 7, 8), levels):
            due(at, add_proj, 1, level)
        for at, level in zip((6, 7, 8), levels[::-1]):
            due(at, spread_proj, 0, level)
        for which in (1, 2, 0):
            due(ends[which][0], finish_sum, which)
        for step, level in enumerate(levels[::-1]):
            for which in (1, 2, 0):
                due(ends[which][1 + step], spread, which, level)

        copies = [
            pltpu.make_async_copy(source, into, attention_sems.at[at])
            for at, (source, into) in enumerate(
                (
                    (qkv_source, qkv),
                    (seg_source, seg_col),
                    (log_source, log_total),
                    (out_source, out_cols),
                    (input_source, input_all),
                )
            )
        ]
        for copy in copies:
            copy.start()
        biases[0][...] = jnp.zeros_like(biases[0])
        for step in range(BLOCKS):
            seg_blocks[step] = seg_row[:, step * BLOCK : (step + 1) * BLOCK]
        final = head_total - 1
        copies[0].wait()
        for head in range(head_total):
            prepare(head)
            take_grads(head)
            if head == 0:
                for copy in copies[1:4]:
                    copy.wait()
            attend_back(head)
            give_grads(head)
            start_trade(head)
            if head == 0:
                copies[4].wait()
            start_proj(head)
        bias_copy(0).start()
        for level in levels:
            add_proj(final, level)
            add_bias(level)
            spread_proj(final - 1, bits - 1 - level)
        for act, *which in rest:
            act(*which)
        for level in levels[::-1]:
            spread_proj(final, level)
        for head in range(head_total):
            finish_proj(head)
            traded_own_copy(head).wait()
            for offset in peers:
                traded_copy(head, offset).wait()

    pl.run_scoped(
        attention_phase,
        pltpu.VMEM(qkv_source.shape, BF16),
        pltpu.VMEM(out_source.shape, F32),
        pltpu.VMEM(log_source.shape, F32),
        pltpu.VMEM(seg_source.shape, jnp.int32),
        pltpu.VMEM(input_source.shape, BF16),
        pltpu.VMEM((head_total, mp_size, 3, half, 2 * HEAD_DIM), BF16),
        pltpu.VMEM((ROW_LEN, 3 * HEAD_DIM), BF16),
        pltpu.VMEM((BLOCKS, 1, BLOCK), jnp.int32),
        pltpu.VMEM((ROW_LEN, HEAD_DIM), BF16),
        pltpu.VMEM((ROW_LEN, HEAD_DIM + EXTRA), BF16),
        pltpu.VMEM((BLOCKS, HEAD_DIM, BLOCK), BF16),
        pltpu.VMEM((ROW_LEN, HEAD_DIM + EXTRA), BF16),
        pltpu.VMEM((ROW_LEN, HEAD_DIM), F32),
        pltpu.VMEM((ROW_LEN, HEAD_DIM), F32),
        pltpu.VMEM((ROW_LEN, HEAD_DIM), F32),
        pltpu.VMEM((3 * HEAD_DIM, width), F32),
    )

    for hop in line.hops:
        if (take_weight, hop) not in done:
            both_sides(take_weight, hop)
    for level in levels:
        for hop in line.hops:
            if (trade_weight, level, hop) not in done:
                both_sides(trade_weight, level, hop)

    def sent_trades(side, hop):
        for level in levels:
            weight_trade_copy(level, side, hop).wait_send()

    for side, hop in line.ways:
        line.if_sent(side, hop)(lambda side=side, hop=hop: weight_copy(side, hop).wait_send())
        line.if_taken(side, hop)(partial(sent_trades, side, hop))
    weight_own_copy.wait()
    for head in range(head_total):
        for offset in peers:
            grads_copy(head, offset).wait_send()
        for level in levels:
            proj_copy(head, level).wait_send()
            proj_spread_copy(head, level).wait_send()
    for level in levels:
        vector_copy(level).wait_send()
        bias_copy(level).wait_send()
        for which in arrays:
            spread_copy(which, level).wait_send()
            for turn in turns:
                level_copy(which, level, turn).wait_send()
    for offset in peers:
        vector_last_copy(offset).wait_send()
        for which in arrays:
            last_copy(which, offset).wait_send()


def rear(frames, heads_low, out_grad, seg_row, in_bias, small, weights, proj_weight, saved, bits):
    local_rows, width = frames.shape
    qkv_low, out_cols = saved[:2]
    mp_size, units = weights[1].shape[:2]
    head_total = out_cols.shape[0]
    half, lanes = local_rows // 2, 2 * HEAD_DIM
    peers = mp_size - 1
    slots = 2**bits
    head_rows = -(-width // mp_size // slots // 16) * 16
    anywhere = pl.BlockSpec(memory_space=pl.ANY)
    blocks = [(width // slots, units), (units // slots, width), (head_rows, width)]
    proj_block = (3 * HEAD_DIM // slots, width)
    bias_block = (8, 2 * 128)
    vector_block = (8 + -(-mp_size // 8) * 8, width)

    def halves(shape, lead=()):
        return [pltpu.VMEM(lead + (slots >> (level + 1),) + shape, BF16) for level in range(bits)]

    def sems(*shapes):
        return [pltpu.SemaphoreType.DMA(shape) for shape in shapes for _ in range(2)]

    piece = pltpu.VMEM((mp_size, head_total, half, lanes), BF16)
    return pl.pallas_call(
        partial(rear_kernel, bits),
        out_shape=(
            jax.ShapeDtypeStruct((local_rows, width), F32),
            jax.ShapeDtypeStruct((local_rows, width), F32),
            *(jax.ShapeDtypeStruct((mp_size, slots) + block, BF16) for block in blocks),
            jax.ShapeDtypeStruct((mp_size,) + proj_weight.shape, BF16),
            jax.ShapeDtypeStruct((head_total, mp_size, 3, half, lanes), BF16),
            *(jax.ShapeDtypeStruct((slots,) + block, BF16) for block in blocks),
            jax.ShapeDtypeStruct((3, head_total * HEAD_DIM, width), BF16),
            jax.ShapeDtypeStruct(vector_block, F32),
            jax.ShapeDtypeStruct(bias_block, F32),
        ),
        in_specs=[whole()] * 6 + [anywhere] * 12,
        out_specs=(anywhere,) * 7 + (whole(),) * 6,
        scratch_shapes=[
            piece,
            pltpu.VMEM((head_total, mp_size, half, lanes), BF16),
            [pltpu.VMEM((2, slots // 2) + block, BF16) for block in blocks],
            [halves(block, (mp_size,)) for block in blocks],
            [pltpu.VMEM((peers, 1) + block, BF16) for block in blocks],
            [pltpu.VMEM((slots,) + proj_block, BF16) for _ in range(head_total)],
            [halves(proj_block) for _ in range(head_total)],
            [pltpu.VMEM((slots,) + proj_block, BF16) for _ in range(head_total)],
            [pltpu.VMEM(vector_block, F32) for _ in range(bits + 1)],
            [pltpu.VMEM(vector_block, F32) for _ in range(bits)],
            pltpu.VMEM((mp_size,) + vector_block, F32),
            [pltpu.VMEM(bias_block, F32) for _ in range(bits + 1)],
            [pltpu.VMEM(bias_block, F32) for _ in range(bits)],
            pltpu.SemaphoreType.DMA((3,)),
            pltpu.SemaphoreType.DMA((mp_size,)),
            pltpu.SemaphoreType.DMA((mp_size,)),
            pltpu.SemaphoreType.DMA((mp_size,)),
            pltpu.SemaphoreType.DMA((2,)),
            pltpu.SemaphoreType.DMA,
            pltpu.SemaphoreType.DMA((2,)),
            pltpu.SemaphoreType.DMA((5,)),
            pltpu.SemaphoreType.DMA,
            *sems((2, peers), (max(bits, 1), 2, peers)),
            pltpu.SemaphoreType.DMA((3, 2)),
            pltpu.SemaphoreType.DMA((head_total,)),
            *sems((head_total, peers)),
            pltpu.SemaphoreType.DMA((head_total,)),
            *sems(
                (head_total, peers),
                (3, bits, mp_size),
                (3, peers),
                (3, bits),
                (2, head_total, bits),
                (bits,),
                (peers,),
                (bits,),
            ),
        ],
        compiler_params=pltpu.CompilerParams(
            collective_id=1, has_side_effects=True, vmem_limit_bytes=REAR_VMEM_BYTES
        ),
        cost_estimate=pl.CostEstimate(
            flops=40 * head_total * ROW_LEN * ROW_LEN * HEAD_DIM,
            bytes_accessed=96 * 1024 * 1024,
            transcendentals=head_total * ROW_LEN * ROW_LEN,
        ),
        name="rear",
    )(seg_row, in_bias, *small, frames, heads_low, out_grad, *weights, proj_weight, *saved)


def finish_kernel(
    vector_sum,
    bias_sum,
    traded,
    proj_all,
    resid_grad,
    in_sum,
    down_sum,
    head_sum,
    proj_sum,
    stream_grad,
    in_grad,
    down_grad,
    out_grad,
    proj_grad,
    query_bias_grad,
    value_bias_grad,
    out_bias_grad,
    in_bias_grad,
    down_bias_grad,
    gain_grad,
    shift_grad,
    traded_buf,
    weight_buf,
    columns,
    low_bufs,
    full_bufs,
    stream_buf,
    sems,
    out_sems,
):
    head_total, mp_size = traded.shape[:2]
    half = traded.shape[3]
    head_cols = head_total * HEAD_DIM
    sums = (in_sum, down_sum, head_sum, proj_sum)
    grads = (in_grad, down_grad, out_grad, proj_grad)
    copies = [
        pltpu.make_async_copy(source, into, sems.at[at])
        for at, (source, into) in enumerate(
            (
                *zip(sums, low_bufs),
                (traded, traded_buf),
                (resid_grad, stream_buf),
                (proj_all, weight_buf),
            )
        )
    ]
    outs = [
        pltpu.make_async_copy(source, into, out_sems.at[at])
        for at, (source, into) in enumerate((*zip(full_bufs, grads), (stream_buf, stream_grad)))
    ]
    for copy in copies:
        copy.start()
    query_bias_grad[...] = bias_sum[0:1, :head_cols]
    value_bias_grad[...] = bias_sum[2:3, :head_cols]
    gain_grad[...] = vector_sum[0:2]
    shift_grad[...] = vector_sum[2:4]
    out_bias_grad[...] = vector_sum[4:5]
    down_bias_grad[...] = vector_sum[5:6]
    in_bias_grad[...] = vector_sum[pl.ds(8 + lax.axis_index("mp"), 1)]
    for at in range(3):
        rows = full_bufs[at].shape[0] // low_bufs[at].shape[0]
        copies[at].wait()
        for slot in range(low_bufs[at].shape[0]):
            full_bufs[at][slot * rows : (slot + 1) * rows] = low_bufs[at][slot, :rows].astype(F32)
        outs[at].start()
    copies[3].wait()
    full_bufs[3][...] = low_bufs[3][...].astype(F32)
    outs[3].start()
    for copy in copies[4:]:
        copy.wait()
    for index in range(mp_size):
        for head in range(head_total):
            for part in range(3):
                at = part * head_cols + head * HEAD_DIM
                for side in range(2):
                    columns[index % 2, side * half : (side + 1) * half, at : at + HEAD_DIM] = (
                        traded_buf[head, index, part, :, side * HEAD_DIM : (side + 1) * HEAD_DIM]
                    )
        stream_buf[...] += dot(columns[index % 2], weight_buf[index])
    outs[4].start()
    for copy in outs:
        copy.wait()


def finish(traded, proj_all, resid_grad, sums):
    head_total, mp_size = traded.shape[:2]
    head_cols = head_total * HEAD_DIM
    local_rows, width = resid_grad.shape
    *sums, vector_sum, bias_sum = sums
    units = sums[0].shape[0] * sums[0].shape[1]
    row = jax.ShapeDtypeStruct((1, width), F32)
    head_row = jax.ShapeDtypeStruct((1, head_cols), F32)
    anywhere = pl.BlockSpec(memory_space=pl.ANY)
    grads = [(units, width), (units, width), (head_cols, width), (3, head_cols, width)]
    return pl.pallas_call(
        finish_kernel,
        out_shape=(
            jax.ShapeDtypeStruct((local_rows, width), F32),
            *(jax.ShapeDtypeStruct(shape, F32) for shape in grads),
            head_row,
            head_row,
            row,
            jax.ShapeDtypeStruct((1, units), F32),
            row,
            jax.ShapeDtypeStruct((2, width), F32),
            jax.ShapeDtypeStruct((2, width), F32),
        ),
        in_specs=[whole()] * 2 + [anywhere] * 7,
        out_specs=(anywhere,) * 5 + (whole(),) * 7,
        scratch_shapes=[
            pltpu.VMEM(traded.shape, BF16),
            pltpu.VMEM(proj_all.shape, BF16),
            pltpu.VMEM((2, local_rows, 3 * head_cols), BF16),
            [pltpu.VMEM(array.shape, array.dtype) for array in sums],
            [pltpu.VMEM(shape, F32) for shape in grads],
            pltpu.VMEM((local_rows, width), F32),
            pltpu.SemaphoreType.DMA((7,)),
            pltpu.SemaphoreType.DMA((5,)),
        ],
        compiler_params=pltpu.CompilerParams(vmem_limit_bytes=VMEM_BYTES),
        cost_estimate=pl.CostEstimate(
            flops=6 * local_rows * width * width, bytes_accessed=24 * 1024 * 1024, transcendentals=0
        ),
        name="finish",
    )(vector_sum, bias_sum, traded, proj_all, resid_grad, *sums)


def dp_groups():
    total = lax.axis_size("dp")
    size = min(8, total)
    groups = [list(range(start, start + size)) for start in range(0, total, size)]
    return (size, groups)


def on_device(
    frames,
    segment_ids,
    qkv_weight,
    q_bias,
    v_bias,
    out_weight,
    out_bias,
    ff_in_weight,
    ff_in_bias,
    ff_out_weight,
    ff_out_bias,
    norm_gain,
    norm_shift,
    out_grad,
):
    local_rows, width = frames.shape
    mp_size = lax.axis_size("mp")
    group, groups = dp_groups()
    bits = group_bits(lax.axis_size("dp"))
    slots = 2**bits

    proj_weight = qkv_weight[0].transpose(0, 2, 1)
    seg_row = segment_ids.reshape(1, ROW_LEN)
    (
        input_all,
        qkv_low,
        in_all,
        down_all,
        out_all,
        in_bias_all,
        seg_col,
        out_cols,
        log_total,
        heads_low,
    ) = front(
        frames,
        proj_weight,
        q_bias,
        v_bias,
        seg_row,
        (ff_in_weight[0], ff_out_weight[0], out_weight[0]),
        ff_in_bias,
        mp_size,
        bits,
    )
    block_out, resid_grad, _, _, _, proj_all, traded, *summed = rear(
        frames,
        heads_low,
        out_grad,
        seg_row,
        in_bias_all,
        (out_bias, ff_out_bias, norm_gain[0], norm_shift[0]),
        (in_all, down_all, out_all),
        proj_weight.reshape(slots, -1, width),
        (qkv_low, out_cols, log_total, seg_col, input_all),
        bits,
    )
    if len(groups) > 1:
        across = [list(range(at, lax.axis_size("dp"), group)) for at in range(group)]
        summed = lax.psum(summed, "dp", axis_index_groups=across)
    (
        stream_grad,
        in_weight_grad,
        down_weight_grad,
        out_weight_grad,
        proj_grad,
        query_bias_grad,
        value_bias_grad,
        head_bias_grad,
        in_bias_grad,
        down_bias_grad,
        gain_grad,
        shift_grad,
    ) = finish(traded, proj_all.reshape(mp_size, -1, width), resid_grad, summed)
    return (
        block_out,
        stream_grad,
        proj_grad.transpose(0, 2, 1)[None],
        query_bias_grad,
        value_bias_grad,
        out_weight_grad[None],
        head_bias_grad,
        in_weight_grad[None],
        in_bias_grad,
        down_weight_grad[None],
        down_bias_grad,
        gain_grad[None],
        shift_grad[None],
    )


def solution(mesh):
    return jax.shard_map(
        on_device,
        mesh=mesh,
        in_specs=(
            P(("dp", "mp"), None),
            P("dp"),
            P(None, None, None, "mp"),
            P(None, "mp"),
            P(None, "mp"),
            P(None, "mp", None),
            P(),
            P(None, None, "mp"),
            P(None, "mp"),
            P(None, "mp", None),
            P(),
            P(),
            P(),
            P(("dp", "mp"), None),
        ),
        out_specs=(
            P(("dp", "mp"), None),
            P(("dp", "mp"), None),
            P(None, None, None, "mp"),
            P(None, "mp"),
            P(None, "mp"),
            P(None, "mp", None),
            P(),
            P(None, None, "mp"),
            P(None, "mp"),
            P(None, "mp", None),
            P(),
            P(),
            P(),
        ),
        check_vma=False,
    )
```

```python
import itertools
from functools import partial

import jax
import jax.numpy as jnp
from jax import lax
from jax.experimental import pallas as pl
from jax.experimental.pallas import tpu as pltpu
from jax.sharding import PartitionSpec as P

HEAD_DIM = 64
ROW_LEN = 2304
BLOCK = 768
BLOCKS = ROW_LEN // BLOCK
EXTRA = 16
SCALE = HEAD_DIM ** (-0.5)
MASKED = -1e30
F32 = jnp.float32
BF16 = jnp.bfloat16
VMEM_BYTES = 56 * 1024 * 1024
REAR_VMEM_BYTES = 63 * 1024 * 1024


def dot_rows(left, right):
    return lax.dot_general(left, right, (((1,), (1,)), ((), ())), preferred_element_type=F32)


def dot_cols(left, right):
    return lax.dot_general(left, right, (((0,), (0,)), ((), ())), preferred_element_type=F32)


def dot(left, right):
    return jnp.dot(left, right, preferred_element_type=F32)


def block_rows(number):
    return pl.ds(pl.multiple_of(number * BLOCK, BLOCK), BLOCK)


def as_pieces(row):
    high = row.astype(BF16).astype(F32)
    middle = (row - high).astype(BF16).astype(F32)
    last = row - high - middle
    place = lax.broadcasted_iota(jnp.int32, (EXTRA, row.shape[1]), 0)
    pieces = jnp.where(place == 0, high, jnp.where(place == 1, middle, jnp.where(place == 2, last, 0.0)))
    return pieces.astype(BF16)


def ones_columns(rows):
    place = lax.broadcasted_iota(jnp.int32, (rows, EXTRA), 1)
    return jnp.where(place < 3, 1.0, 0.0).astype(BF16)


def whole(memory_space=pltpu.VMEM):
    return pl.BlockSpec(memory_space=memory_space)


MESH = pl.DeviceIdType.MESH


def group_bits(dp_size):
    return min(3, dp_size.bit_length() - 1)


def place_in(dp_index, order):
    slot = 0
    for at, bit in enumerate(order):
        slot = slot + (dp_index // 2**bit) % 2 * 2**at
    return slot


def partner_of(dp_index, bit):
    return dp_index + (1 - 2 * ((dp_index // 2**bit) % 2)) * 2**bit


def enter(dp_index, mp_index, mp_size, bits):
    barrier = pltpu.get_barrier_semaphore()
    for offset in range(1, mp_size):
        pl.semaphore_signal(
            barrier, device_id={"mp": lax.rem(mp_index + offset, mp_size)}, device_id_type=MESH
        )
    for bit in range(bits):
        pl.semaphore_signal(
            barrier, device_id={"dp": partner_of(dp_index, bit)}, device_id_type=MESH
        )
    pl.semaphore_wait(barrier, mp_size - 1 + bits)


def send(src, dst, sems, at, device_id):
    return pltpu.make_async_remote_copy(
        src_ref=src,
        dst_ref=dst,
        send_sem=sems[0].at[at],
        recv_sem=sems[1].at[at],
        device_id=device_id,
        device_id_type=MESH,
    )


def gather_orders(bits):
    if bits == 3:
        return ((1, 2, 0), (2, 1, 0), (1, 2), (1, 2, 0))
    return (tuple(range(bits)),) * 4


SIDES = (1, -1)


def inside(index, size):
    return jnp.logical_and(index >= 0, index < size)


class Line:
    def __init__(self, mp_size, me):
        self.size = mp_size
        self.me = me
        self.hops = range(mp_size - 1)
        self.ways = [(side, hop) for hop in self.hops for side in (0, 1)]

    def wrapped(self, index):
        return lax.rem(index + self.size, self.size)

    def chunk(self, side, hop):
        return self.me - SIDES[side] * hop

    def place(self, side, hop):
        return self.wrapped(self.chunk(side, hop))

    def sends(self, side, hop):
        there = inside(self.me + SIDES[side], self.size)
        return jnp.logical_and(there, inside(self.chunk(side, hop), self.size))

    def if_sent(self, side, hop):
        return pl.when(self.sends(side, hop))

    def if_taken(self, side, hop):
        return pl.when(inside(self.chunk(side, hop + 1), self.size))

    def neighbour(self, side):
        return {"mp": self.wrapped(self.me + SIDES[side])}


def front_kernel(
    bits,
    frames,
    qkv_weight,
    q_bias,
    v_bias,
    seg_row,
    in_weight,
    down_weight,
    out_weight,
    in_bias,
    input_all,
    qkv_low,
    in_all,
    down_all,
    out_all,
    bias_all,
    seg_col,
    out_cols,
    log_total,
    heads_low,
    bias_buf,
    key_cols,
    value_buf,
    out_buf,
    staged,
    heads_in,
    own_sems,
    frame_send,
    frame_recv,
    bias_send,
    bias_recv,
    first_send,
    first_recv,
    later_send,
    later_recv,
    heads_own,
    heads_send,
    heads_recv,
):
    mp_size = in_all.shape[0]
    me = lax.axis_index("mp")
    dp_index = lax.axis_index("dp")
    local_rows = frames.shape[0]
    half = local_rows // 2
    head_total = out_cols.shape[0]
    orders = gather_orders(bits)[:3]
    parts = ((in_weight, in_all), (down_weight, down_all), (out_weight, out_all))
    line = Line(mp_size, me)
    hops, ways, wrapped = line.hops, line.ways, line.wrapped
    enter(dp_index, me, mp_size, bits)

    def slots(which, level):
        count = parts[which][0].shape[0] // 2 ** len(orders[which])
        start = place_in(dp_index, orders[which]) // 2**level * 2**level
        return pl.ds(pl.multiple_of(start * count, 16), count * 2**level)

    def first_copy(which, side, hop):
        rows = slots(which, 0)
        place = parts[which][1].at[line.place(side, hop), rows]
        source = parts[which][0].at[rows] if hop == 0 else place
        sems = (first_send, first_recv)
        return send(source, place, sems, (which, side, hop), line.neighbour(side))

    def later_copy(which, level, side, hop):
        held = parts[which][1].at[line.place(side, hop + 1), slots(which, level)]
        partner = {"dp": partner_of(dp_index, orders[which][level])}
        return send(held, held, (later_send, later_recv), (which, level, side, hop), partner)

    def frame_rows(index):
        return pl.ds(pl.multiple_of(wrapped(index) * local_rows, local_rows), local_rows)

    def frame_copy(side, hop):
        place = input_all.at[frame_rows(line.chunk(side, hop))]
        source = frames if hop == 0 else place
        return send(source, place, (frame_send, frame_recv), (side, hop), line.neighbour(side))

    def bias_copy(side, hop):
        place = bias_all.at[line.place(side, hop)]
        source = bias_buf if hop == 0 else place
        return send(source, place, (bias_send, bias_recv), (side, hop), line.neighbour(side))

    def project(index):
        rows = frame_rows(index)
        inputs = input_all[rows]
        for part, bias in enumerate((q_bias, None, v_bias)):
            products = dot_rows(inputs, qkv_weight[part])
            if bias is not None:
                products = products + bias[...].astype(F32)
            qkv_low[part, rows] = products.astype(BF16)

    def start_slices(side, hop):
        for which in range(3):
            first_copy(which, side, hop).start()
        bias_copy(side, hop).start()

    def take_slices(side, hop):
        for which in range(3):
            first_copy(which, side, hop).wait_recv()
        bias_copy(side, hop).wait_recv()
        if 0 < hop < mp_size - 2:
            line.if_sent(side, hop + 1)(partial(start_slices, side, hop + 1))
        for which in range(3):
            if orders[which]:
                later_copy(which, 0, side, hop).start()

    def trade_slices(level, side, hop):
        for which in range(3):
            if level < len(orders[which]):
                later_copy(which, level, side, hop).wait_recv()
            if level + 1 < len(orders[which]):
                later_copy(which, level + 1, side, hop).start()

    def take_hop(hop):
        for side in (0, 1):
            line.if_taken(side, hop)(partial(take_slices, side, hop))

    def trade_hop(level, hop):
        for side in (0, 1):
            line.if_taken(side, hop)(partial(trade_slices, level, side, hop))


    bias_buf[...] = jnp.broadcast_to(in_bias[...], bias_buf.shape)
    for side in (0, 1):
        line.if_sent(side, 0)(partial(start_slices, side, 0))
    for side in (0, 1):
        line.if_sent(side, 0)(lambda side=side: frame_copy(side, 0).start())
    own = [
        pltpu.make_async_copy(shard, gathered.at[me], own_sems.at[at])
        for at, (shard, gathered) in enumerate(parts + ((bias_buf, bias_all),))
    ]
    for copy in own:
        copy.start()
    input_all[frame_rows(me)] = frames[...]
    project(me)
    for step in range(BLOCKS):
        ids = jnp.broadcast_to(seg_row[:, step * BLOCK : (step + 1) * BLOCK].astype(F32), (128, BLOCK))
        seg_col[step * BLOCK : (step + 1) * BLOCK] = ids.T.astype(jnp.int32)

    def take_frames(side, hop):
        frame_copy(side, hop).wait_recv()
        if hop + 1 < mp_size - 1:
            line.if_sent(side, hop + 1)(lambda: frame_copy(side, hop + 1).start())

    def project_taken(side, hop):
        project(line.chunk(side, hop + 1))

    for hop in hops:
        for side in (0, 1):
            line.if_taken(side, hop)(partial(take_frames, side, hop))
        if hop == 0:
            take_hop(0)
        elif hop - 1 < bits:
            trade_hop(hop - 1, 0)
        for side in (0, 1):
            free = line.sends(side, hop)
            if hop + 1 < mp_size - 1:
                free = jnp.logical_and(free, jnp.logical_not(line.sends(side, hop + 1)))
            if mp_size > 2:
                passes = jnp.logical_and(free, line.sends(side, 1))
                pl.when(passes)(partial(start_slices, side, 1))
        for side in (0, 1):
            line.if_taken(side, hop)(partial(project_taken, side, hop))

    schedule = (
        (1, take_hop, 1),
        (3, trade_hop, 0, 1),
        (4, take_hop, 2),
        (6, trade_hop, 1, 1),
        (6, trade_hop, 0, 2),
    )
    events = {}
    done = {(take_hop, 0)} | {(trade_hop, hop - 1, 0) for hop in hops if 0 < hop <= bits}
    for at, act, *which in schedule:
        if which[-1] in hops and (act is take_hop or which[0] < bits):
            events.setdefault((at // BLOCKS, at % BLOCKS), []).append(partial(act, *which))
            done.add((act, *which))

    def attend(head):
        cols = slice(head * HEAD_DIM, (head + 1) * HEAD_DIM)
        lane = lax.broadcasted_iota(jnp.int32, (BLOCK, EXTRA), 1)
        for step in range(BLOCKS):
            rows = slice(step * BLOCK, (step + 1) * BLOCK)
            key_cols[step] = qkv_low[1, rows, cols].T
            value_buf[step, :, :HEAD_DIM] = qkv_low[2, rows, cols]
            value_buf[step, :, HEAD_DIM:] = jnp.where(lane == 0, 1.0, 0.0).astype(BF16)

        def query_block(number, _):
            rows = block_rows(number)
            queries = qkv_low[0, rows, cols] * SCALE

            def scores_of(step):
                ids = seg_row[:, step * BLOCK : (step + 1) * BLOCK]
                same = jnp.concatenate([seg_col[rows]] * (BLOCK // 128), axis=1) == ids
                return jnp.where(same, dot(queries, key_cols[step]), MASKED)

            peak = jnp.full((BLOCK, 1), MASKED, F32)
            mixed = jnp.zeros((BLOCK, HEAD_DIM + EXTRA), F32)
            scores = scores_of(0)
            for step in range(BLOCKS):
                ahead = scores_of(step + 1) if step + 1 < BLOCKS else None
                higher = jnp.maximum(peak, jnp.max(scores, axis=1, keepdims=True))
                soft = jnp.exp(scores - higher).astype(BF16)
                mixed = mixed * jnp.exp(peak - higher) + dot(soft, value_buf[step])
                peak, scores = higher, ahead
            total = mixed[:, HEAD_DIM : HEAD_DIM + 1]
            mixed = mixed[:, :HEAD_DIM] / total
            logs = jnp.broadcast_to(peak + jnp.log(total), (BLOCK, HEAD_DIM))
            both = jnp.concatenate([mixed, logs], axis=1).T
            out_cols[head, number] = both[:HEAD_DIM]
            log_total[head, number] = both[HEAD_DIM : HEAD_DIM + 1]
            out_buf[rows] = mixed.astype(BF16)
            for at in range(BLOCKS):
                if (head, at) in events:

                    @pl.when(number == at)
                    def _():
                        for act in events[(head, at)]:
                            act()

            return 0

        lax.fori_loop(0, BLOCKS, query_block, 0)

    def heads_copy(head, offset):
        return send(
            staged.at[head, wrapped(me + offset)],
            heads_in.at[head, me],
            (heads_send, heads_recv),
            (head, offset - 1),
            {"mp": wrapped(me + offset)},
        )

    def heads_own_copy(head):
        return pltpu.make_async_copy(
            staged.at[head, me], heads_in.at[head, me], heads_own.at[head]
        )

    peers = range(1, mp_size)
    for head in range(head_total):
        attend(head)
        for chunk in range(mp_size):
            for side in range(2):
                start = (2 * chunk + side) * half
                staged[head, chunk, :, side * HEAD_DIM : (side + 1) * HEAD_DIM] = out_buf[
                    start : start + half
                ]
        for offset in peers:
            heads_copy(head, offset).start()
        heads_own_copy(head).start()

    for hop in hops:
        if (take_hop, hop) not in done:
            take_hop(hop)
    for level in range(bits):
        for hop in hops:
            if (trade_hop, level, hop) not in done:
                trade_hop(level, hop)
    for head in range(head_total):
        heads_own_copy(head).wait()
        for offset in peers:
            heads_copy(head, offset).wait_recv()
        for chunk in range(mp_size):
            for side in range(2):
                at = (chunk * head_total + head) * HEAD_DIM
                heads_low[side * half : (side + 1) * half, at : at + HEAD_DIM] = heads_in[
                    head, chunk, :, side * HEAD_DIM : (side + 1) * HEAD_DIM
                ]
        for offset in peers:
            heads_copy(head, offset).wait_send()

    def sent_all(side, hop):
        frame_copy(side, hop).wait_send()
        bias_copy(side, hop).wait_send()
        for which in range(3):
            first_copy(which, side, hop).wait_send()

    def sent_later(side, hop):
        for which in range(3):
            for level in range(len(orders[which])):
                later_copy(which, level, side, hop).wait_send()

    for side, hop in ways:
        line.if_sent(side, hop)(partial(sent_all, side, hop))
        line.if_taken(side, hop)(partial(sent_later, side, hop))
    for copy in own:
        copy.wait()


def front(frames, qkv_weight, q_bias, v_bias, seg_row, weights, in_bias, mp_size, bits):
    local_rows, width = frames.shape
    head_cols = qkv_weight.shape[1]
    head_total = head_cols // HEAD_DIM
    peers = mp_size - 1
    levels = max(bits, 1)
    anywhere = pl.BlockSpec(memory_space=pl.ANY)
    in_weight, down_weight, out_weight = weights

    def sems(*shapes):
        return [pltpu.SemaphoreType.DMA(shape) for shape in shapes for _ in range(2)]

    piece = (head_total, mp_size, local_rows // 2, 2 * HEAD_DIM)
    return pl.pallas_call(
        partial(front_kernel, bits),
        out_shape=(
            jax.ShapeDtypeStruct((ROW_LEN, width), BF16),
            jax.ShapeDtypeStruct((3, ROW_LEN, head_cols), BF16),
            jax.ShapeDtypeStruct((mp_size,) + in_weight.shape, BF16),
            jax.ShapeDtypeStruct((mp_size,) + down_weight.shape, BF16),
            jax.ShapeDtypeStruct((mp_size,) + out_weight.shape, BF16),
            jax.ShapeDtypeStruct((mp_size, 16, in_bias.shape[1]), BF16),
            jax.ShapeDtypeStruct((ROW_LEN, 128), jnp.int32),
            jax.ShapeDtypeStruct((head_total, BLOCKS, HEAD_DIM, BLOCK), F32),
            jax.ShapeDtypeStruct((head_total, BLOCKS, 1, BLOCK), F32),
            jax.ShapeDtypeStruct((local_rows, width), BF16),
        ),
        in_specs=[whole()] * 5 + [anywhere] * 3 + [whole()],
        out_specs=(whole(), whole()) + (anywhere,) * 4 + (whole(),) * 4,
        scratch_shapes=[
            pltpu.VMEM((16, in_bias.shape[1]), BF16),
            pltpu.VMEM((BLOCKS, HEAD_DIM, BLOCK), BF16),
            pltpu.VMEM((BLOCKS, BLOCK, HEAD_DIM + EXTRA), BF16),
            pltpu.VMEM((ROW_LEN, HEAD_DIM), BF16),
            pltpu.VMEM(piece, BF16),
            pltpu.VMEM(piece, BF16),
            pltpu.SemaphoreType.DMA((4,)),
            *sems((2, peers), (2, peers), (3, 2, peers), (3, levels, 2, peers)),
            pltpu.SemaphoreType.DMA((head_total,)),
            *sems((head_total, peers)),
        ],
        compiler_params=pltpu.CompilerParams(
            collective_id=0, has_side_effects=True, vmem_limit_bytes=VMEM_BYTES
        ),
        cost_estimate=pl.CostEstimate(
            flops=16 * head_total * ROW_LEN * ROW_LEN * HEAD_DIM,
            bytes_accessed=32 * 1024 * 1024,
            transcendentals=head_total * ROW_LEN * ROW_LEN,
        ),
        name="front",
    )(frames, qkv_weight, q_bias, v_bias, seg_row, in_weight, down_weight, out_weight, in_bias)


def reduce_orders(bits):
    if bits == 3:
        return ((0, 1, 2), (0, 2, 1), (0, 1, 2))
    return (tuple(range(bits)),) * 3


def norm_rows(inputs, norm_gain, norm_shift):
    row_mean = jnp.mean(inputs, axis=-1, keepdims=True)
    centred = inputs - row_mean
    variance = jnp.mean(centred * centred, axis=-1, keepdims=True)
    inv_std = lax.rsqrt(variance + 1e-05)
    normed = centred * inv_std
    return (normed * norm_gain + norm_shift, normed, inv_std)


def norm_back(cotangent, normed, inv_std, norm_gain):
    scaled = cotangent * norm_gain
    adjusted = (
        scaled
        - jnp.mean(scaled, axis=-1, keepdims=True)
        - normed * jnp.mean(scaled * normed, axis=-1, keepdims=True)
    )
    return adjusted * inv_std


def sum_rows(array):
    return jnp.sum(array.astype(F32), axis=0, keepdims=True)


def rear_kernel(
    bits,
    seg_row,
    in_bias,
    out_bias,
    down_bias,
    norm_gain,
    norm_shift,
    frames,
    heads_low,
    out_grad,
    in_all,
    down_all,
    out_all,
    proj_weight,
    qkv_source,
    out_source,
    log_source,
    seg_source,
    input_source,
    block_out,
    resid_grad,
    in_grads,
    down_grads,
    head_grads,
    proj_all,
    traded,
    in_sum,
    down_sum,
    head_sum,
    proj_sum,
    vector_sum,
    bias_sum,
    grads_out,
    grads_in,
    kept,
    taken,
    last,
    proj,
    proj_taken,
    proj_slots,
    vectors,
    vectors_taken,
    vectors_all,
    biases,
    biases_taken,
    load_sems,
    in_sems,
    down_sems,
    out_sems,
    given_sems,
    head_sem,
    store_sems,
    attention_sems,
    weight_own,
    weight_send,
    weight_recv,
    weight_trade_send,
    weight_trade_recv,
    keep_sems,
    grads_own,
    grads_send,
    grads_recv,
    traded_own,
    traded_send,
    traded_recv,
    level_send,
    level_recv,
    last_send,
    last_recv,
    back_send,
    back_recv,
    proj_send,
    proj_recv,
    vector_send,
    vector_recv,
    vector_last_send,
    vector_last_recv,
    bias_send,
    bias_recv,
):
    mp_size, units, width = down_all.shape
    head_total = grads_out.shape[1]
    half = grads_out.shape[2]
    head_cols = width // mp_size
    slots = 2**bits
    me = lax.axis_index("mp")
    dp_index = lax.axis_index("dp")
    peers = range(1, mp_size)
    turns = range(mp_size)
    levels = list(range(bits))
    orders = reduce_orders(bits)
    partials = (in_grads, down_grads, head_grads)
    sums = (in_sum, down_sum, head_sum)
    arrays = range(3)
    vector = vectors[0]

    def target(offset):
        return lax.rem(me + offset, mp_size)

    def bit_of(which, level):
        return (dp_index // 2 ** orders[which][level]) % 2


    def part_of(turn):
        return target(turn + 1)

    def level_copy(which, level, turn):
        count = 2 ** (bits - 1 - level)
        other = (1 - bit_of(which, level)) * count
        part = pl.ds(part_of(turn), 1)
        source = partials[which] if level == 0 else taken[which][level - 1]
        return send(
            source.at[part, pl.ds(other, count)],
            taken[which][level].at[part],
            (level_send, level_recv),
            (which, level, turn),
            {"dp": partner_of(dp_index, orders[which][level])},
        )

    def keep_copy(which, turn):
        count = 2 ** (bits - 1)
        return pltpu.make_async_copy(
            partials[which].at[part_of(turn), pl.ds(bit_of(which, 0) * count, count)],
            kept[which].at[turn % 2],
            keep_sems.at[which, turn % 2],
        )

    def last_copy(which, side, part):
        return send(
            taken[which][bits - 1].at[part, 0],
            last[which].at[side, part],
            (last_send, last_recv),
            (which, side, part),
            line.neighbour(side),
        )

    def add_last(which, side, part):
        last_copy(which, side, part).wait_recv()
        total = taken[which][bits - 1][part, 0].astype(F32) + last[which][side, part].astype(F32)
        taken[which][bits - 1][part, 0] = total.astype(BF16)

    def pass_on(which, stage):
        for side in (0, 1):
            at = stage if side == 0 else mp_size - 1 - stage
            beyond = range(at + 1, mp_size) if side == 0 else range(at)

            @pl.when(me == at)
            def _():
                for part in beyond:
                    if stage:
                        add_last(which, side, part)
                    last_copy(which, side, part).start()

    def add_level(which, level, turn):
        level_copy(which, level, turn).wait_recv()
        count = 2 ** (bits - 1 - level)
        if level == 0:
            keep_copy(which, turn).wait()
        start = bit_of(which, level) * count
        into = taken[which][level]
        part = part_of(turn)
        for slot in range(count):
            if level == 0:
                mine = kept[which][turn % 2, slot]
            else:
                mine = taken[which][level - 1][part, start + slot]
            into[part, slot] = (into[part, slot].astype(F32) + mine.astype(F32)).astype(BF16)
        if level == 0 and turn + 2 < mp_size:
            keep_copy(which, turn + 2).start()
        if level + 1 < bits:
            level_copy(which, level + 1, turn).start()

    def offer(which, turn):
        level_copy(which, 0, turn).start()
        if turn < 2:
            keep_copy(which, turn).start()

    def slot_of(order):
        return place_in(dp_index, order[::-1])

    def held_slots(order, level):
        count = 2 ** (bits - 1 - level)
        return pl.ds(slot_of(order) // count * count, count)

    def spread_copy(which, level):
        held = sums[which].at[held_slots(orders[which], level)]
        partner = {"dp": partner_of(dp_index, orders[which][level])}
        return send(held, held, (back_send, back_recv), (which, level), partner)

    def finish_sum(which):
        pl.when(me > 0)(lambda: add_last(which, 0, me))
        pl.when(me < mp_size - 1)(lambda: add_last(which, 1, me))
        sums[which][slot_of(orders[which])] = taken[which][bits - 1][me, 0]
        spread_copy(which, bits - 1).start()

    def spread(which, level):
        spread_copy(which, level).wait_recv()
        if level:
            spread_copy(which, level - 1).start()


    def proj_copy(head, level):
        count = 2 ** (bits - 1 - level)
        other = (1 - bit_of(0, level)) * count
        source = proj[head] if level == 0 else proj_taken[head][level - 1]
        return send(
            source.at[pl.ds(other, count)],
            proj_taken[head][level],
            (proj_send, proj_recv),
            (0, head, level),
            {"dp": partner_of(dp_index, orders[0][level])},
        )

    def proj_spread_copy(head, level):
        held = proj_slots[head].at[held_slots(orders[0], level)]
        partner = {"dp": partner_of(dp_index, orders[0][level])}
        return send(held, held, (proj_send, proj_recv), (1, head, level), partner)

    def add_proj(head, level):
        proj_copy(head, level).wait_recv()
        count = 2 ** (bits - 1 - level)
        start = bit_of(0, level) * count
        into = proj_taken[head][level]
        for slot in range(count):
            mine = proj[head][start + slot] if level == 0 else proj_taken[head][level - 1][start + slot]
            into[slot] = (into[slot].astype(F32) + mine.astype(F32)).astype(BF16)
        if level + 1 < bits:
            proj_copy(head, level + 1).start()
        else:
            proj_slots[head][slot_of(orders[0])] = into[0]
            proj_spread_copy(head, level).start()

    def spread_proj(head, level):
        proj_spread_copy(head, level).wait_recv()
        if level:
            proj_spread_copy(head, level - 1).start()


    def vector_copy(level):
        return send(
            vectors[level],
            vectors_taken[level],
            (vector_send, vector_recv),
            level,
            {"dp": partner_of(dp_index, level)},
        )

    def vector_last_copy(offset):
        return send(
            vectors[bits],
            vectors_all.at[me],
            (vector_last_send, vector_last_recv),
            offset - 1,
            {"mp": target(offset)},
        )

    def add_vector(level):
        vector_copy(level).wait_recv()
        vectors[level + 1][...] = vectors[level][...] + vectors_taken[level][...]
        if level + 1 < bits:
            vector_copy(level + 1).start()
        else:
            vectors_all[me] = vectors[bits][...]
            for offset in peers:
                vector_last_copy(offset).start()

    def finish_vector():
        for offset in peers:
            vector_last_copy(offset).wait_recv()
        total = vectors_all[0]
        for index in peers:
            total = total + vectors_all[index]
        vector_sum[...] = total

    def bias_copy(level):
        return send(
            biases[level],
            biases_taken[level],
            (bias_send, bias_recv),
            level,
            {"dp": partner_of(dp_index, level)},
        )

    def add_bias(level):
        bias_copy(level).wait_recv()
        biases[level + 1][...] = biases[level][...] + biases_taken[level][...]
        if level + 1 < bits:
            bias_copy(level + 1).start()
        else:
            bias_sum[...] = biases[bits][...]


    def grads_copy(head, offset):
        return send(
            grads_out.at[target(offset), head],
            grads_in.at[head, me],
            (grads_send, grads_recv),
            (head, offset - 1),
            {"mp": target(offset)},
        )

    def grads_own_copy(head):
        return pltpu.make_async_copy(
            grads_out.at[me, head], grads_in.at[head, me], grads_own.at[head]
        )

    line = Line(mp_size, me)
    order = gather_orders(bits)[3]
    own_slot = place_in(dp_index, order)

    def weight_copy(side, hop):
        place = proj_all.at[line.place(side, hop), pl.ds(own_slot, 1)]
        source = proj_weight.at[pl.ds(own_slot, 1)] if hop == 0 else place
        return send(source, place, (weight_send, weight_recv), (side, hop), line.neighbour(side))

    def weight_trade_copy(level, side, hop):
        held = pl.ds(own_slot // 2**level * 2**level, 2**level)
        place = proj_all.at[line.place(side, hop + 1), held]
        partner = {"dp": partner_of(dp_index, order[level])}
        return send(place, place, (weight_trade_send, weight_trade_recv), (level, side, hop), partner)

    def take_weight(side, hop):
        weight_copy(side, hop).wait_recv()
        if hop + 1 < mp_size - 1:
            line.if_sent(side, hop + 1)(lambda: weight_copy(side, hop + 1).start())
        if bits:
            weight_trade_copy(0, side, hop).start()

    def trade_weight(level, side, hop):
        weight_trade_copy(level, side, hop).wait_recv()
        if level + 1 < bits:
            weight_trade_copy(level + 1, side, hop).start()

    def both_sides(act, *which):
        for side in (0, 1):
            line.if_taken(side, which[-1])(partial(act, *which[:-1], side, which[-1]))

    schedule = (
        (0, take_weight, 0),
        (1, take_weight, 1),
        (2, take_weight, 2),
        (2, trade_weight, 0, 0),
        (3, trade_weight, 0, 1),
        (3, trade_weight, 0, 2),
        (4, trade_weight, 1, 0),
        (6, trade_weight, 1, 1),
        (8, trade_weight, 1, 2),
    )
    done = set()

    def at_point(point, index=None):
        for at, act, *which in schedule:
            if which[-1] not in line.hops or (act is trade_weight and which[0] >= bits):
                continue
            if index is None and at == point:
                both_sides(act, *which)
                done.add((act, *which))
            if index is not None and point <= at < point + mp_size:
                pl.when(index == at - point)(partial(both_sides, act, *which))
                done.add((act, *which))

    def dense_phase(
        frames_buf,
        heads_buf,
        cotangent_buf,
        in_buf,
        down_buf,
        out_buf,
        hidden,
        slope,
        mid_buf,
        normed_buf,
        store_buf,
        low_buf,
        grad_buf,
        given,
        head_buf,
    ):
        loads = [
            pltpu.make_async_copy(source, into, load_sems.at[at])
            for at, (source, into) in enumerate(
                ((frames, frames_buf), (heads_low, heads_buf), (out_grad, cotangent_buf))
            )
        ]
        out_copies = [
            pltpu.make_async_copy(
                out_all.at[index],
                out_buf.at[pl.ds(index * head_cols, head_cols)],
                out_sems.at[index],
            )
            for index in range(mp_size)
        ]

        def in_copy(index):
            return pltpu.make_async_copy(in_all.at[index], in_buf.at[index], in_sems.at[index])

        def down_copy(index):
            return pltpu.make_async_copy(
                down_all.at[index], down_buf.at[index], down_sems.at[index]
            )

        def given_copy(which, turn):
            return pltpu.make_async_copy(
                given.at[turn % 2], partials[which].at[part_of(turn)], given_sems.at[turn % 2]
            )

        def store_copy(at):
            return pltpu.make_async_copy(
                store_buf, (block_out, resid_grad)[at], store_sems.at[at]
            )

        for copy in loads + out_copies:
            copy.start()
        for index in range(mp_size):
            in_copy(index).start()
            down_copy(index).start()
        enter(dp_index, me, mp_size, bits)
        for side in (0, 1):
            line.if_sent(side, 0)(lambda side=side: weight_copy(side, 0).start())
        weight_own_copy.start()
        vector[...] = jnp.zeros_like(vector)
        gains = norm_gain[...].astype(F32)
        shifts = norm_shift[...].astype(F32)
        both = [slice(side * half, (side + 1) * half) for side in range(2)]

        for copy in loads + out_copies:
            copy.wait()
        branch = dot(heads_buf[...], out_buf[...]) + out_bias[...].astype(F32)
        mid, normed, inv_mid = norm_rows(
            frames_buf[...].astype(F32) + branch, gains[:1], shifts[:1]
        )
        mid_buf[...] = mid + down_bias[...].astype(F32)
        normed_buf[...] = normed
        low_buf[...] = mid.astype(BF16)
        at_point(0)

        def feed(index, _):
            in_copy(index).wait()
            down_copy(index).wait()
            for rows in both:
                pre_act = dot(low_buf[rows], in_buf[index]) + in_bias[index, 0:1].astype(F32)
                unit_cdf = 0.5 * (1.0 + lax.erf(pre_act * 0.5**0.5))
                bell = jnp.exp(-0.5 * pre_act * pre_act) * (2.0 * jnp.pi) ** (-0.5)
                slope[index, rows] = (unit_cdf + pre_act * bell).astype(BF16)
                hidden[index, rows] = (pre_act * unit_cdf).astype(BF16)
                mid_buf[rows] += dot(hidden[index, rows], down_buf[index])
            at_point(1, index)
            return 0

        lax.fori_loop(0, mp_size, feed, 0)
        output, normed, inv_out = norm_rows(mid_buf[...], gains[1:], shifts[1:])
        store_buf[...] = output
        store_copy(0).start()

        cotangent = cotangent_buf[...].astype(F32)
        vector[1:2] = sum_rows(cotangent * normed)
        vector[3:4] = sum_rows(cotangent)
        sum_grad = norm_back(cotangent, normed, inv_out, gains[1:])
        mid_buf[...] = sum_grad
        grad_buf[...] = sum_grad.astype(BF16)
        vector[5:6] = sum_rows(grad_buf[...])

        def give(which, turn, result):
            if turn >= 2:
                offer_given(which, turn - 2)
            share = result.shape[0] // slots
            for slot in range(slots):
                given[turn % 2, slot] = result[slot * share : (slot + 1) * share].astype(BF16)
            given_copy(which, turn).start()

        def offer_given(which, turn):
            given_copy(which, turn).wait()
            offer(which, turn)

        for turn in turns:
            index = part_of(turn)
            give(1, turn, dot_cols(hidden[index], grad_buf[...]))
            pre = dot_rows(grad_buf[...], down_buf[index]) * slope[index].astype(F32)
            hidden[index] = pre.astype(BF16)
            vector[pl.ds(8 + index, 1)] = sum_rows(hidden[index])
            mid_buf[...] += dot_rows(hidden[index], in_buf[index])
            at_point(1 + mp_size + turn)
        for turn in turns[-2:]:
            offer_given(1, turn)
        mid_grad = mid_buf[...]
        vector[0:1] = sum_rows(mid_grad * normed_buf[...])
        vector[2:3] = sum_rows(mid_grad)
        resid = norm_back(mid_grad, normed_buf[...], inv_mid, gains[:1])
        store_copy(0).wait()
        store_buf[...] = resid
        store_copy(1).start()
        attn_grad = resid.astype(BF16)
        grad_buf[...] = attn_grad
        vector[4:5] = sum_rows(attn_grad)
        heads_grad = dot_rows(attn_grad, out_buf[...]).astype(BF16)
        for head in range(head_total):
            for index in range(mp_size):
                at = index * head_cols + head * HEAD_DIM
                for side in range(2):
                    grads_out[index, head, :, side * HEAD_DIM : (side + 1) * HEAD_DIM] = (
                        heads_grad[both[side], at : at + HEAD_DIM]
                    )
            if head == 0:
                for offset in peers:
                    grads_copy(0, offset).start()
        for head in range(head_total):
            grads_own_copy(head).start()
        vector_copy(0).start()

        products = dot_cols(heads_buf[...], grad_buf[...]).astype(BF16)
        rows = head_cols // slots
        for index in range(mp_size):
            for slot in range(slots):
                start = index * head_cols + slot * rows
                head_buf[index, slot, :rows] = products[start : start + rows]
                if rows < head_buf.shape[2]:
                    head_buf[index, slot, rows:] = jnp.zeros(
                        (head_buf.shape[2] - rows, width), BF16
                    )
        head_copy = pltpu.make_async_copy(head_buf, head_grads, head_sem)
        head_copy.start()
        normed_low = low_buf[...].T
        for turn in turns:
            give(0, turn, dot(normed_low, hidden[part_of(turn)]))
            if turn == 0:
                head_copy.wait()
                for at in turns:
                    offer(2, at)
                for later in range(1, head_total):
                    for offset in peers:
                        grads_copy(later, offset).start()
        for turn in turns[-2:]:
            offer_given(0, turn)
        store_copy(1).wait()

    weight_own_copy = pltpu.make_async_copy(proj_weight, proj_all.at[me], weight_own)
    rows_low = pltpu.VMEM((2 * half, width), BF16)
    rows_full = pltpu.VMEM((2 * half, width), F32)
    pl.run_scoped(
        dense_phase,
        rows_low,
        rows_low,
        rows_low,
        pltpu.VMEM((mp_size, width, units), BF16),
        pltpu.VMEM((mp_size, units, width), BF16),
        pltpu.VMEM((width, width), BF16),
        pltpu.VMEM((mp_size, 2 * half, units), BF16),
        pltpu.VMEM((mp_size, 2 * half, units), BF16),
        rows_full,
        rows_full,
        rows_full,
        rows_low,
        rows_low,
        pltpu.VMEM((2, slots, units // slots, width), BF16),
        pltpu.VMEM(head_grads.shape, BF16),
    )

    def attention_phase(
        qkv,
        out_cols,
        log_total,
        seg_col,
        input_all,
        staged,
        qkv_grad,
        seg_blocks,
        grads,
        key_buf,
        key_cols,
        value_buf,
        query_sum,
        key_sum,
        value_sum,
        proj_rows,
    ):
        def traded_copy(head, offset):
            return send(
                staged.at[head, target(offset)],
                traded.at[head, me],
                (traded_send, traded_recv),
                (head, offset - 1),
                {"mp": target(offset)},
            )

        def traded_own_copy(head):
            return pltpu.make_async_copy(
                staged.at[head, me], traded.at[head, me], traded_own.at[head]
            )

        def prepare(head):
            cols = slice(head * HEAD_DIM, (head + 1) * HEAD_DIM)
            key_buf[:, :HEAD_DIM] = qkv[1, :, cols]
            key_buf[:, HEAD_DIM:] = ones_columns(ROW_LEN)
            value_buf[:, :HEAD_DIM] = qkv[2, :, cols]
            value_buf[:, HEAD_DIM:] = ones_columns(ROW_LEN)
            for step in range(BLOCKS):
                key_cols[step] = qkv[1, step * BLOCK : (step + 1) * BLOCK, cols].T
            key_sum[...] = jnp.zeros_like(key_sum)
            value_sum[...] = jnp.zeros_like(value_sum)

        def take_grads(head):
            grads_own_copy(head).wait()
            for offset in peers:
                grads_copy(head, offset).wait_recv()
            for chunk in range(mp_size):
                for side in range(2):
                    start = (2 * chunk + side) * half
                    grads[start : start + half] = grads_in[
                        head, chunk, :, side * HEAD_DIM : (side + 1) * HEAD_DIM
                    ]

        def attend_back(head):
            cols = slice(head * HEAD_DIM, (head + 1) * HEAD_DIM)

            def query_block(number, _):
                rows = block_rows(number)
                queries = qkv[0, rows, cols] * SCALE
                grad_rows = grads[rows]
                seg_query = seg_blocks[number]
                grad_cols = grad_rows.astype(F32).T
                row_dot = jnp.sum(grad_cols * out_cols[head, number], axis=0, keepdims=True)
                grad_cols = jnp.concatenate([grad_cols.astype(BF16), as_pieces(-row_dot)], axis=0)
                query_cols = jnp.concatenate(
                    [queries.astype(F32).T.astype(BF16), as_pieces(-log_total[head, number])], axis=0
                )

                def products_of(step):
                    key_rows = slice(step * BLOCK, (step + 1) * BLOCK)
                    same = (
                        jnp.concatenate([seg_col[key_rows]] * (BLOCK // 128), axis=1) == seg_query
                    )
                    scores = jnp.where(same, dot(key_buf[key_rows], query_cols), MASKED)
                    return scores, dot(value_buf[key_rows], grad_cols)

                query_grad = jnp.zeros((HEAD_DIM, BLOCK), F32)
                ahead = products_of(0)
                for step in range(BLOCKS):
                    scores, soft_grad = ahead
                    if step + 1 < BLOCKS:
                        ahead = products_of(step + 1)
                    key_rows = slice(step * BLOCK, (step + 1) * BLOCK)
                    soft = jnp.exp(scores)
                    score_grad = (soft * soft_grad).astype(BF16)
                    value_sum[key_rows] += dot(soft.astype(BF16), grad_rows)
                    key_sum[key_rows] += dot(score_grad, queries)
                    query_grad = query_grad + dot(key_cols[step], score_grad)
                query_sum[rows] = (query_grad * SCALE).T
                for at in range(head * BLOCKS, (head + 1) * BLOCKS):
                    if at in events:

                        @pl.when(number == at - head * BLOCKS)
                        def _():
                            for act in events[at]:
                                act()

                return 0

            lax.fori_loop(0, BLOCKS, query_block, 0)

        def give_grads(head):
            for part, total in enumerate((query_sum, key_sum, value_sum)):
                low = total[...].astype(BF16)
                qkv_grad[:, part * HEAD_DIM : (part + 1) * HEAD_DIM] = low
                if part != 1:
                    cols = slice(head * HEAD_DIM, (head + 1) * HEAD_DIM)
                    sum_low = jnp.sum(low.astype(F32), axis=0, keepdims=True)
                    biases[0][part : part + 1, cols] = sum_low
                for chunk in range(mp_size):
                    for side in range(2):
                        start = (2 * chunk + side) * half
                        staged[head, chunk, part, :, side * HEAD_DIM : (side + 1) * HEAD_DIM] = total[
                            start : start + half
                        ].astype(BF16)

        def start_trade(head):
            for offset in peers:
                traded_copy(head, offset).start()
            traded_own_copy(head).start()

        def start_proj(head):
            products = dot_cols(qkv_grad[...], input_all[...])
            slot_rows = proj[head].shape[1]
            for slot in range(2**bits):
                proj[head][slot] = products[slot * slot_rows : (slot + 1) * slot_rows].astype(BF16)
            proj_copy(head, 0).start()

        def finish_proj(head):
            cols = slice(head * HEAD_DIM, (head + 1) * HEAD_DIM)
            slot_rows = proj_slots[head].shape[1]
            for slot in range(2**bits):
                proj_rows[slot * slot_rows : (slot + 1) * slot_rows] = proj_slots[head][slot].astype(F32)
            for part in range(3):
                rows = proj_rows[part * HEAD_DIM : (part + 1) * HEAD_DIM]
                proj_sum[part, cols] = rows.astype(BF16)

        events = {}
        rest = []

        def due(at, act, *which):
            if at is None:
                rest.append((act, *which))
            else:
                events.setdefault(at, []).append(partial(act, *which))

        for at, level in zip((0, 1, 2), levels):
            due(at, add_vector, level)
        due(3, finish_vector)
        times = {
            1: ((0, 0, 0, 0), (2, 3, 3, 4), (3, 4, 4, 5)),
            2: ((1, 1, 1, 1), (3, 3, 3, 3), (4, 4, 4, 4)),
            0: ((2, 3, 3, 5), (3, 5, 6, 6), (4, 6, 7, 8)),
        }
        stages = {1: (5, 6, 7), 2: (5, 6, 7), 0: (7, 8, None)}
        ends = {1: (8, None, None, None), 2: (8, None, None, None), 0: (None,) * 4}
        for level in levels:
            for which in times:
                for turn, at in zip(turns, times[which][level]):
                    due(at, add_level, which, level, turn)
        for at, level in zip((3, 4, 5), levels):
            due(at, add_proj, 0, level)
        for at, level in zip((6, 7, 8), levels):
            due(at, add_proj, 1, level)
        for at, level in zip((6, 7, 8), levels[::-1]):
            due(at, spread_proj, 0, level)
        for which in (1, 2, 0):
            for stage, at in enumerate(stages[which]):
                due(at, pass_on, which, stage)
        for which in (1, 2, 0):
            due(ends[which][0], finish_sum, which)
        for step, level in enumerate(levels[::-1]):
            for which in (1, 2, 0):
                due(ends[which][1 + step], spread, which, level)

        copies = [
            pltpu.make_async_copy(source, into, attention_sems.at[at])
            for at, (source, into) in enumerate(
                (
                    (qkv_source, qkv),
                    (seg_source, seg_col),
                    (log_source, log_total),
                    (out_source, out_cols),
                    (input_source, input_all),
                )
            )
        ]
        for copy in copies:
            copy.start()
        biases[0][...] = jnp.zeros_like(biases[0])
        for step in range(BLOCKS):
            seg_blocks[step] = seg_row[:, step * BLOCK : (step + 1) * BLOCK]
        final = head_total - 1
        copies[0].wait()
        for head in range(head_total):
            prepare(head)
            take_grads(head)
            if head == 0:
                for copy in copies[1:4]:
                    copy.wait()
            attend_back(head)
            give_grads(head)
            start_trade(head)
            if head == 0:
                copies[4].wait()
            start_proj(head)
        bias_copy(0).start()
        for level in levels:
            add_proj(final, level)
            add_bias(level)
            spread_proj(final - 1, bits - 1 - level)
        for act, *which in rest:
            act(*which)
        for level in levels[::-1]:
            spread_proj(final, level)
        for head in range(head_total):
            finish_proj(head)
            traded_own_copy(head).wait()
            for offset in peers:
                traded_copy(head, offset).wait()

    pl.run_scoped(
        attention_phase,
        pltpu.VMEM(qkv_source.shape, BF16),
        pltpu.VMEM(out_source.shape, F32),
        pltpu.VMEM(log_source.shape, F32),
        pltpu.VMEM(seg_source.shape, jnp.int32),
        pltpu.VMEM(input_source.shape, BF16),
        pltpu.VMEM((head_total, mp_size, 3, half, 2 * HEAD_DIM), BF16),
        pltpu.VMEM((ROW_LEN, 3 * HEAD_DIM), BF16),
        pltpu.VMEM((BLOCKS, 1, BLOCK), jnp.int32),
        pltpu.VMEM((ROW_LEN, HEAD_DIM), BF16),
        pltpu.VMEM((ROW_LEN, HEAD_DIM + EXTRA), BF16),
        pltpu.VMEM((BLOCKS, HEAD_DIM, BLOCK), BF16),
        pltpu.VMEM((ROW_LEN, HEAD_DIM + EXTRA), BF16),
        pltpu.VMEM((ROW_LEN, HEAD_DIM), F32),
        pltpu.VMEM((ROW_LEN, HEAD_DIM), F32),
        pltpu.VMEM((ROW_LEN, HEAD_DIM), F32),
        pltpu.VMEM((3 * HEAD_DIM, width), F32),
    )

    for hop in line.hops:
        if (take_weight, hop) not in done:
            both_sides(take_weight, hop)
    for level in levels:
        for hop in line.hops:
            if (trade_weight, level, hop) not in done:
                both_sides(trade_weight, level, hop)

    def sent_trades(side, hop):
        for level in levels:
            weight_trade_copy(level, side, hop).wait_send()

    for side, hop in line.ways:
        line.if_sent(side, hop)(lambda side=side, hop=hop: weight_copy(side, hop).wait_send())
        line.if_taken(side, hop)(partial(sent_trades, side, hop))
    weight_own_copy.wait()
    for head in range(head_total):
        for offset in peers:
            grads_copy(head, offset).wait_send()
        for level in levels:
            proj_copy(head, level).wait_send()
            proj_spread_copy(head, level).wait_send()
    for level in levels:
        vector_copy(level).wait_send()
        bias_copy(level).wait_send()
        for which in arrays:
            spread_copy(which, level).wait_send()
            for turn in turns:
                level_copy(which, level, turn).wait_send()
    for offset in peers:
        vector_last_copy(offset).wait_send()

    def sent_last(side, part):
        for which in arrays:
            last_copy(which, side, part).wait_send()

    for part in turns:
        pl.when(me < part)(partial(sent_last, 0, part))
        pl.when(me > part)(partial(sent_last, 1, part))


def rear(frames, heads_low, out_grad, seg_row, in_bias, small, weights, proj_weight, saved, bits):
    local_rows, width = frames.shape
    qkv_low, out_cols = saved[:2]
    mp_size, units = weights[1].shape[:2]
    head_total = out_cols.shape[0]
    half, lanes = local_rows // 2, 2 * HEAD_DIM
    peers = mp_size - 1
    slots = 2**bits
    head_rows = -(-width // mp_size // slots // 16) * 16
    anywhere = pl.BlockSpec(memory_space=pl.ANY)
    blocks = [(width // slots, units), (units // slots, width), (head_rows, width)]
    proj_block = (3 * HEAD_DIM // slots, width)
    bias_block = (8, 2 * 128)
    vector_block = (8 + -(-mp_size // 8) * 8, width)

    def halves(shape, lead=()):
        return [pltpu.VMEM(lead + (slots >> (level + 1),) + shape, BF16) for level in range(bits)]

    def sems(*shapes):
        return [pltpu.SemaphoreType.DMA(shape) for shape in shapes for _ in range(2)]

    piece = pltpu.VMEM((mp_size, head_total, half, lanes), BF16)
    return pl.pallas_call(
        partial(rear_kernel, bits),
        out_shape=(
            jax.ShapeDtypeStruct((local_rows, width), F32),
            jax.ShapeDtypeStruct((local_rows, width), F32),
            *(jax.ShapeDtypeStruct((mp_size, slots) + block, BF16) for block in blocks),
            jax.ShapeDtypeStruct((mp_size,) + proj_weight.shape, BF16),
            jax.ShapeDtypeStruct((head_total, mp_size, 3, half, lanes), BF16),
            *(jax.ShapeDtypeStruct((slots,) + block, BF16) for block in blocks),
            jax.ShapeDtypeStruct((3, head_total * HEAD_DIM, width), BF16),
            jax.ShapeDtypeStruct(vector_block, F32),
            jax.ShapeDtypeStruct(bias_block, F32),
        ),
        in_specs=[whole()] * 6 + [anywhere] * 12,
        out_specs=(anywhere,) * 7 + (whole(),) * 6,
        scratch_shapes=[
            piece,
            pltpu.VMEM((head_total, mp_size, half, lanes), BF16),
            [pltpu.VMEM((2, slots // 2) + block, BF16) for block in blocks],
            [halves(block, (mp_size,)) for block in blocks],
            [pltpu.VMEM((2, mp_size) + block, BF16) for block in blocks],
            [pltpu.VMEM((slots,) + proj_block, BF16) for _ in range(head_total)],
            [halves(proj_block) for _ in range(head_total)],
            [pltpu.VMEM((slots,) + proj_block, BF16) for _ in range(head_total)],
            [pltpu.VMEM(vector_block, F32) for _ in range(bits + 1)],
            [pltpu.VMEM(vector_block, F32) for _ in range(bits)],
            pltpu.VMEM((mp_size,) + vector_block, F32),
            [pltpu.VMEM(bias_block, F32) for _ in range(bits + 1)],
            [pltpu.VMEM(bias_block, F32) for _ in range(bits)],
            pltpu.SemaphoreType.DMA((3,)),
            pltpu.SemaphoreType.DMA((mp_size,)),
            pltpu.SemaphoreType.DMA((mp_size,)),
            pltpu.SemaphoreType.DMA((mp_size,)),
            pltpu.SemaphoreType.DMA((2,)),
            pltpu.SemaphoreType.DMA,
            pltpu.SemaphoreType.DMA((2,)),
            pltpu.SemaphoreType.DMA((5,)),
            pltpu.SemaphoreType.DMA,
            *sems((2, peers), (max(bits, 1), 2, peers)),
            pltpu.SemaphoreType.DMA((3, 2)),
            pltpu.SemaphoreType.DMA((head_total,)),
            *sems((head_total, peers)),
            pltpu.SemaphoreType.DMA((head_total,)),
            *sems(
                (head_total, peers),
                (3, bits, mp_size),
                (3, 2, mp_size),
                (3, bits),
                (2, head_total, bits),
                (bits,),
                (peers,),
                (bits,),
            ),
        ],
        compiler_params=pltpu.CompilerParams(
            collective_id=1, has_side_effects=True, vmem_limit_bytes=REAR_VMEM_BYTES
        ),
        cost_estimate=pl.CostEstimate(
            flops=40 * head_total * ROW_LEN * ROW_LEN * HEAD_DIM,
            bytes_accessed=96 * 1024 * 1024,
            transcendentals=head_total * ROW_LEN * ROW_LEN,
        ),
        name="rear",
    )(seg_row, in_bias, *small, frames, heads_low, out_grad, *weights, proj_weight, *saved)


def finish_kernel(
    traded,
    proj_all,
    resid_grad,
    in_sum,
    down_sum,
    head_sum,
    proj_sum,
    vector_sum,
    bias_sum,
    stream_grad,
    in_grad,
    down_grad,
    out_grad,
    proj_grad,
    query_bias_grad,
    value_bias_grad,
    out_bias_grad,
    in_bias_grad,
    down_bias_grad,
    gain_grad,
    shift_grad,
    columns,
    weight_buf,
    sems,
):
    head_total, mp_size = traded.shape[:2]
    half = traded.shape[3]
    head_cols = head_total * HEAD_DIM
    copies = [
        pltpu.make_async_copy(
            proj_all.at[index],
            weight_buf.at[index],
            sems.at[index],
        )
        for index in range(mp_size)
    ]
    for copy in copies:
        copy.start()
    for sums, grad in ((in_sum, in_grad), (down_sum, down_grad), (head_sum, out_grad)):
        rows = grad.shape[0] // sums.shape[0]
        for slot in range(sums.shape[0]):
            grad[slot * rows : (slot + 1) * rows] = sums[slot, :rows].astype(F32)
    proj_grad[...] = proj_sum[...].astype(F32)
    query_bias_grad[...] = bias_sum[0:1, :head_cols]
    value_bias_grad[...] = bias_sum[2:3, :head_cols]
    gain_grad[...] = vector_sum[0:2]
    shift_grad[...] = vector_sum[2:4]
    out_bias_grad[...] = vector_sum[4:5]
    down_bias_grad[...] = vector_sum[5:6]
    in_bias_grad[...] = vector_sum[pl.ds(8 + lax.axis_index("mp"), 1)]
    stream_grad[...] = resid_grad[...]
    for index in range(mp_size):
        for head in range(head_total):
            for part in range(3):
                at = part * head_cols + head * HEAD_DIM
                for side in range(2):
                    columns[side * half : (side + 1) * half, at : at + HEAD_DIM] = traded[
                        head, index, part, :, side * HEAD_DIM : (side + 1) * HEAD_DIM
                    ]
        copies[index].wait()
        stream_grad[...] += dot(columns[...], weight_buf[index])


def finish(traded, proj_all, resid_grad, sums):
    head_total, mp_size = traded.shape[:2]
    head_cols = head_total * HEAD_DIM
    local_rows, width = resid_grad.shape
    units = sums[0].shape[0] * sums[0].shape[1]
    row = jax.ShapeDtypeStruct((1, width), F32)
    head_row = jax.ShapeDtypeStruct((1, head_cols), F32)
    anywhere = pl.BlockSpec(memory_space=pl.ANY)
    return pl.pallas_call(
        finish_kernel,
        out_shape=(
            jax.ShapeDtypeStruct((local_rows, width), F32),
            jax.ShapeDtypeStruct((units, width), F32),
            jax.ShapeDtypeStruct((units, width), F32),
            jax.ShapeDtypeStruct((head_cols, width), F32),
            jax.ShapeDtypeStruct((3, head_cols, width), F32),
            head_row,
            head_row,
            row,
            jax.ShapeDtypeStruct((1, units), F32),
            row,
            jax.ShapeDtypeStruct((2, width), F32),
            jax.ShapeDtypeStruct((2, width), F32),
        ),
        in_specs=[whole(), anywhere] + [whole()] * 7,
        out_specs=(whole(),) * 12,
        scratch_shapes=[
            pltpu.VMEM((local_rows, 3 * head_cols), BF16),
            pltpu.VMEM((mp_size, 3 * head_cols, width), BF16),
            pltpu.SemaphoreType.DMA((mp_size,)),
        ],
        compiler_params=pltpu.CompilerParams(vmem_limit_bytes=VMEM_BYTES),
        cost_estimate=pl.CostEstimate(
            flops=6 * local_rows * width * width, bytes_accessed=24 * 1024 * 1024, transcendentals=0
        ),
        name="finish",
    )(traded, proj_all, resid_grad, *sums)


def dp_groups():
    total = lax.axis_size("dp")
    size = min(8, total)
    groups = [list(range(start, start + size)) for start in range(0, total, size)]
    return (size, groups)


def on_device(
    frames,
    segment_ids,
    qkv_weight,
    q_bias,
    v_bias,
    out_weight,
    out_bias,
    ff_in_weight,
    ff_in_bias,
    ff_out_weight,
    ff_out_bias,
    norm_gain,
    norm_shift,
    out_grad,
):
    local_rows, width = frames.shape
    mp_size = lax.axis_size("mp")
    group, groups = dp_groups()
    bits = group_bits(lax.axis_size("dp"))
    slots = 2**bits

    proj_weight = qkv_weight[0].transpose(0, 2, 1)
    seg_row = segment_ids.reshape(1, ROW_LEN)
    (
        input_all,
        qkv_low,
        in_all,
        down_all,
        out_all,
        in_bias_all,
        seg_col,
        out_cols,
        log_total,
        heads_low,
    ) = front(
        frames,
        proj_weight,
        q_bias,
        v_bias,
        seg_row,
        (ff_in_weight[0], ff_out_weight[0], out_weight[0]),
        ff_in_bias,
        mp_size,
        bits,
    )
    block_out, resid_grad, _, _, _, proj_all, traded, *summed = rear(
        frames,
        heads_low,
        out_grad,
        seg_row,
        in_bias_all,
        (out_bias, ff_out_bias, norm_gain[0], norm_shift[0]),
        (in_all, down_all, out_all),
        proj_weight.reshape(slots, -1, width),
        (qkv_low, out_cols, log_total, seg_col, input_all),
        bits,
    )
    if len(groups) > 1:
        across = [list(range(at, lax.axis_size("dp"), group)) for at in range(group)]
        summed = lax.psum(summed, "dp", axis_index_groups=across)
    (
        stream_grad,
        in_weight_grad,
        down_weight_grad,
        out_weight_grad,
        proj_grad,
        query_bias_grad,
        value_bias_grad,
        head_bias_grad,
        in_bias_grad,
        down_bias_grad,
        gain_grad,
        shift_grad,
    ) = finish(traded, proj_all.reshape(mp_size, -1, width), resid_grad, summed)
    return (
        block_out,
        stream_grad,
        proj_grad.transpose(0, 2, 1)[None],
        query_bias_grad,
        value_bias_grad,
        out_weight_grad[None],
        head_bias_grad,
        in_weight_grad[None],
        in_bias_grad,
        down_weight_grad[None],
        down_bias_grad,
        gain_grad[None],
        shift_grad[None],
    )


def solution(mesh):
    return jax.shard_map(
        on_device,
        mesh=mesh,
        in_specs=(
            P(("dp", "mp"), None),
            P("dp"),
            P(None, None, None, "mp"),
            P(None, "mp"),
            P(None, "mp"),
            P(None, "mp", None),
            P(),
            P(None, None, "mp"),
            P(None, "mp"),
            P(None, "mp", None),
            P(),
            P(),
            P(),
            P(("dp", "mp"), None),
        ),
        out_specs=(
            P(("dp", "mp"), None),
            P(("dp", "mp"), None),
            P(None, None, None, "mp"),
            P(None, "mp"),
            P(None, "mp"),
            P(None, "mp", None),
            P(),
            P(None, None, "mp"),
            P(None, "mp"),
            P(None, "mp", None),
            P(),
            P(),
            P(),
        ),
        check_vma=False,
    )
```

```python
import itertools
from functools import partial

import jax
import jax.numpy as jnp
from jax import lax
from jax.experimental import pallas as pl
from jax.experimental.pallas import tpu as pltpu
from jax.sharding import PartitionSpec as P

HEAD_DIM = 64
ROW_LEN = 2304
BLOCK = 768
BLOCKS = ROW_LEN // BLOCK
EXTRA = 16
SCALE = HEAD_DIM ** (-0.5)
MASKED = -1e30
F32 = jnp.float32
BF16 = jnp.bfloat16
VMEM_BYTES = 56 * 1024 * 1024
REAR_VMEM_BYTES = 63 * 1024 * 1024


def dot_rows(left, right):
    return lax.dot_general(left, right, (((1,), (1,)), ((), ())), preferred_element_type=F32)


def dot_cols(left, right):
    return lax.dot_general(left, right, (((0,), (0,)), ((), ())), preferred_element_type=F32)


def dot(left, right):
    return jnp.dot(left, right, preferred_element_type=F32)


def block_rows(number):
    return pl.ds(pl.multiple_of(number * BLOCK, BLOCK), BLOCK)


def as_pieces(row):
    high = row.astype(BF16).astype(F32)
    middle = (row - high).astype(BF16).astype(F32)
    last = row - high - middle
    place = lax.broadcasted_iota(jnp.int32, (EXTRA, row.shape[1]), 0)
    pieces = jnp.where(place == 0, high, jnp.where(place == 1, middle, jnp.where(place == 2, last, 0.0)))
    return pieces.astype(BF16)


def ones_columns(rows):
    place = lax.broadcasted_iota(jnp.int32, (rows, EXTRA), 1)
    return jnp.where(place < 3, 1.0, 0.0).astype(BF16)


def whole(memory_space=pltpu.VMEM):
    return pl.BlockSpec(memory_space=memory_space)


MESH = pl.DeviceIdType.MESH


def group_bits(dp_size):
    return min(3, dp_size.bit_length() - 1)


def place_in(dp_index, order):
    slot = 0
    for at, bit in enumerate(order):
        slot = slot + (dp_index // 2**bit) % 2 * 2**at
    return slot


def partner_of(dp_index, bit):
    return dp_index + (1 - 2 * ((dp_index // 2**bit) % 2)) * 2**bit


def enter(dp_index, mp_index, mp_size, bits):
    barrier = pltpu.get_barrier_semaphore()
    for offset in range(1, mp_size):
        pl.semaphore_signal(
            barrier, device_id={"mp": lax.rem(mp_index + offset, mp_size)}, device_id_type=MESH
        )
    for bit in range(bits):
        pl.semaphore_signal(
            barrier, device_id={"dp": partner_of(dp_index, bit)}, device_id_type=MESH
        )
    pl.semaphore_wait(barrier, mp_size - 1 + bits)


def send(src, dst, sems, at, device_id):
    return pltpu.make_async_remote_copy(
        src_ref=src,
        dst_ref=dst,
        send_sem=sems[0].at[at],
        recv_sem=sems[1].at[at],
        device_id=device_id,
        device_id_type=MESH,
    )


def gather_orders(bits):
    if bits == 3:
        return ((1, 2, 0), (2, 1, 0), (1, 2), (1, 2, 0))
    return (tuple(range(bits)),) * 4


SIDES = (1, -1)


def inside(index, size):
    return jnp.logical_and(index >= 0, index < size)


class Line:
    def __init__(self, mp_size, me):
        self.size = mp_size
        self.me = me
        self.hops = range(mp_size - 1)
        self.ways = [(side, hop) for hop in self.hops for side in (0, 1)]

    def wrapped(self, index):
        return lax.rem(index + self.size, self.size)

    def chunk(self, side, hop):
        return self.me - SIDES[side] * hop

    def place(self, side, hop):
        return self.wrapped(self.chunk(side, hop))

    def sends(self, side, hop):
        there = inside(self.me + SIDES[side], self.size)
        return jnp.logical_and(there, inside(self.chunk(side, hop), self.size))

    def if_sent(self, side, hop):
        return pl.when(self.sends(side, hop))

    def if_taken(self, side, hop):
        return pl.when(inside(self.chunk(side, hop + 1), self.size))

    def neighbour(self, side):
        return {"mp": self.wrapped(self.me + SIDES[side])}


def front_kernel(
    bits,
    frames,
    qkv_weight,
    q_bias,
    v_bias,
    seg_row,
    in_weight,
    down_weight,
    out_weight,
    in_bias,
    input_all,
    qkv_low,
    in_all,
    down_all,
    out_all,
    bias_all,
    seg_col,
    out_cols,
    log_total,
    heads_low,
    bias_buf,
    key_cols,
    value_buf,
    out_buf,
    staged,
    heads_in,
    own_sems,
    frame_send,
    frame_recv,
    bias_send,
    bias_recv,
    first_send,
    first_recv,
    later_send,
    later_recv,
    heads_own,
    heads_send,
    heads_recv,
):
    mp_size = in_all.shape[0]
    me = lax.axis_index("mp")
    dp_index = lax.axis_index("dp")
    local_rows = frames.shape[0]
    half = local_rows // 2
    head_total = out_cols.shape[0]
    orders = gather_orders(bits)[:3]
    parts = ((in_weight, in_all), (down_weight, down_all), (out_weight, out_all))
    line = Line(mp_size, me)
    hops, ways, wrapped = line.hops, line.ways, line.wrapped
    enter(dp_index, me, mp_size, bits)

    def slots(which, level):
        count = parts[which][0].shape[0] // 2 ** len(orders[which])
        start = place_in(dp_index, orders[which]) // 2**level * 2**level
        return pl.ds(pl.multiple_of(start * count, 16), count * 2**level)

    def first_copy(which, side, hop):
        rows = slots(which, 0)
        place = parts[which][1].at[line.place(side, hop), rows]
        source = parts[which][0].at[rows] if hop == 0 else place
        sems = (first_send, first_recv)
        return send(source, place, sems, (which, side, hop), line.neighbour(side))

    def later_copy(which, level, side, hop):
        held = parts[which][1].at[line.place(side, hop + 1), slots(which, level)]
        partner = {"dp": partner_of(dp_index, orders[which][level])}
        return send(held, held, (later_send, later_recv), (which, level, side, hop), partner)

    def frame_rows(index):
        return pl.ds(pl.multiple_of(wrapped(index) * local_rows, local_rows), local_rows)

    def frame_copy(side, hop):
        place = input_all.at[frame_rows(line.chunk(side, hop))]
        source = frames if hop == 0 else place
        return send(source, place, (frame_send, frame_recv), (side, hop), line.neighbour(side))

    def bias_copy(side, hop):
        place = bias_all.at[line.place(side, hop)]
        source = bias_buf if hop == 0 else place
        return send(source, place, (bias_send, bias_recv), (side, hop), line.neighbour(side))

    def project(index):
        rows = frame_rows(index)
        inputs = input_all[rows]
        for part, bias in enumerate((q_bias, None, v_bias)):
            products = dot_rows(inputs, qkv_weight[part])
            if bias is not None:
                products = products + bias[...].astype(F32)
            qkv_low[part, rows] = products.astype(BF16)

    def start_slices(side, hop):
        for which in range(3):
            first_copy(which, side, hop).start()
        bias_copy(side, hop).start()

    def take_slices(side, hop):
        for which in range(3):
            first_copy(which, side, hop).wait_recv()
        bias_copy(side, hop).wait_recv()
        if 0 < hop < mp_size - 2:
            line.if_sent(side, hop + 1)(partial(start_slices, side, hop + 1))
        for which in range(3):
            if orders[which]:
                later_copy(which, 0, side, hop).start()

    def trade_slices(level, side, hop):
        for which in range(3):
            if level < len(orders[which]):
                later_copy(which, level, side, hop).wait_recv()
            if level + 1 < len(orders[which]):
                later_copy(which, level + 1, side, hop).start()

    def take_hop(hop):
        for side in (0, 1):
            line.if_taken(side, hop)(partial(take_slices, side, hop))

    def trade_hop(level, hop):
        for side in (0, 1):
            line.if_taken(side, hop)(partial(trade_slices, level, side, hop))


    bias_buf[...] = jnp.broadcast_to(in_bias[...], bias_buf.shape)
    for side in (0, 1):
        line.if_sent(side, 0)(partial(start_slices, side, 0))
    for side in (0, 1):
        line.if_sent(side, 0)(lambda side=side: frame_copy(side, 0).start())
    own = [
        pltpu.make_async_copy(shard, gathered.at[me], own_sems.at[at])
        for at, (shard, gathered) in enumerate(parts + ((bias_buf, bias_all),))
    ]
    for copy in own:
        copy.start()
    input_all[frame_rows(me)] = frames[...]
    project(me)
    for step in range(BLOCKS):
        ids = jnp.broadcast_to(seg_row[:, step * BLOCK : (step + 1) * BLOCK].astype(F32), (128, BLOCK))
        seg_col[step * BLOCK : (step + 1) * BLOCK] = ids.T.astype(jnp.int32)

    def take_frames(side, hop):
        frame_copy(side, hop).wait_recv()
        if hop + 1 < mp_size - 1:
            line.if_sent(side, hop + 1)(lambda: frame_copy(side, hop + 1).start())

    def project_taken(side, hop):
        project(line.chunk(side, hop + 1))

    for hop in hops:
        for side in (0, 1):
            line.if_taken(side, hop)(partial(take_frames, side, hop))
        if hop == 0:
            take_hop(0)
        elif hop - 1 < bits:
            trade_hop(hop - 1, 0)
        for side in (0, 1):
            free = line.sends(side, hop)
            if hop + 1 < mp_size - 1:
                free = jnp.logical_and(free, jnp.logical_not(line.sends(side, hop + 1)))
            if mp_size > 2:
                passes = jnp.logical_and(free, line.sends(side, 1))
                pl.when(passes)(partial(start_slices, side, 1))
        for side in (0, 1):
            line.if_taken(side, hop)(partial(project_taken, side, hop))

    schedule = (
        (1, take_hop, 1),
        (3, trade_hop, 0, 1),
        (4, take_hop, 2),
        (6, trade_hop, 1, 1),
        (6, trade_hop, 0, 2),
    )
    events = {}
    done = {(take_hop, 0)} | {(trade_hop, hop - 1, 0) for hop in hops if 0 < hop <= bits}
    for at, act, *which in schedule:
        if which[-1] in hops and (act is take_hop or which[0] < bits):
            events.setdefault((at // BLOCKS, at % BLOCKS), []).append(partial(act, *which))
            done.add((act, *which))

    def attend(head):
        cols = slice(head * HEAD_DIM, (head + 1) * HEAD_DIM)
        lane = lax.broadcasted_iota(jnp.int32, (BLOCK, EXTRA), 1)
        for step in range(BLOCKS):
            rows = slice(step * BLOCK, (step + 1) * BLOCK)
            key_cols[step] = qkv_low[1, rows, cols].T
            value_buf[step, :, :HEAD_DIM] = qkv_low[2, rows, cols]
            value_buf[step, :, HEAD_DIM:] = jnp.where(lane == 0, 1.0, 0.0).astype(BF16)

        def query_block(number, _):
            rows = block_rows(number)
            queries = qkv_low[0, rows, cols] * SCALE

            def scores_of(step):
                ids = seg_row[:, step * BLOCK : (step + 1) * BLOCK]
                same = jnp.concatenate([seg_col[rows]] * (BLOCK // 128), axis=1) == ids
                return jnp.where(same, dot(queries, key_cols[step]), MASKED)

            peak = jnp.full((BLOCK, 1), MASKED, F32)
            mixed = jnp.zeros((BLOCK, HEAD_DIM + EXTRA), F32)
            scores = scores_of(0)
            for step in range(BLOCKS):
                ahead = scores_of(step + 1) if step + 1 < BLOCKS else None
                higher = jnp.maximum(peak, jnp.max(scores, axis=1, keepdims=True))
                soft = jnp.exp(scores - higher).astype(BF16)
                mixed = mixed * jnp.exp(peak - higher) + dot(soft, value_buf[step])
                peak, scores = higher, ahead
            total = mixed[:, HEAD_DIM : HEAD_DIM + 1]
            mixed = mixed[:, :HEAD_DIM] / total
            logs = jnp.broadcast_to(peak + jnp.log(total), (BLOCK, HEAD_DIM))
            both = jnp.concatenate([mixed, logs], axis=1).T
            out_cols[head, number] = both[:HEAD_DIM]
            log_total[head, number] = both[HEAD_DIM : HEAD_DIM + 1]
            out_buf[rows] = mixed.astype(BF16)
            for at in range(BLOCKS):
                if (head, at) in events:

                    @pl.when(number == at)
                    def _():
                        for act in events[(head, at)]:
                            act()

            return 0

        lax.fori_loop(0, BLOCKS, query_block, 0)

    def heads_copy(head, offset):
        return send(
            staged.at[head, wrapped(me + offset)],
            heads_in.at[head, me],
            (heads_send, heads_recv),
            (head, offset - 1),
            {"mp": wrapped(me + offset)},
        )

    def heads_own_copy(head):
        return pltpu.make_async_copy(
            staged.at[head, me], heads_in.at[head, me], heads_own.at[head]
        )

    peers = range(1, mp_size)
    for head in range(head_total):
        attend(head)
        for chunk in range(mp_size):
            for side in range(2):
                start = (2 * chunk + side) * half
                staged[head, chunk, :, side * HEAD_DIM : (side + 1) * HEAD_DIM] = out_buf[
                    start : start + half
                ]
        for offset in peers:
            heads_copy(head, offset).start()
        heads_own_copy(head).start()

    for hop in hops:
        if (take_hop, hop) not in done:
            take_hop(hop)
    for level in range(bits):
        for hop in hops:
            if (trade_hop, level, hop) not in done:
                trade_hop(level, hop)
    for head in range(head_total):
        heads_own_copy(head).wait()
        for offset in peers:
            heads_copy(head, offset).wait_recv()
        for chunk in range(mp_size):
            for side in range(2):
                at = (chunk * head_total + head) * HEAD_DIM
                heads_low[side * half : (side + 1) * half, at : at + HEAD_DIM] = heads_in[
                    head, chunk, :, side * HEAD_DIM : (side + 1) * HEAD_DIM
                ]
        for offset in peers:
            heads_copy(head, offset).wait_send()

    def sent_all(side, hop):
        frame_copy(side, hop).wait_send()
        bias_copy(side, hop).wait_send()
        for which in range(3):
            first_copy(which, side, hop).wait_send()

    def sent_later(side, hop):
        for which in range(3):
            for level in range(len(orders[which])):
                later_copy(which, level, side, hop).wait_send()

    for side, hop in ways:
        line.if_sent(side, hop)(partial(sent_all, side, hop))
        line.if_taken(side, hop)(partial(sent_later, side, hop))
    for copy in own:
        copy.wait()


def front(frames, qkv_weight, q_bias, v_bias, seg_row, weights, in_bias, mp_size, bits):
    local_rows, width = frames.shape
    head_cols = qkv_weight.shape[1]
    head_total = head_cols // HEAD_DIM
    peers = mp_size - 1
    levels = max(bits, 1)
    anywhere = pl.BlockSpec(memory_space=pl.ANY)
    in_weight, down_weight, out_weight = weights

    def sems(*shapes):
        return [pltpu.SemaphoreType.DMA(shape) for shape in shapes for _ in range(2)]

    piece = (head_total, mp_size, local_rows // 2, 2 * HEAD_DIM)
    return pl.pallas_call(
        partial(front_kernel, bits),
        out_shape=(
            jax.ShapeDtypeStruct((ROW_LEN, width), BF16),
            jax.ShapeDtypeStruct((3, ROW_LEN, head_cols), BF16),
            jax.ShapeDtypeStruct((mp_size,) + in_weight.shape, BF16),
            jax.ShapeDtypeStruct((mp_size,) + down_weight.shape, BF16),
            jax.ShapeDtypeStruct((mp_size,) + out_weight.shape, BF16),
            jax.ShapeDtypeStruct((mp_size, 16, in_bias.shape[1]), BF16),
            jax.ShapeDtypeStruct((ROW_LEN, 128), jnp.int32),
            jax.ShapeDtypeStruct((head_total, BLOCKS, HEAD_DIM, BLOCK), F32),
            jax.ShapeDtypeStruct((head_total, BLOCKS, 1, BLOCK), F32),
            jax.ShapeDtypeStruct((local_rows, width), BF16),
        ),
        in_specs=[whole()] * 5 + [anywhere] * 3 + [whole()],
        out_specs=(whole(), whole()) + (anywhere,) * 4 + (whole(),) * 4,
        scratch_shapes=[
            pltpu.VMEM((16, in_bias.shape[1]), BF16),
            pltpu.VMEM((BLOCKS, HEAD_DIM, BLOCK), BF16),
            pltpu.VMEM((BLOCKS, BLOCK, HEAD_DIM + EXTRA), BF16),
            pltpu.VMEM((ROW_LEN, HEAD_DIM), BF16),
            pltpu.VMEM(piece, BF16),
            pltpu.VMEM(piece, BF16),
            pltpu.SemaphoreType.DMA((4,)),
            *sems((2, peers), (2, peers), (3, 2, peers), (3, levels, 2, peers)),
            pltpu.SemaphoreType.DMA((head_total,)),
            *sems((head_total, peers)),
        ],
        compiler_params=pltpu.CompilerParams(
            collective_id=0, has_side_effects=True, vmem_limit_bytes=VMEM_BYTES
        ),
        cost_estimate=pl.CostEstimate(
            flops=16 * head_total * ROW_LEN * ROW_LEN * HEAD_DIM,
            bytes_accessed=32 * 1024 * 1024,
            transcendentals=head_total * ROW_LEN * ROW_LEN,
        ),
        name="front",
    )(frames, qkv_weight, q_bias, v_bias, seg_row, in_weight, down_weight, out_weight, in_bias)


def reduce_orders(bits):
    if bits == 3:
        return ((0, 1, 2), (0, 2, 1), (1, 2, 0))
    return (tuple(range(bits)),) * 3


def norm_rows(inputs, norm_gain, norm_shift):
    row_mean = jnp.mean(inputs, axis=-1, keepdims=True)
    centred = inputs - row_mean
    variance = jnp.mean(centred * centred, axis=-1, keepdims=True)
    inv_std = lax.rsqrt(variance + 1e-05)
    normed = centred * inv_std
    return (normed * norm_gain + norm_shift, normed, inv_std)


def norm_back(cotangent, normed, inv_std, norm_gain):
    scaled = cotangent * norm_gain
    adjusted = (
        scaled
        - jnp.mean(scaled, axis=-1, keepdims=True)
        - normed * jnp.mean(scaled * normed, axis=-1, keepdims=True)
    )
    return adjusted * inv_std


def sum_rows(array):
    return jnp.sum(array.astype(F32), axis=0, keepdims=True)


def rear_kernel(
    bits,
    seg_row,
    in_bias,
    out_bias,
    down_bias,
    norm_gain,
    norm_shift,
    frames,
    heads_low,
    out_grad,
    in_all,
    down_all,
    out_all,
    proj_weight,
    qkv_source,
    out_source,
    log_source,
    seg_source,
    input_source,
    block_out,
    resid_grad,
    in_grads,
    down_grads,
    head_grads,
    proj_all,
    traded,
    in_sum,
    down_sum,
    head_sum,
    proj_sum,
    vector_sum,
    bias_sum,
    grads_out,
    grads_in,
    kept,
    taken,
    last,
    proj,
    proj_taken,
    proj_slots,
    vectors,
    vectors_taken,
    vectors_all,
    biases,
    biases_taken,
    load_sems,
    in_sems,
    down_sems,
    out_sems,
    given_sems,
    head_sem,
    store_sems,
    attention_sems,
    weight_own,
    weight_send,
    weight_recv,
    weight_trade_send,
    weight_trade_recv,
    keep_sems,
    grads_own,
    grads_send,
    grads_recv,
    traded_own,
    traded_send,
    traded_recv,
    level_send,
    level_recv,
    last_send,
    last_recv,
    back_send,
    back_recv,
    proj_send,
    proj_recv,
    vector_send,
    vector_recv,
    vector_last_send,
    vector_last_recv,
    bias_send,
    bias_recv,
):
    mp_size, units, width = down_all.shape
    head_total = grads_out.shape[1]
    half = grads_out.shape[2]
    head_cols = width // mp_size
    slots = 2**bits
    me = lax.axis_index("mp")
    dp_index = lax.axis_index("dp")
    peers = range(1, mp_size)
    turns = range(mp_size)
    levels = list(range(bits))
    orders = reduce_orders(bits)
    partials = (in_grads, down_grads, head_grads)
    sums = (in_sum, down_sum, head_sum)
    arrays = range(3)
    vector = vectors[0]

    def target(offset):
        return lax.rem(me + offset, mp_size)

    def bit_of(which, level):
        return (dp_index // 2 ** orders[which][level]) % 2


    def part_of(turn):
        return target(turn + 1)

    def level_copy(which, level, turn):
        count = 2 ** (bits - 1 - level)
        other = (1 - bit_of(which, level)) * count
        part = pl.ds(part_of(turn), 1)
        source = partials[which] if level == 0 else taken[which][level - 1]
        return send(
            source.at[part, pl.ds(other, count)],
            taken[which][level].at[part],
            (level_send, level_recv),
            (which, level, turn),
            {"dp": partner_of(dp_index, orders[which][level])},
        )

    def keep_copy(which, turn):
        count = 2 ** (bits - 1)
        return pltpu.make_async_copy(
            partials[which].at[part_of(turn), pl.ds(bit_of(which, 0) * count, count)],
            kept[which].at[turn % 2],
            keep_sems.at[which, turn % 2],
        )

    def last_copy(which, offset):
        return send(
            taken[which][bits - 1].at[target(offset)],
            last[which].at[offset - 1],
            (last_send, last_recv),
            (which, offset - 1),
            {"mp": target(offset)},
        )

    def add_level(which, level, turn):
        level_copy(which, level, turn).wait_recv()
        count = 2 ** (bits - 1 - level)
        if level == 0:
            keep_copy(which, turn).wait()
        start = bit_of(which, level) * count
        into = taken[which][level]
        part = part_of(turn)
        for slot in range(count):
            if level == 0:
                mine = kept[which][turn % 2, slot]
            else:
                mine = taken[which][level - 1][part, start + slot]
            into[part, slot] = (into[part, slot].astype(F32) + mine.astype(F32)).astype(BF16)
        if level == 0 and turn + 2 < mp_size:
            keep_copy(which, turn + 2).start()
        if level + 1 < bits:
            level_copy(which, level + 1, turn).start()
        elif turn + 1 < mp_size:
            last_copy(which, turn + 1).start()

    def offer(which, turn):
        level_copy(which, 0, turn).start()
        if turn < 2:
            keep_copy(which, turn).start()

    def slot_of(order):
        return place_in(dp_index, order[::-1])

    def held_slots(order, level):
        count = 2 ** (bits - 1 - level)
        return pl.ds(slot_of(order) // count * count, count)

    def spread_copy(which, level):
        held = sums[which].at[held_slots(orders[which], level)]
        partner = {"dp": partner_of(dp_index, orders[which][level])}
        return send(held, held, (back_send, back_recv), (which, level), partner)

    def finish_sum(which):
        total = taken[which][bits - 1][me, 0].astype(F32)
        for offset in peers:
            last_copy(which, offset).wait_recv()
            total = total + last[which][offset - 1, 0].astype(F32)
        sums[which][slot_of(orders[which])] = total.astype(BF16)
        spread_copy(which, bits - 1).start()

    def spread(which, level):
        spread_copy(which, level).wait_recv()
        if level:
            spread_copy(which, level - 1).start()


    def proj_copy(head, level):
        count = 2 ** (bits - 1 - level)
        other = (1 - bit_of(0, level)) * count
        source = proj[head] if level == 0 else proj_taken[head][level - 1]
        return send(
            source.at[pl.ds(other, count)],
            proj_taken[head][level],
            (proj_send, proj_recv),
            (0, head, level),
            {"dp": partner_of(dp_index, orders[0][level])},
        )

    def proj_spread_copy(head, level):
        held = proj_slots[head].at[held_slots(orders[0], level)]
        partner = {"dp": partner_of(dp_index, orders[0][level])}
        return send(held, held, (proj_send, proj_recv), (1, head, level), partner)

    def add_proj(head, level):
        proj_copy(head, level).wait_recv()
        count = 2 ** (bits - 1 - level)
        start = bit_of(0, level) * count
        into = proj_taken[head][level]
        for slot in range(count):
            mine = proj[head][start + slot] if level == 0 else proj_taken[head][level - 1][start + slot]
            into[slot] = (into[slot].astype(F32) + mine.astype(F32)).astype(BF16)
        if level + 1 < bits:
            proj_copy(head, level + 1).start()
        else:
            proj_slots[head][slot_of(orders[0])] = into[0]
            proj_spread_copy(head, level).start()

    def spread_proj(head, level):
        proj_spread_copy(head, level).wait_recv()
        if level:
            proj_spread_copy(head, level - 1).start()


    def vector_copy(level):
        return send(
            vectors[level],
            vectors_taken[level],
            (vector_send, vector_recv),
            level,
            {"dp": partner_of(dp_index, level)},
        )

    def vector_last_copy(offset):
        return send(
            vectors[bits],
            vectors_all.at[me],
            (vector_last_send, vector_last_recv),
            offset - 1,
            {"mp": target(offset)},
        )

    def add_vector(level):
        vector_copy(level).wait_recv()
        vectors[level + 1][...] = vectors[level][...] + vectors_taken[level][...]
        if level + 1 < bits:
            vector_copy(level + 1).start()
        else:
            vectors_all[me] = vectors[bits][...]
            for offset in peers:
                vector_last_copy(offset).start()

    def finish_vector():
        for offset in peers:
            vector_last_copy(offset).wait_recv()
        total = vectors_all[0]
        for index in peers:
            total = total + vectors_all[index]
        vector_sum[...] = total

    def bias_copy(level):
        return send(
            biases[level],
            biases_taken[level],
            (bias_send, bias_recv),
            level,
            {"dp": partner_of(dp_index, level)},
        )

    def add_bias(level):
        bias_copy(level).wait_recv()
        biases[level + 1][...] = biases[level][...] + biases_taken[level][...]
        if level + 1 < bits:
            bias_copy(level + 1).start()
        else:
            bias_sum[...] = biases[bits][...]


    def grads_copy(head, offset):
        return send(
            grads_out.at[target(offset), head],
            grads_in.at[head, me],
            (grads_send, grads_recv),
            (head, offset - 1),
            {"mp": target(offset)},
        )

    def grads_own_copy(head):
        return pltpu.make_async_copy(
            grads_out.at[me, head], grads_in.at[head, me], grads_own.at[head]
        )

    line = Line(mp_size, me)
    order = gather_orders(bits)[3]
    own_slot = place_in(dp_index, order)

    def weight_copy(side, hop):
        place = proj_all.at[line.place(side, hop), pl.ds(own_slot, 1)]
        source = proj_weight.at[pl.ds(own_slot, 1)] if hop == 0 else place
        return send(source, place, (weight_send, weight_recv), (side, hop), line.neighbour(side))

    def weight_trade_copy(level, side, hop):
        held = pl.ds(own_slot // 2**level * 2**level, 2**level)
        place = proj_all.at[line.place(side, hop + 1), held]
        partner = {"dp": partner_of(dp_index, order[level])}
        return send(place, place, (weight_trade_send, weight_trade_recv), (level, side, hop), partner)

    def take_weight(side, hop):
        weight_copy(side, hop).wait_recv()
        if hop + 1 < mp_size - 1:
            line.if_sent(side, hop + 1)(lambda: weight_copy(side, hop + 1).start())
        if bits:
            weight_trade_copy(0, side, hop).start()

    def trade_weight(level, side, hop):
        weight_trade_copy(level, side, hop).wait_recv()
        if level + 1 < bits:
            weight_trade_copy(level + 1, side, hop).start()

    def both_sides(act, *which):
        for side in (0, 1):
            line.if_taken(side, which[-1])(partial(act, *which[:-1], side, which[-1]))

    schedule = (
        (0, take_weight, 0),
        (1, take_weight, 1),
        (2, take_weight, 2),
        (2, trade_weight, 0, 0),
        (3, trade_weight, 0, 1),
        (3, trade_weight, 0, 2),
        (4, trade_weight, 1, 0),
        (6, trade_weight, 1, 1),
        (8, trade_weight, 1, 2),
    )
    done = set()

    def at_point(point, index=None):
        for at, act, *which in schedule:
            if which[-1] not in line.hops or (act is trade_weight and which[0] >= bits):
                continue
            if index is None and at == point:
                both_sides(act, *which)
                done.add((act, *which))
            if index is not None and point <= at < point + mp_size:
                pl.when(index == at - point)(partial(both_sides, act, *which))
                done.add((act, *which))

    def dense_phase(
        frames_buf,
        heads_buf,
        cotangent_buf,
        in_buf,
        down_buf,
        out_buf,
        hidden,
        slope,
        mid_buf,
        normed_buf,
        store_buf,
        low_buf,
        grad_buf,
        given,
        head_buf,
    ):
        loads = [
            pltpu.make_async_copy(source, into, load_sems.at[at])
            for at, (source, into) in enumerate(
                ((frames, frames_buf), (heads_low, heads_buf), (out_grad, cotangent_buf))
            )
        ]
        out_copies = [
            pltpu.make_async_copy(
                out_all.at[index],
                out_buf.at[pl.ds(index * head_cols, head_cols)],
                out_sems.at[index],
            )
            for index in range(mp_size)
        ]

        def in_copy(index):
            return pltpu.make_async_copy(in_all.at[index], in_buf.at[index], in_sems.at[index])

        def down_copy(index):
            return pltpu.make_async_copy(
                down_all.at[index], down_buf.at[index], down_sems.at[index]
            )

        def given_copy(which, turn):
            return pltpu.make_async_copy(
                given.at[turn % 2], partials[which].at[part_of(turn)], given_sems.at[turn % 2]
            )

        def store_copy(at):
            return pltpu.make_async_copy(
                store_buf, (block_out, resid_grad)[at], store_sems.at[at]
            )

        for copy in loads + out_copies:
            copy.start()
        for index in range(mp_size):
            in_copy(index).start()
            down_copy(index).start()
        enter(dp_index, me, mp_size, bits)
        for side in (0, 1):
            line.if_sent(side, 0)(lambda side=side: weight_copy(side, 0).start())
        weight_own_copy.start()
        vector[...] = jnp.zeros_like(vector)
        gains = norm_gain[...].astype(F32)
        shifts = norm_shift[...].astype(F32)
        both = [slice(side * half, (side + 1) * half) for side in range(2)]

        for copy in loads + out_copies:
            copy.wait()
        branch = dot(heads_buf[...], out_buf[...]) + out_bias[...].astype(F32)
        mid, normed, inv_mid = norm_rows(
            frames_buf[...].astype(F32) + branch, gains[:1], shifts[:1]
        )
        mid_buf[...] = mid + down_bias[...].astype(F32)
        normed_buf[...] = normed
        low_buf[...] = mid.astype(BF16)
        at_point(0)

        def feed(index, _):
            in_copy(index).wait()
            down_copy(index).wait()
            for rows in both:
                pre_act = dot(low_buf[rows], in_buf[index]) + in_bias[index, 0:1].astype(F32)
                unit_cdf = 0.5 * (1.0 + lax.erf(pre_act * 0.5**0.5))
                bell = jnp.exp(-0.5 * pre_act * pre_act) * (2.0 * jnp.pi) ** (-0.5)
                slope[index, rows] = (unit_cdf + pre_act * bell).astype(BF16)
                hidden[index, rows] = (pre_act * unit_cdf).astype(BF16)
                mid_buf[rows] += dot(hidden[index, rows], down_buf[index])
            at_point(1, index)
            return 0

        lax.fori_loop(0, mp_size, feed, 0)
        output, normed, inv_out = norm_rows(mid_buf[...], gains[1:], shifts[1:])
        store_buf[...] = output
        store_copy(0).start()

        cotangent = cotangent_buf[...].astype(F32)
        vector[1:2] = sum_rows(cotangent * normed)
        vector[3:4] = sum_rows(cotangent)
        sum_grad = norm_back(cotangent, normed, inv_out, gains[1:])
        mid_buf[...] = sum_grad
        grad_buf[...] = sum_grad.astype(BF16)
        vector[5:6] = sum_rows(grad_buf[...])

        def give(which, turn, result):
            if turn >= 2:
                offer_given(which, turn - 2)
            share = result.shape[0] // slots
            for slot in range(slots):
                given[turn % 2, slot] = result[slot * share : (slot + 1) * share].astype(BF16)
            given_copy(which, turn).start()

        def offer_given(which, turn):
            given_copy(which, turn).wait()
            offer(which, turn)

        for turn in turns:
            index = part_of(turn)
            give(1, turn, dot_cols(hidden[index], grad_buf[...]))
            pre = dot_rows(grad_buf[...], down_buf[index]) * slope[index].astype(F32)
            hidden[index] = pre.astype(BF16)
            vector[pl.ds(8 + index, 1)] = sum_rows(hidden[index])
            mid_buf[...] += dot_rows(hidden[index], in_buf[index])
            at_point(1 + mp_size + turn)
        for turn in turns[-2:]:
            offer_given(1, turn)
        mid_grad = mid_buf[...]
        vector[0:1] = sum_rows(mid_grad * normed_buf[...])
        vector[2:3] = sum_rows(mid_grad)
        resid = norm_back(mid_grad, normed_buf[...], inv_mid, gains[:1])
        store_copy(0).wait()
        store_buf[...] = resid
        store_copy(1).start()
        attn_grad = resid.astype(BF16)
        grad_buf[...] = attn_grad
        vector[4:5] = sum_rows(attn_grad)
        heads_grad = dot_rows(attn_grad, out_buf[...]).astype(BF16)
        for head in range(head_total):
            for index in range(mp_size):
                at = index * head_cols + head * HEAD_DIM
                for side in range(2):
                    grads_out[index, head, :, side * HEAD_DIM : (side + 1) * HEAD_DIM] = (
                        heads_grad[both[side], at : at + HEAD_DIM]
                    )
            if head == 0:
                for offset in peers:
                    grads_copy(0, offset).start()
        for head in range(head_total):
            grads_own_copy(head).start()
        vector_copy(0).start()

        products = dot_cols(heads_buf[...], grad_buf[...]).astype(BF16)
        rows = head_cols // slots
        for index in range(mp_size):
            for slot in range(slots):
                start = index * head_cols + slot * rows
                head_buf[index, slot, :rows] = products[start : start + rows]
                if rows < head_buf.shape[2]:
                    head_buf[index, slot, rows:] = jnp.zeros(
                        (head_buf.shape[2] - rows, width), BF16
                    )
        head_copy = pltpu.make_async_copy(head_buf, head_grads, head_sem)
        head_copy.start()
        normed_low = low_buf[...].T
        for turn in turns:
            give(0, turn, dot(normed_low, hidden[part_of(turn)]))
            if turn == 0:
                head_copy.wait()
                for at in turns:
                    offer(2, at)
                for later in range(1, head_total):
                    for offset in peers:
                        grads_copy(later, offset).start()
        for turn in turns[-2:]:
            offer_given(0, turn)
        store_copy(1).wait()

    weight_own_copy = pltpu.make_async_copy(proj_weight, proj_all.at[me], weight_own)
    rows_low = pltpu.VMEM((2 * half, width), BF16)
    rows_full = pltpu.VMEM((2 * half, width), F32)
    pl.run_scoped(
        dense_phase,
        rows_low,
        rows_low,
        rows_low,
        pltpu.VMEM((mp_size, width, units), BF16),
        pltpu.VMEM((mp_size, units, width), BF16),
        pltpu.VMEM((width, width), BF16),
        pltpu.VMEM((mp_size, 2 * half, units), BF16),
        pltpu.VMEM((mp_size, 2 * half, units), BF16),
        rows_full,
        rows_full,
        rows_full,
        rows_low,
        rows_low,
        pltpu.VMEM((2, slots, units // slots, width), BF16),
        pltpu.VMEM(head_grads.shape, BF16),
    )

    def attention_phase(
        qkv,
        out_cols,
        log_total,
        seg_col,
        input_all,
        staged,
        qkv_grad,
        seg_blocks,
        grads,
        key_buf,
        key_cols,
        value_buf,
        query_sum,
        key_sum,
        value_sum,
        proj_rows,
    ):
        def traded_copy(head, offset):
            return send(
                staged.at[head, target(offset)],
                traded.at[head, me],
                (traded_send, traded_recv),
                (head, offset - 1),
                {"mp": target(offset)},
            )

        def traded_own_copy(head):
            return pltpu.make_async_copy(
                staged.at[head, me], traded.at[head, me], traded_own.at[head]
            )

        def prepare(head):
            cols = slice(head * HEAD_DIM, (head + 1) * HEAD_DIM)
            key_buf[:, :HEAD_DIM] = qkv[1, :, cols]
            key_buf[:, HEAD_DIM:] = ones_columns(ROW_LEN)
            value_buf[:, :HEAD_DIM] = qkv[2, :, cols]
            value_buf[:, HEAD_DIM:] = ones_columns(ROW_LEN)
            for step in range(BLOCKS):
                key_cols[step] = qkv[1, step * BLOCK : (step + 1) * BLOCK, cols].T
            key_sum[...] = jnp.zeros_like(key_sum)
            value_sum[...] = jnp.zeros_like(value_sum)

        def take_grads(head):
            grads_own_copy(head).wait()
            for offset in peers:
                grads_copy(head, offset).wait_recv()
            for chunk in range(mp_size):
                for side in range(2):
                    start = (2 * chunk + side) * half
                    grads[start : start + half] = grads_in[
                        head, chunk, :, side * HEAD_DIM : (side + 1) * HEAD_DIM
                    ]

        def attend_back(head):
            cols = slice(head * HEAD_DIM, (head + 1) * HEAD_DIM)

            def query_block(number, _):
                rows = block_rows(number)
                queries = qkv[0, rows, cols] * SCALE
                grad_rows = grads[rows]
                seg_query = seg_blocks[number]
                grad_cols = grad_rows.astype(F32).T
                row_dot = jnp.sum(grad_cols * out_cols[head, number], axis=0, keepdims=True)
                grad_cols = jnp.concatenate([grad_cols.astype(BF16), as_pieces(-row_dot)], axis=0)
                query_cols = jnp.concatenate(
                    [queries.astype(F32).T.astype(BF16), as_pieces(-log_total[head, number])], axis=0
                )

                def products_of(step):
                    key_rows = slice(step * BLOCK, (step + 1) * BLOCK)
                    same = (
                        jnp.concatenate([seg_col[key_rows]] * (BLOCK // 128), axis=1) == seg_query
                    )
                    scores = jnp.where(same, dot(key_buf[key_rows], query_cols), MASKED)
                    return scores, dot(value_buf[key_rows], grad_cols)

                query_grad = jnp.zeros((HEAD_DIM, BLOCK), F32)
                ahead = products_of(0)
                for step in range(BLOCKS):
                    scores, soft_grad = ahead
                    if step + 1 < BLOCKS:
                        ahead = products_of(step + 1)
                    key_rows = slice(step * BLOCK, (step + 1) * BLOCK)
                    soft = jnp.exp(scores)
                    score_grad = (soft * soft_grad).astype(BF16)
                    value_sum[key_rows] += dot(soft.astype(BF16), grad_rows)
                    key_sum[key_rows] += dot(score_grad, queries)
                    query_grad = query_grad + dot(key_cols[step], score_grad)
                query_sum[rows] = (query_grad * SCALE).T
                for at in range(head * BLOCKS, (head + 1) * BLOCKS):
                    if at in events:

                        @pl.when(number == at - head * BLOCKS)
                        def _():
                            for act in events[at]:
                                act()

                return 0

            lax.fori_loop(0, BLOCKS, query_block, 0)

        def give_grads(head):
            for part, total in enumerate((query_sum, key_sum, value_sum)):
                low = total[...].astype(BF16)
                qkv_grad[:, part * HEAD_DIM : (part + 1) * HEAD_DIM] = low
                if part != 1:
                    cols = slice(head * HEAD_DIM, (head + 1) * HEAD_DIM)
                    sum_low = jnp.sum(low.astype(F32), axis=0, keepdims=True)
                    biases[0][part : part + 1, cols] = sum_low
                for chunk in range(mp_size):
                    for side in range(2):
                        start = (2 * chunk + side) * half
                        staged[head, chunk, part, :, side * HEAD_DIM : (side + 1) * HEAD_DIM] = total[
                            start : start + half
                        ].astype(BF16)

        def start_trade(head):
            for offset in peers:
                traded_copy(head, offset).start()
            traded_own_copy(head).start()

        def start_proj(head):
            products = dot_cols(qkv_grad[...], input_all[...])
            slot_rows = proj[head].shape[1]
            for slot in range(2**bits):
                proj[head][slot] = products[slot * slot_rows : (slot + 1) * slot_rows].astype(BF16)
            proj_copy(head, 0).start()

        def finish_proj(head):
            cols = slice(head * HEAD_DIM, (head + 1) * HEAD_DIM)
            slot_rows = proj_slots[head].shape[1]
            for slot in range(2**bits):
                proj_rows[slot * slot_rows : (slot + 1) * slot_rows] = proj_slots[head][slot].astype(F32)
            for part in range(3):
                rows = proj_rows[part * HEAD_DIM : (part + 1) * HEAD_DIM]
                proj_sum[part, cols] = rows.astype(BF16)

        events = {}
        rest = []

        def due(at, act, *which):
            if at is None:
                rest.append((act, *which))
            else:
                events.setdefault(at, []).append(partial(act, *which))

        for at, level in zip((0, 1, 2), levels):
            due(at, add_vector, level)
        due(2.5, finish_vector)
        times = {
            1: ((0, 0, 0, 0), (2, 2.5, 3, 4), (2.5, 3, 4, 5)),
            2: ((2.5, 2.5, 2.5, 2.5), (4, 4, 4, 4), (5, 5, 5, 5)),
            0: ((1, 2.5, 3, 4), (2.5, 4, 5, 5.5), (3, 5, 5.5, 6)),
        }
        ends = {1: (5.5, 6, 7, 8), 2: (6, 7, 8, None), 0: (7, 8, None, None)}
        for level in levels:
            for which in times:
                for turn, at in zip(turns, times[which][level]):
                    due(at, add_level, which, level, turn)
        for at, level in zip((3, 4, 5), levels):
            due(at, add_proj, 0, level)
        for at, level in zip((6, 7, 8), levels):
            due(at, add_proj, 1, level)
        for at, level in zip((5.5, 6, 7), levels[::-1]):
            due(at, spread_proj, 0, level)
        for which in (1, 2, 0):
            due(ends[which][0], finish_sum, which)
        for step, level in enumerate(levels[::-1]):
            for which in (0, 1, 2):
                due(ends[which][1 + step], spread, which, level)

        copies = [
            pltpu.make_async_copy(source, into, attention_sems.at[at])
            for at, (source, into) in enumerate(
                (
                    (qkv_source, qkv),
                    (seg_source, seg_col),
                    (log_source, log_total),
                    (out_source, out_cols),
                    (input_source, input_all),
                )
            )
        ]
        for copy in copies:
            copy.start()
        biases[0][...] = jnp.zeros_like(biases[0])
        for step in range(BLOCKS):
            seg_blocks[step] = seg_row[:, step * BLOCK : (step + 1) * BLOCK]
        final = head_total - 1
        copies[0].wait()
        for head in range(head_total):
            prepare(head)
            take_grads(head)
            if head == 0:
                for copy in copies[1:4]:
                    copy.wait()
            attend_back(head)
            give_grads(head)
            start_trade(head)
            if head == 0:
                copies[4].wait()
            start_proj(head)
            for act in events.get((head + 1) * BLOCKS - 0.5, ()):
                act()
        bias_copy(0).start()
        for level in levels:
            add_proj(final, level)
            spread_proj(final - 1, bits - 1 - level)
            if rest:
                act, *which = rest.pop(0)
                act(*which)
            add_bias(level)
        for act, *which in rest:
            act(*which)
        for level in levels[::-1]:
            spread_proj(final, level)
        for head in range(head_total):
            finish_proj(head)
            traded_own_copy(head).wait()
            for offset in peers:
                traded_copy(head, offset).wait()

    pl.run_scoped(
        attention_phase,
        pltpu.VMEM(qkv_source.shape, BF16),
        pltpu.VMEM(out_source.shape, F32),
        pltpu.VMEM(log_source.shape, F32),
        pltpu.VMEM(seg_source.shape, jnp.int32),
        pltpu.VMEM(input_source.shape, BF16),
        pltpu.VMEM((head_total, mp_size, 3, half, 2 * HEAD_DIM), BF16),
        pltpu.VMEM((ROW_LEN, 3 * HEAD_DIM), BF16),
        pltpu.VMEM((BLOCKS, 1, BLOCK), jnp.int32),
        pltpu.VMEM((ROW_LEN, HEAD_DIM), BF16),
        pltpu.VMEM((ROW_LEN, HEAD_DIM + EXTRA), BF16),
        pltpu.VMEM((BLOCKS, HEAD_DIM, BLOCK), BF16),
        pltpu.VMEM((ROW_LEN, HEAD_DIM + EXTRA), BF16),
        pltpu.VMEM((ROW_LEN, HEAD_DIM), F32),
        pltpu.VMEM((ROW_LEN, HEAD_DIM), F32),
        pltpu.VMEM((ROW_LEN, HEAD_DIM), F32),
        pltpu.VMEM((3 * HEAD_DIM, width), F32),
    )

    for hop in line.hops:
        if (take_weight, hop) not in done:
            both_sides(take_weight, hop)
    for level in levels:
        for hop in line.hops:
            if (trade_weight, level, hop) not in done:
                both_sides(trade_weight, level, hop)

    def sent_trades(side, hop):
        for level in levels:
            weight_trade_copy(level, side, hop).wait_send()

    for side, hop in line.ways:
        line.if_sent(side, hop)(lambda side=side, hop=hop: weight_copy(side, hop).wait_send())
        line.if_taken(side, hop)(partial(sent_trades, side, hop))
    weight_own_copy.wait()
    for head in range(head_total):
        for offset in peers:
            grads_copy(head, offset).wait_send()
        for level in levels:
            proj_copy(head, level).wait_send()
            proj_spread_copy(head, level).wait_send()
    for level in levels:
        vector_copy(level).wait_send()
        bias_copy(level).wait_send()
        for which in arrays:
            spread_copy(which, level).wait_send()
            for turn in turns:
                level_copy(which, level, turn).wait_send()
    for offset in peers:
        vector_last_copy(offset).wait_send()
        for which in arrays:
            last_copy(which, offset).wait_send()


def rear(frames, heads_low, out_grad, seg_row, in_bias, small, weights, proj_weight, saved, bits):
    local_rows, width = frames.shape
    qkv_low, out_cols = saved[:2]
    mp_size, units = weights[1].shape[:2]
    head_total = out_cols.shape[0]
    half, lanes = local_rows // 2, 2 * HEAD_DIM
    peers = mp_size - 1
    slots = 2**bits
    head_rows = -(-width // mp_size // slots // 16) * 16
    anywhere = pl.BlockSpec(memory_space=pl.ANY)
    blocks = [(width // slots, units), (units // slots, width), (head_rows, width)]
    proj_block = (3 * HEAD_DIM // slots, width)
    bias_block = (8, 2 * 128)
    vector_block = (8 + -(-mp_size // 8) * 8, width)

    def halves(shape, lead=()):
        return [pltpu.VMEM(lead + (slots >> (level + 1),) + shape, BF16) for level in range(bits)]

    def sems(*shapes):
        return [pltpu.SemaphoreType.DMA(shape) for shape in shapes for _ in range(2)]

    piece = pltpu.VMEM((mp_size, head_total, half, lanes), BF16)
    return pl.pallas_call(
        partial(rear_kernel, bits),
        out_shape=(
            jax.ShapeDtypeStruct((local_rows, width), F32),
            jax.ShapeDtypeStruct((local_rows, width), F32),
            *(jax.ShapeDtypeStruct((mp_size, slots) + block, BF16) for block in blocks),
            jax.ShapeDtypeStruct((mp_size,) + proj_weight.shape, BF16),
            jax.ShapeDtypeStruct((head_total, mp_size, 3, half, lanes), BF16),
            *(jax.ShapeDtypeStruct((slots,) + block, BF16) for block in blocks),
            jax.ShapeDtypeStruct((3, head_total * HEAD_DIM, width), BF16),
            jax.ShapeDtypeStruct(vector_block, F32),
            jax.ShapeDtypeStruct(bias_block, F32),
        ),
        in_specs=[whole()] * 6 + [anywhere] * 12,
        out_specs=(anywhere,) * 7 + (whole(),) * 6,
        scratch_shapes=[
            piece,
            pltpu.VMEM((head_total, mp_size, half, lanes), BF16),
            [pltpu.VMEM((2, slots // 2) + block, BF16) for block in blocks],
            [halves(block, (mp_size,)) for block in blocks],
            [pltpu.VMEM((peers, 1) + block, BF16) for block in blocks],
            [pltpu.VMEM((slots,) + proj_block, BF16) for _ in range(head_total)],
            [halves(proj_block) for _ in range(head_total)],
            [pltpu.VMEM((slots,) + proj_block, BF16) for _ in range(head_total)],
            [pltpu.VMEM(vector_block, F32) for _ in range(bits + 1)],
            [pltpu.VMEM(vector_block, F32) for _ in range(bits)],
            pltpu.VMEM((mp_size,) + vector_block, F32),
            [pltpu.VMEM(bias_block, F32) for _ in range(bits + 1)],
            [pltpu.VMEM(bias_block, F32) for _ in range(bits)],
            pltpu.SemaphoreType.DMA((3,)),
            pltpu.SemaphoreType.DMA((mp_size,)),
            pltpu.SemaphoreType.DMA((mp_size,)),
            pltpu.SemaphoreType.DMA((mp_size,)),
            pltpu.SemaphoreType.DMA((2,)),
            pltpu.SemaphoreType.DMA,
            pltpu.SemaphoreType.DMA((2,)),
            pltpu.SemaphoreType.DMA((5,)),
            pltpu.SemaphoreType.DMA,
            *sems((2, peers), (max(bits, 1), 2, peers)),
            pltpu.SemaphoreType.DMA((3, 2)),
            pltpu.SemaphoreType.DMA((head_total,)),
            *sems((head_total, peers)),
            pltpu.SemaphoreType.DMA((head_total,)),
            *sems(
                (head_total, peers),
                (3, bits, mp_size),
                (3, peers),
                (3, bits),
                (2, head_total, bits),
                (bits,),
                (peers,),
                (bits,),
            ),
        ],
        compiler_params=pltpu.CompilerParams(
            collective_id=1, has_side_effects=True, vmem_limit_bytes=REAR_VMEM_BYTES
        ),
        cost_estimate=pl.CostEstimate(
            flops=40 * head_total * ROW_LEN * ROW_LEN * HEAD_DIM,
            bytes_accessed=96 * 1024 * 1024,
            transcendentals=head_total * ROW_LEN * ROW_LEN,
        ),
        name="rear",
    )(seg_row, in_bias, *small, frames, heads_low, out_grad, *weights, proj_weight, *saved)


def finish_kernel(
    traded,
    proj_all,
    resid_grad,
    in_sum,
    down_sum,
    head_sum,
    proj_sum,
    vector_sum,
    bias_sum,
    stream_grad,
    in_grad,
    down_grad,
    out_grad,
    proj_grad,
    query_bias_grad,
    value_bias_grad,
    out_bias_grad,
    in_bias_grad,
    down_bias_grad,
    gain_grad,
    shift_grad,
    columns,
    weight_buf,
    sems,
):
    head_total, mp_size = traded.shape[:2]
    half = traded.shape[3]
    head_cols = head_total * HEAD_DIM
    copies = [
        pltpu.make_async_copy(
            proj_all.at[index],
            weight_buf.at[index],
            sems.at[index],
        )
        for index in range(mp_size)
    ]
    for copy in copies:
        copy.start()
    for sums, grad in ((in_sum, in_grad), (down_sum, down_grad), (head_sum, out_grad)):
        rows = grad.shape[0] // sums.shape[0]
        for slot in range(sums.shape[0]):
            grad[slot * rows : (slot + 1) * rows] = sums[slot, :rows].astype(F32)
    proj_grad[...] = proj_sum[...].astype(F32)
    query_bias_grad[...] = bias_sum[0:1, :head_cols]
    value_bias_grad[...] = bias_sum[2:3, :head_cols]
    gain_grad[...] = vector_sum[0:2]
    shift_grad[...] = vector_sum[2:4]
    out_bias_grad[...] = vector_sum[4:5]
    down_bias_grad[...] = vector_sum[5:6]
    in_bias_grad[...] = vector_sum[pl.ds(8 + lax.axis_index("mp"), 1)]
    stream_grad[...] = resid_grad[...]
    for index in range(mp_size):
        for head in range(head_total):
            for part in range(3):
                at = part * head_cols + head * HEAD_DIM
                for side in range(2):
                    columns[side * half : (side + 1) * half, at : at + HEAD_DIM] = traded[
                        head, index, part, :, side * HEAD_DIM : (side + 1) * HEAD_DIM
                    ]
        copies[index].wait()
        stream_grad[...] += dot(columns[...], weight_buf[index])


def finish(traded, proj_all, resid_grad, sums):
    head_total, mp_size = traded.shape[:2]
    head_cols = head_total * HEAD_DIM
    local_rows, width = resid_grad.shape
    units = sums[0].shape[0] * sums[0].shape[1]
    row = jax.ShapeDtypeStruct((1, width), F32)
    head_row = jax.ShapeDtypeStruct((1, head_cols), F32)
    anywhere = pl.BlockSpec(memory_space=pl.ANY)
    return pl.pallas_call(
        finish_kernel,
        out_shape=(
            jax.ShapeDtypeStruct((local_rows, width), F32),
            jax.ShapeDtypeStruct((units, width), F32),
            jax.ShapeDtypeStruct((units, width), F32),
            jax.ShapeDtypeStruct((head_cols, width), F32),
            jax.ShapeDtypeStruct((3, head_cols, width), F32),
            head_row,
            head_row,
            row,
            jax.ShapeDtypeStruct((1, units), F32),
            row,
            jax.ShapeDtypeStruct((2, width), F32),
            jax.ShapeDtypeStruct((2, width), F32),
        ),
        in_specs=[whole(), anywhere] + [whole()] * 7,
        out_specs=(whole(),) * 12,
        scratch_shapes=[
            pltpu.VMEM((local_rows, 3 * head_cols), BF16),
            pltpu.VMEM((mp_size, 3 * head_cols, width), BF16),
            pltpu.SemaphoreType.DMA((mp_size,)),
        ],
        compiler_params=pltpu.CompilerParams(vmem_limit_bytes=VMEM_BYTES),
        cost_estimate=pl.CostEstimate(
            flops=6 * local_rows * width * width, bytes_accessed=24 * 1024 * 1024, transcendentals=0
        ),
        name="finish",
    )(traded, proj_all, resid_grad, *sums)


def dp_groups():
    total = lax.axis_size("dp")
    size = min(8, total)
    groups = [list(range(start, start + size)) for start in range(0, total, size)]
    return (size, groups)


def on_device(
    frames,
    segment_ids,
    qkv_weight,
    q_bias,
    v_bias,
    out_weight,
    out_bias,
    ff_in_weight,
    ff_in_bias,
    ff_out_weight,
    ff_out_bias,
    norm_gain,
    norm_shift,
    out_grad,
):
    local_rows, width = frames.shape
    mp_size = lax.axis_size("mp")
    group, groups = dp_groups()
    bits = group_bits(lax.axis_size("dp"))
    slots = 2**bits

    proj_weight = qkv_weight[0].transpose(0, 2, 1)
    seg_row = segment_ids.reshape(1, ROW_LEN)
    (
        input_all,
        qkv_low,
        in_all,
        down_all,
        out_all,
        in_bias_all,
        seg_col,
        out_cols,
        log_total,
        heads_low,
    ) = front(
        frames,
        proj_weight,
        q_bias,
        v_bias,
        seg_row,
        (ff_in_weight[0], ff_out_weight[0], out_weight[0]),
        ff_in_bias,
        mp_size,
        bits,
    )
    block_out, resid_grad, _, _, _, proj_all, traded, *summed = rear(
        frames,
        heads_low,
        out_grad,
        seg_row,
        in_bias_all,
        (out_bias, ff_out_bias, norm_gain[0], norm_shift[0]),
        (in_all, down_all, out_all),
        proj_weight.reshape(slots, -1, width),
        (qkv_low, out_cols, log_total, seg_col, input_all),
        bits,
    )
    if len(groups) > 1:
        across = [list(range(at, lax.axis_size("dp"), group)) for at in range(group)]
        summed = lax.psum(summed, "dp", axis_index_groups=across)
    (
        stream_grad,
        in_weight_grad,
        down_weight_grad,
        out_weight_grad,
        proj_grad,
        query_bias_grad,
        value_bias_grad,
        head_bias_grad,
        in_bias_grad,
        down_bias_grad,
        gain_grad,
        shift_grad,
    ) = finish(traded, proj_all.reshape(mp_size, -1, width), resid_grad, summed)
    return (
        block_out,
        stream_grad,
        proj_grad.transpose(0, 2, 1)[None],
        query_bias_grad,
        value_bias_grad,
        out_weight_grad[None],
        head_bias_grad,
        in_weight_grad[None],
        in_bias_grad,
        down_weight_grad[None],
        down_bias_grad,
        gain_grad[None],
        shift_grad[None],
    )


def solution(mesh):
    return jax.shard_map(
        on_device,
        mesh=mesh,
        in_specs=(
            P(("dp", "mp"), None),
            P("dp"),
            P(None, None, None, "mp"),
            P(None, "mp"),
            P(None, "mp"),
            P(None, "mp", None),
            P(),
            P(None, None, "mp"),
            P(None, "mp"),
            P(None, "mp", None),
            P(),
            P(),
            P(),
            P(("dp", "mp"), None),
        ),
        out_specs=(
            P(("dp", "mp"), None),
            P(("dp", "mp"), None),
            P(None, None, None, "mp"),
            P(None, "mp"),
            P(None, "mp"),
            P(None, "mp", None),
            P(),
            P(None, None, "mp"),
            P(None, "mp"),
            P(None, "mp", None),
            P(),
            P(),
            P(),
        ),
        check_vma=False,
    )
```

```python
import itertools
from functools import partial

import jax
import jax.numpy as jnp
from jax import lax
from jax.experimental import pallas as pl
from jax.experimental.pallas import tpu as pltpu
from jax.sharding import PartitionSpec as P

HEAD_DIM = 64
ROW_LEN = 2304
BLOCK = 768
BLOCKS = ROW_LEN // BLOCK
EXTRA = 16
SCALE = HEAD_DIM ** (-0.5)
MASKED = -1e30
F32 = jnp.float32
BF16 = jnp.bfloat16
VMEM_BYTES = 56 * 1024 * 1024
REAR_VMEM_BYTES = 63 * 1024 * 1024


def dot_rows(left, right):
    return lax.dot_general(left, right, (((1,), (1,)), ((), ())), preferred_element_type=F32)


def dot_cols(left, right):
    return lax.dot_general(left, right, (((0,), (0,)), ((), ())), preferred_element_type=F32)


def dot(left, right):
    return jnp.dot(left, right, preferred_element_type=F32)


def block_rows(number):
    return pl.ds(pl.multiple_of(number * BLOCK, BLOCK), BLOCK)


def as_pieces(row):
    high = row.astype(BF16).astype(F32)
    middle = (row - high).astype(BF16).astype(F32)
    last = row - high - middle
    place = lax.broadcasted_iota(jnp.int32, (EXTRA, row.shape[1]), 0)
    pieces = jnp.where(place == 0, high, jnp.where(place == 1, middle, jnp.where(place == 2, last, 0.0)))
    return pieces.astype(BF16)


def ones_columns(rows):
    place = lax.broadcasted_iota(jnp.int32, (rows, EXTRA), 1)
    return jnp.where(place < 3, 1.0, 0.0).astype(BF16)


def whole(memory_space=pltpu.VMEM):
    return pl.BlockSpec(memory_space=memory_space)


MESH = pl.DeviceIdType.MESH


def group_bits(dp_size):
    return min(3, dp_size.bit_length() - 1)


def place_in(dp_index, order):
    slot = 0
    for at, bit in enumerate(order):
        slot = slot + (dp_index // 2**bit) % 2 * 2**at
    return slot


def partner_of(dp_index, bit):
    return dp_index + (1 - 2 * ((dp_index // 2**bit) % 2)) * 2**bit


def mate_of(dp_index, offset, size):
    place = lax.rem(dp_index, size)
    return dp_index - place + lax.rem(place + offset, size)


def enter(dp_index, mp_index, mp_size, bits, whole_group=False):
    barrier = pltpu.get_barrier_semaphore()
    for offset in range(1, mp_size):
        pl.semaphore_signal(
            barrier, device_id={"mp": lax.rem(mp_index + offset, mp_size)}, device_id_type=MESH
        )
    if whole_group:
        partners = [mate_of(dp_index, offset, 2**bits) for offset in range(1, 2**bits)]
    else:
        partners = [partner_of(dp_index, bit) for bit in range(bits)]
    for partner in partners:
        pl.semaphore_signal(barrier, device_id={"dp": partner}, device_id_type=MESH)
    pl.semaphore_wait(barrier, mp_size - 1 + len(partners))


def send(src, dst, sems, at, device_id):
    return pltpu.make_async_remote_copy(
        src_ref=src,
        dst_ref=dst,
        send_sem=sems[0].at[at],
        recv_sem=sems[1].at[at],
        device_id=device_id,
        device_id_type=MESH,
    )


def gather_orders(bits):
    if bits == 3:
        return ((1, 2, 0), (2, 1, 0), (1, 2), (1, 2, 0))
    return (tuple(range(bits)),) * 4


SIDES = (1, -1)


def inside(index, size):
    return jnp.logical_and(index >= 0, index < size)


class Line:
    def __init__(self, mp_size, me):
        self.size = mp_size
        self.me = me
        self.hops = range(mp_size - 1)
        self.ways = [(side, hop) for hop in self.hops for side in (0, 1)]

    def wrapped(self, index):
        return lax.rem(index + self.size, self.size)

    def chunk(self, side, hop):
        return self.me - SIDES[side] * hop

    def place(self, side, hop):
        return self.wrapped(self.chunk(side, hop))

    def sends(self, side, hop):
        there = inside(self.me + SIDES[side], self.size)
        return jnp.logical_and(there, inside(self.chunk(side, hop), self.size))

    def if_sent(self, side, hop):
        return pl.when(self.sends(side, hop))

    def if_taken(self, side, hop):
        return pl.when(inside(self.chunk(side, hop + 1), self.size))

    def neighbour(self, side):
        return {"mp": self.wrapped(self.me + SIDES[side])}


def front_kernel(
    bits,
    frames,
    qkv_weight,
    q_bias,
    v_bias,
    seg_row,
    in_weight,
    down_weight,
    out_weight,
    in_bias,
    input_all,
    qkv_low,
    in_all,
    down_all,
    out_all,
    bias_all,
    seg_col,
    out_cols,
    log_total,
    heads_low,
    bias_buf,
    key_cols,
    value_buf,
    out_buf,
    staged,
    heads_in,
    own_sems,
    frame_send,
    frame_recv,
    bias_send,
    bias_recv,
    first_send,
    first_recv,
    later_send,
    later_recv,
    heads_own,
    heads_send,
    heads_recv,
):
    mp_size = in_all.shape[0]
    me = lax.axis_index("mp")
    dp_index = lax.axis_index("dp")
    local_rows = frames.shape[0]
    half = local_rows // 2
    head_total = out_cols.shape[0]
    orders = gather_orders(bits)[:3]
    parts = ((in_weight, in_all), (down_weight, down_all), (out_weight, out_all))
    line = Line(mp_size, me)
    hops, ways, wrapped = line.hops, line.ways, line.wrapped
    enter(dp_index, me, mp_size, bits)

    def slots(which, level):
        count = parts[which][0].shape[0] // 2 ** len(orders[which])
        start = place_in(dp_index, orders[which]) // 2**level * 2**level
        return pl.ds(pl.multiple_of(start * count, 16), count * 2**level)

    def first_copy(which, side, hop):
        rows = slots(which, 0)
        place = parts[which][1].at[line.place(side, hop), rows]
        source = parts[which][0].at[rows] if hop == 0 else place
        sems = (first_send, first_recv)
        return send(source, place, sems, (which, side, hop), line.neighbour(side))

    def later_copy(which, level, side, hop):
        held = parts[which][1].at[line.place(side, hop + 1), slots(which, level)]
        partner = {"dp": partner_of(dp_index, orders[which][level])}
        return send(held, held, (later_send, later_recv), (which, level, side, hop), partner)

    def frame_rows(index):
        return pl.ds(pl.multiple_of(wrapped(index) * local_rows, local_rows), local_rows)

    def frame_copy(side, hop):
        place = input_all.at[frame_rows(line.chunk(side, hop))]
        source = frames if hop == 0 else place
        return send(source, place, (frame_send, frame_recv), (side, hop), line.neighbour(side))

    def bias_copy(side, hop):
        place = bias_all.at[line.place(side, hop)]
        source = bias_buf if hop == 0 else place
        return send(source, place, (bias_send, bias_recv), (side, hop), line.neighbour(side))

    def project(index):
        rows = frame_rows(index)
        inputs = input_all[rows]
        for part, bias in enumerate((q_bias, None, v_bias)):
            products = dot_rows(inputs, qkv_weight[part])
            if bias is not None:
                products = products + bias[...].astype(F32)
            qkv_low[part, rows] = products.astype(BF16)

    def start_slices(side, hop):
        for which in range(3):
            first_copy(which, side, hop).start()
        bias_copy(side, hop).start()

    def take_slices(side, hop):
        for which in range(3):
            first_copy(which, side, hop).wait_recv()
        bias_copy(side, hop).wait_recv()
        if 0 < hop < mp_size - 2:
            line.if_sent(side, hop + 1)(partial(start_slices, side, hop + 1))
        for which in range(3):
            if orders[which]:
                later_copy(which, 0, side, hop).start()

    def trade_slices(level, side, hop):
        for which in range(3):
            if level < len(orders[which]):
                later_copy(which, level, side, hop).wait_recv()
            if level + 1 < len(orders[which]):
                later_copy(which, level + 1, side, hop).start()

    def take_hop(hop):
        for side in (0, 1):
            line.if_taken(side, hop)(partial(take_slices, side, hop))

    def trade_hop(level, hop):
        for side in (0, 1):
            line.if_taken(side, hop)(partial(trade_slices, level, side, hop))


    bias_buf[...] = jnp.broadcast_to(in_bias[...], bias_buf.shape)
    for side in (0, 1):
        line.if_sent(side, 0)(partial(start_slices, side, 0))
    for side in (0, 1):
        line.if_sent(side, 0)(lambda side=side: frame_copy(side, 0).start())
    own = [
        pltpu.make_async_copy(shard, gathered.at[me], own_sems.at[at])
        for at, (shard, gathered) in enumerate(parts + ((bias_buf, bias_all),))
    ]
    for copy in own:
        copy.start()
    input_all[frame_rows(me)] = frames[...]
    project(me)
    for step in range(BLOCKS):
        ids = jnp.broadcast_to(seg_row[:, step * BLOCK : (step + 1) * BLOCK].astype(F32), (128, BLOCK))
        seg_col[step * BLOCK : (step + 1) * BLOCK] = ids.T.astype(jnp.int32)

    def take_frames(side, hop):
        frame_copy(side, hop).wait_recv()
        if hop + 1 < mp_size - 1:
            line.if_sent(side, hop + 1)(lambda: frame_copy(side, hop + 1).start())

    def project_taken(side, hop):
        project(line.chunk(side, hop + 1))

    for hop in hops:
        for side in (0, 1):
            line.if_taken(side, hop)(partial(take_frames, side, hop))
        if hop == 0:
            take_hop(0)
        elif hop - 1 < bits:
            trade_hop(hop - 1, 0)
        for side in (0, 1):
            free = line.sends(side, hop)
            if hop + 1 < mp_size - 1:
                free = jnp.logical_and(free, jnp.logical_not(line.sends(side, hop + 1)))
            if mp_size > 2:
                passes = jnp.logical_and(free, line.sends(side, 1))
                pl.when(passes)(partial(start_slices, side, 1))
        for side in (0, 1):
            line.if_taken(side, hop)(partial(project_taken, side, hop))

    schedule = (
        (1, take_hop, 1),
        (3, trade_hop, 0, 1),
        (4, take_hop, 2),
        (6, trade_hop, 1, 1),
        (6, trade_hop, 0, 2),
    )
    events = {}
    done = {(take_hop, 0)} | {(trade_hop, hop - 1, 0) for hop in hops if 0 < hop <= bits}
    for at, act, *which in schedule:
        if which[-1] in hops and (act is take_hop or which[0] < bits):
            events.setdefault((at // BLOCKS, at % BLOCKS), []).append(partial(act, *which))
            done.add((act, *which))

    def attend(head):
        cols = slice(head * HEAD_DIM, (head + 1) * HEAD_DIM)
        lane = lax.broadcasted_iota(jnp.int32, (BLOCK, EXTRA), 1)
        for step in range(BLOCKS):
            rows = slice(step * BLOCK, (step + 1) * BLOCK)
            key_cols[step] = qkv_low[1, rows, cols].T
            value_buf[step, :, :HEAD_DIM] = qkv_low[2, rows, cols]
            value_buf[step, :, HEAD_DIM:] = jnp.where(lane == 0, 1.0, 0.0).astype(BF16)

        def query_block(number, _):
            rows = block_rows(number)
            queries = qkv_low[0, rows, cols] * SCALE

            def scores_of(step):
                ids = seg_row[:, step * BLOCK : (step + 1) * BLOCK]
                same = jnp.concatenate([seg_col[rows]] * (BLOCK // 128), axis=1) == ids
                return jnp.where(same, dot(queries, key_cols[step]), MASKED)

            peak = jnp.full((BLOCK, 1), MASKED, F32)
            mixed = jnp.zeros((BLOCK, HEAD_DIM + EXTRA), F32)
            scores = scores_of(0)
            for step in range(BLOCKS):
                ahead = scores_of(step + 1) if step + 1 < BLOCKS else None
                higher = jnp.maximum(peak, jnp.max(scores, axis=1, keepdims=True))
                soft = jnp.exp(scores - higher).astype(BF16)
                mixed = mixed * jnp.exp(peak - higher) + dot(soft, value_buf[step])
                peak, scores = higher, ahead
            total = mixed[:, HEAD_DIM : HEAD_DIM + 1]
            mixed = mixed[:, :HEAD_DIM] / total
            logs = jnp.broadcast_to(peak + jnp.log(total), (BLOCK, HEAD_DIM))
            both = jnp.concatenate([mixed, logs], axis=1).T
            out_cols[head, number] = both[:HEAD_DIM]
            log_total[head, number] = both[HEAD_DIM : HEAD_DIM + 1]
            out_buf[rows] = mixed.astype(BF16)
            for at in range(BLOCKS):
                if (head, at) in events:

                    @pl.when(number == at)
                    def _():
                        for act in events[(head, at)]:
                            act()

            return 0

        lax.fori_loop(0, BLOCKS, query_block, 0)

    def heads_copy(head, offset):
        return send(
            staged.at[head, wrapped(me + offset)],
            heads_in.at[head, me],
            (heads_send, heads_recv),
            (head, offset - 1),
            {"mp": wrapped(me + offset)},
        )

    def heads_own_copy(head):
        return pltpu.make_async_copy(
            staged.at[head, me], heads_in.at[head, me], heads_own.at[head]
        )

    peers = range(1, mp_size)
    for head in range(head_total):
        attend(head)
        for chunk in range(mp_size):
            for side in range(2):
                start = (2 * chunk + side) * half
                staged[head, chunk, :, side * HEAD_DIM : (side + 1) * HEAD_DIM] = out_buf[
                    start : start + half
                ]
        for offset in peers:
            heads_copy(head, offset).start()
        heads_own_copy(head).start()

    for hop in hops:
        if (take_hop, hop) not in done:
            take_hop(hop)
    for level in range(bits):
        for hop in hops:
            if (trade_hop, level, hop) not in done:
                trade_hop(level, hop)
    for head in range(head_total):
        heads_own_copy(head).wait()
        for offset in peers:
            heads_copy(head, offset).wait_recv()
        for chunk in range(mp_size):
            for side in range(2):
                at = (chunk * head_total + head) * HEAD_DIM
                heads_low[side * half : (side + 1) * half, at : at + HEAD_DIM] = heads_in[
                    head, chunk, :, side * HEAD_DIM : (side + 1) * HEAD_DIM
                ]
        for offset in peers:
            heads_copy(head, offset).wait_send()

    def sent_all(side, hop):
        frame_copy(side, hop).wait_send()
        bias_copy(side, hop).wait_send()
        for which in range(3):
            first_copy(which, side, hop).wait_send()

    def sent_later(side, hop):
        for which in range(3):
            for level in range(len(orders[which])):
                later_copy(which, level, side, hop).wait_send()

    for side, hop in ways:
        line.if_sent(side, hop)(partial(sent_all, side, hop))
        line.if_taken(side, hop)(partial(sent_later, side, hop))
    for copy in own:
        copy.wait()


def front(frames, qkv_weight, q_bias, v_bias, seg_row, weights, in_bias, mp_size, bits):
    local_rows, width = frames.shape
    head_cols = qkv_weight.shape[1]
    head_total = head_cols // HEAD_DIM
    peers = mp_size - 1
    levels = max(bits, 1)
    anywhere = pl.BlockSpec(memory_space=pl.ANY)
    in_weight, down_weight, out_weight = weights

    def sems(*shapes):
        return [pltpu.SemaphoreType.DMA(shape) for shape in shapes for _ in range(2)]

    piece = (head_total, mp_size, local_rows // 2, 2 * HEAD_DIM)
    return pl.pallas_call(
        partial(front_kernel, bits),
        out_shape=(
            jax.ShapeDtypeStruct((ROW_LEN, width), BF16),
            jax.ShapeDtypeStruct((3, ROW_LEN, head_cols), BF16),
            jax.ShapeDtypeStruct((mp_size,) + in_weight.shape, BF16),
            jax.ShapeDtypeStruct((mp_size,) + down_weight.shape, BF16),
            jax.ShapeDtypeStruct((mp_size,) + out_weight.shape, BF16),
            jax.ShapeDtypeStruct((mp_size, 16, in_bias.shape[1]), BF16),
            jax.ShapeDtypeStruct((ROW_LEN, 128), jnp.int32),
            jax.ShapeDtypeStruct((head_total, BLOCKS, HEAD_DIM, BLOCK), F32),
            jax.ShapeDtypeStruct((head_total, BLOCKS, 1, BLOCK), F32),
            jax.ShapeDtypeStruct((local_rows, width), BF16),
        ),
        in_specs=[whole()] * 5 + [anywhere] * 3 + [whole()],
        out_specs=(whole(), whole()) + (anywhere,) * 4 + (whole(),) * 4,
        scratch_shapes=[
            pltpu.VMEM((16, in_bias.shape[1]), BF16),
            pltpu.VMEM((BLOCKS, HEAD_DIM, BLOCK), BF16),
            pltpu.VMEM((BLOCKS, BLOCK, HEAD_DIM + EXTRA), BF16),
            pltpu.VMEM((ROW_LEN, HEAD_DIM), BF16),
            pltpu.VMEM(piece, BF16),
            pltpu.VMEM(piece, BF16),
            pltpu.SemaphoreType.DMA((4,)),
            *sems((2, peers), (2, peers), (3, 2, peers), (3, levels, 2, peers)),
            pltpu.SemaphoreType.DMA((head_total,)),
            *sems((head_total, peers)),
        ],
        compiler_params=pltpu.CompilerParams(
            collective_id=0, has_side_effects=True, vmem_limit_bytes=VMEM_BYTES
        ),
        cost_estimate=pl.CostEstimate(
            flops=16 * head_total * ROW_LEN * ROW_LEN * HEAD_DIM,
            bytes_accessed=32 * 1024 * 1024,
            transcendentals=head_total * ROW_LEN * ROW_LEN,
        ),
        name="front",
    )(frames, qkv_weight, q_bias, v_bias, seg_row, in_weight, down_weight, out_weight, in_bias)


def reduce_orders(bits):
    if bits == 3:
        return ((0, 1, 2), (0, 2, 1), (1, 2, 0))
    return (tuple(range(bits)),) * 3


def norm_rows(inputs, norm_gain, norm_shift):
    row_mean = jnp.mean(inputs, axis=-1, keepdims=True)
    centred = inputs - row_mean
    variance = jnp.mean(centred * centred, axis=-1, keepdims=True)
    inv_std = lax.rsqrt(variance + 1e-05)
    normed = centred * inv_std
    return (normed * norm_gain + norm_shift, normed, inv_std)


def norm_back(cotangent, normed, inv_std, norm_gain):
    scaled = cotangent * norm_gain
    adjusted = (
        scaled
        - jnp.mean(scaled, axis=-1, keepdims=True)
        - normed * jnp.mean(scaled * normed, axis=-1, keepdims=True)
    )
    return adjusted * inv_std


def sum_rows(array):
    return jnp.sum(array.astype(F32), axis=0, keepdims=True)


def rear_kernel(
    bits,
    seg_row,
    in_bias,
    out_bias,
    down_bias,
    norm_gain,
    norm_shift,
    frames,
    heads_low,
    out_grad,
    in_all,
    down_all,
    out_all,
    proj_weight,
    qkv_source,
    out_source,
    log_source,
    seg_source,
    input_source,
    block_out,
    resid_grad,
    in_grads,
    down_grads,
    head_grads,
    proj_all,
    traded,
    in_sum,
    down_sum,
    head_sum,
    proj_sum,
    vector_sum,
    bias_sum,
    grads_out,
    grads_in,
    kept,
    taken,
    last,
    direct,
    proj,
    proj_taken,
    proj_slots,
    vectors,
    vectors_taken,
    vectors_all,
    biases,
    load_sems,
    in_sems,
    down_sems,
    out_sems,
    given_sems,
    head_sem,
    store_sems,
    attention_sems,
    weight_own,
    weight_send,
    weight_recv,
    weight_trade_send,
    weight_trade_recv,
    keep_sems,
    grads_own,
    grads_send,
    grads_recv,
    traded_own,
    traded_send,
    traded_recv,
    level_send,
    level_recv,
    last_send,
    last_recv,
    direct_send,
    direct_recv,
    back_send,
    back_recv,
    proj_send,
    proj_recv,
    vector_send,
    vector_recv,
    vector_last_send,
    vector_last_recv,
    bias_send,
    bias_recv,
):
    mp_size, units, width = down_all.shape
    head_total = grads_out.shape[1]
    half = grads_out.shape[2]
    head_cols = width // mp_size
    slots = 2**bits
    me = lax.axis_index("mp")
    dp_index = lax.axis_index("dp")
    peers = range(1, mp_size)
    turns = range(mp_size)
    levels = list(range(bits))
    orders = reduce_orders(bits)
    partials = (in_grads, down_grads, head_grads)
    sums = (in_sum, down_sum, head_sum)
    arrays = range(3)
    vector = vectors[0]
    place = lax.rem(dp_index, slots)
    mates = range(1, slots)
    odd = lax.rem(me, 2)
    leaving = (2, 3 - 2 * odd, 1 + 2 * odd) if mp_size == 4 else peers

    def target(offset):
        return lax.rem(me + offset, mp_size)

    def bit_of(which, level):
        return (dp_index // 2 ** orders[which][level]) % 2


    def part_of(turn):
        return target(turn + 1)

    def level_copy(which, level, turn):
        count = 2 ** (bits - 1 - level)
        other = (1 - bit_of(which, level)) * count
        part = pl.ds(part_of(turn), 1)
        source = partials[which] if level == 0 else taken[which][level - 1]
        return send(
            source.at[part, pl.ds(other, count)],
            taken[which][level].at[part],
            (level_send, level_recv),
            (which, level, turn),
            {"dp": partner_of(dp_index, orders[which][level])},
        )

    def keep_copy(which, turn):
        count = 2 ** (bits - 1)
        return pltpu.make_async_copy(
            partials[which].at[part_of(turn), pl.ds(bit_of(which, 0) * count, count)],
            kept[which].at[turn % 2],
            keep_sems.at[which, turn % 2],
        )

    def direct_copy(offset):
        return send(
            taken[0][bits - 1].at[target(offset)],
            direct.at[offset - 1],
            (direct_send, direct_recv),
            offset - 1,
            {"mp": target(offset)},
        )

    def last_copy(which, side, part):
        return send(
            taken[which][bits - 1].at[part, 0],
            last[which].at[side, part],
            (last_send, last_recv),
            (which, side, part),
            line.neighbour(side),
        )

    def add_last(which, side, part):
        last_copy(which, side, part).wait_recv()
        total = taken[which][bits - 1][part, 0].astype(F32) + last[which][side, part].astype(F32)
        taken[which][bits - 1][part, 0] = total.astype(BF16)

    def pass_on(which, stage):
        for side in (0, 1):
            at = stage if side == 0 else mp_size - 1 - stage
            beyond = range(at + 1, mp_size) if side == 0 else range(at)

            @pl.when(me == at)
            def _():
                for part in beyond:
                    if stage:
                        add_last(which, side, part)
                    last_copy(which, side, part).start()

    def add_level(which, level, turn):
        level_copy(which, level, turn).wait_recv()
        count = 2 ** (bits - 1 - level)
        if level == 0:
            keep_copy(which, turn).wait()
        start = bit_of(which, level) * count
        into = taken[which][level]
        part = part_of(turn)
        for slot in range(count):
            if level == 0:
                mine = kept[which][turn % 2, slot]
            else:
                mine = taken[which][level - 1][part, start + slot]
            into[part, slot] = (into[part, slot].astype(F32) + mine.astype(F32)).astype(BF16)
        if level == 0 and turn + 2 < mp_size:
            keep_copy(which, turn + 2).start()
        if level + 1 < bits:
            level_copy(which, level + 1, turn).start()
        elif which == 0 and turn + 1 < mp_size:
            direct_copy(turn + 1).start()

    def offer(which, turn):
        level_copy(which, 0, turn).start()
        if turn < 2:
            keep_copy(which, turn).start()

    def slot_of(order):
        return place_in(dp_index, order[::-1])

    def held_slots(order, level):
        count = 2 ** (bits - 1 - level)
        return pl.ds(slot_of(order) // count * count, count)

    def spread_copy(which, level):
        held = sums[which].at[held_slots(orders[which], level)]
        partner = {"dp": partner_of(dp_index, orders[which][level])}
        return send(held, held, (back_send, back_recv), (which, level), partner)

    def finish_sum(which):
        if which == 0:
            total = taken[0][bits - 1][me, 0].astype(F32)
            for offset in peers:
                direct_copy(offset).wait_recv()
                total = total + direct[offset - 1, 0].astype(F32)
            sums[0][slot_of(orders[0])] = total.astype(BF16)
        else:
            pl.when(me > 0)(lambda: add_last(which, 0, me))
            pl.when(me < mp_size - 1)(lambda: add_last(which, 1, me))
            sums[which][slot_of(orders[which])] = taken[which][bits - 1][me, 0]
        spread_copy(which, bits - 1).start()

    def spread(which, level):
        spread_copy(which, level).wait_recv()
        if level:
            spread_copy(which, level - 1).start()


    def mate(offset):
        return {"dp": mate_of(dp_index, offset, slots)}

    def proj_copy(head, offset):
        return send(
            proj[head].at[lax.rem(place + offset, slots)],
            proj_taken[head].at[offset - 1],
            (proj_send, proj_recv),
            (0, head, offset - 1),
            mate(offset),
        )

    def proj_spread_copy(head, offset):
        held = proj_slots[head].at[place]
        return send(held, held, (proj_send, proj_recv), (1, head, offset - 1), mate(offset))

    def sum_proj(head):
        total = proj[head][place].astype(F32)
        for offset in mates:
            proj_copy(head, offset).wait_recv()
            total = total + proj_taken[head][offset - 1].astype(F32)
        proj_slots[head][place] = total.astype(BF16)
        for offset in mates:
            proj_spread_copy(head, offset).start()

    def take_proj(head):
        for offset in mates:
            proj_spread_copy(head, offset).wait_recv()


    def vector_copy(level):
        return send(
            vectors[level],
            vectors_taken[level],
            (vector_send, vector_recv),
            level,
            {"dp": partner_of(dp_index, level)},
        )

    def vector_last_copy(offset):
        return send(
            vectors[bits],
            vectors_all.at[me],
            (vector_last_send, vector_last_recv),
            offset - 1,
            {"mp": target(offset)},
        )

    def add_vector(level):
        vector_copy(level).wait_recv()
        vectors[level + 1][...] = vectors[level][...] + vectors_taken[level][...]
        if level + 1 < bits:
            vector_copy(level + 1).start()
        else:
            vectors_all[me] = vectors[bits][...]
            for offset in peers:
                vector_last_copy(offset).start()

    def finish_vector():
        for offset in peers:
            vector_last_copy(offset).wait_recv()
        total = vectors_all[0]
        for index in peers:
            total = total + vectors_all[index]
        vector_sum[...] = total

    def bias_copy(offset):
        held = biases.at[place]
        return send(held, held, (bias_send, bias_recv), offset - 1, mate(offset))

    def sum_bias():
        for offset in mates:
            bias_copy(offset).wait_recv()
        total = biases[0]
        for at in range(1, slots):
            total = total + biases[at]
        bias_sum[...] = total

    def grads_copy(head, offset):
        return send(
            grads_out.at[target(offset), head],
            grads_in.at[head, me],
            (grads_send, grads_recv),
            (head, offset - 1),
            {"mp": target(offset)},
        )

    def grads_own_copy(head):
        return pltpu.make_async_copy(
            grads_out.at[me, head], grads_in.at[head, me], grads_own.at[head]
        )

    line = Line(mp_size, me)
    order = gather_orders(bits)[3]
    own_slot = place_in(dp_index, order)

    def weight_copy(side, hop):
        place = proj_all.at[line.place(side, hop), pl.ds(own_slot, 1)]
        source = proj_weight.at[pl.ds(own_slot, 1)] if hop == 0 else place
        return send(source, place, (weight_send, weight_recv), (side, hop), line.neighbour(side))

    def weight_trade_copy(level, side, hop):
        held = pl.ds(own_slot // 2**level * 2**level, 2**level)
        place = proj_all.at[line.place(side, hop + 1), held]
        partner = {"dp": partner_of(dp_index, order[level])}
        return send(place, place, (weight_trade_send, weight_trade_recv), (level, side, hop), partner)

    def take_weight(side, hop):
        weight_copy(side, hop).wait_recv()
        if hop + 1 < mp_size - 1:
            line.if_sent(side, hop + 1)(lambda: weight_copy(side, hop + 1).start())
        if bits:
            weight_trade_copy(0, side, hop).start()

    def trade_weight(level, side, hop):
        weight_trade_copy(level, side, hop).wait_recv()
        if level + 1 < bits:
            weight_trade_copy(level + 1, side, hop).start()

    def both_sides(act, *which):
        for side in (0, 1):
            line.if_taken(side, which[-1])(partial(act, *which[:-1], side, which[-1]))

    schedule = (
        (0, take_weight, 0),
        (1, take_weight, 1),
        (2, take_weight, 2),
        (2, trade_weight, 0, 0),
        (3, trade_weight, 0, 1),
        (3, trade_weight, 0, 2),
        (4, trade_weight, 1, 0),
        (6, trade_weight, 1, 1),
        (8, trade_weight, 1, 2),
    )
    done = set()

    def at_point(point, index=None):
        for at, act, *which in schedule:
            if which[-1] not in line.hops or (act is trade_weight and which[0] >= bits):
                continue
            if index is None and at == point:
                both_sides(act, *which)
                done.add((act, *which))
            if index is not None and point <= at < point + mp_size:
                pl.when(index == at - point)(partial(both_sides, act, *which))
                done.add((act, *which))

    def dense_phase(
        frames_buf,
        heads_buf,
        cotangent_buf,
        in_buf,
        down_buf,
        out_buf,
        hidden,
        slope,
        mid_buf,
        normed_buf,
        store_buf,
        low_buf,
        grad_buf,
        given,
        head_buf,
    ):
        loads = [
            pltpu.make_async_copy(source, into, load_sems.at[at])
            for at, (source, into) in enumerate(
                ((frames, frames_buf), (heads_low, heads_buf), (out_grad, cotangent_buf))
            )
        ]
        out_copies = [
            pltpu.make_async_copy(
                out_all.at[index],
                out_buf.at[pl.ds(index * head_cols, head_cols)],
                out_sems.at[index],
            )
            for index in range(mp_size)
        ]

        def in_copy(index):
            return pltpu.make_async_copy(in_all.at[index], in_buf.at[index], in_sems.at[index])

        def down_copy(index):
            return pltpu.make_async_copy(
                down_all.at[index], down_buf.at[index], down_sems.at[index]
            )

        def given_copy(which, turn):
            return pltpu.make_async_copy(
                given.at[turn % 2], partials[which].at[part_of(turn)], given_sems.at[turn % 2]
            )

        def store_copy(at):
            return pltpu.make_async_copy(
                store_buf, (block_out, resid_grad)[at], store_sems.at[at]
            )

        for copy in loads + out_copies:
            copy.start()
        for index in range(mp_size):
            in_copy(index).start()
            down_copy(index).start()
        enter(dp_index, me, mp_size, bits, whole_group=True)
        for side in (0, 1):
            line.if_sent(side, 0)(lambda side=side: weight_copy(side, 0).start())
        weight_own_copy.start()
        vector[...] = jnp.zeros_like(vector)
        gains = norm_gain[...].astype(F32)
        shifts = norm_shift[...].astype(F32)
        both = [slice(side * half, (side + 1) * half) for side in range(2)]

        for copy in loads + out_copies:
            copy.wait()
        branch = dot(heads_buf[...], out_buf[...]) + out_bias[...].astype(F32)
        mid, normed, inv_mid = norm_rows(
            frames_buf[...].astype(F32) + branch, gains[:1], shifts[:1]
        )
        mid_buf[...] = mid + down_bias[...].astype(F32)
        normed_buf[...] = normed
        low_buf[...] = mid.astype(BF16)
        at_point(0)

        def feed(index, _):
            in_copy(index).wait()
            down_copy(index).wait()
            for rows in both:
                pre_act = dot(low_buf[rows], in_buf[index]) + in_bias[index, 0:1].astype(F32)
                unit_cdf = 0.5 * (1.0 + lax.erf(pre_act * 0.5**0.5))
                bell = jnp.exp(-0.5 * pre_act * pre_act) * (2.0 * jnp.pi) ** (-0.5)
                slope[index, rows] = (unit_cdf + pre_act * bell).astype(BF16)
                hidden[index, rows] = (pre_act * unit_cdf).astype(BF16)
                mid_buf[rows] += dot(hidden[index, rows], down_buf[index])
            at_point(1, index)
            return 0

        lax.fori_loop(0, mp_size, feed, 0)
        output, normed, inv_out = norm_rows(mid_buf[...], gains[1:], shifts[1:])
        store_buf[...] = output
        store_copy(0).start()

        cotangent = cotangent_buf[...].astype(F32)
        vector[1:2] = sum_rows(cotangent * normed)
        vector[3:4] = sum_rows(cotangent)
        sum_grad = norm_back(cotangent, normed, inv_out, gains[1:])
        mid_buf[...] = sum_grad
        grad_buf[...] = sum_grad.astype(BF16)
        vector[5:6] = sum_rows(grad_buf[...])

        def give(which, turn, result):
            if turn >= 2:
                offer_given(which, turn - 2)
            share = result.shape[0] // slots
            for slot in range(slots):
                given[turn % 2, slot] = result[slot * share : (slot + 1) * share].astype(BF16)
            given_copy(which, turn).start()

        def offer_given(which, turn):
            given_copy(which, turn).wait()
            offer(which, turn)

        for turn in turns:
            index = part_of(turn)
            give(1, turn, dot_cols(hidden[index], grad_buf[...]))
            pre = dot_rows(grad_buf[...], down_buf[index]) * slope[index].astype(F32)
            hidden[index] = pre.astype(BF16)
            vector[pl.ds(8 + index, 1)] = sum_rows(hidden[index])
            mid_buf[...] += dot_rows(hidden[index], in_buf[index])
            at_point(1 + mp_size + turn)
        for turn in turns[-2:]:
            offer_given(1, turn)
        mid_grad = mid_buf[...]
        vector[0:1] = sum_rows(mid_grad * normed_buf[...])
        vector[2:3] = sum_rows(mid_grad)
        resid = norm_back(mid_grad, normed_buf[...], inv_mid, gains[:1])
        store_copy(0).wait()
        store_buf[...] = resid
        store_copy(1).start()
        attn_grad = resid.astype(BF16)
        grad_buf[...] = attn_grad
        vector[4:5] = sum_rows(attn_grad)
        heads_grad = dot_rows(attn_grad, out_buf[...]).astype(BF16)
        for head in range(head_total):
            for index in range(mp_size):
                at = index * head_cols + head * HEAD_DIM
                for side in range(2):
                    grads_out[index, head, :, side * HEAD_DIM : (side + 1) * HEAD_DIM] = (
                        heads_grad[both[side], at : at + HEAD_DIM]
                    )
            if head == 0:
                for offset in leaving:
                    grads_copy(0, offset).start()
        for head in range(head_total):
            grads_own_copy(head).start()
        vector_copy(0).start()

        products = dot_cols(heads_buf[...], grad_buf[...]).astype(BF16)
        rows = head_cols // slots
        for index in range(mp_size):
            for slot in range(slots):
                start = index * head_cols + slot * rows
                head_buf[index, slot, :rows] = products[start : start + rows]
                if rows < head_buf.shape[2]:
                    head_buf[index, slot, rows:] = jnp.zeros(
                        (head_buf.shape[2] - rows, width), BF16
                    )
        head_copy = pltpu.make_async_copy(head_buf, head_grads, head_sem)
        head_copy.start()
        normed_low = low_buf[...].T
        for turn in turns:
            give(0, turn, dot(normed_low, hidden[part_of(turn)]))
            if turn == 0:
                head_copy.wait()
                for at in turns:
                    offer(2, at)
                for later in range(1, head_total):
                    for offset in leaving:
                        grads_copy(later, offset).start()
        for turn in turns[-2:]:
            offer_given(0, turn)
        store_copy(1).wait()

    weight_own_copy = pltpu.make_async_copy(proj_weight, proj_all.at[me], weight_own)
    rows_low = pltpu.VMEM((2 * half, width), BF16)
    rows_full = pltpu.VMEM((2 * half, width), F32)
    pl.run_scoped(
        dense_phase,
        rows_low,
        rows_low,
        rows_low,
        pltpu.VMEM((mp_size, width, units), BF16),
        pltpu.VMEM((mp_size, units, width), BF16),
        pltpu.VMEM((width, width), BF16),
        pltpu.VMEM((mp_size, 2 * half, units), BF16),
        pltpu.VMEM((mp_size, 2 * half, units), BF16),
        rows_full,
        rows_full,
        rows_full,
        rows_low,
        rows_low,
        pltpu.VMEM((2, slots, units // slots, width), BF16),
        pltpu.VMEM(head_grads.shape, BF16),
    )

    def attention_phase(
        qkv,
        out_cols,
        log_total,
        seg_col,
        input_all,
        staged,
        qkv_grad,
        seg_blocks,
        grads,
        key_buf,
        key_cols,
        value_buf,
        query_sum,
        key_sum,
        value_sum,
        proj_rows,
    ):
        def traded_copy(head, offset):
            return send(
                staged.at[head, target(offset)],
                traded.at[head, me],
                (traded_send, traded_recv),
                (head, offset - 1),
                {"mp": target(offset)},
            )

        def traded_own_copy(head):
            return pltpu.make_async_copy(
                staged.at[head, me], traded.at[head, me], traded_own.at[head]
            )

        def prepare(head):
            cols = slice(head * HEAD_DIM, (head + 1) * HEAD_DIM)
            key_buf[:, :HEAD_DIM] = qkv[1, :, cols]
            key_buf[:, HEAD_DIM:] = ones_columns(ROW_LEN)
            value_buf[:, :HEAD_DIM] = qkv[2, :, cols]
            value_buf[:, HEAD_DIM:] = ones_columns(ROW_LEN)
            for step in range(BLOCKS):
                key_cols[step] = qkv[1, step * BLOCK : (step + 1) * BLOCK, cols].T
            key_sum[...] = jnp.zeros_like(key_sum)
            value_sum[...] = jnp.zeros_like(value_sum)

        def take_grads(head):
            grads_own_copy(head).wait()
            for offset in peers:
                grads_copy(head, offset).wait_recv()
            for chunk in range(mp_size):
                for side in range(2):
                    start = (2 * chunk + side) * half
                    grads[start : start + half] = grads_in[
                        head, chunk, :, side * HEAD_DIM : (side + 1) * HEAD_DIM
                    ]

        def attend_back(head):
            cols = slice(head * HEAD_DIM, (head + 1) * HEAD_DIM)

            def query_block(number, _):
                rows = block_rows(number)
                queries = qkv[0, rows, cols] * SCALE
                grad_rows = grads[rows]
                seg_query = seg_blocks[number]
                grad_cols = grad_rows.astype(F32).T
                row_dot = jnp.sum(grad_cols * out_cols[head, number], axis=0, keepdims=True)
                grad_cols = jnp.concatenate([grad_cols.astype(BF16), as_pieces(-row_dot)], axis=0)
                query_cols = jnp.concatenate(
                    [queries.astype(F32).T.astype(BF16), as_pieces(-log_total[head, number])], axis=0
                )

                def products_of(step):
                    key_rows = slice(step * BLOCK, (step + 1) * BLOCK)
                    same = (
                        jnp.concatenate([seg_col[key_rows]] * (BLOCK // 128), axis=1) == seg_query
                    )
                    scores = jnp.where(same, dot(key_buf[key_rows], query_cols), MASKED)
                    return scores, dot(value_buf[key_rows], grad_cols)

                query_grad = jnp.zeros((HEAD_DIM, BLOCK), F32)
                ahead = products_of(0)
                for step in range(BLOCKS):
                    scores, soft_grad = ahead
                    if step + 1 < BLOCKS:
                        ahead = products_of(step + 1)
                    key_rows = slice(step * BLOCK, (step + 1) * BLOCK)
                    soft = jnp.exp(scores)
                    score_grad = (soft * soft_grad).astype(BF16)
                    value_sum[key_rows] += dot(soft.astype(BF16), grad_rows)
                    key_sum[key_rows] += dot(score_grad, queries)
                    query_grad = query_grad + dot(key_cols[step], score_grad)
                query_sum[rows] = (query_grad * SCALE).T
                for at in range(head * BLOCKS, (head + 1) * BLOCKS):
                    if at in events:

                        @pl.when(number == at - head * BLOCKS)
                        def _():
                            for act in events[at]:
                                act()

                return 0

            lax.fori_loop(0, BLOCKS, query_block, 0)

        def give_grads(head):
            for part, total in enumerate((query_sum, key_sum, value_sum)):
                low = total[...].astype(BF16)
                qkv_grad[:, part * HEAD_DIM : (part + 1) * HEAD_DIM] = low
                if part != 1:
                    cols = slice(head * HEAD_DIM, (head + 1) * HEAD_DIM)
                    sum_low = jnp.sum(low.astype(F32), axis=0, keepdims=True)
                    biases[place, part : part + 1, cols] = sum_low
                for chunk in range(mp_size):
                    for side in range(2):
                        start = (2 * chunk + side) * half
                        staged[head, chunk, part, :, side * HEAD_DIM : (side + 1) * HEAD_DIM] = total[
                            start : start + half
                        ].astype(BF16)

        def start_trade(head):
            for offset in leaving:
                traded_copy(head, offset).start()
            traded_own_copy(head).start()

        def start_proj(head):
            products = dot_cols(qkv_grad[...], input_all[...])
            slot_rows = proj[head].shape[1]
            for slot in range(2**bits):
                proj[head][slot] = products[slot * slot_rows : (slot + 1) * slot_rows].astype(BF16)
            for offset in mates:
                proj_copy(head, offset).start()

        def finish_proj(head):
            cols = slice(head * HEAD_DIM, (head + 1) * HEAD_DIM)
            slot_rows = proj_slots[head].shape[1]
            for slot in range(2**bits):
                proj_rows[slot * slot_rows : (slot + 1) * slot_rows] = proj_slots[head][slot].astype(F32)
            for part in range(3):
                rows = proj_rows[part * HEAD_DIM : (part + 1) * HEAD_DIM]
                proj_sum[part, cols] = rows.astype(BF16)

        events = {}
        rest = []

        def due(at, act, *which):
            if at is None:
                rest.append((act, *which))
            else:
                events.setdefault(at, []).append(partial(act, *which))

        for at, level in zip((0, 1, 2), levels):
            due(at, add_vector, level)
        due(2.5, finish_vector)
        times = {
            1: ((0, 0, 0, 0), (2, 2.5, 3, 4), (2.5, 3, 4, 5)),
            2: ((2.5, 2.5, 2.5, 2.5), (4, 4, 4, 4), (5, 5, 5, 5)),
            0: ((1, 2.5, 3, 4), (2.5, 4, 5, 5.5), (3, 5, 5.5, 6)),
        }
        stages = {1: (4, 5, 5.5), 2: (5, 5.5, 6)}
        ends = {1: (6, 7, 8, None), 2: (7, 8, None, None), 0: (7, 8, None, None)}
        for level in levels:
            for which in times:
                for turn, at in zip(turns, times[which][level]):
                    due(at, add_level, which, level, turn)
        for stage in range(mp_size - 1):
            for which in stages:
                due(stages[which][stage], pass_on, which, stage)
        due(3, sum_proj, 0)
        due(5, take_proj, 0)
        due(6, sum_proj, 1)
        due(8, take_proj, 1)
        for which in (1, 2, 0):
            due(ends[which][0], finish_sum, which)
        for step, level in enumerate(levels[::-1]):
            for which in (0, 1, 2):
                due(ends[which][1 + step], spread, which, level)

        copies = [
            pltpu.make_async_copy(source, into, attention_sems.at[at])
            for at, (source, into) in enumerate(
                (
                    (qkv_source, qkv),
                    (seg_source, seg_col),
                    (log_source, log_total),
                    (out_source, out_cols),
                    (input_source, input_all),
                )
            )
        ]
        for copy in copies:
            copy.start()
        biases[place] = jnp.zeros(bias_sum.shape, F32)
        for step in range(BLOCKS):
            seg_blocks[step] = seg_row[:, step * BLOCK : (step + 1) * BLOCK]
        final = head_total - 1
        copies[0].wait()
        for head in range(head_total):
            prepare(head)
            take_grads(head)
            if head == 0:
                for copy in copies[1:4]:
                    copy.wait()
            attend_back(head)
            give_grads(head)
            start_trade(head)
            if head == 0:
                copies[4].wait()
            start_proj(head)
            for act in events.get((head + 1) * BLOCKS - 0.5, ()):
                act()
        for offset in mates:
            bias_copy(offset).start()
        if rest:
            act, *which = rest.pop(0)
            act(*which)
        sum_proj(final)
        sum_bias()
        for act, *which in rest:
            act(*which)
        take_proj(final)
        for head in range(head_total):
            finish_proj(head)
            traded_own_copy(head).wait()
            for offset in peers:
                traded_copy(head, offset).wait()

    pl.run_scoped(
        attention_phase,
        pltpu.VMEM(qkv_source.shape, BF16),
        pltpu.VMEM(out_source.shape, F32),
        pltpu.VMEM(log_source.shape, F32),
        pltpu.VMEM(seg_source.shape, jnp.int32),
        pltpu.VMEM(input_source.shape, BF16),
        pltpu.VMEM((head_total, mp_size, 3, half, 2 * HEAD_DIM), BF16),
        pltpu.VMEM((ROW_LEN, 3 * HEAD_DIM), BF16),
        pltpu.VMEM((BLOCKS, 1, BLOCK), jnp.int32),
        pltpu.VMEM((ROW_LEN, HEAD_DIM), BF16),
        pltpu.VMEM((ROW_LEN, HEAD_DIM + EXTRA), BF16),
        pltpu.VMEM((BLOCKS, HEAD_DIM, BLOCK), BF16),
        pltpu.VMEM((ROW_LEN, HEAD_DIM + EXTRA), BF16),
        pltpu.VMEM((ROW_LEN, HEAD_DIM), F32),
        pltpu.VMEM((ROW_LEN, HEAD_DIM), F32),
        pltpu.VMEM((ROW_LEN, HEAD_DIM), F32),
        pltpu.VMEM((3 * HEAD_DIM, width), F32),
    )

    for hop in line.hops:
        if (take_weight, hop) not in done:
            both_sides(take_weight, hop)
    for level in levels:
        for hop in line.hops:
            if (trade_weight, level, hop) not in done:
                both_sides(trade_weight, level, hop)

    def sent_trades(side, hop):
        for level in levels:
            weight_trade_copy(level, side, hop).wait_send()

    for side, hop in line.ways:
        line.if_sent(side, hop)(lambda side=side, hop=hop: weight_copy(side, hop).wait_send())
        line.if_taken(side, hop)(partial(sent_trades, side, hop))
    weight_own_copy.wait()
    for head in range(head_total):
        for offset in peers:
            grads_copy(head, offset).wait_send()
        for offset in mates:
            proj_copy(head, offset).wait_send()
            proj_spread_copy(head, offset).wait_send()
    for offset in mates:
        bias_copy(offset).wait_send()
    for level in levels:
        vector_copy(level).wait_send()
        for which in arrays:
            spread_copy(which, level).wait_send()
            for turn in turns:
                level_copy(which, level, turn).wait_send()
    for offset in peers:
        vector_last_copy(offset).wait_send()
        direct_copy(offset).wait_send()

    def sent_last(side, part):
        for which in (1, 2):
            last_copy(which, side, part).wait_send()

    for part in turns:
        pl.when(me < part)(partial(sent_last, 0, part))
        pl.when(me > part)(partial(sent_last, 1, part))


def rear(frames, heads_low, out_grad, seg_row, in_bias, small, weights, proj_weight, saved, bits):
    local_rows, width = frames.shape
    qkv_low, out_cols = saved[:2]
    mp_size, units = weights[1].shape[:2]
    head_total = out_cols.shape[0]
    half, lanes = local_rows // 2, 2 * HEAD_DIM
    peers = mp_size - 1
    slots = 2**bits
    head_rows = -(-width // mp_size // slots // 16) * 16
    anywhere = pl.BlockSpec(memory_space=pl.ANY)
    blocks = [(width // slots, units), (units // slots, width), (head_rows, width)]
    proj_block = (3 * HEAD_DIM // slots, width)
    bias_block = (8, 2 * 128)
    vector_block = (8 + -(-mp_size // 8) * 8, width)

    def halves(shape, lead=()):
        return [pltpu.VMEM(lead + (slots >> (level + 1),) + shape, BF16) for level in range(bits)]

    def sems(*shapes):
        return [pltpu.SemaphoreType.DMA(shape) for shape in shapes for _ in range(2)]

    piece = pltpu.VMEM((mp_size, head_total, half, lanes), BF16)
    return pl.pallas_call(
        partial(rear_kernel, bits),
        out_shape=(
            jax.ShapeDtypeStruct((local_rows, width), F32),
            jax.ShapeDtypeStruct((local_rows, width), F32),
            *(jax.ShapeDtypeStruct((mp_size, slots) + block, BF16) for block in blocks),
            jax.ShapeDtypeStruct((mp_size,) + proj_weight.shape, BF16),
            jax.ShapeDtypeStruct((head_total, mp_size, 3, half, lanes), BF16),
            *(jax.ShapeDtypeStruct((slots,) + block, BF16) for block in blocks),
            jax.ShapeDtypeStruct((3, head_total * HEAD_DIM, width), BF16),
            jax.ShapeDtypeStruct(vector_block, F32),
            jax.ShapeDtypeStruct(bias_block, F32),
        ),
        in_specs=[whole()] * 6 + [anywhere] * 12,
        out_specs=(anywhere,) * 7 + (whole(),) * 6,
        scratch_shapes=[
            piece,
            pltpu.VMEM((head_total, mp_size, half, lanes), BF16),
            [pltpu.VMEM((2, slots // 2) + block, BF16) for block in blocks],
            [halves(block, (mp_size,)) for block in blocks],
            [pltpu.VMEM((2, mp_size) + block, BF16) for block in blocks],
            pltpu.VMEM((peers, 1) + blocks[0], BF16),
            [pltpu.VMEM((slots,) + proj_block, BF16) for _ in range(head_total)],
            [pltpu.VMEM((slots - 1,) + proj_block, BF16) for _ in range(head_total)],
            [pltpu.VMEM((slots,) + proj_block, BF16) for _ in range(head_total)],
            [pltpu.VMEM(vector_block, F32) for _ in range(bits + 1)],
            [pltpu.VMEM(vector_block, F32) for _ in range(bits)],
            pltpu.VMEM((mp_size,) + vector_block, F32),
            pltpu.VMEM((slots,) + bias_block, F32),
            pltpu.SemaphoreType.DMA((3,)),
            pltpu.SemaphoreType.DMA((mp_size,)),
            pltpu.SemaphoreType.DMA((mp_size,)),
            pltpu.SemaphoreType.DMA((mp_size,)),
            pltpu.SemaphoreType.DMA((2,)),
            pltpu.SemaphoreType.DMA,
            pltpu.SemaphoreType.DMA((2,)),
            pltpu.SemaphoreType.DMA((5,)),
            pltpu.SemaphoreType.DMA,
            *sems((2, peers), (max(bits, 1), 2, peers)),
            pltpu.SemaphoreType.DMA((3, 2)),
            pltpu.SemaphoreType.DMA((head_total,)),
            *sems((head_total, peers)),
            pltpu.SemaphoreType.DMA((head_total,)),
            *sems(
                (head_total, peers),
                (3, bits, mp_size),
                (3, 2, mp_size),
                (peers,),
                (3, bits),
                (2, head_total, slots - 1),
                (bits,),
                (peers,),
                (slots - 1,),
            ),
        ],
        compiler_params=pltpu.CompilerParams(
            collective_id=1, has_side_effects=True, vmem_limit_bytes=REAR_VMEM_BYTES
        ),
        cost_estimate=pl.CostEstimate(
            flops=40 * head_total * ROW_LEN * ROW_LEN * HEAD_DIM,
            bytes_accessed=96 * 1024 * 1024,
            transcendentals=head_total * ROW_LEN * ROW_LEN,
        ),
        name="rear",
    )(seg_row, in_bias, *small, frames, heads_low, out_grad, *weights, proj_weight, *saved)


def finish_kernel(
    traded,
    proj_all,
    resid_grad,
    in_sum,
    down_sum,
    head_sum,
    proj_sum,
    vector_sum,
    bias_sum,
    stream_grad,
    in_grad,
    down_grad,
    out_grad,
    proj_grad,
    query_bias_grad,
    value_bias_grad,
    out_bias_grad,
    in_bias_grad,
    down_bias_grad,
    gain_grad,
    shift_grad,
    columns,
    weight_buf,
    sems,
):
    head_total, mp_size = traded.shape[:2]
    half = traded.shape[3]
    head_cols = head_total * HEAD_DIM
    copies = [
        pltpu.make_async_copy(
            proj_all.at[index],
            weight_buf.at[index],
            sems.at[index],
        )
        for index in range(mp_size)
    ]
    for copy in copies:
        copy.start()
    for sums, grad in ((in_sum, in_grad), (down_sum, down_grad), (head_sum, out_grad)):
        rows = grad.shape[0] // sums.shape[0]
        for slot in range(sums.shape[0]):
            grad[slot * rows : (slot + 1) * rows] = sums[slot, :rows].astype(F32)
    proj_grad[...] = proj_sum[...].astype(F32)
    query_bias_grad[...] = bias_sum[0:1, :head_cols]
    value_bias_grad[...] = bias_sum[2:3, :head_cols]
    gain_grad[...] = vector_sum[0:2]
    shift_grad[...] = vector_sum[2:4]
    out_bias_grad[...] = vector_sum[4:5]
    down_bias_grad[...] = vector_sum[5:6]
    in_bias_grad[...] = vector_sum[pl.ds(8 + lax.axis_index("mp"), 1)]
    stream_grad[...] = resid_grad[...]
    for index in range(mp_size):
        for head in range(head_total):
            for part in range(3):
                at = part * head_cols + head * HEAD_DIM
                for side in range(2):
                    columns[side * half : (side + 1) * half, at : at + HEAD_DIM] = traded[
                        head, index, part, :, side * HEAD_DIM : (side + 1) * HEAD_DIM
                    ]
        copies[index].wait()
        stream_grad[...] += dot(columns[...], weight_buf[index])


def finish(traded, proj_all, resid_grad, sums):
    head_total, mp_size = traded.shape[:2]
    head_cols = head_total * HEAD_DIM
    local_rows, width = resid_grad.shape
    units = sums[0].shape[0] * sums[0].shape[1]
    row = jax.ShapeDtypeStruct((1, width), F32)
    head_row = jax.ShapeDtypeStruct((1, head_cols), F32)
    anywhere = pl.BlockSpec(memory_space=pl.ANY)
    return pl.pallas_call(
        finish_kernel,
        out_shape=(
            jax.ShapeDtypeStruct((local_rows, width), F32),
            jax.ShapeDtypeStruct((units, width), F32),
            jax.ShapeDtypeStruct((units, width), F32),
            jax.ShapeDtypeStruct((head_cols, width), F32),
            jax.ShapeDtypeStruct((3, head_cols, width), F32),
            head_row,
            head_row,
            row,
            jax.ShapeDtypeStruct((1, units), F32),
            row,
            jax.ShapeDtypeStruct((2, width), F32),
            jax.ShapeDtypeStruct((2, width), F32),
        ),
        in_specs=[whole(), anywhere] + [whole()] * 7,
        out_specs=(whole(),) * 12,
        scratch_shapes=[
            pltpu.VMEM((local_rows, 3 * head_cols), BF16),
            pltpu.VMEM((mp_size, 3 * head_cols, width), BF16),
            pltpu.SemaphoreType.DMA((mp_size,)),
        ],
        compiler_params=pltpu.CompilerParams(vmem_limit_bytes=VMEM_BYTES),
        cost_estimate=pl.CostEstimate(
            flops=6 * local_rows * width * width, bytes_accessed=24 * 1024 * 1024, transcendentals=0
        ),
        name="finish",
    )(traded, proj_all, resid_grad, *sums)


def dp_groups():
    total = lax.axis_size("dp")
    size = min(8, total)
    groups = [list(range(start, start + size)) for start in range(0, total, size)]
    return (size, groups)


def on_device(
    frames,
    segment_ids,
    qkv_weight,
    q_bias,
    v_bias,
    out_weight,
    out_bias,
    ff_in_weight,
    ff_in_bias,
    ff_out_weight,
    ff_out_bias,
    norm_gain,
    norm_shift,
    out_grad,
):
    local_rows, width = frames.shape
    mp_size = lax.axis_size("mp")
    group, groups = dp_groups()
    bits = group_bits(lax.axis_size("dp"))
    slots = 2**bits

    proj_weight = qkv_weight[0].transpose(0, 2, 1)
    seg_row = segment_ids.reshape(1, ROW_LEN)
    (
        input_all,
        qkv_low,
        in_all,
        down_all,
        out_all,
        in_bias_all,
        seg_col,
        out_cols,
        log_total,
        heads_low,
    ) = front(
        frames,
        proj_weight,
        q_bias,
        v_bias,
        seg_row,
        (ff_in_weight[0], ff_out_weight[0], out_weight[0]),
        ff_in_bias,
        mp_size,
        bits,
    )
    block_out, resid_grad, _, _, _, proj_all, traded, *summed = rear(
        frames,
        heads_low,
        out_grad,
        seg_row,
        in_bias_all,
        (out_bias, ff_out_bias, norm_gain[0], norm_shift[0]),
        (in_all, down_all, out_all),
        proj_weight.reshape(slots, -1, width),
        (qkv_low, out_cols, log_total, seg_col, input_all),
        bits,
    )
    if len(groups) > 1:
        across = [list(range(at, lax.axis_size("dp"), group)) for at in range(group)]
        summed = lax.psum(summed, "dp", axis_index_groups=across)
    (
        stream_grad,
        in_weight_grad,
        down_weight_grad,
        out_weight_grad,
        proj_grad,
        query_bias_grad,
        value_bias_grad,
        head_bias_grad,
        in_bias_grad,
        down_bias_grad,
        gain_grad,
        shift_grad,
    ) = finish(traded, proj_all.reshape(mp_size, -1, width), resid_grad, summed)
    return (
        block_out,
        stream_grad,
        proj_grad.transpose(0, 2, 1)[None],
        query_bias_grad,
        value_bias_grad,
        out_weight_grad[None],
        head_bias_grad,
        in_weight_grad[None],
        in_bias_grad,
        down_weight_grad[None],
        down_bias_grad,
        gain_grad[None],
        shift_grad[None],
    )


def solution(mesh):
    return jax.shard_map(
        on_device,
        mesh=mesh,
        in_specs=(
            P(("dp", "mp"), None),
            P("dp"),
            P(None, None, None, "mp"),
            P(None, "mp"),
            P(None, "mp"),
            P(None, "mp", None),
            P(),
            P(None, None, "mp"),
            P(None, "mp"),
            P(None, "mp", None),
            P(),
            P(),
            P(),
            P(("dp", "mp"), None),
        ),
        out_specs=(
            P(("dp", "mp"), None),
            P(("dp", "mp"), None),
            P(None, None, None, "mp"),
            P(None, "mp"),
            P(None, "mp"),
            P(None, "mp", None),
            P(),
            P(None, None, "mp"),
            P(None, "mp"),
            P(None, "mp", None),
            P(),
            P(),
            P(),
        ),
        check_vma=False,
    )
```

```python
import itertools
from functools import partial

import jax
import jax.numpy as jnp
from jax import lax
from jax.experimental import pallas as pl
from jax.experimental.pallas import tpu as pltpu
from jax.sharding import PartitionSpec as P

HEAD_DIM = 64
ROW_LEN = 2304
BLOCK = 768
BLOCKS = ROW_LEN // BLOCK
EXTRA = 16
SCALE = HEAD_DIM ** (-0.5)
MASKED = -1e30
F32 = jnp.float32
BF16 = jnp.bfloat16
VMEM_BYTES = 56 * 1024 * 1024
REAR_VMEM_BYTES = 63 * 1024 * 1024


def dot_rows(left, right):
    return lax.dot_general(left, right, (((1,), (1,)), ((), ())), preferred_element_type=F32)


def dot_cols(left, right):
    return lax.dot_general(left, right, (((0,), (0,)), ((), ())), preferred_element_type=F32)


def dot(left, right):
    return jnp.dot(left, right, preferred_element_type=F32)


def block_rows(number):
    return pl.ds(pl.multiple_of(number * BLOCK, BLOCK), BLOCK)


def as_pieces(row):
    high = row.astype(BF16).astype(F32)
    middle = (row - high).astype(BF16).astype(F32)
    last = row - high - middle
    place = lax.broadcasted_iota(jnp.int32, (EXTRA, row.shape[1]), 0)
    pieces = jnp.where(place == 0, high, jnp.where(place == 1, middle, jnp.where(place == 2, last, 0.0)))
    return pieces.astype(BF16)


def ones_columns(rows):
    place = lax.broadcasted_iota(jnp.int32, (rows, EXTRA), 1)
    return jnp.where(place < 3, 1.0, 0.0).astype(BF16)


def whole(memory_space=pltpu.VMEM):
    return pl.BlockSpec(memory_space=memory_space)


MESH = pl.DeviceIdType.MESH


def group_bits(dp_size):
    return min(3, dp_size.bit_length() - 1)


def place_in(dp_index, order):
    slot = 0
    for at, bit in enumerate(order):
        slot = slot + (dp_index // 2**bit) % 2 * 2**at
    return slot


def partner_of(dp_index, bit):
    return dp_index + (1 - 2 * ((dp_index // 2**bit) % 2)) * 2**bit


def mate_of(dp_index, offset, size):
    place = lax.rem(dp_index, size)
    return dp_index - place + lax.rem(place + offset, size)


def enter(dp_index, mp_index, mp_size, bits, whole_group=False):
    barrier = pltpu.get_barrier_semaphore()
    for offset in range(1, mp_size):
        pl.semaphore_signal(
            barrier, device_id={"mp": lax.rem(mp_index + offset, mp_size)}, device_id_type=MESH
        )
    if whole_group:
        partners = [mate_of(dp_index, offset, 2**bits) for offset in range(1, 2**bits)]
    else:
        partners = [partner_of(dp_index, bit) for bit in range(bits)]
    for partner in partners:
        pl.semaphore_signal(barrier, device_id={"dp": partner}, device_id_type=MESH)
    pl.semaphore_wait(barrier, mp_size - 1 + len(partners))


def send(src, dst, sems, at, device_id):
    return pltpu.make_async_remote_copy(
        src_ref=src,
        dst_ref=dst,
        send_sem=sems[0].at[at],
        recv_sem=sems[1].at[at],
        device_id=device_id,
        device_id_type=MESH,
    )


def gather_orders(bits):
    if bits == 3:
        return ((1, 2, 0), (2, 1, 0), (1, 2), (1, 2, 0))
    return (tuple(range(bits)),) * 4


SIDES = (1, -1)


def inside(index, size):
    return jnp.logical_and(index >= 0, index < size)


class Line:
    def __init__(self, mp_size, me):
        self.size = mp_size
        self.me = me
        self.hops = range(mp_size - 1)
        self.ways = [(side, hop) for hop in self.hops for side in (0, 1)]

    def wrapped(self, index):
        return lax.rem(index + self.size, self.size)

    def chunk(self, side, hop):
        return self.me - SIDES[side] * hop

    def place(self, side, hop):
        return self.wrapped(self.chunk(side, hop))

    def sends(self, side, hop):
        there = inside(self.me + SIDES[side], self.size)
        return jnp.logical_and(there, inside(self.chunk(side, hop), self.size))

    def if_sent(self, side, hop):
        return pl.when(self.sends(side, hop))

    def if_taken(self, side, hop):
        return pl.when(inside(self.chunk(side, hop + 1), self.size))

    def neighbour(self, side):
        return {"mp": self.wrapped(self.me + SIDES[side])}


def front_kernel(
    bits,
    frames,
    qkv_weight,
    q_bias,
    v_bias,
    seg_row,
    in_weight,
    down_weight,
    out_weight,
    in_bias,
    input_all,
    qkv_low,
    in_all,
    down_all,
    out_all,
    bias_all,
    seg_col,
    out_cols,
    log_total,
    heads_low,
    bias_buf,
    key_cols,
    value_buf,
    out_buf,
    staged,
    heads_in,
    own_sems,
    frame_send,
    frame_recv,
    bias_send,
    bias_recv,
    first_send,
    first_recv,
    later_send,
    later_recv,
    heads_own,
    heads_send,
    heads_recv,
):
    mp_size = in_all.shape[0]
    me = lax.axis_index("mp")
    dp_index = lax.axis_index("dp")
    local_rows = frames.shape[0]
    half = local_rows // 2
    head_total = out_cols.shape[0]
    orders = gather_orders(bits)[:3]
    parts = ((in_weight, in_all), (down_weight, down_all), (out_weight, out_all))
    line = Line(mp_size, me)
    hops, ways, wrapped = line.hops, line.ways, line.wrapped
    enter(dp_index, me, mp_size, bits)

    def slots(which, level):
        count = parts[which][0].shape[0] // 2 ** len(orders[which])
        start = place_in(dp_index, orders[which]) // 2**level * 2**level
        return pl.ds(pl.multiple_of(start * count, 16), count * 2**level)

    def first_copy(which, side, hop):
        rows = slots(which, 0)
        place = parts[which][1].at[line.place(side, hop), rows]
        source = parts[which][0].at[rows] if hop == 0 else place
        sems = (first_send, first_recv)
        return send(source, place, sems, (which, side, hop), line.neighbour(side))

    def later_copy(which, level, side, hop):
        held = parts[which][1].at[line.place(side, hop + 1), slots(which, level)]
        partner = {"dp": partner_of(dp_index, orders[which][level])}
        return send(held, held, (later_send, later_recv), (which, level, side, hop), partner)

    def frame_rows(index):
        return pl.ds(pl.multiple_of(wrapped(index) * local_rows, local_rows), local_rows)

    def frame_copy(side, hop):
        place = input_all.at[frame_rows(line.chunk(side, hop))]
        source = frames if hop == 0 else place
        return send(source, place, (frame_send, frame_recv), (side, hop), line.neighbour(side))

    def bias_copy(side, hop):
        place = bias_all.at[line.place(side, hop)]
        source = bias_buf if hop == 0 else place
        return send(source, place, (bias_send, bias_recv), (side, hop), line.neighbour(side))

    def project(index):
        rows = frame_rows(index)
        inputs = input_all[rows]
        for part, bias in enumerate((q_bias, None, v_bias)):
            products = dot_rows(inputs, qkv_weight[part])
            if bias is not None:
                products = products + bias[...].astype(F32)
            qkv_low[part, rows] = products.astype(BF16)

    def start_slices(side, hop):
        for which in range(3):
            first_copy(which, side, hop).start()
        bias_copy(side, hop).start()

    def take_slices(side, hop):
        for which in range(3):
            first_copy(which, side, hop).wait_recv()
        bias_copy(side, hop).wait_recv()
        if 0 < hop < mp_size - 2:
            line.if_sent(side, hop + 1)(partial(start_slices, side, hop + 1))
        for which in range(3):
            if orders[which]:
                later_copy(which, 0, side, hop).start()

    def trade_slices(level, side, hop):
        for which in range(3):
            if level < len(orders[which]):
                later_copy(which, level, side, hop).wait_recv()
            if level + 1 < len(orders[which]):
                later_copy(which, level + 1, side, hop).start()

    def take_hop(hop):
        for side in (0, 1):
            line.if_taken(side, hop)(partial(take_slices, side, hop))

    def trade_hop(level, hop):
        for side in (0, 1):
            line.if_taken(side, hop)(partial(trade_slices, level, side, hop))


    bias_buf[...] = jnp.broadcast_to(in_bias[...], bias_buf.shape)
    for side in (0, 1):
        line.if_sent(side, 0)(partial(start_slices, side, 0))
    for side in (0, 1):
        line.if_sent(side, 0)(lambda side=side: frame_copy(side, 0).start())
    own = [
        pltpu.make_async_copy(shard, gathered.at[me], own_sems.at[at])
        for at, (shard, gathered) in enumerate(parts + ((bias_buf, bias_all),))
    ]
    for copy in own:
        copy.start()
    input_all[frame_rows(me)] = frames[...]
    project(me)
    for step in range(BLOCKS):
        ids = jnp.broadcast_to(seg_row[:, step * BLOCK : (step + 1) * BLOCK].astype(F32), (128, BLOCK))
        seg_col[step * BLOCK : (step + 1) * BLOCK] = ids.T.astype(jnp.int32)

    def take_frames(side, hop):
        frame_copy(side, hop).wait_recv()
        if hop + 1 < mp_size - 1:
            line.if_sent(side, hop + 1)(lambda: frame_copy(side, hop + 1).start())

    def project_taken(side, hop):
        project(line.chunk(side, hop + 1))

    for hop in hops:
        for side in (0, 1):
            line.if_taken(side, hop)(partial(take_frames, side, hop))
        if hop == 0:
            take_hop(0)
        elif hop - 1 < bits:
            trade_hop(hop - 1, 0)
        for side in (0, 1):
            free = line.sends(side, hop)
            if hop + 1 < mp_size - 1:
                free = jnp.logical_and(free, jnp.logical_not(line.sends(side, hop + 1)))
            if mp_size > 2:
                passes = jnp.logical_and(free, line.sends(side, 1))
                pl.when(passes)(partial(start_slices, side, 1))
        for side in (0, 1):
            line.if_taken(side, hop)(partial(project_taken, side, hop))

    schedule = (
        (1, take_hop, 1),
        (3, trade_hop, 0, 1),
        (4, take_hop, 2),
        (6, trade_hop, 1, 1),
        (6, trade_hop, 0, 2),
    )
    events = {}
    done = {(take_hop, 0)} | {(trade_hop, hop - 1, 0) for hop in hops if 0 < hop <= bits}
    for at, act, *which in schedule:
        if which[-1] in hops and (act is take_hop or which[0] < bits):
            events.setdefault((at // BLOCKS, at % BLOCKS), []).append(partial(act, *which))
            done.add((act, *which))

    def attend(head):
        cols = slice(head * HEAD_DIM, (head + 1) * HEAD_DIM)
        lane = lax.broadcasted_iota(jnp.int32, (BLOCK, EXTRA), 1)
        for step in range(BLOCKS):
            rows = slice(step * BLOCK, (step + 1) * BLOCK)
            key_cols[step] = qkv_low[1, rows, cols].T
            value_buf[step, :, :HEAD_DIM] = qkv_low[2, rows, cols]
            value_buf[step, :, HEAD_DIM:] = jnp.where(lane == 0, 1.0, 0.0).astype(BF16)

        def query_block(number, _):
            rows = block_rows(number)
            queries = qkv_low[0, rows, cols] * SCALE

            def scores_of(step):
                ids = seg_row[:, step * BLOCK : (step + 1) * BLOCK]
                same = jnp.concatenate([seg_col[rows]] * (BLOCK // 128), axis=1) == ids
                return jnp.where(same, dot(queries, key_cols[step]), MASKED)

            peak = jnp.full((BLOCK, 1), MASKED, F32)
            mixed = jnp.zeros((BLOCK, HEAD_DIM + EXTRA), F32)
            scores = scores_of(0)
            for step in range(BLOCKS):
                ahead = scores_of(step + 1) if step + 1 < BLOCKS else None
                higher = jnp.maximum(peak, jnp.max(scores, axis=1, keepdims=True))
                soft = jnp.exp(scores - higher).astype(BF16)
                mixed = mixed * jnp.exp(peak - higher) + dot(soft, value_buf[step])
                peak, scores = higher, ahead
            total = mixed[:, HEAD_DIM : HEAD_DIM + 1]
            mixed = mixed[:, :HEAD_DIM] / total
            logs = jnp.broadcast_to(peak + jnp.log(total), (BLOCK, HEAD_DIM))
            both = jnp.concatenate([mixed, logs], axis=1).T
            out_cols[head, number] = both[:HEAD_DIM]
            log_total[head, number] = both[HEAD_DIM : HEAD_DIM + 1]
            out_buf[rows] = mixed.astype(BF16)
            for at in range(BLOCKS):
                if (head, at) in events:

                    @pl.when(number == at)
                    def _():
                        for act in events[(head, at)]:
                            act()

            return 0

        lax.fori_loop(0, BLOCKS, query_block, 0)

    def heads_copy(head, offset):
        return send(
            staged.at[head, wrapped(me + offset)],
            heads_in.at[head, me],
            (heads_send, heads_recv),
            (head, offset - 1),
            {"mp": wrapped(me + offset)},
        )

    def heads_own_copy(head):
        return pltpu.make_async_copy(
            staged.at[head, me], heads_in.at[head, me], heads_own.at[head]
        )

    peers = range(1, mp_size)
    for head in range(head_total):
        attend(head)
        for chunk in range(mp_size):
            for side in range(2):
                start = (2 * chunk + side) * half
                staged[head, chunk, :, side * HEAD_DIM : (side + 1) * HEAD_DIM] = out_buf[
                    start : start + half
                ]
        for offset in peers:
            heads_copy(head, offset).start()
        heads_own_copy(head).start()

    for hop in hops:
        if (take_hop, hop) not in done:
            take_hop(hop)
    for level in range(bits):
        for hop in hops:
            if (trade_hop, level, hop) not in done:
                trade_hop(level, hop)
    for head in range(head_total):
        heads_own_copy(head).wait()
        for offset in peers:
            heads_copy(head, offset).wait_recv()
        for chunk in range(mp_size):
            for side in range(2):
                at = (chunk * head_total + head) * HEAD_DIM
                heads_low[side * half : (side + 1) * half, at : at + HEAD_DIM] = heads_in[
                    head, chunk, :, side * HEAD_DIM : (side + 1) * HEAD_DIM
                ]
        for offset in peers:
            heads_copy(head, offset).wait_send()

    def sent_all(side, hop):
        frame_copy(side, hop).wait_send()
        bias_copy(side, hop).wait_send()
        for which in range(3):
            first_copy(which, side, hop).wait_send()

    def sent_later(side, hop):
        for which in range(3):
            for level in range(len(orders[which])):
                later_copy(which, level, side, hop).wait_send()

    for side, hop in ways:
        line.if_sent(side, hop)(partial(sent_all, side, hop))
        line.if_taken(side, hop)(partial(sent_later, side, hop))
    for copy in own:
        copy.wait()


def front(frames, qkv_weight, q_bias, v_bias, seg_row, weights, in_bias, mp_size, bits):
    local_rows, width = frames.shape
    head_cols = qkv_weight.shape[1]
    head_total = head_cols // HEAD_DIM
    peers = mp_size - 1
    levels = max(bits, 1)
    anywhere = pl.BlockSpec(memory_space=pl.ANY)
    in_weight, down_weight, out_weight = weights

    def sems(*shapes):
        return [pltpu.SemaphoreType.DMA(shape) for shape in shapes for _ in range(2)]

    piece = (head_total, mp_size, local_rows // 2, 2 * HEAD_DIM)
    return pl.pallas_call(
        partial(front_kernel, bits),
        out_shape=(
            jax.ShapeDtypeStruct((ROW_LEN, width), BF16),
            jax.ShapeDtypeStruct((3, ROW_LEN, head_cols), BF16),
            jax.ShapeDtypeStruct((mp_size,) + in_weight.shape, BF16),
            jax.ShapeDtypeStruct((mp_size,) + down_weight.shape, BF16),
            jax.ShapeDtypeStruct((mp_size,) + out_weight.shape, BF16),
            jax.ShapeDtypeStruct((mp_size, 16, in_bias.shape[1]), BF16),
            jax.ShapeDtypeStruct((ROW_LEN, 128), jnp.int32),
            jax.ShapeDtypeStruct((head_total, BLOCKS, HEAD_DIM, BLOCK), F32),
            jax.ShapeDtypeStruct((head_total, BLOCKS, 1, BLOCK), F32),
            jax.ShapeDtypeStruct((local_rows, width), BF16),
        ),
        in_specs=[whole()] * 5 + [anywhere] * 3 + [whole()],
        out_specs=(whole(), whole()) + (anywhere,) * 4 + (whole(),) * 4,
        scratch_shapes=[
            pltpu.VMEM((16, in_bias.shape[1]), BF16),
            pltpu.VMEM((BLOCKS, HEAD_DIM, BLOCK), BF16),
            pltpu.VMEM((BLOCKS, BLOCK, HEAD_DIM + EXTRA), BF16),
            pltpu.VMEM((ROW_LEN, HEAD_DIM), BF16),
            pltpu.VMEM(piece, BF16),
            pltpu.VMEM(piece, BF16),
            pltpu.SemaphoreType.DMA((4,)),
            *sems((2, peers), (2, peers), (3, 2, peers), (3, levels, 2, peers)),
            pltpu.SemaphoreType.DMA((head_total,)),
            *sems((head_total, peers)),
        ],
        compiler_params=pltpu.CompilerParams(
            collective_id=0, has_side_effects=True, vmem_limit_bytes=VMEM_BYTES
        ),
        cost_estimate=pl.CostEstimate(
            flops=16 * head_total * ROW_LEN * ROW_LEN * HEAD_DIM,
            bytes_accessed=32 * 1024 * 1024,
            transcendentals=head_total * ROW_LEN * ROW_LEN,
        ),
        name="front",
    )(frames, qkv_weight, q_bias, v_bias, seg_row, in_weight, down_weight, out_weight, in_bias)


def reduce_orders(bits):
    if bits == 3:
        return ((0, 1, 2), (0, 2, 1), (1, 2, 0))
    return (tuple(range(bits)),) * 3


def norm_rows(inputs, norm_gain, norm_shift):
    row_mean = jnp.mean(inputs, axis=-1, keepdims=True)
    centred = inputs - row_mean
    variance = jnp.mean(centred * centred, axis=-1, keepdims=True)
    inv_std = lax.rsqrt(variance + 1e-05)
    normed = centred * inv_std
    return (normed * norm_gain + norm_shift, normed, inv_std)


def norm_back(cotangent, normed, inv_std, norm_gain):
    scaled = cotangent * norm_gain
    adjusted = (
        scaled
        - jnp.mean(scaled, axis=-1, keepdims=True)
        - normed * jnp.mean(scaled * normed, axis=-1, keepdims=True)
    )
    return adjusted * inv_std


def sum_rows(array):
    return jnp.sum(array.astype(F32), axis=0, keepdims=True)


def rear_kernel(
    bits,
    seg_row,
    in_bias,
    out_bias,
    down_bias,
    norm_gain,
    norm_shift,
    frames,
    heads_low,
    out_grad,
    in_all,
    down_all,
    out_all,
    proj_weight,
    qkv_source,
    out_source,
    log_source,
    seg_source,
    input_source,
    block_out,
    resid_grad,
    in_grads,
    down_grads,
    head_grads,
    proj_all,
    traded,
    in_sum,
    down_sum,
    head_sum,
    proj_sum,
    vector_sum,
    bias_sum,
    grads_out,
    grads_in,
    kept,
    taken,
    last,
    proj,
    proj_taken,
    proj_slots,
    vectors,
    vectors_taken,
    vectors_all,
    biases,
    load_sems,
    in_sems,
    down_sems,
    out_sems,
    given_sems,
    head_sem,
    store_sems,
    attention_sems,
    weight_own,
    weight_send,
    weight_recv,
    weight_trade_send,
    weight_trade_recv,
    keep_sems,
    grads_own,
    grads_send,
    grads_recv,
    traded_own,
    traded_send,
    traded_recv,
    level_send,
    level_recv,
    last_send,
    last_recv,
    back_send,
    back_recv,
    proj_send,
    proj_recv,
    vector_send,
    vector_recv,
    vector_last_send,
    vector_last_recv,
    bias_send,
    bias_recv,
):
    mp_size, units, width = down_all.shape
    head_total = grads_out.shape[1]
    half = grads_out.shape[2]
    head_cols = width // mp_size
    slots = 2**bits
    me = lax.axis_index("mp")
    dp_index = lax.axis_index("dp")
    peers = range(1, mp_size)
    turns = range(mp_size)
    levels = list(range(bits))
    orders = reduce_orders(bits)
    partials = (in_grads, down_grads, head_grads)
    sums = (in_sum, down_sum, head_sum)
    arrays = range(3)
    vector = vectors[0]
    place = lax.rem(dp_index, slots)
    mates = range(1, slots)
    odd = lax.rem(me, 2)
    leaving = (2, 3 - 2 * odd, 1 + 2 * odd) if mp_size == 4 else peers

    def target(offset):
        return lax.rem(me + offset, mp_size)

    def bit_of(which, level):
        return (dp_index // 2 ** orders[which][level]) % 2


    def part_of(turn):
        return target(turn + 1)

    def level_copy(which, level, turn):
        count = 2 ** (bits - 1 - level)
        other = (1 - bit_of(which, level)) * count
        part = pl.ds(part_of(turn), 1)
        source = partials[which] if level == 0 else taken[which][level - 1]
        return send(
            source.at[part, pl.ds(other, count)],
            taken[which][level].at[part],
            (level_send, level_recv),
            (which, level, turn),
            {"dp": partner_of(dp_index, orders[which][level])},
        )

    def keep_copy(which, turn):
        count = 2 ** (bits - 1)
        return pltpu.make_async_copy(
            partials[which].at[part_of(turn), pl.ds(bit_of(which, 0) * count, count)],
            kept[which].at[turn % 2],
            keep_sems.at[which, turn % 2],
        )

    def last_copy(which, offset):
        return send(
            taken[which][bits - 1].at[target(offset)],
            last[which].at[offset - 1],
            (last_send, last_recv),
            (which, offset - 1),
            {"mp": target(offset)},
        )

    def add_level(which, level, turn):
        level_copy(which, level, turn).wait_recv()
        count = 2 ** (bits - 1 - level)
        if level == 0:
            keep_copy(which, turn).wait()
        start = bit_of(which, level) * count
        into = taken[which][level]
        part = part_of(turn)
        for slot in range(count):
            if level == 0:
                mine = kept[which][turn % 2, slot]
            else:
                mine = taken[which][level - 1][part, start + slot]
            into[part, slot] = (into[part, slot].astype(F32) + mine.astype(F32)).astype(BF16)
        if level == 0 and turn + 2 < mp_size:
            keep_copy(which, turn + 2).start()
        if level + 1 < bits:
            level_copy(which, level + 1, turn).start()
        elif turn + 1 < mp_size:
            last_copy(which, turn + 1).start()

    def offer(which, turn):
        level_copy(which, 0, turn).start()
        if turn < 2:
            keep_copy(which, turn).start()

    def slot_of(order):
        return place_in(dp_index, order[::-1])

    def held_slots(order, level):
        count = 2 ** (bits - 1 - level)
        return pl.ds(slot_of(order) // count * count, count)

    def spread_copy(which, level):
        held = sums[which].at[held_slots(orders[which], level)]
        partner = {"dp": partner_of(dp_index, orders[which][level])}
        return send(held, held, (back_send, back_recv), (which, level), partner)

    def finish_sum(which):
        total = taken[which][bits - 1][me, 0].astype(F32)
        for offset in peers:
            last_copy(which, offset).wait_recv()
            total = total + last[which][offset - 1, 0].astype(F32)
        sums[which][slot_of(orders[which])] = total.astype(BF16)
        spread_copy(which, bits - 1).start()

    def spread(which, level):
        spread_copy(which, level).wait_recv()
        if level:
            spread_copy(which, level - 1).start()


    def mate(offset):
        return {"dp": mate_of(dp_index, offset, slots)}

    def proj_copy(head, offset):
        return send(
            proj[head].at[lax.rem(place + offset, slots)],
            proj_taken[head].at[offset - 1],
            (proj_send, proj_recv),
            (0, head, offset - 1),
            mate(offset),
        )

    def proj_spread_copy(head, offset):
        held = proj_slots[head].at[place]
        return send(held, held, (proj_send, proj_recv), (1, head, offset - 1), mate(offset))

    def sum_proj(head):
        total = proj[head][place].astype(F32)
        for offset in mates:
            proj_copy(head, offset).wait_recv()
            total = total + proj_taken[head][offset - 1].astype(F32)
        proj_slots[head][place] = total.astype(BF16)
        for offset in mates:
            proj_spread_copy(head, offset).start()

    def take_proj(head):
        for offset in mates:
            proj_spread_copy(head, offset).wait_recv()


    def vector_copy(level):
        return send(
            vectors[level],
            vectors_taken[level],
            (vector_send, vector_recv),
            level,
            {"dp": partner_of(dp_index, level)},
        )

    def vector_last_copy(offset):
        return send(
            vectors[bits],
            vectors_all.at[me],
            (vector_last_send, vector_last_recv),
            offset - 1,
            {"mp": target(offset)},
        )

    def add_vector(level):
        vector_copy(level).wait_recv()
        vectors[level + 1][...] = vectors[level][...] + vectors_taken[level][...]
        if level + 1 < bits:
            vector_copy(level + 1).start()
        else:
            vectors_all[me] = vectors[bits][...]
            for offset in peers:
                vector_last_copy(offset).start()

    def finish_vector():
        for offset in peers:
            vector_last_copy(offset).wait_recv()
        total = vectors_all[0]
        for index in peers:
            total = total + vectors_all[index]
        vector_sum[...] = total

    def bias_copy(offset):
        held = biases.at[place]
        return send(held, held, (bias_send, bias_recv), offset - 1, mate(offset))

    def sum_bias():
        for offset in mates:
            bias_copy(offset).wait_recv()
        total = biases[0]
        for at in range(1, slots):
            total = total + biases[at]
        bias_sum[...] = total

    def grads_copy(head, offset):
        return send(
            grads_out.at[target(offset), head],
            grads_in.at[head, me],
            (grads_send, grads_recv),
            (head, offset - 1),
            {"mp": target(offset)},
        )

    def grads_own_copy(head):
        return pltpu.make_async_copy(
            grads_out.at[me, head], grads_in.at[head, me], grads_own.at[head]
        )

    line = Line(mp_size, me)
    order = gather_orders(bits)[3]
    own_slot = place_in(dp_index, order)

    def weight_copy(side, hop):
        place = proj_all.at[line.place(side, hop), pl.ds(own_slot, 1)]
        source = proj_weight.at[pl.ds(own_slot, 1)] if hop == 0 else place
        return send(source, place, (weight_send, weight_recv), (side, hop), line.neighbour(side))

    def weight_trade_copy(level, side, hop):
        held = pl.ds(own_slot // 2**level * 2**level, 2**level)
        place = proj_all.at[line.place(side, hop + 1), held]
        partner = {"dp": partner_of(dp_index, order[level])}
        return send(place, place, (weight_trade_send, weight_trade_recv), (level, side, hop), partner)

    def take_weight(side, hop):
        weight_copy(side, hop).wait_recv()
        if hop + 1 < mp_size - 1:
            line.if_sent(side, hop + 1)(lambda: weight_copy(side, hop + 1).start())
        if bits:
            weight_trade_copy(0, side, hop).start()

    def trade_weight(level, side, hop):
        weight_trade_copy(level, side, hop).wait_recv()
        if level + 1 < bits:
            weight_trade_copy(level + 1, side, hop).start()

    def both_sides(act, *which):
        for side in (0, 1):
            line.if_taken(side, which[-1])(partial(act, *which[:-1], side, which[-1]))

    schedule = (
        (0, take_weight, 0),
        (1, take_weight, 1),
        (2, take_weight, 2),
        (2, trade_weight, 0, 0),
        (3, trade_weight, 0, 1),
        (3, trade_weight, 0, 2),
        (4, trade_weight, 1, 0),
        (6, trade_weight, 1, 1),
        (8, trade_weight, 1, 2),
    )
    done = set()

    def at_point(point, index=None):
        for at, act, *which in schedule:
            if which[-1] not in line.hops or (act is trade_weight and which[0] >= bits):
                continue
            if index is None and at == point:
                both_sides(act, *which)
                done.add((act, *which))
            if index is not None and point <= at < point + mp_size:
                pl.when(index == at - point)(partial(both_sides, act, *which))
                done.add((act, *which))

    def dense_phase(
        frames_buf,
        heads_buf,
        cotangent_buf,
        in_buf,
        down_buf,
        out_buf,
        hidden,
        slope,
        mid_buf,
        normed_buf,
        store_buf,
        low_buf,
        grad_buf,
        given,
        head_buf,
    ):
        loads = [
            pltpu.make_async_copy(source, into, load_sems.at[at])
            for at, (source, into) in enumerate(
                ((frames, frames_buf), (heads_low, heads_buf), (out_grad, cotangent_buf))
            )
        ]
        out_copies = [
            pltpu.make_async_copy(
                out_all.at[index],
                out_buf.at[pl.ds(index * head_cols, head_cols)],
                out_sems.at[index],
            )
            for index in range(mp_size)
        ]

        def in_copy(index):
            return pltpu.make_async_copy(in_all.at[index], in_buf.at[index], in_sems.at[index])

        def down_copy(index):
            return pltpu.make_async_copy(
                down_all.at[index], down_buf.at[index], down_sems.at[index]
            )

        def given_copy(which, turn):
            return pltpu.make_async_copy(
                given.at[turn % 2], partials[which].at[part_of(turn)], given_sems.at[turn % 2]
            )

        def store_copy(at):
            return pltpu.make_async_copy(
                store_buf, (block_out, resid_grad)[at], store_sems.at[at]
            )

        for copy in loads + out_copies:
            copy.start()
        for index in range(mp_size):
            in_copy(index).start()
            down_copy(index).start()
        enter(dp_index, me, mp_size, bits, whole_group=True)
        for side in (0, 1):
            line.if_sent(side, 0)(lambda side=side: weight_copy(side, 0).start())
        weight_own_copy.start()
        vector[...] = jnp.zeros_like(vector)
        gains = norm_gain[...].astype(F32)
        shifts = norm_shift[...].astype(F32)
        both = [slice(side * half, (side + 1) * half) for side in range(2)]

        for copy in loads + out_copies:
            copy.wait()
        branch = dot(heads_buf[...], out_buf[...]) + out_bias[...].astype(F32)
        mid, normed, inv_mid = norm_rows(
            frames_buf[...].astype(F32) + branch, gains[:1], shifts[:1]
        )
        mid_buf[...] = mid + down_bias[...].astype(F32)
        normed_buf[...] = normed
        low_buf[...] = mid.astype(BF16)
        at_point(0)

        def feed(index, _):
            in_copy(index).wait()
            down_copy(index).wait()
            for rows in both:
                pre_act = dot(low_buf[rows], in_buf[index]) + in_bias[index, 0:1].astype(F32)
                unit_cdf = 0.5 * (1.0 + lax.erf(pre_act * 0.5**0.5))
                bell = jnp.exp(-0.5 * pre_act * pre_act) * (2.0 * jnp.pi) ** (-0.5)
                slope[index, rows] = (unit_cdf + pre_act * bell).astype(BF16)
                hidden[index, rows] = (pre_act * unit_cdf).astype(BF16)
                mid_buf[rows] += dot(hidden[index, rows], down_buf[index])
            at_point(1, index)
            return 0

        lax.fori_loop(0, mp_size, feed, 0)
        output, normed, inv_out = norm_rows(mid_buf[...], gains[1:], shifts[1:])
        store_buf[...] = output
        store_copy(0).start()

        cotangent = cotangent_buf[...].astype(F32)
        vector[1:2] = sum_rows(cotangent * normed)
        vector[3:4] = sum_rows(cotangent)
        sum_grad = norm_back(cotangent, normed, inv_out, gains[1:])
        mid_buf[...] = sum_grad
        grad_buf[...] = sum_grad.astype(BF16)
        vector[5:6] = sum_rows(grad_buf[...])

        def give(which, turn, result):
            if turn >= 2:
                offer_given(which, turn - 2)
            share = result.shape[0] // slots
            for slot in range(slots):
                given[turn % 2, slot] = result[slot * share : (slot + 1) * share].astype(BF16)
            given_copy(which, turn).start()

        def offer_given(which, turn):
            given_copy(which, turn).wait()
            offer(which, turn)

        for turn in turns:
            index = part_of(turn)
            give(1, turn, dot_cols(hidden[index], grad_buf[...]))
            pre = dot_rows(grad_buf[...], down_buf[index]) * slope[index].astype(F32)
            hidden[index] = pre.astype(BF16)
            vector[pl.ds(8 + index, 1)] = sum_rows(hidden[index])
            mid_buf[...] += dot_rows(hidden[index], in_buf[index])
            at_point(1 + mp_size + turn)
        for turn in turns[-2:]:
            offer_given(1, turn)
        mid_grad = mid_buf[...]
        vector[0:1] = sum_rows(mid_grad * normed_buf[...])
        vector[2:3] = sum_rows(mid_grad)
        resid = norm_back(mid_grad, normed_buf[...], inv_mid, gains[:1])
        store_copy(0).wait()
        store_buf[...] = resid
        store_copy(1).start()
        attn_grad = resid.astype(BF16)
        grad_buf[...] = attn_grad
        vector[4:5] = sum_rows(attn_grad)
        heads_grad = dot_rows(attn_grad, out_buf[...]).astype(BF16)
        for head in range(head_total):
            for index in range(mp_size):
                at = index * head_cols + head * HEAD_DIM
                for side in range(2):
                    grads_out[index, head, :, side * HEAD_DIM : (side + 1) * HEAD_DIM] = (
                        heads_grad[both[side], at : at + HEAD_DIM]
                    )
            if head == 0:
                for offset in leaving:
                    grads_copy(0, offset).start()
        for head in range(head_total):
            grads_own_copy(head).start()
        vector_copy(0).start()

        products = dot_cols(heads_buf[...], grad_buf[...]).astype(BF16)
        rows = head_cols // slots
        for index in range(mp_size):
            for slot in range(slots):
                start = index * head_cols + slot * rows
                head_buf[index, slot, :rows] = products[start : start + rows]
                if rows < head_buf.shape[2]:
                    head_buf[index, slot, rows:] = jnp.zeros(
                        (head_buf.shape[2] - rows, width), BF16
                    )
        head_copy = pltpu.make_async_copy(head_buf, head_grads, head_sem)
        head_copy.start()
        normed_low = low_buf[...].T
        for turn in turns:
            give(0, turn, dot(normed_low, hidden[part_of(turn)]))
            if turn == 0:
                head_copy.wait()
                for at in turns:
                    offer(2, at)
                for later in range(1, head_total):
                    for offset in leaving:
                        grads_copy(later, offset).start()
        for turn in turns[-2:]:
            offer_given(0, turn)
        store_copy(1).wait()

    weight_own_copy = pltpu.make_async_copy(proj_weight, proj_all.at[me], weight_own)
    rows_low = pltpu.VMEM((2 * half, width), BF16)
    rows_full = pltpu.VMEM((2 * half, width), F32)
    pl.run_scoped(
        dense_phase,
        rows_low,
        rows_low,
        rows_low,
        pltpu.VMEM((mp_size, width, units), BF16),
        pltpu.VMEM((mp_size, units, width), BF16),
        pltpu.VMEM((width, width), BF16),
        pltpu.VMEM((mp_size, 2 * half, units), BF16),
        pltpu.VMEM((mp_size, 2 * half, units), BF16),
        rows_full,
        rows_full,
        rows_full,
        rows_low,
        rows_low,
        pltpu.VMEM((2, slots, units // slots, width), BF16),
        pltpu.VMEM(head_grads.shape, BF16),
    )

    def attention_phase(
        qkv,
        out_cols,
        log_total,
        seg_col,
        input_all,
        staged,
        qkv_grad,
        seg_blocks,
        grads,
        key_buf,
        key_cols,
        value_buf,
        query_sum,
        key_sum,
        value_sum,
        proj_rows,
    ):
        def traded_copy(head, offset):
            return send(
                staged.at[head, target(offset)],
                traded.at[head, me],
                (traded_send, traded_recv),
                (head, offset - 1),
                {"mp": target(offset)},
            )

        def traded_own_copy(head):
            return pltpu.make_async_copy(
                staged.at[head, me], traded.at[head, me], traded_own.at[head]
            )

        def prepare(head):
            cols = slice(head * HEAD_DIM, (head + 1) * HEAD_DIM)
            key_buf[:, :HEAD_DIM] = qkv[1, :, cols]
            key_buf[:, HEAD_DIM:] = ones_columns(ROW_LEN)
            value_buf[:, :HEAD_DIM] = qkv[2, :, cols]
            value_buf[:, HEAD_DIM:] = ones_columns(ROW_LEN)
            for step in range(BLOCKS):
                key_cols[step] = qkv[1, step * BLOCK : (step + 1) * BLOCK, cols].T
            key_sum[...] = jnp.zeros_like(key_sum)
            value_sum[...] = jnp.zeros_like(value_sum)

        def take_grads(head):
            grads_own_copy(head).wait()
            for offset in peers:
                grads_copy(head, offset).wait_recv()
            for chunk in range(mp_size):
                for side in range(2):
                    start = (2 * chunk + side) * half
                    grads[start : start + half] = grads_in[
                        head, chunk, :, side * HEAD_DIM : (side + 1) * HEAD_DIM
                    ]

        def attend_back(head):
            cols = slice(head * HEAD_DIM, (head + 1) * HEAD_DIM)

            def query_block(number, _):
                rows = block_rows(number)
                queries = qkv[0, rows, cols] * SCALE
                grad_rows = grads[rows]
                seg_query = seg_blocks[number]
                grad_cols = grad_rows.astype(F32).T
                row_dot = jnp.sum(grad_cols * out_cols[head, number], axis=0, keepdims=True)
                grad_cols = jnp.concatenate([grad_cols.astype(BF16), as_pieces(-row_dot)], axis=0)
                query_cols = jnp.concatenate(
                    [queries.astype(F32).T.astype(BF16), as_pieces(-log_total[head, number])], axis=0
                )

                def products_of(step):
                    key_rows = slice(step * BLOCK, (step + 1) * BLOCK)
                    same = (
                        jnp.concatenate([seg_col[key_rows]] * (BLOCK // 128), axis=1) == seg_query
                    )
                    scores = jnp.where(same, dot(key_buf[key_rows], query_cols), MASKED)
                    return scores, dot(value_buf[key_rows], grad_cols)

                query_grad = jnp.zeros((HEAD_DIM, BLOCK), F32)
                ahead = products_of(0)
                for step in range(BLOCKS):
                    scores, soft_grad = ahead
                    if step + 1 < BLOCKS:
                        ahead = products_of(step + 1)
                    key_rows = slice(step * BLOCK, (step + 1) * BLOCK)
                    soft = jnp.exp(scores)
                    score_grad = (soft * soft_grad).astype(BF16)
                    value_sum[key_rows] += dot(soft.astype(BF16), grad_rows)
                    key_sum[key_rows] += dot(score_grad, queries)
                    query_grad = query_grad + dot(key_cols[step], score_grad)
                query_sum[rows] = (query_grad * SCALE).T
                for at in range(head * BLOCKS, (head + 1) * BLOCKS):
                    if at in events:

                        @pl.when(number == at - head * BLOCKS)
                        def _():
                            for act in events[at]:
                                act()

                return 0

            lax.fori_loop(0, BLOCKS, query_block, 0)

        def give_grads(head):
            for part, total in enumerate((query_sum, key_sum, value_sum)):
                low = total[...].astype(BF16)
                qkv_grad[:, part * HEAD_DIM : (part + 1) * HEAD_DIM] = low
                if part != 1:
                    cols = slice(head * HEAD_DIM, (head + 1) * HEAD_DIM)
                    sum_low = jnp.sum(low.astype(F32), axis=0, keepdims=True)
                    biases[place, part : part + 1, cols] = sum_low
                for chunk in range(mp_size):
                    for side in range(2):
                        start = (2 * chunk + side) * half
                        staged[head, chunk, part, :, side * HEAD_DIM : (side + 1) * HEAD_DIM] = total[
                            start : start + half
                        ].astype(BF16)

        def start_trade(head):
            for offset in leaving:
                traded_copy(head, offset).start()
            traded_own_copy(head).start()

        def start_proj(head):
            products = dot_cols(qkv_grad[...], input_all[...])
            slot_rows = proj[head].shape[1]
            for slot in range(2**bits):
                proj[head][slot] = products[slot * slot_rows : (slot + 1) * slot_rows].astype(BF16)
            for offset in mates:
                proj_copy(head, offset).start()

        def finish_proj(head):
            cols = slice(head * HEAD_DIM, (head + 1) * HEAD_DIM)
            slot_rows = proj_slots[head].shape[1]
            for slot in range(2**bits):
                proj_rows[slot * slot_rows : (slot + 1) * slot_rows] = proj_slots[head][slot].astype(F32)
            for part in range(3):
                rows = proj_rows[part * HEAD_DIM : (part + 1) * HEAD_DIM]
                proj_sum[part, cols] = rows.astype(BF16)

        events = {}
        rest = []

        def due(at, act, *which):
            if at is None:
                rest.append((act, *which))
            else:
                events.setdefault(at, []).append(partial(act, *which))

        for at, level in zip((0, 1, 2), levels):
            due(at, add_vector, level)
        due(2.5, finish_vector)
        times = {
            1: ((0, 0, 0, 0), (2, 2, 2.5, 3), (2.5, 2.5, 3, 4)),
            2: ((2, 2, 2, 2), (3, 3, 3, 3), (4, 4, 4, 4)),
            0: ((1, 2, 2.5, 3), (2, 3, 4, 4), (2.5, 4, 5, 5.5)),
        }
        ends = {1: (5, 5.5, 6, 7), 2: (5.5, 6, 7, 8), 0: (6, 7, 8, None)}
        for level in levels:
            for which in times:
                for turn, at in zip(turns, times[which][level]):
                    due(at, add_level, which, level, turn)
        due(3, sum_proj, 0)
        due(5, take_proj, 0)
        due(6, sum_proj, 1)
        due(8, take_proj, 1)
        for which in (1, 2, 0):
            due(ends[which][0], finish_sum, which)
        for step, level in enumerate(levels[::-1]):
            for which in (0, 1, 2):
                due(ends[which][1 + step], spread, which, level)

        copies = [
            pltpu.make_async_copy(source, into, attention_sems.at[at])
            for at, (source, into) in enumerate(
                (
                    (qkv_source, qkv),
                    (seg_source, seg_col),
                    (log_source, log_total),
                    (out_source, out_cols),
                    (input_source, input_all),
                )
            )
        ]
        for copy in copies:
            copy.start()
        biases[place] = jnp.zeros(bias_sum.shape, F32)
        for step in range(BLOCKS):
            seg_blocks[step] = seg_row[:, step * BLOCK : (step + 1) * BLOCK]
        final = head_total - 1
        copies[0].wait()
        for head in range(head_total):
            prepare(head)
            take_grads(head)
            if head == 0:
                for copy in copies[1:4]:
                    copy.wait()
            attend_back(head)
            give_grads(head)
            start_trade(head)
            if head == 0:
                copies[4].wait()
            start_proj(head)
            for act in events.get((head + 1) * BLOCKS - 0.5, ()):
                act()
        for offset in mates:
            bias_copy(offset).start()
        if rest:
            act, *which = rest.pop(0)
            act(*which)
        sum_proj(final)
        sum_bias()
        for act, *which in rest:
            act(*which)
        take_proj(final)
        for head in range(head_total):
            finish_proj(head)
            traded_own_copy(head).wait()
            for offset in peers:
                traded_copy(head, offset).wait()

    pl.run_scoped(
        attention_phase,
        pltpu.VMEM(qkv_source.shape, BF16),
        pltpu.VMEM(out_source.shape, F32),
        pltpu.VMEM(log_source.shape, F32),
        pltpu.VMEM(seg_source.shape, jnp.int32),
        pltpu.VMEM(input_source.shape, BF16),
        pltpu.VMEM((head_total, mp_size, 3, half, 2 * HEAD_DIM), BF16),
        pltpu.VMEM((ROW_LEN, 3 * HEAD_DIM), BF16),
        pltpu.VMEM((BLOCKS, 1, BLOCK), jnp.int32),
        pltpu.VMEM((ROW_LEN, HEAD_DIM), BF16),
        pltpu.VMEM((ROW_LEN, HEAD_DIM + EXTRA), BF16),
        pltpu.VMEM((BLOCKS, HEAD_DIM, BLOCK), BF16),
        pltpu.VMEM((ROW_LEN, HEAD_DIM + EXTRA), BF16),
        pltpu.VMEM((ROW_LEN, HEAD_DIM), F32),
        pltpu.VMEM((ROW_LEN, HEAD_DIM), F32),
        pltpu.VMEM((ROW_LEN, HEAD_DIM), F32),
        pltpu.VMEM((3 * HEAD_DIM, width), F32),
    )

    for hop in line.hops:
        if (take_weight, hop) not in done:
            both_sides(take_weight, hop)
    for level in levels:
        for hop in line.hops:
            if (trade_weight, level, hop) not in done:
                both_sides(trade_weight, level, hop)

    def sent_trades(side, hop):
        for level in levels:
            weight_trade_copy(level, side, hop).wait_send()

    for side, hop in line.ways:
        line.if_sent(side, hop)(lambda side=side, hop=hop: weight_copy(side, hop).wait_send())
        line.if_taken(side, hop)(partial(sent_trades, side, hop))
    weight_own_copy.wait()
    for head in range(head_total):
        for offset in peers:
            grads_copy(head, offset).wait_send()
        for offset in mates:
            proj_copy(head, offset).wait_send()
            proj_spread_copy(head, offset).wait_send()
    for offset in mates:
        bias_copy(offset).wait_send()
    for level in levels:
        vector_copy(level).wait_send()
        for which in arrays:
            spread_copy(which, level).wait_send()
            for turn in turns:
                level_copy(which, level, turn).wait_send()
    for offset in peers:
        vector_last_copy(offset).wait_send()
        for which in arrays:
            last_copy(which, offset).wait_send()


def rear(frames, heads_low, out_grad, seg_row, in_bias, small, weights, proj_weight, saved, bits):
    local_rows, width = frames.shape
    qkv_low, out_cols = saved[:2]
    mp_size, units = weights[1].shape[:2]
    head_total = out_cols.shape[0]
    half, lanes = local_rows // 2, 2 * HEAD_DIM
    peers = mp_size - 1
    slots = 2**bits
    head_rows = -(-width // mp_size // slots // 16) * 16
    anywhere = pl.BlockSpec(memory_space=pl.ANY)
    blocks = [(width // slots, units), (units // slots, width), (head_rows, width)]
    proj_block = (3 * HEAD_DIM // slots, width)
    bias_block = (8, 2 * 128)
    vector_block = (8 + -(-mp_size // 8) * 8, width)

    def halves(shape, lead=()):
        return [pltpu.VMEM(lead + (slots >> (level + 1),) + shape, BF16) for level in range(bits)]

    def sems(*shapes):
        return [pltpu.SemaphoreType.DMA(shape) for shape in shapes for _ in range(2)]

    piece = pltpu.VMEM((mp_size, head_total, half, lanes), BF16)
    return pl.pallas_call(
        partial(rear_kernel, bits),
        out_shape=(
            jax.ShapeDtypeStruct((local_rows, width), F32),
            jax.ShapeDtypeStruct((local_rows, width), F32),
            *(jax.ShapeDtypeStruct((mp_size, slots) + block, BF16) for block in blocks),
            jax.ShapeDtypeStruct((mp_size,) + proj_weight.shape, BF16),
            jax.ShapeDtypeStruct((head_total, mp_size, 3, half, lanes), BF16),
            *(jax.ShapeDtypeStruct((slots,) + block, BF16) for block in blocks),
            jax.ShapeDtypeStruct((3, head_total * HEAD_DIM, width), BF16),
            jax.ShapeDtypeStruct(vector_block, F32),
            jax.ShapeDtypeStruct(bias_block, F32),
        ),
        in_specs=[whole()] * 6 + [anywhere] * 12,
        out_specs=(anywhere,) * 7 + (whole(),) * 6,
        scratch_shapes=[
            piece,
            pltpu.VMEM((head_total, mp_size, half, lanes), BF16),
            [pltpu.VMEM((2, slots // 2) + block, BF16) for block in blocks],
            [halves(block, (mp_size,)) for block in blocks],
            [pltpu.VMEM((peers, 1) + block, BF16) for block in blocks],
            [pltpu.VMEM((slots,) + proj_block, BF16) for _ in range(head_total)],
            [pltpu.VMEM((slots - 1,) + proj_block, BF16) for _ in range(head_total)],
            [pltpu.VMEM((slots,) + proj_block, BF16) for _ in range(head_total)],
            [pltpu.VMEM(vector_block, F32) for _ in range(bits + 1)],
            [pltpu.VMEM(vector_block, F32) for _ in range(bits)],
            pltpu.VMEM((mp_size,) + vector_block, F32),
            pltpu.VMEM((slots,) + bias_block, F32),
            pltpu.SemaphoreType.DMA((3,)),
            pltpu.SemaphoreType.DMA((mp_size,)),
            pltpu.SemaphoreType.DMA((mp_size,)),
            pltpu.SemaphoreType.DMA((mp_size,)),
            pltpu.SemaphoreType.DMA((2,)),
            pltpu.SemaphoreType.DMA,
            pltpu.SemaphoreType.DMA((2,)),
            pltpu.SemaphoreType.DMA((5,)),
            pltpu.SemaphoreType.DMA,
            *sems((2, peers), (max(bits, 1), 2, peers)),
            pltpu.SemaphoreType.DMA((3, 2)),
            pltpu.SemaphoreType.DMA((head_total,)),
            *sems((head_total, peers)),
            pltpu.SemaphoreType.DMA((head_total,)),
            *sems(
                (head_total, peers),
                (3, bits, mp_size),
                (3, peers),
                (3, bits),
                (2, head_total, slots - 1),
                (bits,),
                (peers,),
                (slots - 1,),
            ),
        ],
        compiler_params=pltpu.CompilerParams(
            collective_id=1, has_side_effects=True, vmem_limit_bytes=REAR_VMEM_BYTES
        ),
        cost_estimate=pl.CostEstimate(
            flops=40 * head_total * ROW_LEN * ROW_LEN * HEAD_DIM,
            bytes_accessed=96 * 1024 * 1024,
            transcendentals=head_total * ROW_LEN * ROW_LEN,
        ),
        name="rear",
    )(seg_row, in_bias, *small, frames, heads_low, out_grad, *weights, proj_weight, *saved)


def finish_kernel(
    traded,
    proj_all,
    resid_grad,
    in_sum,
    down_sum,
    head_sum,
    proj_sum,
    vector_sum,
    bias_sum,
    stream_grad,
    in_grad,
    down_grad,
    out_grad,
    proj_grad,
    query_bias_grad,
    value_bias_grad,
    out_bias_grad,
    in_bias_grad,
    down_bias_grad,
    gain_grad,
    shift_grad,
    columns,
    weight_buf,
    sems,
):
    head_total, mp_size = traded.shape[:2]
    half = traded.shape[3]
    head_cols = head_total * HEAD_DIM
    copies = [
        pltpu.make_async_copy(
            proj_all.at[index],
            weight_buf.at[index],
            sems.at[index],
        )
        for index in range(mp_size)
    ]
    for copy in copies:
        copy.start()
    for sums, grad in ((in_sum, in_grad), (down_sum, down_grad), (head_sum, out_grad)):
        rows = grad.shape[0] // sums.shape[0]
        for slot in range(sums.shape[0]):
            grad[slot * rows : (slot + 1) * rows] = sums[slot, :rows].astype(F32)
    proj_grad[...] = proj_sum[...].astype(F32)
    query_bias_grad[...] = bias_sum[0:1, :head_cols]
    value_bias_grad[...] = bias_sum[2:3, :head_cols]
    gain_grad[...] = vector_sum[0:2]
    shift_grad[...] = vector_sum[2:4]
    out_bias_grad[...] = vector_sum[4:5]
    down_bias_grad[...] = vector_sum[5:6]
    in_bias_grad[...] = vector_sum[pl.ds(8 + lax.axis_index("mp"), 1)]
    stream_grad[...] = resid_grad[...]
    for index in range(mp_size):
        for head in range(head_total):
            for part in range(3):
                at = part * head_cols + head * HEAD_DIM
                for side in range(2):
                    columns[side * half : (side + 1) * half, at : at + HEAD_DIM] = traded[
                        head, index, part, :, side * HEAD_DIM : (side + 1) * HEAD_DIM
                    ]
        copies[index].wait()
        stream_grad[...] += dot(columns[...], weight_buf[index])


def finish(traded, proj_all, resid_grad, sums):
    head_total, mp_size = traded.shape[:2]
    head_cols = head_total * HEAD_DIM
    local_rows, width = resid_grad.shape
    units = sums[0].shape[0] * sums[0].shape[1]
    row = jax.ShapeDtypeStruct((1, width), F32)
    head_row = jax.ShapeDtypeStruct((1, head_cols), F32)
    anywhere = pl.BlockSpec(memory_space=pl.ANY)
    return pl.pallas_call(
        finish_kernel,
        out_shape=(
            jax.ShapeDtypeStruct((local_rows, width), F32),
            jax.ShapeDtypeStruct((units, width), F32),
            jax.ShapeDtypeStruct((units, width), F32),
            jax.ShapeDtypeStruct((head_cols, width), F32),
            jax.ShapeDtypeStruct((3, head_cols, width), F32),
            head_row,
            head_row,
            row,
            jax.ShapeDtypeStruct((1, units), F32),
            row,
            jax.ShapeDtypeStruct((2, width), F32),
            jax.ShapeDtypeStruct((2, width), F32),
        ),
        in_specs=[whole(), anywhere] + [whole()] * 7,
        out_specs=(whole(),) * 12,
        scratch_shapes=[
            pltpu.VMEM((local_rows, 3 * head_cols), BF16),
            pltpu.VMEM((mp_size, 3 * head_cols, width), BF16),
            pltpu.SemaphoreType.DMA((mp_size,)),
        ],
        compiler_params=pltpu.CompilerParams(vmem_limit_bytes=VMEM_BYTES),
        cost_estimate=pl.CostEstimate(
            flops=6 * local_rows * width * width, bytes_accessed=24 * 1024 * 1024, transcendentals=0
        ),
        name="finish",
    )(traded, proj_all, resid_grad, *sums)


def dp_groups():
    total = lax.axis_size("dp")
    size = min(8, total)
    groups = [list(range(start, start + size)) for start in range(0, total, size)]
    return (size, groups)


def on_device(
    frames,
    segment_ids,
    qkv_weight,
    q_bias,
    v_bias,
    out_weight,
    out_bias,
    ff_in_weight,
    ff_in_bias,
    ff_out_weight,
    ff_out_bias,
    norm_gain,
    norm_shift,
    out_grad,
):
    local_rows, width = frames.shape
    mp_size = lax.axis_size("mp")
    group, groups = dp_groups()
    bits = group_bits(lax.axis_size("dp"))
    slots = 2**bits

    proj_weight = qkv_weight[0].transpose(0, 2, 1)
    seg_row = segment_ids.reshape(1, ROW_LEN)
    (
        input_all,
        qkv_low,
        in_all,
        down_all,
        out_all,
        in_bias_all,
        seg_col,
        out_cols,
        log_total,
        heads_low,
    ) = front(
        frames,
        proj_weight,
        q_bias,
        v_bias,
        seg_row,
        (ff_in_weight[0], ff_out_weight[0], out_weight[0]),
        ff_in_bias,
        mp_size,
        bits,
    )
    block_out, resid_grad, _, _, _, proj_all, traded, *summed = rear(
        frames,
        heads_low,
        out_grad,
        seg_row,
        in_bias_all,
        (out_bias, ff_out_bias, norm_gain[0], norm_shift[0]),
        (in_all, down_all, out_all),
        proj_weight.reshape(slots, -1, width),
        (qkv_low, out_cols, log_total, seg_col, input_all),
        bits,
    )
    if len(groups) > 1:
        across = [list(range(at, lax.axis_size("dp"), group)) for at in range(group)]
        summed = lax.psum(summed, "dp", axis_index_groups=across)
    (
        stream_grad,
        in_weight_grad,
        down_weight_grad,
        out_weight_grad,
        proj_grad,
        query_bias_grad,
        value_bias_grad,
        head_bias_grad,
        in_bias_grad,
        down_bias_grad,
        gain_grad,
        shift_grad,
    ) = finish(traded, proj_all.reshape(mp_size, -1, width), resid_grad, summed)
    return (
        block_out,
        stream_grad,
        proj_grad.transpose(0, 2, 1)[None],
        query_bias_grad,
        value_bias_grad,
        out_weight_grad[None],
        head_bias_grad,
        in_weight_grad[None],
        in_bias_grad,
        down_weight_grad[None],
        down_bias_grad,
        gain_grad[None],
        shift_grad[None],
    )


def solution(mesh):
    return jax.shard_map(
        on_device,
        mesh=mesh,
        in_specs=(
            P(("dp", "mp"), None),
            P("dp"),
            P(None, None, None, "mp"),
            P(None, "mp"),
            P(None, "mp"),
            P(None, "mp", None),
            P(),
            P(None, None, "mp"),
            P(None, "mp"),
            P(None, "mp", None),
            P(),
            P(),
            P(),
            P(("dp", "mp"), None),
        ),
        out_specs=(
            P(("dp", "mp"), None),
            P(("dp", "mp"), None),
            P(None, None, None, "mp"),
            P(None, "mp"),
            P(None, "mp"),
            P(None, "mp", None),
            P(),
            P(None, None, "mp"),
            P(None, "mp"),
            P(None, "mp", None),
            P(),
            P(),
            P(),
        ),
        check_vma=False,
    )
```

```python
import itertools
from functools import partial

import jax
import jax.numpy as jnp
from jax import lax
from jax.experimental import pallas as pl
from jax.experimental.pallas import tpu as pltpu
from jax.sharding import PartitionSpec as P

HEAD_DIM = 64
ROW_LEN = 2304
BLOCK = 768
BLOCKS = ROW_LEN // BLOCK
EXTRA = 16
SCALE = HEAD_DIM ** (-0.5)
MASKED = -1e30
F32 = jnp.float32
BF16 = jnp.bfloat16
VMEM_BYTES = 56 * 1024 * 1024
REAR_VMEM_BYTES = 63 * 1024 * 1024


def dot_rows(left, right):
    return lax.dot_general(left, right, (((1,), (1,)), ((), ())), preferred_element_type=F32)


def dot_cols(left, right):
    return lax.dot_general(left, right, (((0,), (0,)), ((), ())), preferred_element_type=F32)


def dot(left, right):
    return jnp.dot(left, right, preferred_element_type=F32)


def block_rows(number):
    return pl.ds(pl.multiple_of(number * BLOCK, BLOCK), BLOCK)


def as_pieces(row):
    high = row.astype(BF16).astype(F32)
    middle = (row - high).astype(BF16).astype(F32)
    last = row - high - middle
    place = lax.broadcasted_iota(jnp.int32, (EXTRA, row.shape[1]), 0)
    pieces = jnp.where(place == 0, high, jnp.where(place == 1, middle, jnp.where(place == 2, last, 0.0)))
    return pieces.astype(BF16)


def ones_columns(rows):
    place = lax.broadcasted_iota(jnp.int32, (rows, EXTRA), 1)
    return jnp.where(place < 3, 1.0, 0.0).astype(BF16)


def whole(memory_space=pltpu.VMEM):
    return pl.BlockSpec(memory_space=memory_space)


MESH = pl.DeviceIdType.MESH


def group_bits(dp_size):
    return min(3, dp_size.bit_length() - 1)


def place_in(dp_index, order):
    slot = 0
    for at, bit in enumerate(order):
        slot = slot + (dp_index // 2**bit) % 2 * 2**at
    return slot


def partner_of(dp_index, bit):
    return dp_index + (1 - 2 * ((dp_index // 2**bit) % 2)) * 2**bit


def mate_of(dp_index, offset, size):
    place = lax.rem(dp_index, size)
    return dp_index - place + lax.rem(place + offset, size)


def enter(dp_index, mp_index, mp_size, bits, whole_group=False):
    barrier = pltpu.get_barrier_semaphore()
    for offset in range(1, mp_size):
        pl.semaphore_signal(
            barrier, device_id={"mp": lax.rem(mp_index + offset, mp_size)}, device_id_type=MESH
        )
    if whole_group:
        partners = [mate_of(dp_index, offset, 2**bits) for offset in range(1, 2**bits)]
    else:
        partners = [partner_of(dp_index, bit) for bit in range(bits)]
    for partner in partners:
        pl.semaphore_signal(barrier, device_id={"dp": partner}, device_id_type=MESH)
    pl.semaphore_wait(barrier, mp_size - 1 + len(partners))


def send(src, dst, sems, at, device_id):
    return pltpu.make_async_remote_copy(
        src_ref=src,
        dst_ref=dst,
        send_sem=sems[0].at[at],
        recv_sem=sems[1].at[at],
        device_id=device_id,
        device_id_type=MESH,
    )


def gather_orders(bits):
    if bits == 3:
        return ((1, 2, 0), (2, 1, 0), (1, 2), (1, 2, 0))
    return (tuple(range(bits)),) * 4


SIDES = (1, -1)


def inside(index, size):
    return jnp.logical_and(index >= 0, index < size)


class Line:
    def __init__(self, mp_size, me):
        self.size = mp_size
        self.me = me
        self.hops = range(mp_size - 1)
        self.ways = [(side, hop) for hop in self.hops for side in (0, 1)]

    def wrapped(self, index):
        return lax.rem(index + self.size, self.size)

    def chunk(self, side, hop):
        return self.me - SIDES[side] * hop

    def place(self, side, hop):
        return self.wrapped(self.chunk(side, hop))

    def sends(self, side, hop):
        there = inside(self.me + SIDES[side], self.size)
        return jnp.logical_and(there, inside(self.chunk(side, hop), self.size))

    def if_sent(self, side, hop):
        return pl.when(self.sends(side, hop))

    def if_taken(self, side, hop):
        return pl.when(inside(self.chunk(side, hop + 1), self.size))

    def neighbour(self, side):
        return {"mp": self.wrapped(self.me + SIDES[side])}


def front_kernel(
    bits,
    frames,
    qkv_weight,
    q_bias,
    v_bias,
    seg_row,
    in_weight,
    down_weight,
    out_weight,
    in_bias,
    input_all,
    qkv_low,
    in_all,
    down_all,
    out_all,
    bias_all,
    seg_col,
    out_cols,
    log_total,
    heads_low,
    bias_buf,
    key_cols,
    value_buf,
    out_buf,
    staged,
    heads_in,
    own_sems,
    frame_send,
    frame_recv,
    bias_send,
    bias_recv,
    first_send,
    first_recv,
    later_send,
    later_recv,
    heads_own,
    heads_send,
    heads_recv,
):
    mp_size = in_all.shape[0]
    me = lax.axis_index("mp")
    dp_index = lax.axis_index("dp")
    local_rows = frames.shape[0]
    half = local_rows // 2
    head_total = out_cols.shape[0]
    orders = gather_orders(bits)[:3]
    parts = ((in_weight, in_all), (down_weight, down_all), (out_weight, out_all))
    line = Line(mp_size, me)
    hops, ways, wrapped = line.hops, line.ways, line.wrapped
    enter(dp_index, me, mp_size, bits)

    def slots(which, level):
        count = parts[which][0].shape[0] // 2 ** len(orders[which])
        start = place_in(dp_index, orders[which]) // 2**level * 2**level
        return pl.ds(pl.multiple_of(start * count, 16), count * 2**level)

    def first_copy(which, side, hop):
        rows = slots(which, 0)
        place = parts[which][1].at[line.place(side, hop), rows]
        source = parts[which][0].at[rows] if hop == 0 else place
        sems = (first_send, first_recv)
        return send(source, place, sems, (which, side, hop), line.neighbour(side))

    def later_copy(which, level, side, hop):
        held = parts[which][1].at[line.place(side, hop + 1), slots(which, level)]
        partner = {"dp": partner_of(dp_index, orders[which][level])}
        return send(held, held, (later_send, later_recv), (which, level, side, hop), partner)

    def frame_rows(index):
        return pl.ds(pl.multiple_of(wrapped(index) * local_rows, local_rows), local_rows)

    def frame_copy(side, hop):
        place = input_all.at[frame_rows(line.chunk(side, hop))]
        source = frames if hop == 0 else place
        return send(source, place, (frame_send, frame_recv), (side, hop), line.neighbour(side))

    def bias_copy(side, hop):
        place = bias_all.at[line.place(side, hop)]
        source = bias_buf if hop == 0 else place
        return send(source, place, (bias_send, bias_recv), (side, hop), line.neighbour(side))

    def project(index):
        rows = frame_rows(index)
        inputs = input_all[rows]
        for part, bias in enumerate((q_bias, None, v_bias)):
            products = dot_rows(inputs, qkv_weight[part])
            if bias is not None:
                products = products + bias[...].astype(F32)
            qkv_low[part, rows] = products.astype(BF16)

    def start_slices(side, hop):
        for which in range(3):
            first_copy(which, side, hop).start()
        bias_copy(side, hop).start()

    def take_slices(side, hop):
        for which in range(3):
            first_copy(which, side, hop).wait_recv()
        bias_copy(side, hop).wait_recv()
        if 0 < hop < mp_size - 2:
            line.if_sent(side, hop + 1)(partial(start_slices, side, hop + 1))
        for which in range(3):
            if orders[which]:
                later_copy(which, 0, side, hop).start()

    def trade_slices(level, side, hop):
        for which in range(3):
            if level < len(orders[which]):
                later_copy(which, level, side, hop).wait_recv()
            if level + 1 < len(orders[which]):
                later_copy(which, level + 1, side, hop).start()

    def take_hop(hop):
        for side in (0, 1):
            line.if_taken(side, hop)(partial(take_slices, side, hop))

    def trade_hop(level, hop):
        for side in (0, 1):
            line.if_taken(side, hop)(partial(trade_slices, level, side, hop))


    bias_buf[...] = jnp.broadcast_to(in_bias[...], bias_buf.shape)
    for side in (0, 1):
        line.if_sent(side, 0)(partial(start_slices, side, 0))
    for side in (0, 1):
        line.if_sent(side, 0)(lambda side=side: frame_copy(side, 0).start())
    own = [
        pltpu.make_async_copy(shard, gathered.at[me], own_sems.at[at])
        for at, (shard, gathered) in enumerate(parts + ((bias_buf, bias_all),))
    ]
    for copy in own:
        copy.start()
    input_all[frame_rows(me)] = frames[...]
    project(me)
    for step in range(BLOCKS):
        ids = jnp.broadcast_to(seg_row[:, step * BLOCK : (step + 1) * BLOCK].astype(F32), (128, BLOCK))
        seg_col[step * BLOCK : (step + 1) * BLOCK] = ids.T.astype(jnp.int32)

    def take_frames(side, hop):
        frame_copy(side, hop).wait_recv()
        if hop + 1 < mp_size - 1:
            line.if_sent(side, hop + 1)(lambda: frame_copy(side, hop + 1).start())

    def project_taken(side, hop):
        project(line.chunk(side, hop + 1))

    for hop in hops:
        for side in (0, 1):
            line.if_taken(side, hop)(partial(take_frames, side, hop))
        if hop == 0:
            take_hop(0)
        elif hop - 1 < bits:
            trade_hop(hop - 1, 0)
        for side in (0, 1):
            free = line.sends(side, hop)
            if hop + 1 < mp_size - 1:
                free = jnp.logical_and(free, jnp.logical_not(line.sends(side, hop + 1)))
            if mp_size > 2:
                passes = jnp.logical_and(free, line.sends(side, 1))
                pl.when(passes)(partial(start_slices, side, 1))
        for side in (0, 1):
            line.if_taken(side, hop)(partial(project_taken, side, hop))

    schedule = (
        (1, take_hop, 1),
        (3, trade_hop, 0, 1),
        (4, take_hop, 2),
        (6, trade_hop, 1, 1),
        (6, trade_hop, 0, 2),
    )
    events = {}
    done = {(take_hop, 0)} | {(trade_hop, hop - 1, 0) for hop in hops if 0 < hop <= bits}
    for at, act, *which in schedule:
        if which[-1] in hops and (act is take_hop or which[0] < bits):
            events.setdefault((at // BLOCKS, at % BLOCKS), []).append(partial(act, *which))
            done.add((act, *which))

    def attend(head):
        cols = slice(head * HEAD_DIM, (head + 1) * HEAD_DIM)
        lane = lax.broadcasted_iota(jnp.int32, (BLOCK, EXTRA), 1)
        for step in range(BLOCKS):
            rows = slice(step * BLOCK, (step + 1) * BLOCK)
            key_cols[step] = qkv_low[1, rows, cols].T
            value_buf[step, :, :HEAD_DIM] = qkv_low[2, rows, cols]
            value_buf[step, :, HEAD_DIM:] = jnp.where(lane == 0, 1.0, 0.0).astype(BF16)

        def query_block(number, _):
            rows = block_rows(number)
            queries = qkv_low[0, rows, cols] * SCALE

            def scores_of(step):
                ids = seg_row[:, step * BLOCK : (step + 1) * BLOCK]
                same = jnp.concatenate([seg_col[rows]] * (BLOCK // 128), axis=1) == ids
                return jnp.where(same, dot(queries, key_cols[step]), MASKED)

            peak = jnp.full((BLOCK, 1), MASKED, F32)
            mixed = jnp.zeros((BLOCK, HEAD_DIM + EXTRA), F32)
            scores = scores_of(0)
            for step in range(BLOCKS):
                ahead = scores_of(step + 1) if step + 1 < BLOCKS else None
                higher = jnp.maximum(peak, jnp.max(scores, axis=1, keepdims=True))
                soft = jnp.exp(scores - higher).astype(BF16)
                mixed = mixed * jnp.exp(peak - higher) + dot(soft, value_buf[step])
                peak, scores = higher, ahead
            total = mixed[:, HEAD_DIM : HEAD_DIM + 1]
            mixed = mixed[:, :HEAD_DIM] / total
            logs = jnp.broadcast_to(peak + jnp.log(total), (BLOCK, HEAD_DIM))
            both = jnp.concatenate([mixed, logs], axis=1).T
            out_cols[head, number] = both[:HEAD_DIM]
            log_total[head, number] = both[HEAD_DIM : HEAD_DIM + 1]
            out_buf[rows] = mixed.astype(BF16)
            for at in range(BLOCKS):
                if (head, at) in events:

                    @pl.when(number == at)
                    def _():
                        for act in events[(head, at)]:
                            act()

            return 0

        lax.fori_loop(0, BLOCKS, query_block, 0)

    def heads_copy(head, offset):
        return send(
            staged.at[head, wrapped(me + offset)],
            heads_in.at[head, me],
            (heads_send, heads_recv),
            (head, offset - 1),
            {"mp": wrapped(me + offset)},
        )

    def heads_own_copy(head):
        return pltpu.make_async_copy(
            staged.at[head, me], heads_in.at[head, me], heads_own.at[head]
        )

    peers = range(1, mp_size)
    for head in range(head_total):
        attend(head)
        for chunk in range(mp_size):
            for side in range(2):
                start = (2 * chunk + side) * half
                staged[head, chunk, :, side * HEAD_DIM : (side + 1) * HEAD_DIM] = out_buf[
                    start : start + half
                ]
        for offset in peers:
            heads_copy(head, offset).start()
        heads_own_copy(head).start()

    for hop in hops:
        if (take_hop, hop) not in done:
            take_hop(hop)
    for level in range(bits):
        for hop in hops:
            if (trade_hop, level, hop) not in done:
                trade_hop(level, hop)
    for head in range(head_total):
        heads_own_copy(head).wait()
        for offset in peers:
            heads_copy(head, offset).wait_recv()
        for chunk in range(mp_size):
            for side in range(2):
                at = (chunk * head_total + head) * HEAD_DIM
                heads_low[side * half : (side + 1) * half, at : at + HEAD_DIM] = heads_in[
                    head, chunk, :, side * HEAD_DIM : (side + 1) * HEAD_DIM
                ]
        for offset in peers:
            heads_copy(head, offset).wait_send()

    def sent_all(side, hop):
        frame_copy(side, hop).wait_send()
        bias_copy(side, hop).wait_send()
        for which in range(3):
            first_copy(which, side, hop).wait_send()

    def sent_later(side, hop):
        for which in range(3):
            for level in range(len(orders[which])):
                later_copy(which, level, side, hop).wait_send()

    for side, hop in ways:
        line.if_sent(side, hop)(partial(sent_all, side, hop))
        line.if_taken(side, hop)(partial(sent_later, side, hop))
    for copy in own:
        copy.wait()


def front(frames, qkv_weight, q_bias, v_bias, seg_row, weights, in_bias, mp_size, bits):
    local_rows, width = frames.shape
    head_cols = qkv_weight.shape[1]
    head_total = head_cols // HEAD_DIM
    peers = mp_size - 1
    levels = max(bits, 1)
    anywhere = pl.BlockSpec(memory_space=pl.ANY)
    in_weight, down_weight, out_weight = weights

    def sems(*shapes):
        return [pltpu.SemaphoreType.DMA(shape) for shape in shapes for _ in range(2)]

    piece = (head_total, mp_size, local_rows // 2, 2 * HEAD_DIM)
    return pl.pallas_call(
        partial(front_kernel, bits),
        out_shape=(
            jax.ShapeDtypeStruct((ROW_LEN, width), BF16),
            jax.ShapeDtypeStruct((3, ROW_LEN, head_cols), BF16),
            jax.ShapeDtypeStruct((mp_size,) + in_weight.shape, BF16),
            jax.ShapeDtypeStruct((mp_size,) + down_weight.shape, BF16),
            jax.ShapeDtypeStruct((mp_size,) + out_weight.shape, BF16),
            jax.ShapeDtypeStruct((mp_size, 16, in_bias.shape[1]), BF16),
            jax.ShapeDtypeStruct((ROW_LEN, 128), jnp.int32),
            jax.ShapeDtypeStruct((head_total, BLOCKS, HEAD_DIM, BLOCK), F32),
            jax.ShapeDtypeStruct((head_total, BLOCKS, 1, BLOCK), F32),
            jax.ShapeDtypeStruct((local_rows, width), BF16),
        ),
        in_specs=[whole()] * 5 + [anywhere] * 3 + [whole()],
        out_specs=(whole(), whole()) + (anywhere,) * 4 + (whole(),) * 4,
        scratch_shapes=[
            pltpu.VMEM((16, in_bias.shape[1]), BF16),
            pltpu.VMEM((BLOCKS, HEAD_DIM, BLOCK), BF16),
            pltpu.VMEM((BLOCKS, BLOCK, HEAD_DIM + EXTRA), BF16),
            pltpu.VMEM((ROW_LEN, HEAD_DIM), BF16),
            pltpu.VMEM(piece, BF16),
            pltpu.VMEM(piece, BF16),
            pltpu.SemaphoreType.DMA((4,)),
            *sems((2, peers), (2, peers), (3, 2, peers), (3, levels, 2, peers)),
            pltpu.SemaphoreType.DMA((head_total,)),
            *sems((head_total, peers)),
        ],
        compiler_params=pltpu.CompilerParams(
            collective_id=0, has_side_effects=True, vmem_limit_bytes=VMEM_BYTES
        ),
        cost_estimate=pl.CostEstimate(
            flops=16 * head_total * ROW_LEN * ROW_LEN * HEAD_DIM,
            bytes_accessed=32 * 1024 * 1024,
            transcendentals=head_total * ROW_LEN * ROW_LEN,
        ),
        name="front",
    )(frames, qkv_weight, q_bias, v_bias, seg_row, in_weight, down_weight, out_weight, in_bias)


def reduce_orders(bits):
    if bits == 3:
        return ((0, 1, 2), (0, 2, 1), (1, 2, 0))
    return (tuple(range(bits)),) * 3


def norm_rows(inputs, norm_gain, norm_shift):
    row_mean = jnp.mean(inputs, axis=-1, keepdims=True)
    centred = inputs - row_mean
    variance = jnp.mean(centred * centred, axis=-1, keepdims=True)
    inv_std = lax.rsqrt(variance + 1e-05)
    normed = centred * inv_std
    return (normed * norm_gain + norm_shift, normed, inv_std)


def norm_back(cotangent, normed, inv_std, norm_gain):
    scaled = cotangent * norm_gain
    adjusted = (
        scaled
        - jnp.mean(scaled, axis=-1, keepdims=True)
        - normed * jnp.mean(scaled * normed, axis=-1, keepdims=True)
    )
    return adjusted * inv_std


def sum_rows(array):
    return jnp.sum(array.astype(F32), axis=0, keepdims=True)


def rear_kernel(
    bits,
    seg_row,
    in_bias,
    out_bias,
    down_bias,
    norm_gain,
    norm_shift,
    frames,
    heads_low,
    out_grad,
    in_all,
    down_all,
    out_all,
    proj_weight,
    qkv_source,
    out_source,
    log_source,
    seg_source,
    input_source,
    block_out,
    resid_grad,
    in_grads,
    down_grads,
    head_grads,
    proj_all,
    traded,
    in_sum,
    down_sum,
    head_sum,
    proj_sum,
    vector_sum,
    bias_sum,
    grads_out,
    grads_in,
    kept,
    taken,
    last,
    proj,
    proj_taken,
    proj_slots,
    vectors,
    vectors_taken,
    vectors_all,
    biases,
    load_sems,
    in_sems,
    down_sems,
    out_sems,
    given_sems,
    head_sem,
    store_sems,
    attention_sems,
    weight_own,
    weight_send,
    weight_recv,
    weight_trade_send,
    weight_trade_recv,
    keep_sems,
    grads_own,
    grads_send,
    grads_recv,
    traded_own,
    traded_send,
    traded_recv,
    level_send,
    level_recv,
    last_send,
    last_recv,
    back_send,
    back_recv,
    proj_send,
    proj_recv,
    vector_send,
    vector_recv,
    vector_last_send,
    vector_last_recv,
    bias_send,
    bias_recv,
):
    mp_size, units, width = down_all.shape
    head_total = grads_out.shape[1]
    half = grads_out.shape[2]
    head_cols = width // mp_size
    slots = 2**bits
    me = lax.axis_index("mp")
    dp_index = lax.axis_index("dp")
    peers = range(1, mp_size)
    turns = range(mp_size)
    levels = list(range(bits))
    orders = reduce_orders(bits)
    partials = (in_grads, down_grads, head_grads)
    sums = (in_sum, down_sum, head_sum)
    arrays = range(3)
    vector = vectors[0]
    place = lax.rem(dp_index, slots)
    mates = range(1, slots)
    odd = lax.rem(me, 2)
    leaving = (2, 3 - 2 * odd, 1 + 2 * odd) if mp_size == 4 else peers

    def target(offset):
        return lax.rem(me + offset, mp_size)

    def bit_of(which, level):
        return (dp_index // 2 ** orders[which][level]) % 2


    def part_of(turn):
        return target(turn + 1)

    def level_copy(which, level, turn):
        count = 2 ** (bits - 1 - level)
        other = (1 - bit_of(which, level)) * count
        part = pl.ds(part_of(turn), 1)
        source = partials[which] if level == 0 else taken[which][level - 1]
        return send(
            source.at[part, pl.ds(other, count)],
            taken[which][level].at[part],
            (level_send, level_recv),
            (which, level, turn),
            {"dp": partner_of(dp_index, orders[which][level])},
        )

    def keep_copy(which, turn):
        count = 2 ** (bits - 1)
        return pltpu.make_async_copy(
            partials[which].at[part_of(turn), pl.ds(bit_of(which, 0) * count, count)],
            kept[which].at[turn % 2],
            keep_sems.at[which, turn % 2],
        )

    def last_copy(which, offset):
        return send(
            taken[which][bits - 1].at[target(offset)],
            last[which].at[offset - 1],
            (last_send, last_recv),
            (which, offset - 1),
            {"mp": target(offset)},
        )

    def add_level(which, level, turn):
        level_copy(which, level, turn).wait_recv()
        count = 2 ** (bits - 1 - level)
        if level == 0:
            keep_copy(which, turn).wait()
        start = bit_of(which, level) * count
        into = taken[which][level]
        part = part_of(turn)
        for slot in range(count):
            if level == 0:
                mine = kept[which][turn % 2, slot]
            else:
                mine = taken[which][level - 1][part, start + slot]
            into[part, slot] = into[part, slot] + mine
        if level == 0 and turn + 2 < mp_size:
            keep_copy(which, turn + 2).start()
        if level + 1 < bits:
            level_copy(which, level + 1, turn).start()
        elif turn + 1 < mp_size:
            last_copy(which, turn + 1).start()

    def offer(which, turn):
        level_copy(which, 0, turn).start()
        if turn < 2:
            keep_copy(which, turn).start()

    def slot_of(order):
        return place_in(dp_index, order[::-1])

    def held_slots(order, level):
        count = 2 ** (bits - 1 - level)
        return pl.ds(slot_of(order) // count * count, count)

    def spread_copy(which, level):
        held = sums[which].at[held_slots(orders[which], level)]
        partner = {"dp": partner_of(dp_index, orders[which][level])}
        return send(held, held, (back_send, back_recv), (which, level), partner)

    def finish_sum(which):
        total = taken[which][bits - 1][me, 0].astype(F32)
        for offset in peers:
            last_copy(which, offset).wait_recv()
            total = total + last[which][offset - 1, 0].astype(F32)
        sums[which][slot_of(orders[which])] = total.astype(BF16)
        spread_copy(which, bits - 1).start()

    def spread(which, level):
        spread_copy(which, level).wait_recv()
        if level:
            spread_copy(which, level - 1).start()


    def mate(offset):
        return {"dp": mate_of(dp_index, offset, slots)}

    def proj_copy(head, offset):
        return send(
            proj[head].at[lax.rem(place + offset, slots)],
            proj_taken[head].at[offset - 1],
            (proj_send, proj_recv),
            (0, head, offset - 1),
            mate(offset),
        )

    def proj_spread_copy(head, offset):
        held = proj_slots[head].at[place]
        return send(held, held, (proj_send, proj_recv), (1, head, offset - 1), mate(offset))

    def sum_proj(head):
        total = proj[head][place].astype(F32)
        for offset in mates:
            proj_copy(head, offset).wait_recv()
            total = total + proj_taken[head][offset - 1].astype(F32)
        proj_slots[head][place] = total.astype(BF16)
        for offset in mates:
            proj_spread_copy(head, offset).start()

    def take_proj(head):
        for offset in mates:
            proj_spread_copy(head, offset).wait_recv()


    def vector_copy(level):
        return send(
            vectors[level],
            vectors_taken[level],
            (vector_send, vector_recv),
            level,
            {"dp": partner_of(dp_index, level)},
        )

    def vector_last_copy(offset):
        return send(
            vectors[bits],
            vectors_all.at[me],
            (vector_last_send, vector_last_recv),
            offset - 1,
            {"mp": target(offset)},
        )

    def add_vector(level):
        vector_copy(level).wait_recv()
        vectors[level + 1][...] = vectors[level][...] + vectors_taken[level][...]
        if level + 1 < bits:
            vector_copy(level + 1).start()
        else:
            vectors_all[me] = vectors[bits][...]
            for offset in peers:
                vector_last_copy(offset).start()

    def finish_vector():
        for offset in peers:
            vector_last_copy(offset).wait_recv()
        total = vectors_all[0]
        for index in peers:
            total = total + vectors_all[index]
        vector_sum[...] = total

    def bias_copy(offset):
        held = biases.at[place]
        return send(held, held, (bias_send, bias_recv), offset - 1, mate(offset))

    def sum_bias():
        for offset in mates:
            bias_copy(offset).wait_recv()
        total = biases[0]
        for at in range(1, slots):
            total = total + biases[at]
        bias_sum[...] = total

    def grads_copy(head, offset):
        return send(
            grads_out.at[target(offset), head],
            grads_in.at[head, me],
            (grads_send, grads_recv),
            (head, offset - 1),
            {"mp": target(offset)},
        )

    def grads_own_copy(head):
        return pltpu.make_async_copy(
            grads_out.at[me, head], grads_in.at[head, me], grads_own.at[head]
        )

    line = Line(mp_size, me)
    order = gather_orders(bits)[3]
    own_slot = place_in(dp_index, order)

    def weight_copy(side, hop):
        place = proj_all.at[line.place(side, hop), pl.ds(own_slot, 1)]
        source = proj_weight.at[pl.ds(own_slot, 1)] if hop == 0 else place
        return send(source, place, (weight_send, weight_recv), (side, hop), line.neighbour(side))

    def weight_trade_copy(level, side, hop):
        held = pl.ds(own_slot // 2**level * 2**level, 2**level)
        place = proj_all.at[line.place(side, hop + 1), held]
        partner = {"dp": partner_of(dp_index, order[level])}
        return send(place, place, (weight_trade_send, weight_trade_recv), (level, side, hop), partner)

    def take_weight(side, hop):
        weight_copy(side, hop).wait_recv()
        if hop + 1 < mp_size - 1:
            line.if_sent(side, hop + 1)(lambda: weight_copy(side, hop + 1).start())
        if bits:
            weight_trade_copy(0, side, hop).start()

    def trade_weight(level, side, hop):
        weight_trade_copy(level, side, hop).wait_recv()
        if level + 1 < bits:
            weight_trade_copy(level + 1, side, hop).start()

    def both_sides(act, *which):
        for side in (0, 1):
            line.if_taken(side, which[-1])(partial(act, *which[:-1], side, which[-1]))

    schedule = (
        (0, take_weight, 0),
        (1, take_weight, 1),
        (2, take_weight, 2),
        (2, trade_weight, 0, 0),
        (3, trade_weight, 0, 1),
        (3, trade_weight, 0, 2),
        (4, trade_weight, 1, 0),
        (6, trade_weight, 1, 1),
        (8, trade_weight, 1, 2),
    )
    done = set()

    def at_point(point, index=None):
        for at, act, *which in schedule:
            if which[-1] not in line.hops or (act is trade_weight and which[0] >= bits):
                continue
            if index is None and at == point:
                both_sides(act, *which)
                done.add((act, *which))
            if index is not None and point <= at < point + mp_size:
                pl.when(index == at - point)(partial(both_sides, act, *which))
                done.add((act, *which))

    def dense_phase(
        frames_buf,
        heads_buf,
        cotangent_buf,
        in_buf,
        down_buf,
        out_buf,
        hidden,
        slope,
        mid_buf,
        normed_buf,
        store_buf,
        low_buf,
        grad_buf,
        given,
        head_buf,
    ):
        loads = [
            pltpu.make_async_copy(source, into, load_sems.at[at])
            for at, (source, into) in enumerate(
                ((frames, frames_buf), (heads_low, heads_buf), (out_grad, cotangent_buf))
            )
        ]
        out_copies = [
            pltpu.make_async_copy(
                out_all.at[index],
                out_buf.at[pl.ds(index * head_cols, head_cols)],
                out_sems.at[index],
            )
            for index in range(mp_size)
        ]

        def in_copy(index):
            return pltpu.make_async_copy(in_all.at[index], in_buf.at[index], in_sems.at[index])

        def down_copy(index):
            return pltpu.make_async_copy(
                down_all.at[index], down_buf.at[index], down_sems.at[index]
            )

        def given_copy(which, turn):
            return pltpu.make_async_copy(
                given.at[turn % 2], partials[which].at[part_of(turn)], given_sems.at[turn % 2]
            )

        def store_copy(at):
            return pltpu.make_async_copy(
                store_buf, (block_out, resid_grad)[at], store_sems.at[at]
            )

        for copy in loads + out_copies:
            copy.start()
        for index in range(mp_size):
            in_copy(index).start()
            down_copy(index).start()
        enter(dp_index, me, mp_size, bits, whole_group=True)
        for side in (0, 1):
            line.if_sent(side, 0)(lambda side=side: weight_copy(side, 0).start())
        weight_own_copy.start()
        vector[...] = jnp.zeros_like(vector)
        gains = norm_gain[...].astype(F32)
        shifts = norm_shift[...].astype(F32)
        both = [slice(side * half, (side + 1) * half) for side in range(2)]

        for copy in loads + out_copies:
            copy.wait()
        branch = dot(heads_buf[...], out_buf[...]) + out_bias[...].astype(F32)
        mid, normed, inv_mid = norm_rows(
            frames_buf[...].astype(F32) + branch, gains[:1], shifts[:1]
        )
        mid_buf[...] = mid + down_bias[...].astype(F32)
        normed_buf[...] = normed
        low_buf[...] = mid.astype(BF16)
        at_point(0)

        def feed(index, _):
            in_copy(index).wait()
            down_copy(index).wait()
            for rows in both:
                pre_act = dot(low_buf[rows], in_buf[index]) + in_bias[index, 0:1].astype(F32)
                unit_cdf = 0.5 * (1.0 + lax.erf(pre_act * 0.5**0.5))
                bell = jnp.exp(-0.5 * pre_act * pre_act) * (2.0 * jnp.pi) ** (-0.5)
                slope[index, rows] = (unit_cdf + pre_act * bell).astype(BF16)
                hidden[index, rows] = (pre_act * unit_cdf).astype(BF16)
                mid_buf[rows] += dot(hidden[index, rows], down_buf[index])
            at_point(1, index)
            return 0

        lax.fori_loop(0, mp_size, feed, 0)
        output, normed, inv_out = norm_rows(mid_buf[...], gains[1:], shifts[1:])
        store_buf[...] = output
        store_copy(0).start()

        cotangent = cotangent_buf[...].astype(F32)
        vector[1:2] = sum_rows(cotangent * normed)
        vector[3:4] = sum_rows(cotangent)
        sum_grad = norm_back(cotangent, normed, inv_out, gains[1:])
        mid_buf[...] = sum_grad
        grad_buf[...] = sum_grad.astype(BF16)
        vector[5:6] = sum_rows(grad_buf[...])

        def give(which, turn, result):
            if turn >= 2:
                offer_given(which, turn - 2)
            share = result.shape[0] // slots
            for slot in range(slots):
                given[turn % 2, slot] = result[slot * share : (slot + 1) * share].astype(BF16)
            given_copy(which, turn).start()

        def offer_given(which, turn):
            given_copy(which, turn).wait()
            offer(which, turn)

        for turn in turns:
            index = part_of(turn)
            give(1, turn, dot_cols(hidden[index], grad_buf[...]))
            pre = dot_rows(grad_buf[...], down_buf[index]) * slope[index].astype(F32)
            hidden[index] = pre.astype(BF16)
            vector[pl.ds(8 + index, 1)] = sum_rows(hidden[index])
            mid_buf[...] += dot_rows(hidden[index], in_buf[index])
            at_point(1 + mp_size + turn)
        for turn in turns[-2:]:
            offer_given(1, turn)
        mid_grad = mid_buf[...]
        vector[0:1] = sum_rows(mid_grad * normed_buf[...])
        vector[2:3] = sum_rows(mid_grad)
        resid = norm_back(mid_grad, normed_buf[...], inv_mid, gains[:1])
        store_copy(0).wait()
        store_buf[...] = resid
        store_copy(1).start()
        attn_grad = resid.astype(BF16)
        grad_buf[...] = attn_grad
        vector[4:5] = sum_rows(attn_grad)
        heads_grad = dot_rows(attn_grad, out_buf[...]).astype(BF16)
        for head in range(head_total):
            for index in range(mp_size):
                at = index * head_cols + head * HEAD_DIM
                for side in range(2):
                    grads_out[index, head, :, side * HEAD_DIM : (side + 1) * HEAD_DIM] = (
                        heads_grad[both[side], at : at + HEAD_DIM]
                    )
            if head == 0:
                for offset in leaving:
                    grads_copy(0, offset).start()
        for head in range(head_total):
            grads_own_copy(head).start()
        vector_copy(0).start()

        products = dot_cols(heads_buf[...], grad_buf[...]).astype(BF16)
        rows = head_cols // slots
        for index in range(mp_size):
            for slot in range(slots):
                start = index * head_cols + slot * rows
                head_buf[index, slot, :rows] = products[start : start + rows]
                if rows < head_buf.shape[2]:
                    head_buf[index, slot, rows:] = jnp.zeros(
                        (head_buf.shape[2] - rows, width), BF16
                    )
        head_copy = pltpu.make_async_copy(head_buf, head_grads, head_sem)
        head_copy.start()
        normed_low = low_buf[...].T
        for turn in turns:
            give(0, turn, dot(normed_low, hidden[part_of(turn)]))
            if turn == 0:
                head_copy.wait()
                for at in turns:
                    offer(2, at)
                for later in range(1, head_total):
                    for offset in leaving:
                        grads_copy(later, offset).start()
        for turn in turns[-2:]:
            offer_given(0, turn)
        store_copy(1).wait()

    weight_own_copy = pltpu.make_async_copy(proj_weight, proj_all.at[me], weight_own)
    rows_low = pltpu.VMEM((2 * half, width), BF16)
    rows_full = pltpu.VMEM((2 * half, width), F32)
    pl.run_scoped(
        dense_phase,
        rows_low,
        rows_low,
        rows_low,
        pltpu.VMEM((mp_size, width, units), BF16),
        pltpu.VMEM((mp_size, units, width), BF16),
        pltpu.VMEM((width, width), BF16),
        pltpu.VMEM((mp_size, 2 * half, units), BF16),
        pltpu.VMEM((mp_size, 2 * half, units), BF16),
        rows_full,
        rows_full,
        rows_full,
        rows_low,
        rows_low,
        pltpu.VMEM((2, slots, units // slots, width), BF16),
        pltpu.VMEM(head_grads.shape, BF16),
    )

    def attention_phase(
        qkv,
        out_cols,
        log_total,
        seg_col,
        input_all,
        staged,
        qkv_grad,
        seg_blocks,
        grads,
        key_buf,
        key_cols,
        value_buf,
        query_sum,
        key_sum,
        value_sum,
        proj_rows,
    ):
        def traded_copy(head, offset):
            return send(
                staged.at[head, target(offset)],
                traded.at[head, me],
                (traded_send, traded_recv),
                (head, offset - 1),
                {"mp": target(offset)},
            )

        def traded_own_copy(head):
            return pltpu.make_async_copy(
                staged.at[head, me], traded.at[head, me], traded_own.at[head]
            )

        def prepare(head):
            cols = slice(head * HEAD_DIM, (head + 1) * HEAD_DIM)
            key_buf[:, :HEAD_DIM] = qkv[1, :, cols]
            if head == 0:
                key_buf[:, HEAD_DIM:] = ones_columns(ROW_LEN)
                value_buf[:, HEAD_DIM:] = ones_columns(ROW_LEN)
            value_buf[:, :HEAD_DIM] = qkv[2, :, cols]
            for step in range(BLOCKS):
                key_cols[step] = qkv[1, step * BLOCK : (step + 1) * BLOCK, cols].T
            key_sum[...] = jnp.zeros_like(key_sum)
            value_sum[...] = jnp.zeros_like(value_sum)

        def take_grads(head):
            grads_own_copy(head).wait()
            for offset in peers:
                grads_copy(head, offset).wait_recv()
            for chunk in range(mp_size):
                for side in range(2):
                    start = (2 * chunk + side) * half
                    grads[start : start + half] = grads_in[
                        head, chunk, :, side * HEAD_DIM : (side + 1) * HEAD_DIM
                    ]

        def attend_back(head):
            cols = slice(head * HEAD_DIM, (head + 1) * HEAD_DIM)

            def query_block(number, _):
                rows = block_rows(number)
                queries = qkv[0, rows, cols] * SCALE
                grad_rows = grads[rows]
                seg_query = seg_blocks[number]
                grad_cols = grad_rows.astype(F32).T
                row_dot = jnp.sum(grad_cols * out_cols[head, number], axis=0, keepdims=True)
                grad_cols = jnp.concatenate([grad_cols.astype(BF16), as_pieces(-row_dot)], axis=0)
                query_cols = jnp.concatenate(
                    [queries.astype(F32).T.astype(BF16), as_pieces(-log_total[head, number])], axis=0
                )

                def products_of(step):
                    key_rows = slice(step * BLOCK, (step + 1) * BLOCK)
                    same = (
                        jnp.concatenate([seg_col[key_rows]] * (BLOCK // 128), axis=1) == seg_query
                    )
                    scores = jnp.where(same, dot(key_buf[key_rows], query_cols), MASKED)
                    return scores, dot(value_buf[key_rows], grad_cols)

                query_grad = jnp.zeros((HEAD_DIM, BLOCK), F32)
                ahead = products_of(0)
                for step in range(BLOCKS):
                    scores, soft_grad = ahead
                    if step + 1 < BLOCKS:
                        ahead = products_of(step + 1)
                    key_rows = slice(step * BLOCK, (step + 1) * BLOCK)
                    soft = jnp.exp(scores)
                    score_grad = (soft * soft_grad).astype(BF16)
                    value_sum[key_rows] += dot(soft.astype(BF16), grad_rows)
                    key_sum[key_rows] += dot(score_grad, queries)
                    query_grad = query_grad + dot(key_cols[step], score_grad)
                query_sum[rows] = (query_grad * SCALE).T
                for at in range(head * BLOCKS, (head + 1) * BLOCKS):
                    if at in events:

                        @pl.when(number == at - head * BLOCKS)
                        def _():
                            for act in events[at]:
                                act()

                return 0

            lax.fori_loop(0, BLOCKS, query_block, 0)

        def give_grads(head):
            for part, total in enumerate((query_sum, key_sum, value_sum)):
                low = total[...].astype(BF16)
                qkv_grad[:, part * HEAD_DIM : (part + 1) * HEAD_DIM] = low
                if part != 1:
                    cols = slice(head * HEAD_DIM, (head + 1) * HEAD_DIM)
                    sum_low = jnp.sum(low.astype(F32), axis=0, keepdims=True)
                    biases[place, part : part + 1, cols] = sum_low
                for chunk in range(mp_size):
                    for side in range(2):
                        start = (2 * chunk + side) * half
                        staged[head, chunk, part, :, side * HEAD_DIM : (side + 1) * HEAD_DIM] = total[
                            start : start + half
                        ].astype(BF16)

        def start_trade(head):
            for offset in leaving:
                traded_copy(head, offset).start()
            traded_own_copy(head).start()

        def start_proj(head):
            products = dot_cols(qkv_grad[...], input_all[...])
            slot_rows = proj[head].shape[1]
            for slot in range(2**bits):
                proj[head][slot] = products[slot * slot_rows : (slot + 1) * slot_rows].astype(BF16)
            for offset in mates:
                proj_copy(head, offset).start()

        def finish_proj(head):
            cols = slice(head * HEAD_DIM, (head + 1) * HEAD_DIM)
            slot_rows = proj_slots[head].shape[1]
            for slot in range(2**bits):
                proj_rows[slot * slot_rows : (slot + 1) * slot_rows] = proj_slots[head][slot].astype(F32)
            for part in range(3):
                rows = proj_rows[part * HEAD_DIM : (part + 1) * HEAD_DIM]
                proj_sum[part, cols] = rows.astype(BF16)

        events = {}
        rest = []

        def due(at, act, *which):
            if at is None:
                rest.append((act, *which))
            else:
                events.setdefault(at, []).append(partial(act, *which))

        for at, level in zip((0, 1, 2), levels):
            due(at, add_vector, level)
        due(2.5, finish_vector)
        times = {
            1: ((0, 0, 0, 0), (2, 2, 2.5, 3), (2.5, 2.5, 3, 4)),
            2: ((2, 2, 2, 2), (3, 3, 3, 3), (4, 4, 4, 4)),
            0: ((1, 2, 2.5, 3), (2, 3, 4, 4), (2.5, 4, 5, 5.5)),
        }
        ends = {1: (5, 5.5, 6, 7), 2: (5.5, 6, 7, 8), 0: (6, 7, 8, None)}
        for level in levels:
            for which in times:
                for turn, at in zip(turns, times[which][level]):
                    due(at, add_level, which, level, turn)
        due(3, sum_proj, 0)
        due(5, take_proj, 0)
        due(5, finish_proj, 0)
        due(6, sum_proj, 1)
        due(8, take_proj, 1)
        due(8, finish_proj, 1)
        for which in (1, 2, 0):
            due(ends[which][0], finish_sum, which)
        for step, level in enumerate(levels[::-1]):
            for which in (0, 1, 2):
                due(ends[which][1 + step], spread, which, level)

        copies = [
            pltpu.make_async_copy(source, into, attention_sems.at[at])
            for at, (source, into) in enumerate(
                (
                    (qkv_source, qkv),
                    (seg_source, seg_col),
                    (log_source, log_total),
                    (out_source, out_cols),
                    (input_source, input_all),
                )
            )
        ]
        for copy in copies:
            copy.start()
        biases[place] = jnp.zeros(bias_sum.shape, F32)
        for step in range(BLOCKS):
            seg_blocks[step] = seg_row[:, step * BLOCK : (step + 1) * BLOCK]
        final = head_total - 1
        copies[0].wait()
        for head in range(head_total):
            prepare(head)
            take_grads(head)
            if head == 0:
                for copy in copies[1:4]:
                    copy.wait()
            attend_back(head)
            give_grads(head)
            start_trade(head)
            if head == 0:
                copies[4].wait()
            start_proj(head)
            for act in events.get((head + 1) * BLOCKS - 0.5, ()):
                act()
        for offset in mates:
            bias_copy(offset).start()
        if rest:
            act, *which = rest.pop(0)
            act(*which)
        sum_proj(final)
        sum_bias()
        for act, *which in rest:
            act(*which)
        take_proj(final)
        finish_proj(final)
        for head in range(head_total):
            traded_own_copy(head).wait()
            for offset in peers:
                traded_copy(head, offset).wait()

    pl.run_scoped(
        attention_phase,
        pltpu.VMEM(qkv_source.shape, BF16),
        pltpu.VMEM(out_source.shape, F32),
        pltpu.VMEM(log_source.shape, F32),
        pltpu.VMEM(seg_source.shape, jnp.int32),
        pltpu.VMEM(input_source.shape, BF16),
        pltpu.VMEM((head_total, mp_size, 3, half, 2 * HEAD_DIM), BF16),
        pltpu.VMEM((ROW_LEN, 3 * HEAD_DIM), BF16),
        pltpu.VMEM((BLOCKS, 1, BLOCK), jnp.int32),
        pltpu.VMEM((ROW_LEN, HEAD_DIM), BF16),
        pltpu.VMEM((ROW_LEN, HEAD_DIM + EXTRA), BF16),
        pltpu.VMEM((BLOCKS, HEAD_DIM, BLOCK), BF16),
        pltpu.VMEM((ROW_LEN, HEAD_DIM + EXTRA), BF16),
        pltpu.VMEM((ROW_LEN, HEAD_DIM), F32),
        pltpu.VMEM((ROW_LEN, HEAD_DIM), F32),
        pltpu.VMEM((ROW_LEN, HEAD_DIM), F32),
        pltpu.VMEM((3 * HEAD_DIM, width), F32),
    )

    for hop in line.hops:
        if (take_weight, hop) not in done:
            both_sides(take_weight, hop)
    for level in levels:
        for hop in line.hops:
            if (trade_weight, level, hop) not in done:
                both_sides(trade_weight, level, hop)

    def sent_trades(side, hop):
        for level in levels:
            weight_trade_copy(level, side, hop).wait_send()

    for side, hop in line.ways:
        line.if_sent(side, hop)(lambda side=side, hop=hop: weight_copy(side, hop).wait_send())
        line.if_taken(side, hop)(partial(sent_trades, side, hop))
    weight_own_copy.wait()
    for head in range(head_total):
        for offset in peers:
            grads_copy(head, offset).wait_send()
        for offset in mates:
            proj_copy(head, offset).wait_send()
            proj_spread_copy(head, offset).wait_send()
    for offset in mates:
        bias_copy(offset).wait_send()
    for level in levels:
        vector_copy(level).wait_send()
        for which in arrays:
            spread_copy(which, level).wait_send()
            for turn in turns:
                level_copy(which, level, turn).wait_send()
    for offset in peers:
        vector_last_copy(offset).wait_send()
        for which in arrays:
            last_copy(which, offset).wait_send()


def rear(frames, heads_low, out_grad, seg_row, in_bias, small, weights, proj_weight, saved, bits):
    local_rows, width = frames.shape
    qkv_low, out_cols = saved[:2]
    mp_size, units = weights[1].shape[:2]
    head_total = out_cols.shape[0]
    half, lanes = local_rows // 2, 2 * HEAD_DIM
    peers = mp_size - 1
    slots = 2**bits
    head_rows = -(-width // mp_size // slots // 16) * 16
    anywhere = pl.BlockSpec(memory_space=pl.ANY)
    blocks = [(width // slots, units), (units // slots, width), (head_rows, width)]
    proj_block = (3 * HEAD_DIM // slots, width)
    bias_block = (8, 2 * 128)
    vector_block = (8 + -(-mp_size // 8) * 8, width)

    def halves(shape, lead=()):
        return [pltpu.VMEM(lead + (slots >> (level + 1),) + shape, BF16) for level in range(bits)]

    def sems(*shapes):
        return [pltpu.SemaphoreType.DMA(shape) for shape in shapes for _ in range(2)]

    piece = pltpu.VMEM((mp_size, head_total, half, lanes), BF16)
    return pl.pallas_call(
        partial(rear_kernel, bits),
        out_shape=(
            jax.ShapeDtypeStruct((local_rows, width), F32),
            jax.ShapeDtypeStruct((local_rows, width), F32),
            *(jax.ShapeDtypeStruct((mp_size, slots) + block, BF16) for block in blocks),
            jax.ShapeDtypeStruct((mp_size,) + proj_weight.shape, BF16),
            jax.ShapeDtypeStruct((head_total, mp_size, 3, half, lanes), BF16),
            *(jax.ShapeDtypeStruct((slots,) + block, BF16) for block in blocks),
            jax.ShapeDtypeStruct((3, head_total * HEAD_DIM, width), BF16),
            jax.ShapeDtypeStruct(vector_block, F32),
            jax.ShapeDtypeStruct(bias_block, F32),
        ),
        in_specs=[whole()] * 6 + [anywhere] * 12,
        out_specs=(anywhere,) * 7 + (whole(),) * 6,
        scratch_shapes=[
            piece,
            pltpu.VMEM((head_total, mp_size, half, lanes), BF16),
            [pltpu.VMEM((2, slots // 2) + block, BF16) for block in blocks],
            [halves(block, (mp_size,)) for block in blocks],
            [pltpu.VMEM((peers, 1) + block, BF16) for block in blocks],
            [pltpu.VMEM((slots,) + proj_block, BF16) for _ in range(head_total)],
            [pltpu.VMEM((slots - 1,) + proj_block, BF16) for _ in range(head_total)],
            [pltpu.VMEM((slots,) + proj_block, BF16) for _ in range(head_total)],
            [pltpu.VMEM(vector_block, F32) for _ in range(bits + 1)],
            [pltpu.VMEM(vector_block, F32) for _ in range(bits)],
            pltpu.VMEM((mp_size,) + vector_block, F32),
            pltpu.VMEM((slots,) + bias_block, F32),
            pltpu.SemaphoreType.DMA((3,)),
            pltpu.SemaphoreType.DMA((mp_size,)),
            pltpu.SemaphoreType.DMA((mp_size,)),
            pltpu.SemaphoreType.DMA((mp_size,)),
            pltpu.SemaphoreType.DMA((2,)),
            pltpu.SemaphoreType.DMA,
            pltpu.SemaphoreType.DMA((2,)),
            pltpu.SemaphoreType.DMA((5,)),
            pltpu.SemaphoreType.DMA,
            *sems((2, peers), (max(bits, 1), 2, peers)),
            pltpu.SemaphoreType.DMA((3, 2)),
            pltpu.SemaphoreType.DMA((head_total,)),
            *sems((head_total, peers)),
            pltpu.SemaphoreType.DMA((head_total,)),
            *sems(
                (head_total, peers),
                (3, bits, mp_size),
                (3, peers),
                (3, bits),
                (2, head_total, slots - 1),
                (bits,),
                (peers,),
                (slots - 1,),
            ),
        ],
        compiler_params=pltpu.CompilerParams(
            collective_id=1, has_side_effects=True, vmem_limit_bytes=REAR_VMEM_BYTES
        ),
        cost_estimate=pl.CostEstimate(
            flops=40 * head_total * ROW_LEN * ROW_LEN * HEAD_DIM,
            bytes_accessed=96 * 1024 * 1024,
            transcendentals=head_total * ROW_LEN * ROW_LEN,
        ),
        name="rear",
    )(seg_row, in_bias, *small, frames, heads_low, out_grad, *weights, proj_weight, *saved)


def finish_kernel(
    traded,
    proj_all,
    resid_grad,
    in_sum,
    down_sum,
    head_sum,
    proj_sum,
    vector_sum,
    bias_sum,
    stream_grad,
    in_grad,
    down_grad,
    out_grad,
    proj_grad,
    query_bias_grad,
    value_bias_grad,
    out_bias_grad,
    in_bias_grad,
    down_bias_grad,
    gain_grad,
    shift_grad,
    columns,
    weight_buf,
    sems,
):
    head_total, mp_size = traded.shape[:2]
    half = traded.shape[3]
    head_cols = head_total * HEAD_DIM
    copies = [
        pltpu.make_async_copy(
            proj_all.at[index],
            weight_buf.at[index],
            sems.at[index],
        )
        for index in range(mp_size)
    ]
    for copy in copies:
        copy.start()
    for sums, grad in ((in_sum, in_grad), (down_sum, down_grad), (head_sum, out_grad)):
        rows = grad.shape[0] // sums.shape[0]
        for slot in range(sums.shape[0]):
            grad[slot * rows : (slot + 1) * rows] = sums[slot, :rows].astype(F32)
    proj_grad[...] = proj_sum[...].astype(F32)
    query_bias_grad[...] = bias_sum[0:1, :head_cols]
    value_bias_grad[...] = bias_sum[2:3, :head_cols]
    gain_grad[...] = vector_sum[0:2]
    shift_grad[...] = vector_sum[2:4]
    out_bias_grad[...] = vector_sum[4:5]
    down_bias_grad[...] = vector_sum[5:6]
    in_bias_grad[...] = vector_sum[pl.ds(8 + lax.axis_index("mp"), 1)]
    stream_grad[...] = resid_grad[...]
    for index in range(mp_size):
        for head in range(head_total):
            for part in range(3):
                at = part * head_cols + head * HEAD_DIM
                for side in range(2):
                    columns[side * half : (side + 1) * half, at : at + HEAD_DIM] = traded[
                        head, index, part, :, side * HEAD_DIM : (side + 1) * HEAD_DIM
                    ]
        copies[index].wait()
        stream_grad[...] += dot(columns[...], weight_buf[index])


def finish(traded, proj_all, resid_grad, sums):
    head_total, mp_size = traded.shape[:2]
    head_cols = head_total * HEAD_DIM
    local_rows, width = resid_grad.shape
    units = sums[0].shape[0] * sums[0].shape[1]
    row = jax.ShapeDtypeStruct((1, width), F32)
    head_row = jax.ShapeDtypeStruct((1, head_cols), F32)
    anywhere = pl.BlockSpec(memory_space=pl.ANY)
    return pl.pallas_call(
        finish_kernel,
        out_shape=(
            jax.ShapeDtypeStruct((local_rows, width), F32),
            jax.ShapeDtypeStruct((units, width), F32),
            jax.ShapeDtypeStruct((units, width), F32),
            jax.ShapeDtypeStruct((head_cols, width), F32),
            jax.ShapeDtypeStruct((3, head_cols, width), F32),
            head_row,
            head_row,
            row,
            jax.ShapeDtypeStruct((1, units), F32),
            row,
            jax.ShapeDtypeStruct((2, width), F32),
            jax.ShapeDtypeStruct((2, width), F32),
        ),
        in_specs=[whole(), anywhere] + [whole()] * 7,
        out_specs=(whole(),) * 12,
        scratch_shapes=[
            pltpu.VMEM((local_rows, 3 * head_cols), BF16),
            pltpu.VMEM((mp_size, 3 * head_cols, width), BF16),
            pltpu.SemaphoreType.DMA((mp_size,)),
        ],
        compiler_params=pltpu.CompilerParams(vmem_limit_bytes=VMEM_BYTES),
        cost_estimate=pl.CostEstimate(
            flops=6 * local_rows * width * width, bytes_accessed=24 * 1024 * 1024, transcendentals=0
        ),
        name="finish",
    )(traded, proj_all, resid_grad, *sums)


def dp_groups():
    total = lax.axis_size("dp")
    size = min(8, total)
    groups = [list(range(start, start + size)) for start in range(0, total, size)]
    return (size, groups)


def on_device(
    frames,
    segment_ids,
    qkv_weight,
    q_bias,
    v_bias,
    out_weight,
    out_bias,
    ff_in_weight,
    ff_in_bias,
    ff_out_weight,
    ff_out_bias,
    norm_gain,
    norm_shift,
    out_grad,
):
    local_rows, width = frames.shape
    mp_size = lax.axis_size("mp")
    group, groups = dp_groups()
    bits = group_bits(lax.axis_size("dp"))
    slots = 2**bits

    proj_weight = qkv_weight[0].transpose(0, 2, 1)
    seg_row = segment_ids.reshape(1, ROW_LEN)
    (
        input_all,
        qkv_low,
        in_all,
        down_all,
        out_all,
        in_bias_all,
        seg_col,
        out_cols,
        log_total,
        heads_low,
    ) = front(
        frames,
        proj_weight,
        q_bias,
        v_bias,
        seg_row,
        (ff_in_weight[0], ff_out_weight[0], out_weight[0]),
        ff_in_bias,
        mp_size,
        bits,
    )
    block_out, resid_grad, _, _, _, proj_all, traded, *summed = rear(
        frames,
        heads_low,
        out_grad,
        seg_row,
        in_bias_all,
        (out_bias, ff_out_bias, norm_gain[0], norm_shift[0]),
        (in_all, down_all, out_all),
        proj_weight.reshape(slots, -1, width),
        (qkv_low, out_cols, log_total, seg_col, input_all),
        bits,
    )
    if len(groups) > 1:
        across = [list(range(at, lax.axis_size("dp"), group)) for at in range(group)]
        summed = lax.psum(summed, "dp", axis_index_groups=across)
    (
        stream_grad,
        in_weight_grad,
        down_weight_grad,
        out_weight_grad,
        proj_grad,
        query_bias_grad,
        value_bias_grad,
        head_bias_grad,
        in_bias_grad,
        down_bias_grad,
        gain_grad,
        shift_grad,
    ) = finish(traded, proj_all.reshape(mp_size, -1, width), resid_grad, summed)
    return (
        block_out,
        stream_grad,
        proj_grad.transpose(0, 2, 1)[None],
        query_bias_grad,
        value_bias_grad,
        out_weight_grad[None],
        head_bias_grad,
        in_weight_grad[None],
        in_bias_grad,
        down_weight_grad[None],
        down_bias_grad,
        gain_grad[None],
        shift_grad[None],
    )


def solution(mesh):
    return jax.shard_map(
        on_device,
        mesh=mesh,
        in_specs=(
            P(("dp", "mp"), None),
            P("dp"),
            P(None, None, None, "mp"),
            P(None, "mp"),
            P(None, "mp"),
            P(None, "mp", None),
            P(),
            P(None, None, "mp"),
            P(None, "mp"),
            P(None, "mp", None),
            P(),
            P(),
            P(),
            P(("dp", "mp"), None),
        ),
        out_specs=(
            P(("dp", "mp"), None),
            P(("dp", "mp"), None),
            P(None, None, None, "mp"),
            P(None, "mp"),
            P(None, "mp"),
            P(None, "mp", None),
            P(),
            P(None, None, "mp"),
            P(None, "mp"),
            P(None, "mp", None),
            P(),
            P(),
            P(),
        ),
        check_vma=False,
    )
```

```python
import itertools
from functools import partial

import jax
import jax.numpy as jnp
from jax import lax
from jax.experimental import pallas as pl
from jax.experimental.pallas import tpu as pltpu
from jax.sharding import PartitionSpec as P

HEAD_DIM = 64
ROW_LEN = 2304
BLOCK = 768
BLOCKS = ROW_LEN // BLOCK
EXTRA = 16
SCALE = HEAD_DIM ** (-0.5)
MASKED = -1e30
F32 = jnp.float32
BF16 = jnp.bfloat16
VMEM_BYTES = 56 * 1024 * 1024
REAR_VMEM_BYTES = 63 * 1024 * 1024


def dot_rows(left, right):
    return lax.dot_general(left, right, (((1,), (1,)), ((), ())), preferred_element_type=F32)


def dot_cols(left, right):
    return lax.dot_general(left, right, (((0,), (0,)), ((), ())), preferred_element_type=F32)


def dot(left, right):
    return jnp.dot(left, right, preferred_element_type=F32)


def block_rows(number):
    return pl.ds(pl.multiple_of(number * BLOCK, BLOCK), BLOCK)


def as_pieces(row):
    high = row.astype(BF16).astype(F32)
    middle = (row - high).astype(BF16).astype(F32)
    last = row - high - middle
    place = lax.broadcasted_iota(jnp.int32, (EXTRA, row.shape[1]), 0)
    pieces = jnp.where(place == 0, high, jnp.where(place == 1, middle, jnp.where(place == 2, last, 0.0)))
    return pieces.astype(BF16)


def ones_columns(rows):
    place = lax.broadcasted_iota(jnp.int32, (rows, EXTRA), 1)
    return jnp.where(place < 3, 1.0, 0.0).astype(BF16)


def whole(memory_space=pltpu.VMEM):
    return pl.BlockSpec(memory_space=memory_space)


MESH = pl.DeviceIdType.MESH


def group_bits(dp_size):
    return min(3, dp_size.bit_length() - 1)


def place_in(dp_index, order):
    slot = 0
    for at, bit in enumerate(order):
        slot = slot + (dp_index // 2**bit) % 2 * 2**at
    return slot


def partner_of(dp_index, bit):
    return dp_index + (1 - 2 * ((dp_index // 2**bit) % 2)) * 2**bit


def enter(dp_index, mp_index, mp_size, bits):
    barrier = pltpu.get_barrier_semaphore()
    for offset in range(1, mp_size):
        pl.semaphore_signal(
            barrier, device_id={"mp": lax.rem(mp_index + offset, mp_size)}, device_id_type=MESH
        )
    for bit in range(bits):
        pl.semaphore_signal(
            barrier, device_id={"dp": partner_of(dp_index, bit)}, device_id_type=MESH
        )
    pl.semaphore_wait(barrier, mp_size - 1 + bits)


def send(src, dst, sems, at, device_id):
    return pltpu.make_async_remote_copy(
        src_ref=src,
        dst_ref=dst,
        send_sem=sems[0].at[at],
        recv_sem=sems[1].at[at],
        device_id=device_id,
        device_id_type=MESH,
    )


def gather_orders(bits):
    if bits == 3:
        return ((1, 2, 0), (2, 1, 0), (1, 2), (1, 2, 0))
    return (tuple(range(bits)),) * 4


SIDES = (1, -1)


def inside(index, size):
    return jnp.logical_and(index >= 0, index < size)


class Line:
    def __init__(self, mp_size, me):
        self.size = mp_size
        self.me = me
        self.hops = range(mp_size - 1)
        self.ways = [(side, hop) for hop in self.hops for side in (0, 1)]

    def wrapped(self, index):
        return lax.rem(index + self.size, self.size)

    def chunk(self, side, hop):
        return self.me - SIDES[side] * hop

    def place(self, side, hop):
        return self.wrapped(self.chunk(side, hop))

    def sends(self, side, hop):
        there = inside(self.me + SIDES[side], self.size)
        return jnp.logical_and(there, inside(self.chunk(side, hop), self.size))

    def if_sent(self, side, hop):
        return pl.when(self.sends(side, hop))

    def if_taken(self, side, hop):
        return pl.when(inside(self.chunk(side, hop + 1), self.size))

    def neighbour(self, side):
        return {"mp": self.wrapped(self.me + SIDES[side])}


def front_kernel(
    bits,
    frames,
    qkv_weight,
    q_bias,
    v_bias,
    seg_row,
    in_weight,
    down_weight,
    out_weight,
    in_bias,
    input_all,
    qkv_low,
    in_all,
    down_all,
    out_all,
    bias_all,
    seg_col,
    out_cols,
    log_total,
    heads_low,
    bias_buf,
    key_cols,
    value_buf,
    out_buf,
    staged,
    heads_in,
    own_sems,
    frame_send,
    frame_recv,
    bias_send,
    bias_recv,
    first_send,
    first_recv,
    later_send,
    later_recv,
    heads_own,
    heads_send,
    heads_recv,
):
    mp_size = in_all.shape[0]
    me = lax.axis_index("mp")
    dp_index = lax.axis_index("dp")
    local_rows = frames.shape[0]
    half = local_rows // 2
    head_total = out_cols.shape[0]
    orders = gather_orders(bits)[:3]
    parts = ((in_weight, in_all), (down_weight, down_all), (out_weight, out_all))
    line = Line(mp_size, me)
    hops, ways, wrapped = line.hops, line.ways, line.wrapped
    enter(dp_index, me, mp_size, bits)

    def slots(which, level):
        count = parts[which][0].shape[0] // 2 ** len(orders[which])
        start = place_in(dp_index, orders[which]) // 2**level * 2**level
        return pl.ds(pl.multiple_of(start * count, 16), count * 2**level)

    def first_copy(which, side, hop):
        rows = slots(which, 0)
        place = parts[which][1].at[line.place(side, hop), rows]
        source = parts[which][0].at[rows] if hop == 0 else place
        sems = (first_send, first_recv)
        return send(source, place, sems, (which, side, hop), line.neighbour(side))

    def later_copy(which, level, side, hop):
        held = parts[which][1].at[line.place(side, hop + 1), slots(which, level)]
        partner = {"dp": partner_of(dp_index, orders[which][level])}
        return send(held, held, (later_send, later_recv), (which, level, side, hop), partner)

    def frame_rows(index):
        return pl.ds(pl.multiple_of(wrapped(index) * local_rows, local_rows), local_rows)

    def frame_copy(side, hop):
        place = input_all.at[frame_rows(line.chunk(side, hop))]
        source = frames if hop == 0 else place
        return send(source, place, (frame_send, frame_recv), (side, hop), line.neighbour(side))

    def bias_copy(side, hop):
        place = bias_all.at[line.place(side, hop)]
        source = bias_buf if hop == 0 else place
        return send(source, place, (bias_send, bias_recv), (side, hop), line.neighbour(side))

    def project(index):
        rows = frame_rows(index)
        inputs = input_all[rows]
        for part, bias in enumerate((q_bias, None, v_bias)):
            products = dot_rows(inputs, qkv_weight[part])
            if bias is not None:
                products = products + bias[...].astype(F32)
            qkv_low[part, rows] = products.astype(BF16)

    def start_slices(side, hop):
        for which in range(3):
            first_copy(which, side, hop).start()
        bias_copy(side, hop).start()

    def take_slices(side, hop):
        for which in range(3):
            first_copy(which, side, hop).wait_recv()
        bias_copy(side, hop).wait_recv()
        if 0 < hop < mp_size - 2:
            line.if_sent(side, hop + 1)(partial(start_slices, side, hop + 1))
        for which in range(3):
            if orders[which]:
                later_copy(which, 0, side, hop).start()

    def trade_slices(level, side, hop):
        for which in range(3):
            if level < len(orders[which]):
                later_copy(which, level, side, hop).wait_recv()
            if level + 1 < len(orders[which]):
                later_copy(which, level + 1, side, hop).start()

    def take_hop(hop):
        for side in (0, 1):
            line.if_taken(side, hop)(partial(take_slices, side, hop))

    def trade_hop(level, hop):
        for side in (0, 1):
            line.if_taken(side, hop)(partial(trade_slices, level, side, hop))


    bias_buf[...] = jnp.broadcast_to(in_bias[...], bias_buf.shape)
    for side in (0, 1):
        line.if_sent(side, 0)(partial(start_slices, side, 0))
    for side in (0, 1):
        line.if_sent(side, 0)(lambda side=side: frame_copy(side, 0).start())
    own = [
        pltpu.make_async_copy(shard, gathered.at[me], own_sems.at[at])
        for at, (shard, gathered) in enumerate(parts + ((bias_buf, bias_all),))
    ]
    for copy in own:
        copy.start()
    input_all[frame_rows(me)] = frames[...]
    project(me)
    for step in range(BLOCKS):
        ids = jnp.broadcast_to(seg_row[:, step * BLOCK : (step + 1) * BLOCK].astype(F32), (128, BLOCK))
        seg_col[step * BLOCK : (step + 1) * BLOCK] = ids.T.astype(jnp.int32)

    def take_frames(side, hop):
        frame_copy(side, hop).wait_recv()
        if hop + 1 < mp_size - 1:
            line.if_sent(side, hop + 1)(lambda: frame_copy(side, hop + 1).start())

    def project_taken(side, hop):
        project(line.chunk(side, hop + 1))

    for hop in hops:
        for side in (0, 1):
            line.if_taken(side, hop)(partial(take_frames, side, hop))
        if hop == 0:
            take_hop(0)
        elif hop - 1 < bits:
            trade_hop(hop - 1, 0)
        for side in (0, 1):
            free = line.sends(side, hop)
            if hop + 1 < mp_size - 1:
                free = jnp.logical_and(free, jnp.logical_not(line.sends(side, hop + 1)))
            if mp_size > 2:
                passes = jnp.logical_and(free, line.sends(side, 1))
                pl.when(passes)(partial(start_slices, side, 1))
        for side in (0, 1):
            line.if_taken(side, hop)(partial(project_taken, side, hop))

    schedule = (
        (1, take_hop, 1),
        (3, trade_hop, 0, 1),
        (4, take_hop, 2),
        (6, trade_hop, 1, 1),
        (6, trade_hop, 0, 2),
    )
    events = {}
    done = {(take_hop, 0)} | {(trade_hop, hop - 1, 0) for hop in hops if 0 < hop <= bits}
    for at, act, *which in schedule:
        if which[-1] in hops and (act is take_hop or which[0] < bits):
            events.setdefault((at // BLOCKS, at % BLOCKS), []).append(partial(act, *which))
            done.add((act, *which))

    def attend(head):
        cols = slice(head * HEAD_DIM, (head + 1) * HEAD_DIM)
        lane = lax.broadcasted_iota(jnp.int32, (BLOCK, EXTRA), 1)
        for step in range(BLOCKS):
            rows = slice(step * BLOCK, (step + 1) * BLOCK)
            key_cols[step] = qkv_low[1, rows, cols].T
            value_buf[step, :, :HEAD_DIM] = qkv_low[2, rows, cols]
            value_buf[step, :, HEAD_DIM:] = jnp.where(lane == 0, 1.0, 0.0).astype(BF16)

        def query_block(number, _):
            rows = block_rows(number)
            queries = qkv_low[0, rows, cols] * SCALE

            def scores_of(step):
                ids = seg_row[:, step * BLOCK : (step + 1) * BLOCK]
                same = jnp.concatenate([seg_col[rows]] * (BLOCK // 128), axis=1) == ids
                return jnp.where(same, dot(queries, key_cols[step]), MASKED)

            peak = jnp.full((BLOCK, 1), MASKED, F32)
            mixed = jnp.zeros((BLOCK, HEAD_DIM + EXTRA), F32)
            scores = scores_of(0)
            for step in range(BLOCKS):
                ahead = scores_of(step + 1) if step + 1 < BLOCKS else None
                higher = jnp.maximum(peak, jnp.max(scores, axis=1, keepdims=True))
                soft = jnp.exp(scores - higher).astype(BF16)
                mixed = mixed * jnp.exp(peak - higher) + dot(soft, value_buf[step])
                peak, scores = higher, ahead
            total = mixed[:, HEAD_DIM : HEAD_DIM + 1]
            mixed = mixed[:, :HEAD_DIM] / total
            logs = jnp.broadcast_to(peak + jnp.log(total), (BLOCK, HEAD_DIM))
            both = jnp.concatenate([mixed, logs], axis=1).T
            out_cols[head, number] = both[:HEAD_DIM]
            log_total[head, number] = both[HEAD_DIM : HEAD_DIM + 1]
            out_buf[rows] = mixed.astype(BF16)
            for at in range(BLOCKS):
                if (head, at) in events:

                    @pl.when(number == at)
                    def _():
                        for act in events[(head, at)]:
                            act()

            return 0

        lax.fori_loop(0, BLOCKS, query_block, 0)

    def heads_copy(head, offset):
        return send(
            staged.at[head, wrapped(me + offset)],
            heads_in.at[head, me],
            (heads_send, heads_recv),
            (head, offset - 1),
            {"mp": wrapped(me + offset)},
        )

    def heads_own_copy(head):
        return pltpu.make_async_copy(
            staged.at[head, me], heads_in.at[head, me], heads_own.at[head]
        )

    peers = range(1, mp_size)
    for head in range(head_total):
        attend(head)
        for chunk in range(mp_size):
            for side in range(2):
                start = (2 * chunk + side) * half
                staged[head, chunk, :, side * HEAD_DIM : (side + 1) * HEAD_DIM] = out_buf[
                    start : start + half
                ]
        for offset in peers:
            heads_copy(head, offset).start()
        heads_own_copy(head).start()

    for hop in hops:
        if (take_hop, hop) not in done:
            take_hop(hop)
    for level in range(bits):
        for hop in hops:
            if (trade_hop, level, hop) not in done:
                trade_hop(level, hop)
    for head in range(head_total):
        heads_own_copy(head).wait()
        for offset in peers:
            heads_copy(head, offset).wait_recv()
        for chunk in range(mp_size):
            for side in range(2):
                at = (chunk * head_total + head) * HEAD_DIM
                heads_low[side * half : (side + 1) * half, at : at + HEAD_DIM] = heads_in[
                    head, chunk, :, side * HEAD_DIM : (side + 1) * HEAD_DIM
                ]
        for offset in peers:
            heads_copy(head, offset).wait_send()

    def sent_all(side, hop):
        frame_copy(side, hop).wait_send()
        bias_copy(side, hop).wait_send()
        for which in range(3):
            first_copy(which, side, hop).wait_send()

    def sent_later(side, hop):
        for which in range(3):
            for level in range(len(orders[which])):
                later_copy(which, level, side, hop).wait_send()

    for side, hop in ways:
        line.if_sent(side, hop)(partial(sent_all, side, hop))
        line.if_taken(side, hop)(partial(sent_later, side, hop))
    for copy in own:
        copy.wait()


def front(frames, qkv_weight, q_bias, v_bias, seg_row, weights, in_bias, mp_size, bits):
    local_rows, width = frames.shape
    head_cols = qkv_weight.shape[1]
    head_total = head_cols // HEAD_DIM
    peers = mp_size - 1
    levels = max(bits, 1)
    anywhere = pl.BlockSpec(memory_space=pl.ANY)
    in_weight, down_weight, out_weight = weights

    def sems(*shapes):
        return [pltpu.SemaphoreType.DMA(shape) for shape in shapes for _ in range(2)]

    piece = (head_total, mp_size, local_rows // 2, 2 * HEAD_DIM)
    return pl.pallas_call(
        partial(front_kernel, bits),
        out_shape=(
            jax.ShapeDtypeStruct((ROW_LEN, width), BF16),
            jax.ShapeDtypeStruct((3, ROW_LEN, head_cols), BF16),
            jax.ShapeDtypeStruct((mp_size,) + in_weight.shape, BF16),
            jax.ShapeDtypeStruct((mp_size,) + down_weight.shape, BF16),
            jax.ShapeDtypeStruct((mp_size,) + out_weight.shape, BF16),
            jax.ShapeDtypeStruct((mp_size, 16, in_bias.shape[1]), BF16),
            jax.ShapeDtypeStruct((ROW_LEN, 128), jnp.int32),
            jax.ShapeDtypeStruct((head_total, BLOCKS, HEAD_DIM, BLOCK), F32),
            jax.ShapeDtypeStruct((head_total, BLOCKS, 1, BLOCK), F32),
            jax.ShapeDtypeStruct((local_rows, width), BF16),
        ),
        in_specs=[whole()] * 5 + [anywhere] * 3 + [whole()],
        out_specs=(whole(), whole()) + (anywhere,) * 4 + (whole(),) * 4,
        scratch_shapes=[
            pltpu.VMEM((16, in_bias.shape[1]), BF16),
            pltpu.VMEM((BLOCKS, HEAD_DIM, BLOCK), BF16),
            pltpu.VMEM((BLOCKS, BLOCK, HEAD_DIM + EXTRA), BF16),
            pltpu.VMEM((ROW_LEN, HEAD_DIM), BF16),
            pltpu.VMEM(piece, BF16),
            pltpu.VMEM(piece, BF16),
            pltpu.SemaphoreType.DMA((4,)),
            *sems((2, peers), (2, peers), (3, 2, peers), (3, levels, 2, peers)),
            pltpu.SemaphoreType.DMA((head_total,)),
            *sems((head_total, peers)),
        ],
        compiler_params=pltpu.CompilerParams(
            collective_id=0, has_side_effects=True, vmem_limit_bytes=VMEM_BYTES
        ),
        cost_estimate=pl.CostEstimate(
            flops=16 * head_total * ROW_LEN * ROW_LEN * HEAD_DIM,
            bytes_accessed=32 * 1024 * 1024,
            transcendentals=head_total * ROW_LEN * ROW_LEN,
        ),
        name="front",
    )(frames, qkv_weight, q_bias, v_bias, seg_row, in_weight, down_weight, out_weight, in_bias)


def reduce_orders(bits):
    if bits == 3:
        return ((0, 1, 2), (0, 2, 1), (0, 1, 2))
    return (tuple(range(bits)),) * 3


def norm_rows(inputs, norm_gain, norm_shift):
    row_mean = jnp.mean(inputs, axis=-1, keepdims=True)
    centred = inputs - row_mean
    variance = jnp.mean(centred * centred, axis=-1, keepdims=True)
    inv_std = lax.rsqrt(variance + 1e-05)
    normed = centred * inv_std
    return (normed * norm_gain + norm_shift, normed, inv_std)


def norm_back(cotangent, normed, inv_std, norm_gain):
    scaled = cotangent * norm_gain
    adjusted = (
        scaled
        - jnp.mean(scaled, axis=-1, keepdims=True)
        - normed * jnp.mean(scaled * normed, axis=-1, keepdims=True)
    )
    return adjusted * inv_std


def sum_rows(array):
    return jnp.sum(array.astype(F32), axis=0, keepdims=True)


def rear_kernel(
    bits,
    seg_row,
    in_bias,
    out_bias,
    down_bias,
    norm_gain,
    norm_shift,
    frames,
    heads_low,
    out_grad,
    in_all,
    down_all,
    out_all,
    proj_weight,
    qkv_source,
    out_source,
    log_source,
    seg_source,
    input_source,
    block_out,
    resid_grad,
    in_grads,
    down_grads,
    head_grads,
    proj_all,
    traded,
    in_sum,
    down_sum,
    head_sum,
    proj_sum,
    vector_sum,
    bias_sum,
    grads_out,
    grads_in,
    kept,
    taken,
    last,
    proj,
    proj_taken,
    proj_slots,
    vectors,
    vectors_taken,
    vectors_all,
    biases,
    biases_taken,
    load_sems,
    in_sems,
    down_sems,
    out_sems,
    given_sems,
    head_sem,
    store_sems,
    attention_sems,
    weight_own,
    weight_send,
    weight_recv,
    weight_trade_send,
    weight_trade_recv,
    keep_sems,
    grads_own,
    grads_send,
    grads_recv,
    traded_own,
    traded_send,
    traded_recv,
    level_send,
    level_recv,
    last_send,
    last_recv,
    back_send,
    back_recv,
    proj_send,
    proj_recv,
    vector_send,
    vector_recv,
    vector_last_send,
    vector_last_recv,
    bias_send,
    bias_recv,
):
    mp_size, units, width = down_all.shape
    head_total = grads_out.shape[1]
    half = grads_out.shape[2]
    head_cols = width // mp_size
    slots = 2**bits
    me = lax.axis_index("mp")
    dp_index = lax.axis_index("dp")
    peers = range(1, mp_size)
    turns = range(mp_size)
    levels = list(range(bits))
    orders = reduce_orders(bits)
    partials = (in_grads, down_grads, head_grads)
    sums = (in_sum, down_sum, head_sum)
    arrays = range(3)
    vector = vectors[0]

    def target(offset):
        return lax.rem(me + offset, mp_size)

    def bit_of(which, level):
        return (dp_index // 2 ** orders[which][level]) % 2


    def part_of(turn):
        return target(turn + 1)

    def level_copy(which, level, turn):
        count = 2 ** (bits - 1 - level)
        other = (1 - bit_of(which, level)) * count
        part = pl.ds(part_of(turn), 1)
        source = partials[which] if level == 0 else taken[which][level - 1]
        return send(
            source.at[part, pl.ds(other, count)],
            taken[which][level].at[part],
            (level_send, level_recv),
            (which, level, turn),
            {"dp": partner_of(dp_index, orders[which][level])},
        )

    def keep_copy(which, turn):
        count = 2 ** (bits - 1)
        return pltpu.make_async_copy(
            partials[which].at[part_of(turn), pl.ds(bit_of(which, 0) * count, count)],
            kept[which].at[turn % 2],
            keep_sems.at[which, turn % 2],
        )

    def last_copy(which, offset):
        return send(
            taken[which][bits - 1].at[target(offset)],
            last[which].at[offset - 1],
            (last_send, last_recv),
            (which, offset - 1),
            {"mp": target(offset)},
        )

    def add_level(which, level, turn):
        level_copy(which, level, turn).wait_recv()
        count = 2 ** (bits - 1 - level)
        if level == 0:
            keep_copy(which, turn).wait()
        start = bit_of(which, level) * count
        into = taken[which][level]
        part = part_of(turn)
        for slot in range(count):
            if level == 0:
                mine = kept[which][turn % 2, slot]
            else:
                mine = taken[which][level - 1][part, start + slot]
            into[part, slot] = into[part, slot] + mine
        if level == 0 and turn + 2 < mp_size:
            keep_copy(which, turn + 2).start()
        if level + 1 < bits:
            level_copy(which, level + 1, turn).start()
        elif turn + 1 < mp_size:
            last_copy(which, turn + 1).start()

    def offer(which, turn):
        level_copy(which, 0, turn).start()
        if turn < 2:
            keep_copy(which, turn).start()

    def slot_of(order):
        return place_in(dp_index, order[::-1])

    def held_slots(order, level):
        count = 2 ** (bits - 1 - level)
        return pl.ds(slot_of(order) // count * count, count)

    def spread_copy(which, level):
        held = sums[which].at[held_slots(orders[which], level)]
        partner = {"dp": partner_of(dp_index, orders[which][level])}
        return send(held, held, (back_send, back_recv), (which, level), partner)

    def finish_sum(which):
        total = taken[which][bits - 1][me, 0].astype(F32)
        for offset in peers:
            last_copy(which, offset).wait_recv()
            total = total + last[which][offset - 1, 0].astype(F32)
        sums[which][slot_of(orders[which])] = total.astype(BF16)
        spread_copy(which, bits - 1).start()

    def spread(which, level):
        spread_copy(which, level).wait_recv()
        if level:
            spread_copy(which, level - 1).start()


    def proj_copy(head, level):
        count = 2 ** (bits - 1 - level)
        other = (1 - bit_of(0, level)) * count
        source = proj[head] if level == 0 else proj_taken[head][level - 1]
        return send(
            source.at[pl.ds(other, count)],
            proj_taken[head][level],
            (proj_send, proj_recv),
            (0, head, level),
            {"dp": partner_of(dp_index, orders[0][level])},
        )

    def proj_spread_copy(head, level):
        held = proj_slots[head].at[held_slots(orders[0], level)]
        partner = {"dp": partner_of(dp_index, orders[0][level])}
        return send(held, held, (proj_send, proj_recv), (1, head, level), partner)

    def add_proj(head, level):
        proj_copy(head, level).wait_recv()
        count = 2 ** (bits - 1 - level)
        start = bit_of(0, level) * count
        into = proj_taken[head][level]
        for slot in range(count):
            mine = proj[head][start + slot] if level == 0 else proj_taken[head][level - 1][start + slot]
            into[slot] = (into[slot].astype(F32) + mine.astype(F32)).astype(BF16)
        if level + 1 < bits:
            proj_copy(head, level + 1).start()
        else:
            proj_slots[head][slot_of(orders[0])] = into[0]
            proj_spread_copy(head, level).start()

    def spread_proj(head, level):
        proj_spread_copy(head, level).wait_recv()
        if level:
            proj_spread_copy(head, level - 1).start()


    def vector_copy(level):
        return send(
            vectors[level],
            vectors_taken[level],
            (vector_send, vector_recv),
            level,
            {"dp": partner_of(dp_index, level)},
        )

    def vector_last_copy(offset):
        return send(
            vectors[bits],
            vectors_all.at[me],
            (vector_last_send, vector_last_recv),
            offset - 1,
            {"mp": target(offset)},
        )

    def add_vector(level):
        vector_copy(level).wait_recv()
        vectors[level + 1][...] = vectors[level][...] + vectors_taken[level][...]
        if level + 1 < bits:
            vector_copy(level + 1).start()
        else:
            vectors_all[me] = vectors[bits][...]
            for offset in peers:
                vector_last_copy(offset).start()

    def finish_vector():
        for offset in peers:
            vector_last_copy(offset).wait_recv()
        total = vectors_all[0]
        for index in peers:
            total = total + vectors_all[index]
        vector_sum[...] = total

    def bias_copy(level):
        return send(
            biases[level],
            biases_taken[level],
            (bias_send, bias_recv),
            level,
            {"dp": partner_of(dp_index, level)},
        )

    def add_bias(level):
        bias_copy(level).wait_recv()
        biases[level + 1][...] = biases[level][...] + biases_taken[level][...]
        if level + 1 < bits:
            bias_copy(level + 1).start()
        else:
            bias_sum[...] = biases[bits][...]


    def grads_copy(head, offset):
        return send(
            grads_out.at[target(offset), head],
            grads_in.at[head, me],
            (grads_send, grads_recv),
            (head, offset - 1),
            {"mp": target(offset)},
        )

    def grads_own_copy(head):
        return pltpu.make_async_copy(
            grads_out.at[me, head], grads_in.at[head, me], grads_own.at[head]
        )

    line = Line(mp_size, me)
    order = gather_orders(bits)[3]
    own_slot = place_in(dp_index, order)

    def weight_copy(side, hop):
        place = proj_all.at[line.place(side, hop), pl.ds(own_slot, 1)]
        source = proj_weight.at[pl.ds(own_slot, 1)] if hop == 0 else place
        return send(source, place, (weight_send, weight_recv), (side, hop), line.neighbour(side))

    def weight_trade_copy(level, side, hop):
        held = pl.ds(own_slot // 2**level * 2**level, 2**level)
        place = proj_all.at[line.place(side, hop + 1), held]
        partner = {"dp": partner_of(dp_index, order[level])}
        return send(place, place, (weight_trade_send, weight_trade_recv), (level, side, hop), partner)

    def take_weight(side, hop):
        weight_copy(side, hop).wait_recv()
        if hop + 1 < mp_size - 1:
            line.if_sent(side, hop + 1)(lambda: weight_copy(side, hop + 1).start())
        if bits:
            weight_trade_copy(0, side, hop).start()

    def trade_weight(level, side, hop):
        weight_trade_copy(level, side, hop).wait_recv()
        if level + 1 < bits:
            weight_trade_copy(level + 1, side, hop).start()

    def both_sides(act, *which):
        for side in (0, 1):
            line.if_taken(side, which[-1])(partial(act, *which[:-1], side, which[-1]))

    schedule = (
        (0, take_weight, 0),
        (1, take_weight, 1),
        (2, take_weight, 2),
        (2, trade_weight, 0, 0),
        (3, trade_weight, 0, 1),
        (3, trade_weight, 0, 2),
        (4, trade_weight, 1, 0),
        (6, trade_weight, 1, 1),
        (8, trade_weight, 1, 2),
    )
    done = set()

    def at_point(point, index=None):
        for at, act, *which in schedule:
            if which[-1] not in line.hops or (act is trade_weight and which[0] >= bits):
                continue
            if index is None and at == point:
                both_sides(act, *which)
                done.add((act, *which))
            if index is not None and point <= at < point + mp_size:
                pl.when(index == at - point)(partial(both_sides, act, *which))
                done.add((act, *which))

    def dense_phase(
        frames_buf,
        heads_buf,
        cotangent_buf,
        in_buf,
        down_buf,
        out_buf,
        hidden,
        slope,
        mid_buf,
        normed_buf,
        store_buf,
        low_buf,
        grad_buf,
        given,
        head_buf,
    ):
        loads = [
            pltpu.make_async_copy(source, into, load_sems.at[at])
            for at, (source, into) in enumerate(
                ((frames, frames_buf), (heads_low, heads_buf), (out_grad, cotangent_buf))
            )
        ]
        out_copies = [
            pltpu.make_async_copy(
                out_all.at[index],
                out_buf.at[pl.ds(index * head_cols, head_cols)],
                out_sems.at[index],
            )
            for index in range(mp_size)
        ]

        def in_copy(index):
            return pltpu.make_async_copy(in_all.at[index], in_buf.at[index], in_sems.at[index])

        def down_copy(index):
            return pltpu.make_async_copy(
                down_all.at[index], down_buf.at[index], down_sems.at[index]
            )

        def given_copy(which, turn):
            return pltpu.make_async_copy(
                given.at[turn % 2], partials[which].at[part_of(turn)], given_sems.at[turn % 2]
            )

        def store_copy(at):
            return pltpu.make_async_copy(
                store_buf, (block_out, resid_grad)[at], store_sems.at[at]
            )

        for copy in loads + out_copies:
            copy.start()
        for index in range(mp_size):
            in_copy(index).start()
            down_copy(index).start()
        enter(dp_index, me, mp_size, bits)
        for side in (0, 1):
            line.if_sent(side, 0)(lambda side=side: weight_copy(side, 0).start())
        weight_own_copy.start()
        vector[...] = jnp.zeros_like(vector)
        gains = norm_gain[...].astype(F32)
        shifts = norm_shift[...].astype(F32)
        both = [slice(side * half, (side + 1) * half) for side in range(2)]

        for copy in loads + out_copies:
            copy.wait()
        branch = dot(heads_buf[...], out_buf[...]) + out_bias[...].astype(F32)
        mid, normed, inv_mid = norm_rows(
            frames_buf[...].astype(F32) + branch, gains[:1], shifts[:1]
        )
        mid_buf[...] = mid + down_bias[...].astype(F32)
        normed_buf[...] = normed
        low_buf[...] = mid.astype(BF16)
        at_point(0)

        def feed(index, _):
            in_copy(index).wait()
            down_copy(index).wait()
            for rows in both:
                pre_act = dot(low_buf[rows], in_buf[index]) + in_bias[index, 0:1].astype(F32)
                unit_cdf = 0.5 * (1.0 + lax.erf(pre_act * 0.5**0.5))
                bell = jnp.exp(-0.5 * pre_act * pre_act) * (2.0 * jnp.pi) ** (-0.5)
                slope[index, rows] = (unit_cdf + pre_act * bell).astype(BF16)
                hidden[index, rows] = (pre_act * unit_cdf).astype(BF16)
                mid_buf[rows] += dot(hidden[index, rows], down_buf[index])
            at_point(1, index)
            return 0

        lax.fori_loop(0, mp_size, feed, 0)
        output, normed, inv_out = norm_rows(mid_buf[...], gains[1:], shifts[1:])
        store_buf[...] = output
        store_copy(0).start()

        cotangent = cotangent_buf[...].astype(F32)
        vector[1:2] = sum_rows(cotangent * normed)
        vector[3:4] = sum_rows(cotangent)
        sum_grad = norm_back(cotangent, normed, inv_out, gains[1:])
        mid_buf[...] = sum_grad
        grad_buf[...] = sum_grad.astype(BF16)
        vector[5:6] = sum_rows(grad_buf[...])

        def give(which, turn, result):
            if turn >= 2:
                offer_given(which, turn - 2)
            share = result.shape[0] // slots
            for slot in range(slots):
                given[turn % 2, slot] = result[slot * share : (slot + 1) * share].astype(BF16)
            given_copy(which, turn).start()

        def offer_given(which, turn):
            given_copy(which, turn).wait()
            offer(which, turn)

        for turn in turns:
            index = part_of(turn)
            give(1, turn, dot_cols(hidden[index], grad_buf[...]))
            pre = dot_rows(grad_buf[...], down_buf[index]) * slope[index].astype(F32)
            hidden[index] = pre.astype(BF16)
            vector[pl.ds(8 + index, 1)] = sum_rows(hidden[index])
            mid_buf[...] += dot_rows(hidden[index], in_buf[index])
            at_point(1 + mp_size + turn)
        for turn in turns[-2:]:
            offer_given(1, turn)
        mid_grad = mid_buf[...]
        vector[0:1] = sum_rows(mid_grad * normed_buf[...])
        vector[2:3] = sum_rows(mid_grad)
        resid = norm_back(mid_grad, normed_buf[...], inv_mid, gains[:1])
        store_copy(0).wait()
        store_buf[...] = resid
        store_copy(1).start()
        attn_grad = resid.astype(BF16)
        grad_buf[...] = attn_grad
        vector[4:5] = sum_rows(attn_grad)
        heads_grad = dot_rows(attn_grad, out_buf[...]).astype(BF16)
        for head in range(head_total):
            for index in range(mp_size):
                at = index * head_cols + head * HEAD_DIM
                for side in range(2):
                    grads_out[index, head, :, side * HEAD_DIM : (side + 1) * HEAD_DIM] = (
                        heads_grad[both[side], at : at + HEAD_DIM]
                    )
            if head == 0:
                for offset in peers:
                    grads_copy(0, offset).start()
        for head in range(head_total):
            grads_own_copy(head).start()
        vector_copy(0).start()

        products = dot_cols(heads_buf[...], grad_buf[...]).astype(BF16)
        rows = head_cols // slots
        for index in range(mp_size):
            for slot in range(slots):
                start = index * head_cols + slot * rows
                head_buf[index, slot, :rows] = products[start : start + rows]
                if rows < head_buf.shape[2]:
                    head_buf[index, slot, rows:] = jnp.zeros(
                        (head_buf.shape[2] - rows, width), BF16
                    )
        head_copy = pltpu.make_async_copy(head_buf, head_grads, head_sem)
        head_copy.start()
        normed_low = low_buf[...].T
        for turn in turns:
            give(0, turn, dot(normed_low, hidden[part_of(turn)]))
            if turn == 0:
                head_copy.wait()
                for at in turns:
                    offer(2, at)
                for later in range(1, head_total):
                    for offset in peers:
                        grads_copy(later, offset).start()
        for turn in turns[-2:]:
            offer_given(0, turn)
        store_copy(1).wait()

    weight_own_copy = pltpu.make_async_copy(proj_weight, proj_all.at[me], weight_own)
    rows_low = pltpu.VMEM((2 * half, width), BF16)
    rows_full = pltpu.VMEM((2 * half, width), F32)
    pl.run_scoped(
        dense_phase,
        rows_low,
        rows_low,
        rows_low,
        pltpu.VMEM((mp_size, width, units), BF16),
        pltpu.VMEM((mp_size, units, width), BF16),
        pltpu.VMEM((width, width), BF16),
        pltpu.VMEM((mp_size, 2 * half, units), BF16),
        pltpu.VMEM((mp_size, 2 * half, units), BF16),
        rows_full,
        rows_full,
        rows_full,
        rows_low,
        rows_low,
        pltpu.VMEM((2, slots, units // slots, width), BF16),
        pltpu.VMEM(head_grads.shape, BF16),
    )

    def attention_phase(
        qkv,
        out_cols,
        log_total,
        seg_col,
        input_all,
        staged,
        qkv_grad,
        seg_blocks,
        grads,
        key_buf,
        key_cols,
        value_buf,
        query_sum,
        key_sum,
        value_sum,
        proj_rows,
    ):
        def traded_copy(head, offset):
            return send(
                staged.at[head, target(offset)],
                traded.at[head, me],
                (traded_send, traded_recv),
                (head, offset - 1),
                {"mp": target(offset)},
            )

        def traded_own_copy(head):
            return pltpu.make_async_copy(
                staged.at[head, me], traded.at[head, me], traded_own.at[head]
            )

        def prepare(head):
            cols = slice(head * HEAD_DIM, (head + 1) * HEAD_DIM)
            key_buf[:, :HEAD_DIM] = qkv[1, :, cols]
            key_buf[:, HEAD_DIM:] = ones_columns(ROW_LEN)
            value_buf[:, :HEAD_DIM] = qkv[2, :, cols]
            value_buf[:, HEAD_DIM:] = ones_columns(ROW_LEN)
            for step in range(BLOCKS):
                key_cols[step] = qkv[1, step * BLOCK : (step + 1) * BLOCK, cols].T
            key_sum[...] = jnp.zeros_like(key_sum)
            value_sum[...] = jnp.zeros_like(value_sum)

        def take_grads(head):
            grads_own_copy(head).wait()
            for offset in peers:
                grads_copy(head, offset).wait_recv()
            for chunk in range(mp_size):
                for side in range(2):
                    start = (2 * chunk + side) * half
                    grads[start : start + half] = grads_in[
                        head, chunk, :, side * HEAD_DIM : (side + 1) * HEAD_DIM
                    ]

        def attend_back(head):
            cols = slice(head * HEAD_DIM, (head + 1) * HEAD_DIM)

            def query_block(number, _):
                rows = block_rows(number)
                queries = qkv[0, rows, cols] * SCALE
                grad_rows = grads[rows]
                seg_query = seg_blocks[number]
                grad_cols = grad_rows.astype(F32).T
                row_dot = jnp.sum(grad_cols * out_cols[head, number], axis=0, keepdims=True)
                grad_cols = jnp.concatenate([grad_cols.astype(BF16), as_pieces(-row_dot)], axis=0)
                query_cols = jnp.concatenate(
                    [queries.astype(F32).T.astype(BF16), as_pieces(-log_total[head, number])], axis=0
                )

                def products_of(step):
                    key_rows = slice(step * BLOCK, (step + 1) * BLOCK)
                    same = (
                        jnp.concatenate([seg_col[key_rows]] * (BLOCK // 128), axis=1) == seg_query
                    )
                    scores = jnp.where(same, dot(key_buf[key_rows], query_cols), MASKED)
                    return scores, dot(value_buf[key_rows], grad_cols)

                query_grad = jnp.zeros((HEAD_DIM, BLOCK), F32)
                ahead = products_of(0)
                for step in range(BLOCKS):
                    scores, soft_grad = ahead
                    if step + 1 < BLOCKS:
                        ahead = products_of(step + 1)
                    key_rows = slice(step * BLOCK, (step + 1) * BLOCK)
                    soft = jnp.exp(scores)
                    score_grad = (soft * soft_grad).astype(BF16)
                    value_sum[key_rows] += dot(soft.astype(BF16), grad_rows)
                    key_sum[key_rows] += dot(score_grad, queries)
                    query_grad = query_grad + dot(key_cols[step], score_grad)
                query_sum[rows] = (query_grad * SCALE).T
                for at in range(head * BLOCKS, (head + 1) * BLOCKS):
                    if at in events:

                        @pl.when(number == at - head * BLOCKS)
                        def _():
                            for act in events[at]:
                                act()

                return 0

            lax.fori_loop(0, BLOCKS, query_block, 0)

        def give_grads(head):
            for part, total in enumerate((query_sum, key_sum, value_sum)):
                low = total[...].astype(BF16)
                qkv_grad[:, part * HEAD_DIM : (part + 1) * HEAD_DIM] = low
                if part != 1:
                    cols = slice(head * HEAD_DIM, (head + 1) * HEAD_DIM)
                    sum_low = jnp.sum(low.astype(F32), axis=0, keepdims=True)
                    biases[0][part : part + 1, cols] = sum_low
                for chunk in range(mp_size):
                    for side in range(2):
                        start = (2 * chunk + side) * half
                        staged[head, chunk, part, :, side * HEAD_DIM : (side + 1) * HEAD_DIM] = total[
                            start : start + half
                        ].astype(BF16)

        def start_trade(head):
            for offset in peers:
                traded_copy(head, offset).start()
            traded_own_copy(head).start()

        def start_proj(head):
            products = dot_cols(qkv_grad[...], input_all[...])
            slot_rows = proj[head].shape[1]
            for slot in range(2**bits):
                proj[head][slot] = products[slot * slot_rows : (slot + 1) * slot_rows].astype(BF16)
            proj_copy(head, 0).start()

        def finish_proj(head):
            cols = slice(head * HEAD_DIM, (head + 1) * HEAD_DIM)
            slot_rows = proj_slots[head].shape[1]
            for slot in range(2**bits):
                proj_rows[slot * slot_rows : (slot + 1) * slot_rows] = proj_slots[head][slot].astype(F32)
            for part in range(3):
                rows = proj_rows[part * HEAD_DIM : (part + 1) * HEAD_DIM]
                proj_sum[part, cols] = rows.astype(BF16)

        events = {}
        rest = []

        def due(at, act, *which):
            if at is None:
                rest.append((act, *which))
            else:
                events.setdefault(at, []).append(partial(act, *which))

        for at, level in zip((0, 1, 2), levels):
            due(at, add_vector, level)
        due(3, finish_vector)
        times = {
            1: ((0, 0, 0, 0), (2, 3, 3, 4), (3, 4, 4, 5)),
            2: ((1, 1, 1, 1), (3, 3, 3, 3), (4, 4, 4, 4)),
            0: ((2, 3, 3, 5), (3, 5, 6, 6), (4, 6, 7, 8)),
        }
        ends = {1: (7, 8, None, None), 2: (7, 8, None, None), 0: (None, None, None, None)}
        for level in levels:
            for which in times:
                for turn, at in zip(turns, times[which][level]):
                    due(at, add_level, which, level, turn)
        for at, level in zip((3, 4, 5), levels):
            due(at, add_proj, 0, level)
        for at, level in zip((6, 7, 8), levels):
            due(at, add_proj, 1, level)
        for at, level in zip((6, 7, 8), levels[::-1]):
            due(at, spread_proj, 0, level)
        for which in (1, 2, 0):
            due(ends[which][0], finish_sum, which)
        for step, level in enumerate(levels[::-1]):
            for which in (1, 2, 0):
                due(ends[which][1 + step], spread, which, level)

        copies = [
            pltpu.make_async_copy(source, into, attention_sems.at[at])
            for at, (source, into) in enumerate(
                (
                    (qkv_source, qkv),
                    (seg_source, seg_col),
                    (log_source, log_total),
                    (out_source, out_cols),
                    (input_source, input_all),
                )
            )
        ]
        for copy in copies:
            copy.start()
        biases[0][...] = jnp.zeros_like(biases[0])
        for step in range(BLOCKS):
            seg_blocks[step] = seg_row[:, step * BLOCK : (step + 1) * BLOCK]
        final = head_total - 1
        copies[0].wait()
        for head in range(head_total):
            prepare(head)
            take_grads(head)
            if head == 0:
                for copy in copies[1:4]:
                    copy.wait()
            attend_back(head)
            give_grads(head)
            start_trade(head)
            if head == 0:
                copies[4].wait()
            start_proj(head)
        bias_copy(0).start()
        for level in levels:
            add_proj(final, level)
            add_bias(level)
            spread_proj(final - 1, bits - 1 - level)
        for act, *which in rest:
            act(*which)
        for level in levels[::-1]:
            spread_proj(final, level)
        for head in range(head_total):
            finish_proj(head)
            traded_own_copy(head).wait()
            for offset in peers:
                traded_copy(head, offset).wait()

    pl.run_scoped(
        attention_phase,
        pltpu.VMEM(qkv_source.shape, BF16),
        pltpu.VMEM(out_source.shape, F32),
        pltpu.VMEM(log_source.shape, F32),
        pltpu.VMEM(seg_source.shape, jnp.int32),
        pltpu.VMEM(input_source.shape, BF16),
        pltpu.VMEM((head_total, mp_size, 3, half, 2 * HEAD_DIM), BF16),
        pltpu.VMEM((ROW_LEN, 3 * HEAD_DIM), BF16),
        pltpu.VMEM((BLOCKS, 1, BLOCK), jnp.int32),
        pltpu.VMEM((ROW_LEN, HEAD_DIM), BF16),
        pltpu.VMEM((ROW_LEN, HEAD_DIM + EXTRA), BF16),
        pltpu.VMEM((BLOCKS, HEAD_DIM, BLOCK), BF16),
        pltpu.VMEM((ROW_LEN, HEAD_DIM + EXTRA), BF16),
        pltpu.VMEM((ROW_LEN, HEAD_DIM), F32),
        pltpu.VMEM((ROW_LEN, HEAD_DIM), F32),
        pltpu.VMEM((ROW_LEN, HEAD_DIM), F32),
        pltpu.VMEM((3 * HEAD_DIM, width), F32),
    )

    for hop in line.hops:
        if (take_weight, hop) not in done:
            both_sides(take_weight, hop)
    for level in levels:
        for hop in line.hops:
            if (trade_weight, level, hop) not in done:
                both_sides(trade_weight, level, hop)

    def sent_trades(side, hop):
        for level in levels:
            weight_trade_copy(level, side, hop).wait_send()

    for side, hop in line.ways:
        line.if_sent(side, hop)(lambda side=side, hop=hop: weight_copy(side, hop).wait_send())
        line.if_taken(side, hop)(partial(sent_trades, side, hop))
    weight_own_copy.wait()
    for head in range(head_total):
        for offset in peers:
            grads_copy(head, offset).wait_send()
        for level in levels:
            proj_copy(head, level).wait_send()
            proj_spread_copy(head, level).wait_send()
    for level in levels:
        vector_copy(level).wait_send()
        bias_copy(level).wait_send()
        for which in arrays:
            spread_copy(which, level).wait_send()
            for turn in turns:
                level_copy(which, level, turn).wait_send()
    for offset in peers:
        vector_last_copy(offset).wait_send()
        for which in arrays:
            last_copy(which, offset).wait_send()


def rear(frames, heads_low, out_grad, seg_row, in_bias, small, weights, proj_weight, saved, bits):
    local_rows, width = frames.shape
    qkv_low, out_cols = saved[:2]
    mp_size, units = weights[1].shape[:2]
    head_total = out_cols.shape[0]
    half, lanes = local_rows // 2, 2 * HEAD_DIM
    peers = mp_size - 1
    slots = 2**bits
    head_rows = -(-width // mp_size // slots // 16) * 16
    anywhere = pl.BlockSpec(memory_space=pl.ANY)
    blocks = [(width // slots, units), (units // slots, width), (head_rows, width)]
    proj_block = (3 * HEAD_DIM // slots, width)
    bias_block = (8, 2 * 128)
    vector_block = (8 + -(-mp_size // 8) * 8, width)

    def halves(shape, lead=()):
        return [pltpu.VMEM(lead + (slots >> (level + 1),) + shape, BF16) for level in range(bits)]

    def sems(*shapes):
        return [pltpu.SemaphoreType.DMA(shape) for shape in shapes for _ in range(2)]

    piece = pltpu.VMEM((mp_size, head_total, half, lanes), BF16)
    return pl.pallas_call(
        partial(rear_kernel, bits),
        out_shape=(
            jax.ShapeDtypeStruct((local_rows, width), F32),
            jax.ShapeDtypeStruct((local_rows, width), F32),
            *(jax.ShapeDtypeStruct((mp_size, slots) + block, BF16) for block in blocks),
            jax.ShapeDtypeStruct((mp_size,) + proj_weight.shape, BF16),
            jax.ShapeDtypeStruct((head_total, mp_size, 3, half, lanes), BF16),
            *(jax.ShapeDtypeStruct((slots,) + block, BF16) for block in blocks),
            jax.ShapeDtypeStruct((3, head_total * HEAD_DIM, width), BF16),
            jax.ShapeDtypeStruct(vector_block, F32),
            jax.ShapeDtypeStruct(bias_block, F32),
        ),
        in_specs=[whole()] * 6 + [anywhere] * 12,
        out_specs=(anywhere,) * 7 + (whole(),) * 6,
        scratch_shapes=[
            piece,
            pltpu.VMEM((head_total, mp_size, half, lanes), BF16),
            [pltpu.VMEM((2, slots // 2) + block, BF16) for block in blocks],
            [halves(block, (mp_size,)) for block in blocks],
            [pltpu.VMEM((peers, 1) + block, BF16) for block in blocks],
            [pltpu.VMEM((slots,) + proj_block, BF16) for _ in range(head_total)],
            [halves(proj_block) for _ in range(head_total)],
            [pltpu.VMEM((slots,) + proj_block, BF16) for _ in range(head_total)],
            [pltpu.VMEM(vector_block, F32) for _ in range(bits + 1)],
            [pltpu.VMEM(vector_block, F32) for _ in range(bits)],
            pltpu.VMEM((mp_size,) + vector_block, F32),
            [pltpu.VMEM(bias_block, F32) for _ in range(bits + 1)],
            [pltpu.VMEM(bias_block, F32) for _ in range(bits)],
            pltpu.SemaphoreType.DMA((3,)),
            pltpu.SemaphoreType.DMA((mp_size,)),
            pltpu.SemaphoreType.DMA((mp_size,)),
            pltpu.SemaphoreType.DMA((mp_size,)),
            pltpu.SemaphoreType.DMA((2,)),
            pltpu.SemaphoreType.DMA,
            pltpu.SemaphoreType.DMA((2,)),
            pltpu.SemaphoreType.DMA((5,)),
            pltpu.SemaphoreType.DMA,
            *sems((2, peers), (max(bits, 1), 2, peers)),
            pltpu.SemaphoreType.DMA((3, 2)),
            pltpu.SemaphoreType.DMA((head_total,)),
            *sems((head_total, peers)),
            pltpu.SemaphoreType.DMA((head_total,)),
            *sems(
                (head_total, peers),
                (3, bits, mp_size),
                (3, peers),
                (3, bits),
                (2, head_total, bits),
                (bits,),
                (peers,),
                (bits,),
            ),
        ],
        compiler_params=pltpu.CompilerParams(
            collective_id=1, has_side_effects=True, vmem_limit_bytes=REAR_VMEM_BYTES
        ),
        cost_estimate=pl.CostEstimate(
            flops=40 * head_total * ROW_LEN * ROW_LEN * HEAD_DIM,
            bytes_accessed=96 * 1024 * 1024,
            transcendentals=head_total * ROW_LEN * ROW_LEN,
        ),
        name="rear",
    )(seg_row, in_bias, *small, frames, heads_low, out_grad, *weights, proj_weight, *saved)


def finish_kernel(
    traded,
    proj_all,
    resid_grad,
    in_sum,
    down_sum,
    head_sum,
    proj_sum,
    vector_sum,
    bias_sum,
    stream_grad,
    in_grad,
    down_grad,
    out_grad,
    proj_grad,
    query_bias_grad,
    value_bias_grad,
    out_bias_grad,
    in_bias_grad,
    down_bias_grad,
    gain_grad,
    shift_grad,
    columns,
    weight_buf,
    sems,
):
    head_total, mp_size = traded.shape[:2]
    half = traded.shape[3]
    head_cols = head_total * HEAD_DIM
    copies = [
        pltpu.make_async_copy(
            proj_all.at[index],
            weight_buf.at[index],
            sems.at[index],
        )
        for index in range(mp_size)
    ]
    for copy in copies:
        copy.start()
    for sums, grad in ((in_sum, in_grad), (down_sum, down_grad), (head_sum, out_grad)):
        rows = grad.shape[0] // sums.shape[0]
        for slot in range(sums.shape[0]):
            grad[slot * rows : (slot + 1) * rows] = sums[slot, :rows].astype(F32)
    proj_grad[...] = proj_sum[...].astype(F32)
    query_bias_grad[...] = bias_sum[0:1, :head_cols]
    value_bias_grad[...] = bias_sum[2:3, :head_cols]
    gain_grad[...] = vector_sum[0:2]
    shift_grad[...] = vector_sum[2:4]
    out_bias_grad[...] = vector_sum[4:5]
    down_bias_grad[...] = vector_sum[5:6]
    in_bias_grad[...] = vector_sum[pl.ds(8 + lax.axis_index("mp"), 1)]
    stream_grad[...] = resid_grad[...]
    for index in range(mp_size):
        for head in range(head_total):
            for part in range(3):
                at = part * head_cols + head * HEAD_DIM
                for side in range(2):
                    columns[side * half : (side + 1) * half, at : at + HEAD_DIM] = traded[
                        head, index, part, :, side * HEAD_DIM : (side + 1) * HEAD_DIM
                    ]
        copies[index].wait()
        stream_grad[...] += dot(columns[...], weight_buf[index])


def finish(traded, proj_all, resid_grad, sums):
    head_total, mp_size = traded.shape[:2]
    head_cols = head_total * HEAD_DIM
    local_rows, width = resid_grad.shape
    units = sums[0].shape[0] * sums[0].shape[1]
    row = jax.ShapeDtypeStruct((1, width), F32)
    head_row = jax.ShapeDtypeStruct((1, head_cols), F32)
    anywhere = pl.BlockSpec(memory_space=pl.ANY)
    return pl.pallas_call(
        finish_kernel,
        out_shape=(
            jax.ShapeDtypeStruct((local_rows, width), F32),
            jax.ShapeDtypeStruct((units, width), F32),
            jax.ShapeDtypeStruct((units, width), F32),
            jax.ShapeDtypeStruct((head_cols, width), F32),
            jax.ShapeDtypeStruct((3, head_cols, width), F32),
            head_row,
            head_row,
            row,
            jax.ShapeDtypeStruct((1, units), F32),
            row,
            jax.ShapeDtypeStruct((2, width), F32),
            jax.ShapeDtypeStruct((2, width), F32),
        ),
        in_specs=[whole(), anywhere] + [whole()] * 7,
        out_specs=(whole(),) * 12,
        scratch_shapes=[
            pltpu.VMEM((local_rows, 3 * head_cols), BF16),
            pltpu.VMEM((mp_size, 3 * head_cols, width), BF16),
            pltpu.SemaphoreType.DMA((mp_size,)),
        ],
        compiler_params=pltpu.CompilerParams(vmem_limit_bytes=VMEM_BYTES),
        cost_estimate=pl.CostEstimate(
            flops=6 * local_rows * width * width, bytes_accessed=24 * 1024 * 1024, transcendentals=0
        ),
        name="finish",
    )(traded, proj_all, resid_grad, *sums)


def dp_groups():
    total = lax.axis_size("dp")
    size = min(8, total)
    groups = [list(range(start, start + size)) for start in range(0, total, size)]
    return (size, groups)


def on_device(
    frames,
    segment_ids,
    qkv_weight,
    q_bias,
    v_bias,
    out_weight,
    out_bias,
    ff_in_weight,
    ff_in_bias,
    ff_out_weight,
    ff_out_bias,
    norm_gain,
    norm_shift,
    out_grad,
):
    local_rows, width = frames.shape
    mp_size = lax.axis_size("mp")
    group, groups = dp_groups()
    bits = group_bits(lax.axis_size("dp"))
    slots = 2**bits

    proj_weight = qkv_weight[0].transpose(0, 2, 1)
    seg_row = segment_ids.reshape(1, ROW_LEN)
    (
        input_all,
        qkv_low,
        in_all,
        down_all,
        out_all,
        in_bias_all,
        seg_col,
        out_cols,
        log_total,
        heads_low,
    ) = front(
        frames,
        proj_weight,
        q_bias,
        v_bias,
        seg_row,
        (ff_in_weight[0], ff_out_weight[0], out_weight[0]),
        ff_in_bias,
        mp_size,
        bits,
    )
    block_out, resid_grad, _, _, _, proj_all, traded, *summed = rear(
        frames,
        heads_low,
        out_grad,
        seg_row,
        in_bias_all,
        (out_bias, ff_out_bias, norm_gain[0], norm_shift[0]),
        (in_all, down_all, out_all),
        proj_weight.reshape(slots, -1, width),
        (qkv_low, out_cols, log_total, seg_col, input_all),
        bits,
    )
    if len(groups) > 1:
        across = [list(range(at, lax.axis_size("dp"), group)) for at in range(group)]
        summed = lax.psum(summed, "dp", axis_index_groups=across)
    (
        stream_grad,
        in_weight_grad,
        down_weight_grad,
        out_weight_grad,
        proj_grad,
        query_bias_grad,
        value_bias_grad,
        head_bias_grad,
        in_bias_grad,
        down_bias_grad,
        gain_grad,
        shift_grad,
    ) = finish(traded, proj_all.reshape(mp_size, -1, width), resid_grad, summed)
    return (
        block_out,
        stream_grad,
        proj_grad.transpose(0, 2, 1)[None],
        query_bias_grad,
        value_bias_grad,
        out_weight_grad[None],
        head_bias_grad,
        in_weight_grad[None],
        in_bias_grad,
        down_weight_grad[None],
        down_bias_grad,
        gain_grad[None],
        shift_grad[None],
    )


def solution(mesh):
    return jax.shard_map(
        on_device,
        mesh=mesh,
        in_specs=(
            P(("dp", "mp"), None),
            P("dp"),
            P(None, None, None, "mp"),
            P(None, "mp"),
            P(None, "mp"),
            P(None, "mp", None),
            P(),
            P(None, None, "mp"),
            P(None, "mp"),
            P(None, "mp", None),
            P(),
            P(),
            P(),
            P(("dp", "mp"), None),
        ),
        out_specs=(
            P(("dp", "mp"), None),
            P(("dp", "mp"), None),
            P(None, None, None, "mp"),
            P(None, "mp"),
            P(None, "mp"),
            P(None, "mp", None),
            P(),
            P(None, None, "mp"),
            P(None, "mp"),
            P(None, "mp", None),
            P(),
            P(),
            P(),
        ),
        check_vma=False,
    )
```
